32 devices in a mesh: row: 2 (over x), col: 16 (over z, y, core).
Axes of the slice: x: 2, y: 2, z: 4, core: 2. Of those that a mesh axis runs over, the one named last changes fastest.
Arguments:
- image: bfloat16 [32, 1024, 96], P('row', 'col'), may hold values from -6 to 6
- kernels: float32 [2, 7, 7, 96], replicated, may hold values from -0.875 to 0.875
- gains: float32 [2, 96], replicated, may hold values from 0.5 to 1.5
- up_weights: bfloat16 [2, 96, 384], replicated, may hold values from -0.625 to 0.625
- down_weights: bfloat16 [2, 384, 96], replicated, may hold values from -0.3125 to 0.3125
- cotangent: bfloat16 [32, 1024, 96], P('row', 'col'), may hold values from -6 to 6
Outputs:
- output: bfloat16 [32, 1024, 96], P('row', 'col')
- grad_image: bfloat16 [32, 1024, 96], P('row', 'col')
- grad_kernels: float32 [2, 7, 7, 96], replicated
- grad_gains: float32 [2, 96], replicated
- grad_up: float32 [2, 96, 384], P(None, 'row', 'col')
- grad_down: float32 [2, 384, 96], P(None, 'col', 'row')
The draws below stay inside these ranges and needn't reach their ends.
All inputs are finite; a program needn't handle non-finite values.
Results may differ from the reference program's by a relative error of at most 0.029.
Values may be sent and summed in bfloat16 or wider, within the bound.
No kernel may reach another device: no remote copies, remote signals or barrier semaphores. Data moves between devices by JAX's collectives and lax.ppermute only.
A program may use at most 64 MiB of HBM per device.

```python
import math
import jax
import jax.numpy as jnp
from jax import lax

C = 96
FF = 384
KERNEL = 7
LAYERS = 2
ROWS_DEV = 16
NH = 32
NW = 1024


def level_of(stream_key, extent, pieces, low, high):
    level = 1.0
    for position, parts in pieces:
        heights = jax.random.uniform(jax.random.fold_in(jax.random.fold_in(stream_key, 6), position), (parts,), jnp.float32, low / len(pieces), high / len(pieces))
        level = level * jnp.repeat(jnp.exp(heights), extent[position] // parts).reshape((-1,) + (1,) * (len(extent) - 1 - position))
    return level


def normal_values(key, shape, deviation, bound, pieces=(), kind=jnp.bfloat16):
    values = deviation * jax.random.normal(key, shape, jnp.float32)
    if pieces:
        values = values * level_of(key, shape, pieces, -0.22, 0.18)
    return jnp.clip(values, -bound, bound).astype(kind)


def setup_inputs(seed: int = 0) -> dict:
    splits = jax.random.split(jax.random.key(seed), 7)
    return {
        "image": normal_values(splits[0], (NH, NW, C), 1.0, 6.0, ((0, 2), (1, 16))),
        "kernels": normal_values(splits[1], (LAYERS, KERNEL, KERNEL, C), (KERNEL * KERNEL) ** -0.5, 0.875, (), jnp.float32),
        "gains": jnp.clip(jax.random.uniform(splits[2], (LAYERS, C), jnp.float32, 0.5, 1.5), 0.5, 1.5),
        "up_weights": normal_values(splits[3], (LAYERS, C, FF), C ** -0.5, 0.625),
        "down_weights": normal_values(splits[4], (LAYERS, FF, C), FF ** -0.5, 0.3125),
        "cotangent": normal_values(splits[5], (NH, NW, C), 1.0, 6.0, ((0, 2), (1, 16))),
    }


epsilon = 1e-06
inv_sqrt_two = 0.7071067811865476
inv_sqrt_two_pi = 0.3989422804014327

def depthwise(padded, kernel, tile_rows, tile_cols):
    padded_f = padded.astype(jnp.float32)
    tap_count = kernel.shape[0]
    accumulated = jnp.zeros((tile_rows, tile_cols, padded.shape[2]), jnp.float32)
    for tap_row in range(tap_count):
        for tap_col in range(tap_count):
            accumulated = accumulated + padded_f[tap_row:tap_row + tile_rows, tap_col:tap_col + tile_cols] * kernel[tap_row, tap_col]
    return accumulated

def flipped_conv(padded, kernel, tile_rows, tile_cols):
    padded_f = padded.astype(jnp.float32)
    tap_count = kernel.shape[0]
    last_tap = tap_count - 1
    accumulated = jnp.zeros((tile_rows, tile_cols, padded.shape[2]), jnp.float32)
    for tap_row in range(tap_count):
        for tap_col in range(tap_count):
            start_row = last_tap - tap_row
            start_col = last_tap - tap_col
            accumulated = accumulated + padded_f[start_row:start_row + tile_rows, start_col:start_col + tile_cols] * kernel[tap_row, tap_col]
    return accumulated

def kernel_grad(padded, conv_grad, tile_rows, tile_cols, tap_count):
    padded_f = padded.astype(jnp.float32)
    grad_f = conv_grad.astype(jnp.float32)
    rows_out = []
    for tap_row in range(tap_count):
        entries = []
        for tap_col in range(tap_count):
            entries.append(lax.optimization_barrier(jnp.sum(padded_f[tap_row:tap_row + tile_rows, tap_col:tap_col + tile_cols] * grad_f, axis=(0, 1))))
        rows_out.append(jnp.stack(entries))
    return jnp.stack(rows_out)

def normalize(conv_out):
    centred = conv_out - lax.optimization_barrier(jnp.mean(conv_out, axis=-1, keepdims=True))
    variance = lax.optimization_barrier(jnp.mean(centred * centred, axis=-1, keepdims=True))
    inverse_std = lax.rsqrt(variance + epsilon)
    return (centred * inverse_std, inverse_std)

def gelu_parts(pre):
    normal_cdf = 0.5 * (1.0 + lax.erf(pre * inv_sqrt_two))
    density = jnp.exp(-0.5 * pre * pre) * inv_sqrt_two_pi
    return (pre * normal_cdf, normal_cdf + pre * density)

def mixing(padded, kernel, gain, up_weight, tile_rows, tile_cols):
    conv_out = depthwise(padded, kernel, tile_rows, tile_cols)
    unit_vals, inverse_std = normalize(conv_out)
    normed = (unit_vals * gain).astype(jnp.bfloat16).reshape(tile_rows * tile_cols, -1)
    pre = jnp.dot(normed, up_weight, preferred_element_type=jnp.float32)
    gelu_value, gelu_slope = gelu_parts(pre)
    return (unit_vals, inverse_std, normed, gelu_value.astype(jnp.bfloat16), gelu_slope)

def forward_rows(padded, kernel, gain, up_weight, down_weight, tile_rows, tile_cols):
    unit_vals, inverse_std, normed, hidden, gelu_slope = mixing(padded, kernel, gain, up_weight, tile_rows, tile_cols)
    halo_width = kernel.shape[0] // 2
    residual = padded[halo_width:halo_width + tile_rows, halo_width:halo_width + tile_cols].astype(jnp.float32)
    branch = jnp.dot(hidden, down_weight, preferred_element_type=jnp.float32).reshape(residual.shape)
    return (residual + branch).astype(jnp.bfloat16)

def backward_rows(padded, upstream, kernel, gain, up_weight, down_weight, tile_rows, tile_cols):
    unit_vals, inverse_std, normed, hidden, gelu_slope = mixing(padded, kernel, gain, up_weight, tile_rows, tile_cols)
    channels = upstream.shape[2]
    flat_grad = upstream.reshape(tile_rows * tile_cols, channels)
    down_term = jnp.dot(hidden.T, flat_grad, preferred_element_type=jnp.float32)
    hidden_grad = jnp.dot(flat_grad, down_weight.T, preferred_element_type=jnp.float32)
    pre_grad = (hidden_grad * gelu_slope).astype(jnp.bfloat16)
    up_term = jnp.dot(normed.T, pre_grad, preferred_element_type=jnp.float32)
    normed_grad = jnp.dot(pre_grad, up_weight.T, preferred_element_type=jnp.float32).reshape(tile_rows, tile_cols, channels)
    gain_term = lax.optimization_barrier(jnp.sum(normed_grad * unit_vals, axis=(0, 1)))
    unit_grad = normed_grad * gain
    conv_grad = inverse_std * (unit_grad - lax.optimization_barrier(jnp.mean(unit_grad, axis=-1, keepdims=True)) - unit_vals * lax.optimization_barrier(jnp.mean(unit_grad * unit_vals, axis=-1, keepdims=True)))
    conv_grad = conv_grad.astype(jnp.bfloat16)
    kernel_term = kernel_grad(padded, conv_grad, tile_rows, tile_cols, kernel.shape[0])
    return (conv_grad, kernel_term, gain_term, up_term, down_term)

def reference(image, kernels, gains, up_weights, down_weights, cotangent):
    halo_width = KERNEL // 2
    block_count = NH // ROWS_DEV
    block_ids = jnp.arange(block_count, dtype=jnp.int32)
    factor = 1.0 / math.sqrt(NH * NW)
    padding = ((halo_width, halo_width), (halo_width, halo_width), (0, 0))
    current = image
    stored = []
    for layer_index in range(LAYERS):
        padded = jnp.pad(current, padding)
        stored.append(padded)

        def forward_block(block_index, padded=padded, layer_index=layer_index):
            start = (block_index * ROWS_DEV).astype(jnp.int32)
            anchor = jnp.zeros((), jnp.int32)
            slab = lax.dynamic_slice(padded, (start, anchor, anchor), (ROWS_DEV + 2 * halo_width, NW + 2 * halo_width, C))
            return forward_rows(slab, kernels[layer_index], gains[layer_index], up_weights[layer_index], down_weights[layer_index], ROWS_DEV, NW)
        current = lax.map(forward_block, block_ids).reshape(NH, NW, C)
    output = current
    gradient = cotangent
    kernel_list = [None] * LAYERS
    gain_list = [None] * LAYERS
    up_list = [None] * LAYERS
    down_list = [None] * LAYERS
    for layer_index in reversed(range(LAYERS)):
        padded = stored[layer_index]

        def backward_block(block_index, padded=padded, gradient=gradient, layer_index=layer_index):
            start = (block_index * ROWS_DEV).astype(jnp.int32)
            anchor = jnp.zeros((), jnp.int32)
            slab = lax.dynamic_slice(padded, (start, anchor, anchor), (ROWS_DEV + 2 * halo_width, NW + 2 * halo_width, C))
            upstream = lax.dynamic_slice(gradient, (start, anchor, anchor), (ROWS_DEV, NW, C))
            return backward_rows(slab, upstream, kernels[layer_index], gains[layer_index], up_weights[layer_index], down_weights[layer_index], ROWS_DEV, NW)
        conv_grads, kernel_terms, gain_terms, up_terms, down_terms = lax.map(backward_block, block_ids)
        kernel_list[layer_index] = lax.optimization_barrier(jnp.sum(kernel_terms, axis=0)) * factor
        gain_list[layer_index] = lax.optimization_barrier(jnp.sum(gain_terms, axis=0)) * factor
        up_list[layer_index] = lax.optimization_barrier(jnp.sum(up_terms, axis=0)) * factor
        down_list[layer_index] = lax.optimization_barrier(jnp.sum(down_terms, axis=0)) * factor
        padded_grad = jnp.pad(conv_grads.reshape(NH, NW, C), padding)

        def input_block(block_index, padded_grad=padded_grad, gradient=gradient, layer_index=layer_index):
            start = (block_index * ROWS_DEV).astype(jnp.int32)
            anchor = jnp.zeros((), jnp.int32)
            slab = lax.dynamic_slice(padded_grad, (start, anchor, anchor), (ROWS_DEV + 2 * halo_width, NW + 2 * halo_width, C))
            upstream = lax.dynamic_slice(gradient, (start, anchor, anchor), (ROWS_DEV, NW, C))
            return (upstream.astype(jnp.float32) + flipped_conv(slab, kernels[layer_index], ROWS_DEV, NW)).astype(jnp.bfloat16)
        gradient = lax.map(input_block, block_ids).reshape(NH, NW, C)
    return (output, gradient, jnp.stack(kernel_list), jnp.stack(gain_list), jnp.stack(up_list), jnp.stack(down_list))
```

```python
import math

import jax
import jax.numpy as jnp
from jax import lax
from jax.sharding import PartitionSpec as P

epsilon = 1e-06
inv_sqrt_two = 0.7071067811865476
inv_sqrt_two_pi = 0.3989422804014327


def swap_pairs(row_count, col_count, row_start, col_start):
    def partner(index, start, count):
        if start is None:
            return index
        other = index + 1 if (index - start) % 2 == 0 else index - 1
        return other if 0 <= other < count else None

    pairs = []
    for r in range(row_count):
        for c in range(col_count):
            pr, pc = (partner(r, row_start, row_count), partner(c, col_start, col_count))
            if pr is not None and pc is not None:
                pairs.append((r * col_count + c, pr * col_count + pc))
    return pairs


def extended(array, sides, width):
    row_count, col_count = (lax.axis_size("row"), lax.axis_size("col"))
    rows, cols, _ = array.shape
    even_row, even_col = (lax.axis_index("row") % 2 == 0, lax.axis_index("col") % 2 == 0)
    first_cols, last_cols = (array[:, :width], array[:, cols - width :])
    facing_cols = {
        0: jnp.where(even_col, last_cols, first_cols),
        1: jnp.where(even_col, first_cols, last_cols),
        None: array,
    }

    def swapped(row_start, col_start):
        strip = facing_cols[col_start]
        if row_start is not None:
            low, high = (strip[:width], strip[rows - width :])
            strip = jnp.where(even_row == (row_start == 0), high, low)
        pairs = swap_pairs(row_count, col_count, row_start, col_start)
        return lax.ppermute(strip, ("row", "col"), pairs)

    def band(row_start):
        middle = array if row_start is None else swapped(row_start, None)
        near, far = (swapped(row_start, 0), swapped(row_start, 1))
        left, right = (jnp.where(even_col, far, near), jnp.where(even_col, near, far))
        return jnp.concatenate([left, middle, right], axis=1)

    near = band(0)
    far = band(1) if row_count > 2 else jnp.zeros_like(near)
    above, below = (jnp.where(even_row, far, near), jnp.where(even_row, near, far))
    return jnp.concatenate([above, band(None), below], axis=0)


def contract_leading(left, right):
    return lax.dot_general(
        left, right, (((0,), (0,)), ((), ())), preferred_element_type=jnp.float32
    )


def contract_trailing(left, right):
    return lax.dot_general(
        left, right, (((1,), (1,)), ((), ())), preferred_element_type=jnp.float32
    )


def depthwise(padded, kernel, tile_rows, tile_cols):
    padded_f = padded.astype(jnp.float32)
    tap_count = kernel.shape[0]
    accumulated = jnp.zeros((tile_rows, tile_cols, padded.shape[2]), jnp.float32)
    for tap_row in range(tap_count):
        for tap_col in range(tap_count):
            accumulated = (
                accumulated
                + padded_f[tap_row : tap_row + tile_rows, tap_col : tap_col + tile_cols]
                * kernel[tap_row, tap_col]
            )
    return accumulated


def flipped_conv(padded, kernel, tile_rows, tile_cols):
    padded_f = padded.astype(jnp.float32)
    tap_count = kernel.shape[0]
    last_tap = tap_count - 1
    accumulated = jnp.zeros((tile_rows, tile_cols, padded.shape[2]), jnp.float32)
    for tap_row in range(tap_count):
        for tap_col in range(tap_count):
            start_row = last_tap - tap_row
            start_col = last_tap - tap_col
            accumulated = (
                accumulated
                + padded_f[start_row : start_row + tile_rows, start_col : start_col + tile_cols]
                * kernel[tap_row, tap_col]
            )
    return accumulated


def kernel_grad(padded, conv_grad, tile_rows, tile_cols, tap_count):
    padded_f = padded.astype(jnp.float32)
    grad_f = conv_grad.astype(jnp.float32)
    rows_out = []
    for tap_row in range(tap_count):
        entries = []
        for tap_col in range(tap_count):
            entries.append(
                jnp.sum(
                    padded_f[tap_row : tap_row + tile_rows, tap_col : tap_col + tile_cols] * grad_f,
                    axis=(0, 1),
                )
            )
        rows_out.append(jnp.stack(entries))
    return jnp.stack(rows_out)


def normalize(conv_out):
    centred = conv_out - jnp.mean(conv_out, axis=-1, keepdims=True)
    variance = jnp.mean(centred * centred, axis=-1, keepdims=True)
    inverse_std = lax.rsqrt(variance + epsilon)
    return (centred * inverse_std, inverse_std)


def gelu_parts(pre):
    normal_cdf = 0.5 * (1.0 + lax.erf(pre * inv_sqrt_two))
    density = jnp.exp(-0.5 * pre * pre) * inv_sqrt_two_pi
    return (pre * normal_cdf, normal_cdf + pre * density)


def mixing(padded, kernel, gain, up_weight, tile_rows, tile_cols):
    conv_out = depthwise(padded, kernel, tile_rows, tile_cols)
    unit_vals, inverse_std = normalize(conv_out)
    normed = (unit_vals * gain).astype(jnp.bfloat16).reshape(tile_rows * tile_cols, -1)
    pre = jnp.dot(normed, up_weight, preferred_element_type=jnp.float32)
    gelu_value, gelu_slope = gelu_parts(pre)
    return (unit_vals, inverse_std, normed, gelu_value.astype(jnp.bfloat16), gelu_slope)


def backward_rows(
    padded, upstream, saved, kernel, gain, up_weight, down_weight, tile_rows, tile_cols
):
    unit_vals, inverse_std, normed, hidden, gelu_slope = saved
    channels = upstream.shape[2]
    flat_grad = upstream.reshape(tile_rows * tile_cols, channels)
    down_term = contract_leading(hidden, flat_grad)
    hidden_grad = contract_trailing(flat_grad, down_weight)
    pre_grad = (hidden_grad * gelu_slope).astype(jnp.bfloat16)
    up_term = contract_leading(normed, pre_grad)
    normed_grad = contract_trailing(pre_grad, up_weight).reshape(tile_rows, tile_cols, channels)
    gain_term = jnp.sum(normed_grad * unit_vals, axis=(0, 1))
    unit_grad = normed_grad * gain
    conv_grad = inverse_std * (
        unit_grad
        - jnp.mean(unit_grad, axis=-1, keepdims=True)
        - unit_vals * jnp.mean(unit_grad * unit_vals, axis=-1, keepdims=True)
    )
    conv_grad = conv_grad.astype(jnp.bfloat16)
    kernel_term = kernel_grad(padded, conv_grad, tile_rows, tile_cols, kernel.shape[0])
    return (conv_grad, kernel_term, gain_term, up_term, down_term)


def deliver(kernel_total, gain_total, up_total, down_total):
    axes = ("row", "col")
    row_count, col_count = (lax.axis_size("row"), lax.axis_size("col"))
    count = row_count * col_count
    layers, channels, units = up_total.shape
    half, part = (channels // row_count, units // col_count)
    up = up_total.reshape(layers, row_count, half, col_count, part).transpose(1, 3, 0, 2, 4)
    down = down_total.reshape(layers, col_count, part, row_count, half).transpose(3, 1, 0, 2, 4)
    size = layers * half * part
    small = jnp.concatenate([kernel_total.reshape(-1), gain_total.reshape(-1)])
    share = -(-small.shape[0] // (count * 128)) * 128
    small = jnp.pad(small, (0, share * count - small.shape[0])).reshape(count, share)
    packed = jnp.concatenate([up.reshape(count, size), down.reshape(count, size), small], axis=1)
    width = packed.shape[1]
    packed = jnp.pad(packed, ((0, 0), (0, -width % 128)))
    packed = packed.astype(jnp.bfloat16).reshape(count, -1, 128)
    got = lax.all_to_all(packed, axes, 0, 0, tiled=True)
    total = jnp.sum(got.astype(jnp.float32), axis=0).reshape(-1)
    up_part = total[:size].reshape(layers, half, part)
    down_part = total[size : 2 * size].reshape(layers, part, half)
    mine = total[2 * size : width]
    copies = jnp.broadcast_to(mine.reshape(1, -1, 128), (count, share // 128, 128))
    every = lax.all_to_all(copies, axes, 0, 0, tiled=True).reshape(-1)
    kernel_size = kernel_total.size
    kernel_out = every[:kernel_size].reshape(kernel_total.shape)
    gain_out = every[kernel_size : kernel_size + gain_total.size].reshape(gain_total.shape)
    return (kernel_out, gain_out, up_part, down_part)


def per_device(image, kernels, gains, up_weights, down_weights, cotangent):
    tile_rows, tile_cols, channels = image.shape
    layer_count = kernels.shape[0]
    halo_width = kernels.shape[1] // 2
    pixel_total = tile_rows * tile_cols * lax.axis_size("row") * lax.axis_size("col")
    factor = 1.0 / math.sqrt(pixel_total)
    current = image
    stored = []
    saved_list = []
    for layer_index in range(layer_count):
        padded = extended(current, (("row", 0), ("col", 1)), halo_width)
        stored.append(padded)
        saved = mixing(
            padded,
            kernels[layer_index],
            gains[layer_index],
            up_weights[layer_index],
            tile_rows,
            tile_cols,
        )
        saved_list.append(saved)
        branch = jnp.dot(
            saved[3], down_weights[layer_index], preferred_element_type=jnp.float32
        ).reshape(tile_rows, tile_cols, channels)
        current = (current.astype(jnp.float32) + branch).astype(jnp.bfloat16)
    gradient = cotangent
    kernel_list = [None] * layer_count
    gain_list = [None] * layer_count
    up_list = [None] * layer_count
    down_list = [None] * layer_count
    for layer_index in reversed(range(layer_count)):
        padded = stored[layer_index]
        saved = saved_list[layer_index]
        conv_grad, kernel_term, gain_term, up_term, down_term = backward_rows(
            padded,
            gradient,
            saved,
            kernels[layer_index],
            gains[layer_index],
            up_weights[layer_index],
            down_weights[layer_index],
            tile_rows,
            tile_cols,
        )
        kernel_list[layer_index] = kernel_term * factor
        gain_list[layer_index] = gain_term * factor
        up_list[layer_index], down_list[layer_index] = (up_term * factor, down_term * factor)
        padded_grad = extended(conv_grad, (("row", 0), ("col", 1)), halo_width)
        gradient = (
            gradient.astype(jnp.float32)
            + flipped_conv(padded_grad, kernels[layer_index], tile_rows, tile_cols)
        ).astype(jnp.bfloat16)
    sums = deliver(
        jnp.stack(kernel_list), jnp.stack(gain_list), jnp.stack(up_list), jnp.stack(down_list)
    )
    return (current, gradient) + sums


def solution(mesh):
    placed = (P("row", "col", None), P(), P(), P(), P(), P("row", "col", None))
    return jax.shard_map(
        per_device,
        mesh=mesh,
        in_specs=placed,
        out_specs=(
            P("row", "col", None),
            P("row", "col", None),
            P(),
            P(),
            P(None, "row", "col"),
            P(None, "col", "row"),
        ),
        check_vma=False,
    )
```

```python
import functools
import math

import jax
import jax.numpy as jnp
from jax import lax
from jax.experimental import pallas as pl
from jax.experimental.pallas import tpu as pltpu
from jax.sharding import PartitionSpec as P

epsilon = 1e-06
inv_sqrt_two = 0.7071067811865476
inv_sqrt_two_pi = 0.3989422804014327
LANES = 128
SIDE = 8
f32, bf16 = (jnp.float32, jnp.bfloat16)


def ceil8(n):
    return -(-n // 8) * 8


def combos(row_count):
    listed = [(None, 0), (None, 1), (0, None), (0, 0), (0, 1)]
    if row_count > 2:
        listed += [(1, None), (1, 0), (1, 1)]
    return listed


def partner(index, start, count):
    if start is None:
        return index
    other = index + 1 if (index - start) % 2 == 0 else index - 1
    return other if 0 <= other < count else None


def swap_pairs(row_count, col_count, row_start, col_start):
    pairs = []
    for r in range(row_count):
        for c in range(col_count):
            pr, pc = (partner(r, row_start, row_count), partner(c, col_start, col_count))
            if pr is None:
                pr, pc = (r, c ^ 1)
            elif pc is None:
                pr, pc = (r ^ 1 if row_start is None else pr, c)
            pairs.append((r * col_count + c, pr * col_count + pc))
    return pairs


def exchange(strips, row_count, col_count):
    return [
        lax.ppermute(strip, ("row", "col"), swap_pairs(row_count, col_count, rs, cs))
        for strip, (rs, cs) in zip(strips, combos(row_count))
    ]


class Place:
    def __init__(self, row_count, col_count):
        row, col = (lax.axis_index("row"), lax.axis_index("col"))
        self.even_row, self.even_col = (lax.rem(row, 2) == 0, lax.rem(col, 2) == 0)
        self.has = {
            "above": row > 0,
            "below": row < row_count - 1,
            "left": col > 0,
            "right": col < col_count - 1,
        }
        self.row_count = row_count


def write_strips(place, outs, takes):
    for out, (rs, cs) in zip(outs, combos(place.row_count)):
        at = 0
        for take, radius, rows, cols in takes:
            row_sets = [slice(0, rows)] * 2
            col_sets = [slice(0, cols)] * 2
            if rs is not None:
                row_sets = [slice(rows - radius, rows), slice(0, radius)]
                if rs == 1:
                    row_sets = row_sets[::-1]
            if cs is not None:
                col_sets = [slice(cols - SIDE, cols), slice(0, SIDE)]
                if cs == 1:
                    col_sets = col_sets[::-1]
            count = row_sets[0].stop - row_sets[0].start
            for i in range(count):
                parts = {}
                for er in (0, 1):
                    for ec in (0, 1):
                        key = (row_sets[er].start + i, col_sets[ec].start, col_sets[ec].stop)
                        if key not in parts:
                            parts[key] = take(*key)
                        parts[er, ec] = parts[key]
                if cs is None:
                    pick = [parts[0, 0], parts[1, 0]]
                else:
                    pick = [jnp.where(place.even_col, parts[e, 0], parts[e, 1]) for e in (0, 1)]
                value = pick[0] if rs is None else jnp.where(place.even_row, pick[0], pick[1])
                out[at + i] = value.astype(out.dtype)
            at += count


def strip_shapes(row_count, rows, cols, channels, radii):
    shapes = []
    for rs, cs in combos(row_count):
        height = sum(rows if rs is None else radius for radius in radii)
        shapes.append((height, cols if cs is None else SIDE, channels))
    return shapes


def received(place, strips, row_sections):
    table = dict(zip(combos(place.row_count), strips))
    full_start, band_start = row_sections

    def along(rs, cs, i):
        return table[rs, cs][(full_start if rs is None else band_start) + i].astype(f32)

    def column(rs, side, i):
        if side is None:
            return along(rs, None, i)
        near, far = (along(rs, 0, i), along(rs, 1, i))
        if side == "left":
            return jnp.where(place.even_col, far, near)
        return jnp.where(place.even_col, near, far)

    def read(vertical, side, i):
        if vertical is None:
            value = column(None, side, i)
        elif place.row_count == 2:
            value = column(0, side, i)
        else:
            near, far = (column(0, side, i), column(1, side, i))
            if vertical == "above":
                value = jnp.where(place.even_row, far, near)
            else:
                value = jnp.where(place.even_row, near, far)
        if vertical is not None:
            value = jnp.where(place.has[vertical], value, 0.0)
        if side is not None:
            value = jnp.where(place.has[side], value, 0.0)
        return value

    return read


def assemble(place, target, own, read, radius, rows, cols, channels):
    width = cols + 2 * SIDE
    target[...] = jnp.zeros(target.shape, f32)
    for vertical, start, count in (("above", 0, radius), (None, radius, rows), ("below", radius + rows, radius)):
        for i in range(count):
            base = (start + i) * width
            middle = own(i) if vertical is None else read(vertical, None, i)
            target[base + SIDE : base + SIDE + cols, 0:channels] = middle
            target[base : base + SIDE, 0:channels] = read(vertical, "left", i)
            target[base + SIDE + cols : base + width, 0:channels] = read(vertical, "right", i)


def spread_taps(kernel_ref, layer, target, flipped):
    size, channels = (kernel_ref.shape[1], kernel_ref.shape[3])
    target[...] = jnp.zeros(target.shape, f32)
    for a in range(size):
        for b in range(size):
            t = (size - 1 - a) * size + size - 1 - b if flipped else a * size + b
            row = kernel_ref[layer, a, b : b + 1, :]
            target[t * 8 : t * 8 + 8, 0:channels] = jnp.broadcast_to(row, (8, channels))


def conv_group(src, base, stride, rows_out, taps, size):
    total = [None] * rows_out
    for b in range(size):
        weights = [taps[(a * size + b) * 8 : (a * size + b) * 8 + 8, :] for a in range(size)]
        for i in range(rows_out + size - 1):
            x = src[pl.ds(base + i * stride + b, 8), :]
            for a in range(size):
                r = i - a
                if 0 <= r < rows_out:
                    term = x * weights[a]
                    total[r] = term if total[r] is None else total[r] + term
    return total


def kernel_sums(src, src_base, src_stride, grad, grad_base, grad_stride, rows, cols, size, sums):
    sums[...] = jnp.zeros(sums.shape, f32)

    def group(g, carry):
        at = pl.multiple_of(g * 8, 8)
        grads = [grad[pl.ds(grad_base + i * grad_stride + at, 8), :] for i in range(rows)]
        for b in range(size):
            total = [None] * size
            for i in range(rows + size - 1):
                x = src[pl.ds(src_base + i * src_stride + at + b, 8), :]
                for a in range(size):
                    r = i - a
                    if 0 <= r < rows:
                        term = x * grads[r]
                        total[a] = term if total[a] is None else total[a] + term
            for a in range(size):
                t = (a * size + b) * 8
                sums[t : t + 8, :] += total[a]
        return carry

    lax.fori_loop(0, cols // 8, group, 0)


def lane_total(x):
    high = x.astype(bf16)
    low = (x - high.astype(f32)).astype(bf16)
    both = jnp.concatenate([high, low], axis=1)
    ones = jnp.ones((2 * LANES, LANES), bf16)
    return jnp.dot(both, ones, preferred_element_type=f32)


def layer_norm(conv, channels):
    lane = lax.broadcasted_iota(jnp.int32, conv.shape, 1)
    centred = jnp.where(lane < channels, conv - lane_total(conv) * (1.0 / channels), 0.0)
    variance = lane_total(centred * centred) * (1.0 / channels)
    inverse = lax.rsqrt(variance + epsilon)
    return (centred * inverse, inverse)


def norm_backward(normed_grad, unit, inverse, gain, channels):
    m = normed_grad * gain
    mean = lane_total(m) * (1.0 / channels)
    along = lane_total(m * unit) * (1.0 / channels)
    lane = lax.broadcasted_iota(jnp.int32, m.shape, 1)
    return jnp.where(lane < channels, inverse * (m - mean - unit * along), 0.0)


def gelu_parts(v):
    t = 1.0 / (1.0 + (0.3275911 * inv_sqrt_two) * jnp.abs(v))
    bell = jnp.exp(-0.5 * v * v)
    series = 0.5 * 1.061405429 * t + 0.5 * -1.453152027
    series = series * t + 0.5 * 1.421413741
    series = series * t + 0.5 * -0.284496736
    series = series * t + 0.5 * 0.254829592
    tail = series * t * bell
    cdf = jnp.where(v >= 0.0, 1.0 - tail, tail)
    return (v * cdf, cdf + v * (bell * inv_sqrt_two_pi))


def dot(x, w):
    return jnp.dot(x, w, preferred_element_type=f32)


def dot_leading(x, y):
    return lax.dot_general(x, y, (((0,), (0,)), ((), ())), preferred_element_type=f32)


def pad_lanes(x):
    rows, channels = x.shape
    return jnp.concatenate([x, jnp.zeros((rows, LANES - channels), x.dtype)], axis=1)


def load_weights(up_ref, down_ref, layer, up, down, up_t, down_t):
    channels, units = up_ref.shape[1:]
    up_f = jnp.concatenate([up_ref[layer].astype(f32), jnp.zeros((LANES - channels, units), f32)], axis=0)
    down_f = pad_lanes(down_ref[layer].astype(f32))
    if up is not None:
        up[...] = up_f.astype(bf16)
        down[...] = down_f.astype(bf16)
    if up_t is not None:
        up_t[...] = up_f.T.astype(bf16)
        down_t[...] = down_f.T.astype(bf16)


def round16(x):
    return x.astype(bf16).astype(f32)


def strips_kernel(dims, image, cot, *outs):
    place = Place(dims.row_count, dims.col_count)

    def take(ref):
        return lambda i, lo, hi: ref[i].astype(f32)[lo:hi]

    write_strips(
        place,
        outs,
        [(take(image), 2 * dims.h, dims.rows, dims.cols), (take(cot), dims.h, dims.rows, dims.cols)],
    )


def first_kernel(dims, *refs):
    count = len(combos(dims.row_count))
    image, cot, kernels, gains, up_w, down_w = refs[:6]
    strips = refs[6 : 6 + count]
    refs = refs[6 + count :]
    (output, x0, x1, unit0, inv0, hidden0, slope0, grad1, normed1, pre_grad1, hidden1, gain_sum) = refs[:12]
    outs = refs[12 : 12 + count]
    conv, taps, up, down, up_t, down_t = refs[12 + count :]
    place = Place(dims.row_count, dims.col_count)
    rows, cols, channels, h, size = (dims.rows, dims.cols, dims.channels, dims.h, dims.size)
    ext_rows, ext_cols, wide = (dims.ext_rows, dims.ext_cols, dims.wide)
    read = received(place, strips, (0, 0))
    assemble(place, x0, lambda i: image[i].astype(f32), read, 2 * h, rows, cols, channels)

    spread_taps(kernels, 0, taps, False)
    load_weights(up_w, down_w, 0, up, down, None, None)

    def conv0(g, carry):
        at = pl.multiple_of(g * 8, 8)
        total = conv_group(x0, at + 1, wide, ext_rows, taps, size)
        for r in range(ext_rows):
            conv[pl.ds(r * ext_cols + at, 8), :] = total[r]
            x1[pl.ds(r * ext_cols + at, 8), :] = x0[pl.ds((r + h) * wide + at + 4, 8), :]
        return carry

    lax.fori_loop(0, ext_cols // 8, conv0, 0)
    gain = pad_lanes(gains[0:1, :])
    step = dims.ext_step

    def mix0(k, carry):
        px = pl.ds(pl.multiple_of(k * step, 16), step)
        unit, inverse = layer_norm(conv[px, :], channels)
        unit0[px, :] = unit.astype(bf16)
        inv0[px, :] = inverse
        pre = dot((unit * gain).astype(bf16), up[...])
        value, slope = gelu_parts(pre)
        hidden = value.astype(bf16)
        hidden0[px, :] = hidden
        slope0[px, :] = slope.astype(bf16)
        x1[px, :] = round16(x1[px, :] + dot(hidden, down[...]))
        return carry

    lax.fori_loop(0, ext_rows * ext_cols // step, mix0, 0)
    clear_outside(place, x1, dims)

    spread_taps(kernels, 1, taps, False)
    load_weights(up_w, down_w, 1, up, down, up_t, down_t)

    def conv1(g, carry):
        at = pl.multiple_of(g * 8, 8)
        total = conv_group(x1, at + 1, ext_cols, rows, taps, size)
        for r in range(rows):
            conv[pl.ds(r * cols + at, 8), :] = total[r]
        return carry

    lax.fori_loop(0, cols // 8, conv1, 0)
    gain1 = pad_lanes(gains[1:2, :])
    gain_sum[...] = jnp.zeros(gain_sum.shape, f32)
    lines = dims.line_step
    step1 = lines * cols

    def mix1(k, carry):
        px = pl.ds(pl.multiple_of(k * step1, step1), step1)
        unit, inverse = layer_norm(conv[px, :], channels)
        normed = (unit * gain1).astype(bf16)
        normed1[px, :] = normed
        value, slope = gelu_parts(dot(normed, up[...]))
        hidden = value.astype(bf16)
        hidden1[px, :] = hidden
        branch = dot(hidden, down[...])
        for i in range(lines):
            start = (k * lines + i + h) * ext_cols + 4
            line = x1[pl.ds(start, cols), :] + branch[i * cols : (i + 1) * cols]
            output[k * lines + i] = line[:, :channels].astype(bf16)
        upstream = pad_lanes(cot[pl.ds(k * lines, lines)].reshape(step1, channels))
        pre_grad = (dot(upstream, down_t[...]) * slope).astype(bf16)
        pre_grad1[px, :] = pre_grad
        normed_grad = dot(pre_grad, up_t[...])
        product = normed_grad * unit
        gain_sum[...] += jnp.sum(product.reshape(step1 // 8, 8, LANES), axis=0)
        grad1[px, :] = round16(norm_backward(normed_grad, unit, inverse, gain1, channels))
        return carry

    lax.fori_loop(0, rows // lines, mix1, 0)

    def take(i, lo, hi):
        return grad1[i * cols + lo : i * cols + hi, 0:channels]

    write_strips(place, outs, [(take, 2 * h, rows, cols)])


def clear_outside(place, flat, dims):
    h, ext_rows, ext_cols = (dims.h, dims.ext_rows, dims.ext_cols)
    margin = (ext_cols - dims.cols) // 2

    @pl.when(jnp.logical_not(place.has["above"]))
    def _():
        flat[0 : h * ext_cols, :] = jnp.zeros((h * ext_cols, LANES), f32)

    @pl.when(jnp.logical_not(place.has["below"]))
    def _():
        flat[(ext_rows - h) * ext_cols :, :] = jnp.zeros((h * ext_cols, LANES), f32)

    @pl.when(jnp.logical_not(place.has["left"]))
    def _():
        for r in range(ext_rows):
            flat[r * ext_cols : r * ext_cols + margin, :] = jnp.zeros((margin, LANES), f32)

    @pl.when(jnp.logical_not(place.has["right"]))
    def _():
        for r in range(ext_rows):
            flat[(r + 1) * ext_cols - margin : (r + 1) * ext_cols, :] = jnp.zeros((margin, LANES), f32)


def sums_kernel(dims, x1, grad1, normed1, pre_grad1, hidden1, cot, gain_part, taps_sum, up_sum, down_sum, sums):
    kernel_sums(x1, 1, dims.ext_cols, grad1, 0, dims.cols, dims.rows, dims.cols, dims.size, sums)
    store_sums(dims, sums, gain_part[...], taps_sum)
    upstream = pad_lanes(cot[...].reshape(dims.rows * dims.cols, dims.channels))
    up_sum[...] = dot_leading(normed1[...], pre_grad1[...]).T
    down_sum[...] = dot_leading(upstream, hidden1[...]).T


def store_sums(dims, sums, gain_part, target):
    taps = dims.size * dims.size
    target[...] = jnp.zeros(target.shape, f32)
    for t in range(taps):
        target[t : t + 1, :] = jnp.sum(sums[t * 8 : t * 8 + 8, :], axis=0, keepdims=True)
    target[taps : taps + 1, :] = jnp.sum(gain_part, axis=0, keepdims=True)


def third_kernel(dims, *refs):
    count = len(combos(dims.row_count))
    (grad1, cot, kernels, gains, up_w, down_w, x0, unit0, inv0, hidden0, slope0) = refs[:11]
    (taps_sum1, up_sum1, down_sum1) = refs[11:14]
    strips = refs[14 : 14 + count]
    cot_strips = refs[14 + count : 14 + 2 * count]
    (grad0, middle, packed) = refs[14 + 2 * count : 17 + 2 * count]
    (wide_grad, upstream, own, taps, up_t, down_t, sums, up_acc, down_acc, gain_sum, small, table) = refs[17 + 2 * count :]
    place = Place(dims.row_count, dims.col_count)
    rows, cols, channels, h, size = (dims.rows, dims.cols, dims.channels, dims.h, dims.size)
    ext_rows, ext_cols, wide = (dims.ext_rows, dims.ext_cols, dims.wide)
    read = received(place, strips, (0, 0))
    assemble(
        place, wide_grad, lambda i: grad1[i * cols : (i + 1) * cols, 0:channels], read, 2 * h, rows, cols, channels
    )
    read_cot = received(place, cot_strips, (rows, 2 * h))
    margin = (ext_cols - cols) // 2
    upstream[...] = jnp.zeros(upstream.shape, f32)
    for vertical, start, n in (("above", 0, h), (None, h, rows), ("below", h + rows, h)):
        for i in range(n):
            base = (start + i) * ext_cols
            line = cot[i].astype(f32) if vertical is None else read_cot(vertical, None, i)
            upstream[base + margin : base + margin + cols, 0:channels] = line
            upstream[base : base + margin, 0:channels] = read_cot(vertical, "left", i)[SIDE - margin :]
            upstream[base + margin + cols : base + ext_cols, 0:channels] = read_cot(vertical, "right", i)[:margin]

    spread_taps(kernels, 1, taps, True)
    load_weights(up_w, down_w, 0, None, None, up_t, down_t)

    def conv1(g, carry):
        at = pl.multiple_of(g * 8, 8)
        total = conv_group(wide_grad, at + 1, wide, ext_rows, taps, size)
        col = lax.broadcasted_iota(jnp.int32, (8, LANES), 0) + (at - margin)
        inside = jnp.where(jnp.logical_and(col >= 0, col < cols), 1.0, 0.0)
        for r in range(ext_rows):
            px = pl.ds(r * ext_cols + at, 8)
            upstream[px, :] = upstream[px, :] + total[r]
            own[px, :] = inside if h <= r < h + rows else jnp.zeros((8, LANES), f32)
        return carry

    lax.fori_loop(0, ext_cols // 8, conv1, 0)
    for i in range(rows):
        base = (i + h) * ext_cols + margin
        middle[i * cols : (i + 1) * cols, :] = round16(upstream[base : base + cols, :])

    gain = pad_lanes(gains[0:1, :])
    gain_sum[...] = jnp.zeros(gain_sum.shape, f32)
    up_acc[...] = jnp.zeros(up_acc.shape, f32)
    down_acc[...] = jnp.zeros(down_acc.shape, f32)
    step = dims.ext_step

    def mix0(k, carry):
        px = pl.ds(pl.multiple_of(k * step, 16), step)
        flow = upstream[px, :].astype(bf16)
        mine = own[px, :]
        mine16 = mine.astype(bf16)
        unit = unit0[px, :].astype(f32)
        pre_grad = (dot(flow, down_t[...]) * slope0[px, :].astype(f32)).astype(bf16)
        normed_grad = dot(pre_grad, up_t[...])
        normed = (unit * gain * mine).astype(bf16)
        up_acc[...] += dot_leading(normed, pre_grad)
        down_acc[...] += dot_leading(flow * mine16, hidden0[px, :])
        product = normed_grad * unit * mine
        gain_sum[...] += jnp.sum(product.reshape(step // 8, 8, LANES), axis=0)
        grad0[px, :] = round16(norm_backward(normed_grad, unit, inv0[px, :], gain, channels))
        return carry

    lax.fori_loop(0, ext_rows * ext_cols // step, mix0, 0)
    clear_outside(place, grad0, dims)
    kernel_sums(
        x0, h * wide + SIDE - h, wide, grad0, h * ext_cols + margin, ext_cols, rows, cols, size, sums
    )
    store_sums(dims, sums, gain_sum[...], small)

    layer_rows, part, half, share = (dims.layer_rows, dims.part, dims.half, dims.share)
    units = up_acc.shape[1]
    table[...] = jnp.zeros(table.shape, f32)
    taps_rows = size * size + 1
    for layer, source in ((0, small), (1, taps_sum1)):
        for t in range(taps_rows):
            place_at = layer * taps_rows + t
            line = (place_at // share) * 8 + place_at % share
            table[line : line + 1, :] = source[t : t + 1, :] * dims.factor
    up0 = up_acc[...].T * dims.factor
    down0 = down_acc[...].T * dims.factor
    lane = lax.broadcasted_iota(jnp.int32, (units, LANES), 1)
    tall = wide_grad
    for r in range(dims.row_count):
        for layer, (u, d) in enumerate(((up0, down0), (up_sum1[...] * dims.factor, down_sum1[...] * dims.factor))):
            first = pltpu.roll(u, (LANES - r * half) % LANES, 1) if r else u
            shift = (half - r * half) % LANES
            second = pltpu.roll(d, shift, 1) if shift else d
            joined = jnp.where(lane < half, first, jnp.where(lane < 2 * half, second, 0.0))
            tall[layer * (units + 8) : layer * (units + 8) + units, :] = joined

        def slab(c, carry, r=r):
            dev = r * dims.col_count + c
            rows_of = [tall[pl.ds(layer * (units + 8) + c * part, layer_rows), :] for layer in range(2)]
            whole = jnp.concatenate(rows_of, axis=0)
            extra = table[pl.ds(pl.multiple_of(dev * 8, 8), 8), :]
            quarter = lax.broadcasted_iota(jnp.int32, (8, LANES), 1)
            pieces = [jnp.where(quarter >= 96, pltpu.roll(extra, s, 1), 0.0) for s in (96, 64, 32)]
            pieces.append(jnp.zeros((whole.shape[0] - 24, LANES), f32))
            whole = jnp.where(
                lax.broadcasted_iota(jnp.int32, whole.shape, 1) >= 96, jnp.concatenate(pieces, axis=0), whole
            )
            packed[dev] = whole.astype(bf16)
            return carry

        lax.fori_loop(0, dims.col_count, slab, 0)


def image_kernel(dims, grad0, middle, kernels, out, taps, work):
    rows, cols, size = (dims.rows, dims.cols, dims.size)
    spread_taps(kernels, 0, taps, True)

    def conv0(g, carry):
        at = pl.multiple_of(g * 8, 8)
        total = conv_group(grad0, at + 1, dims.ext_cols, rows, taps, size)
        for r in range(rows):
            work[pl.ds(r * cols + at, 8), :] = middle[pl.ds(r * cols + at, 8), :] + total[r]
        return carry

    lax.fori_loop(0, cols // 8, conv0, 0)
    for r in range(rows):
        out[r] = work[r * cols : (r + 1) * cols, 0 : dims.channels].astype(bf16)


def owner_kernel(dims, got, up_out, down_out, copies):
    total = got[0].astype(f32)
    for d in range(1, got.shape[0]):
        total = total + got[d].astype(f32)
    half, part = (dims.half, dims.part)
    for layer in range(2):
        block = total[layer * dims.layer_rows : (layer + 1) * dims.layer_rows]
        up_out[layer] = block.T[:half, :part]
        down_out[layer] = block[:part, half : 2 * half]
    lane = lax.broadcasted_iota(jnp.int32, (8, LANES), 1)
    line = jnp.where(lane < 32, pltpu.roll(total[0:8], 32, 1), 0.0)
    line = jnp.where(jnp.logical_and(lane >= 32, lane < 64), pltpu.roll(total[8:16], 64, 1), line)
    line = jnp.where(jnp.logical_and(lane >= 64, lane < 96), pltpu.roll(total[16:24], 96, 1), line)
    for d in range(copies.shape[0]):
        copies[d] = line[: dims.share]


def unpack_kernel(dims, every, kernel_out, gain_out):
    size, channels = (dims.size, dims.channels)
    for layer in range(2):
        for t in range(size * size + 1):
            at = layer * (size * size + 1) + t
            row = every[at // dims.share, at % dims.share : at % dims.share + 1, 0:channels]
            if t < size * size:
                kernel_out[layer, t // size, t % size : t % size + 1, :] = row
            else:
                gain_out[layer : layer + 1, :] = row


class Dims:
    pass


def dims_of(image, kernels, up_weights):
    d = Dims()
    d.row_count, d.col_count = (lax.axis_size("row"), lax.axis_size("col"))
    d.rows, d.cols, d.channels = image.shape
    d.size = kernels.shape[1]
    d.h = d.size // 2
    d.ext_rows, d.ext_cols = (d.rows + 2 * d.h, d.cols + 8)
    d.wide = d.cols + 2 * SIDE
    total = d.ext_rows * d.ext_cols
    d.ext_step = max(s for s in range(16, 600, 16) if total % s == 0)
    d.line_step = 4
    d.half = d.channels // d.row_count
    d.part = up_weights.shape[2] // d.col_count
    d.layer_rows = ceil8(d.part)
    d.count = d.row_count * d.col_count
    d.share = -(-2 * (d.size * d.size + 1) // d.count)
    d.factor = 1.0 / math.sqrt(d.rows * d.cols * d.count)
    return d


def run(kernel, outs, scratch, *args):
    shapes = [jax.ShapeDtypeStruct(shape, kind) for shape, kind in outs]
    space = pl.BlockSpec(memory_space=pltpu.VMEM)
    return pl.pallas_call(
        kernel,
        out_shape=shapes,
        in_specs=[space] * len(args),
        out_specs=[space] * len(shapes),
        scratch_shapes=[pltpu.VMEM(shape, kind) for shape, kind in scratch],
        compiler_params=pltpu.CompilerParams(vmem_limit_bytes=48 * 1024 * 1024),
    )(*args)


def per_device(image, kernels, gains, up_weights, down_weights, cotangent):
    d = dims_of(image, kernels, up_weights)
    bind = functools.partial
    rows, cols, channels = image.shape
    units = up_weights.shape[2]
    tile, ext, wide = (rows * cols, d.ext_rows * d.ext_cols, (rows + 4 * d.h) * d.wide)
    taps = ((d.size * d.size * 8, LANES), f32)
    sums_rows = ceil8(d.size * d.size + 1)

    shapes = strip_shapes(d.row_count, rows, cols, channels, (2 * d.h, d.h))
    strips = run(bind(strips_kernel, d), [(s, bf16) for s in shapes], [], image, cotangent)
    strips = exchange(strips, d.row_count, d.col_count)

    grad_shapes = strip_shapes(d.row_count, rows, cols, channels, (2 * d.h,))
    first = run(
        bind(first_kernel, d),
        [
            (image.shape, bf16),
            ((wide, LANES), f32),
            ((ext, LANES), f32),
            ((ext, LANES), bf16),
            ((ext, LANES), f32),
            ((ext, units), bf16),
            ((ext, units), bf16),
            ((tile, LANES), f32),
            ((tile, LANES), bf16),
            ((tile, units), bf16),
            ((tile, units), bf16),
            ((8, LANES), f32),
        ]
        + [(s, bf16) for s in grad_shapes],
        [
            ((ext, LANES), f32),
            taps,
            ((LANES, units), bf16),
            ((units, LANES), bf16),
            ((units, LANES), bf16),
            ((LANES, units), bf16),
        ],
        image,
        cotangent,
        kernels,
        gains,
        up_weights,
        down_weights,
        *strips,
    )
    (output, x0, x1, unit0, inv0, hidden0, slope0, grad1, normed1, pre_grad1, hidden1, gain_part) = first[:12]
    grad_strips = exchange(first[12:], d.row_count, d.col_count)

    taps_sum1, up_sum1, down_sum1 = run(
        bind(sums_kernel, d),
        [((sums_rows, LANES), f32), ((units, LANES), f32), ((units, LANES), f32)],
        [taps],
        x1,
        grad1,
        normed1,
        pre_grad1,
        hidden1,
        cotangent,
        gain_part,
    )

    grad0, middle, packed = run(
        bind(third_kernel, d),
        [((ext, LANES), f32), ((tile, LANES), f32), ((d.count, 2 * d.layer_rows, LANES), bf16)],
        [
            ((max(wide, 2 * (units + 16)), LANES), f32),
            ((ext, LANES), f32),
            ((ext, LANES), f32),
            taps,
            ((units, LANES), bf16),
            ((LANES, units), bf16),
            taps,
            ((LANES, units), f32),
            ((LANES, units), f32),
            ((8, LANES), f32),
            ((sums_rows, LANES), f32),
            ((d.count * 8, LANES), f32),
        ],
        grad1,
        cotangent,
        kernels,
        gains,
        up_weights,
        down_weights,
        x0,
        unit0,
        inv0,
        hidden0,
        slope0,
        taps_sum1,
        up_sum1,
        down_sum1,
        *grad_strips,
        *strips,
    )
    axes = ("row", "col")
    got = lax.all_to_all(packed, axes, 0, 0, tiled=True)
    (gradient,) = run(bind(image_kernel, d), [(image.shape, bf16)], [taps, ((tile, LANES), f32)], grad0, middle, kernels)
    up_out, down_out, copies = run(
        bind(owner_kernel, d),
        [((2, d.half, d.part), f32), ((2, d.part, d.half), f32), ((d.count, d.share, LANES), f32)],
        [],
        got,
    )
    every = lax.all_to_all(copies, axes, 0, 0, tiled=True)
    kernel_out, gain_out = run(bind(unpack_kernel, d), [(kernels.shape, f32), (gains.shape, f32)], [], every)
    return (output, gradient, kernel_out, gain_out, up_out, down_out)


def solution(mesh):
    placed = (P("row", "col", None), P(), P(), P(), P(), P("row", "col", None))
    return jax.shard_map(
        per_device,
        mesh=mesh,
        in_specs=placed,
        out_specs=(
            P("row", "col", None),
            P("row", "col", None),
            P(),
            P(),
            P(None, "row", "col"),
            P(None, "col", "row"),
        ),
        check_vma=False,
    )
```

```python
import functools
import math

import jax
import jax.numpy as jnp
from jax import lax
from jax.experimental import pallas as pl
from jax.experimental.pallas import tpu as pltpu
from jax.sharding import PartitionSpec as P

epsilon = 1e-06
inv_sqrt_two = 0.7071067811865476
inv_sqrt_two_pi = 0.3989422804014327
LANES = 128
SIDE = 8
f32, bf16 = (jnp.float32, jnp.bfloat16)


def ceil8(n):
    return -(-n // 8) * 8


def combos(row_count):
    listed = [(None, 0), (None, 1), (0, None), (0, 0), (0, 1)]
    if row_count > 2:
        listed += [(1, None), (1, 0), (1, 1)]
    return listed


def partner(index, start, count):
    if start is None:
        return index
    other = index + 1 if (index - start) % 2 == 0 else index - 1
    return other if 0 <= other < count else None


def swap_pairs(row_count, col_count, row_start, col_start):
    pairs = []
    for r in range(row_count):
        for c in range(col_count):
            pr, pc = (partner(r, row_start, row_count), partner(c, col_start, col_count))
            if pr is None:
                pr, pc = (r, c ^ 1)
            elif pc is None:
                pr, pc = (r ^ 1 if row_start is None else pr, c)
            pairs.append((r * col_count + c, pr * col_count + pc))
    return pairs


def exchange(strips, row_count, col_count):
    return [
        lax.ppermute(strip, ("row", "col"), swap_pairs(row_count, col_count, rs, cs))
        for strip, (rs, cs) in zip(strips, combos(row_count))
    ]


class Place:
    def __init__(self, row_count, col_count):
        row, col = (lax.axis_index("row"), lax.axis_index("col"))
        self.even_row, self.even_col = (lax.rem(row, 2) == 0, lax.rem(col, 2) == 0)
        self.has = {
            "above": row > 0,
            "below": row < row_count - 1,
            "left": col > 0,
            "right": col < col_count - 1,
        }
        self.row_count = row_count


def write_strips(place, outs, takes):
    for out, (rs, cs) in zip(outs, combos(place.row_count)):
        at = 0
        for take, radius, rows, cols in takes:
            row_sets = [slice(0, rows)] * 2
            col_sets = [slice(0, cols)] * 2
            if rs is not None:
                row_sets = [slice(rows - radius, rows), slice(0, radius)]
                if rs == 1:
                    row_sets = row_sets[::-1]
            if cs is not None:
                col_sets = [slice(cols - SIDE, cols), slice(0, SIDE)]
                if cs == 1:
                    col_sets = col_sets[::-1]
            count = row_sets[0].stop - row_sets[0].start
            for i in range(count):
                parts = {}
                for er in (0, 1):
                    for ec in (0, 1):
                        key = (row_sets[er].start + i, col_sets[ec].start, col_sets[ec].stop)
                        if key not in parts:
                            parts[key] = take(*key)
                        parts[er, ec] = parts[key]
                if cs is None:
                    pick = [parts[0, 0], parts[1, 0]]
                else:
                    pick = [jnp.where(place.even_col, parts[e, 0], parts[e, 1]) for e in (0, 1)]
                value = pick[0] if rs is None else jnp.where(place.even_row, pick[0], pick[1])
                out[at + i] = value.astype(out.dtype)
            at += count


def strip_shapes(row_count, rows, cols, channels, radii):
    shapes = []
    for rs, cs in combos(row_count):
        height = sum(rows if rs is None else radius for radius in radii)
        shapes.append((height, cols if cs is None else SIDE, channels))
    return shapes


def received(place, strips, row_sections):
    table = dict(zip(combos(place.row_count), strips))
    full_start, band_start = row_sections

    def along(rs, cs, i):
        return table[rs, cs][(full_start if rs is None else band_start) + i].astype(f32)

    def column(rs, side, i):
        if side is None:
            return along(rs, None, i)
        near, far = (along(rs, 0, i), along(rs, 1, i))
        if side == "left":
            return jnp.where(place.even_col, far, near)
        return jnp.where(place.even_col, near, far)

    def read(vertical, side, i):
        if vertical is None:
            value = column(None, side, i)
        elif place.row_count == 2:
            value = column(0, side, i)
        else:
            near, far = (column(0, side, i), column(1, side, i))
            if vertical == "above":
                value = jnp.where(place.even_row, far, near)
            else:
                value = jnp.where(place.even_row, near, far)
        if vertical is not None:
            value = jnp.where(place.has[vertical], value, 0.0)
        if side is not None:
            value = jnp.where(place.has[side], value, 0.0)
        return value

    return read


def assemble(place, target, own, read, radius, rows, cols, channels):
    width = cols + 2 * SIDE
    target[...] = jnp.zeros(target.shape, f32)
    for vertical, start, count in (("above", 0, radius), (None, radius, rows), ("below", radius + rows, radius)):
        for i in range(count):
            base = (start + i) * width
            middle = own(i) if vertical is None else read(vertical, None, i)
            target[base + SIDE : base + SIDE + cols, 0:channels] = middle
            target[base : base + SIDE, 0:channels] = read(vertical, "left", i)
            target[base + SIDE + cols : base + width, 0:channels] = read(vertical, "right", i)


def spread_taps(kernel_ref, layer, target):
    size, channels = (kernel_ref.shape[0], kernel_ref.shape[3])
    target[...] = jnp.zeros(target.shape, f32)
    for a in range(size):
        for b in range(size):
            t = a * size + b
            row = kernel_ref[a, b, layer : layer + 1, :]
            target[t * 8 : t * 8 + 8, 0:channels] = jnp.broadcast_to(row, (8, channels))


def conv_group(src, base, stride, rows_out, taps, size, flipped=False):
    total = [None] * rows_out
    for b in range(size):
        order = [a * size + b for a in range(size)]
        if flipped:
            order = [size * size - 1 - t for t in order]
        weights = [taps[t * 8 : t * 8 + 8, :] for t in order]
        for i in range(rows_out + size - 1):
            x = src[pl.ds(base + i * stride + b, 8), :]
            for a in range(size):
                r = i - a
                if 0 <= r < rows_out:
                    term = x * weights[a]
                    total[r] = term if total[r] is None else total[r] + term
    return total


def kernel_sums(src, src_base, src_stride, grad, grad_base, grad_stride, rows, cols, size, sums):
    sums[...] = jnp.zeros(sums.shape, f32)

    def group(g, carry):
        at = pl.multiple_of(g * 8, 8)
        grads = [grad[pl.ds(grad_base + i * grad_stride + at, 8), :] for i in range(rows)]
        for b in range(size):
            total = [None] * size
            for i in range(rows + size - 1):
                x = src[pl.ds(src_base + i * src_stride + at + b, 8), :]
                for a in range(size):
                    r = i - a
                    if 0 <= r < rows:
                        term = x * grads[r]
                        total[a] = term if total[a] is None else total[a] + term
            for a in range(size):
                t = (a * size + b) * 8
                sums[t : t + 8, :] += total[a]
        return carry

    lax.fori_loop(0, cols // 8, group, 0)


def lane_total(x):
    high = x.astype(bf16)
    low = (x - high.astype(f32)).astype(bf16)
    both = jnp.concatenate([high, low], axis=1)
    ones = jnp.ones((2 * LANES, LANES), bf16)
    return jnp.dot(both, ones, preferred_element_type=f32)


def layer_norm(conv, channels):
    lane = lax.broadcasted_iota(jnp.int32, conv.shape, 1)
    centred = jnp.where(lane < channels, conv - lane_total(conv) * (1.0 / channels), 0.0)
    variance = lane_total(centred * centred) * (1.0 / channels)
    inverse = lax.rsqrt(variance + epsilon)
    return (centred * inverse, inverse)


def norm_backward(normed_grad, unit, inverse, gain, channels):
    m = normed_grad * gain
    mean = lane_total(m) * (1.0 / channels)
    along = lane_total(m * unit) * (1.0 / channels)
    lane = lax.broadcasted_iota(jnp.int32, m.shape, 1)
    return jnp.where(lane < channels, inverse * (m - mean - unit * along), 0.0)


def gelu_parts(v):
    t = 1.0 / (1.0 + (0.3275911 * inv_sqrt_two) * jnp.abs(v))
    bell = jnp.exp(-0.5 * v * v)
    series = 0.5 * 1.061405429 * t + 0.5 * -1.453152027
    series = series * t + 0.5 * 1.421413741
    series = series * t + 0.5 * -0.284496736
    series = series * t + 0.5 * 0.254829592
    tail = series * t * bell
    cdf = jnp.where(v >= 0.0, 1.0 - tail, tail)
    return (v * cdf, cdf + v * (bell * inv_sqrt_two_pi))


def dot(x, w):
    return jnp.dot(x, w, preferred_element_type=f32)


def dot_leading(x, y):
    return lax.dot_general(x, y, (((0,), (0,)), ((), ())), preferred_element_type=f32)


def pad_lanes(x):
    rows, channels = x.shape
    return jnp.concatenate([x, jnp.zeros((rows, LANES - channels), x.dtype)], axis=1)


def load_weights(up_ref, down_t_ref, layer, up, down, up_t, down_t):
    channels, units = up_ref.shape[1:]
    blank = jnp.zeros((LANES - channels, units), f32)
    up_f = jnp.concatenate([up_ref[layer].astype(f32), blank], axis=0)
    down_f = jnp.concatenate([down_t_ref[layer].astype(f32), blank], axis=0)
    up[layer] = up_f.astype(bf16)
    down_t[layer] = down_f.astype(bf16)
    up_t[layer] = up_f.T.astype(bf16)
    down[layer] = down_f.T.astype(bf16)


def round16(x):
    return x.astype(bf16).astype(f32)


def fetch(sources, targets, sems):
    copies = [pltpu.make_async_copy(a, b, sems.at[i]) for i, (a, b) in enumerate(zip(sources, targets))]
    for copy in copies:
        copy.start()
    for copy in copies:
        copy.wait()


def strips_kernel(dims, image_in, cot_in, image, cot, *refs):
    outs, sems = (refs[:-1], refs[-1])
    place = Place(dims.row_count, dims.col_count)
    fetch((image_in, cot_in), (image, cot), sems)

    def take(ref):
        return lambda i, lo, hi: ref[i].astype(f32)[lo:hi]

    write_strips(
        place,
        outs,
        [(take(image), 2 * dims.h, dims.rows, dims.cols), (take(cot), dims.h, dims.rows, dims.cols)],
    )


def weights_kernel(up_in, down_t_in, kernels_in, gains_in, up, down, up_t, down_t, taps0, taps1, gains, *refs):
    up_w, down_w, kernels, sems = refs
    fetch((up_in, down_t_in, kernels_in, gains_in), (up_w, down_w, kernels, gains), sems)
    spread_taps(kernels, 0, taps0)
    spread_taps(kernels, 1, taps1)
    for layer in range(2):
        load_weights(up_w, down_w, layer, up, down, up_t, down_t)


def first_kernel(dims, *refs):
    count = len(combos(dims.row_count))
    image, cot, taps0, taps1, gains, up, down, up_t, down_t = refs[:9]
    strips = refs[9 : 9 + count]
    refs = refs[9 + count :]
    (output, x0, x1, unit0, inv0, hidden0, slope0, grad1, normed1, pre_grad1, hidden1, gain_sum) = refs[:12]
    outs = refs[12 : 12 + count]
    (conv,) = refs[12 + count :]
    place = Place(dims.row_count, dims.col_count)
    rows, cols, channels, h, size = (dims.rows, dims.cols, dims.channels, dims.h, dims.size)
    ext_rows, ext_cols, wide = (dims.ext_rows, dims.ext_cols, dims.wide)
    skip = dims.skipped_rows(place)
    read = received(place, strips, (0, 0))
    assemble(place, x0, lambda i: image[i].astype(f32), read, 2 * h, rows, cols, channels)

    x1[...] = jnp.zeros(x1.shape, f32)
    if dims.ext_pad > ext_rows * ext_cols:
        conv[ext_rows * ext_cols :, :] = jnp.zeros((dims.ext_pad - ext_rows * ext_cols, LANES), f32)
    frame = pl.multiple_of(skip * ext_cols, 8)

    def conv0(g, carry):
        at = pl.multiple_of(g * 8, 8)
        base = pl.multiple_of(skip * wide, 8) + at
        total = conv_group(x0, base + 1, wide, ext_rows, taps0, size)
        for r in range(ext_rows):
            conv[pl.ds(r * ext_cols + at, 8), :] = total[r]
            x1[pl.ds(frame + r * ext_cols + at, 8), :] = x0[pl.ds(base + (r + h) * wide + 4, 8), :]
        return carry

    lax.fori_loop(0, ext_cols // 8, conv0, 0)
    gain = pad_lanes(gains[0:1, :])
    step = dims.ext_step

    def mix0(k, carry):
        px = pl.ds(pl.multiple_of(k * step, 16), step)
        px_frame = pl.ds(frame + pl.multiple_of(k * step, 16), step)
        unit, inverse = layer_norm(conv[px, :], channels)
        unit0[px, :] = unit.astype(bf16)
        inv0[px, :] = inverse
        pre = dot((unit * gain).astype(bf16), up[0])
        value, slope = gelu_parts(pre)
        hidden = value.astype(bf16)
        hidden0[px, :] = hidden
        slope0[px, :] = slope.astype(bf16)
        x1[px_frame, :] = round16(x1[px_frame, :] + dot(hidden, down[0]))
        return carry

    lax.fori_loop(0, dims.ext_pad // step, mix0, 0)
    clear_outside(place, x1, dims)

    def conv1(g, carry):
        at = pl.multiple_of(g * 8, 8)
        total = conv_group(x1, at + 1, ext_cols, rows, taps1, size)
        for r in range(rows):
            conv[pl.ds(r * cols + at, 8), :] = total[r]
        return carry

    lax.fori_loop(0, cols // 8, conv1, 0)
    gain1 = pad_lanes(gains[1:2, :])
    gain_sum[...] = jnp.zeros(gain_sum.shape, f32)
    lines = dims.line_step
    step1 = lines * cols

    def mix1(k, carry):
        px = pl.ds(pl.multiple_of(k * step1, step1), step1)
        unit, inverse = layer_norm(conv[px, :], channels)
        normed = (unit * gain1).astype(bf16)
        normed1[px, :] = normed
        value, slope = gelu_parts(dot(normed, up[1]))
        hidden = value.astype(bf16)
        hidden1[px, :] = hidden
        branch = dot(hidden, down[1])
        for i in range(lines):
            start = (k * lines + i + h) * ext_cols + 4
            line = x1[pl.ds(start, cols), :] + branch[i * cols : (i + 1) * cols]
            output[k * lines + i] = line[:, :channels].astype(bf16)
        upstream = pad_lanes(cot[pl.ds(k * lines, lines)].reshape(step1, channels))
        pre_grad = (dot(upstream, down_t[1]) * slope).astype(bf16)
        pre_grad1[px, :] = pre_grad
        normed_grad = dot(pre_grad, up_t[1])
        product = normed_grad * unit
        gain_sum[...] += jnp.sum(product.reshape(step1 // 8, 8, LANES), axis=0)
        grad1[px, :] = round16(norm_backward(normed_grad, unit, inverse, gain1, channels))
        return carry

    lax.fori_loop(0, rows // lines, mix1, 0)

    def take(i, lo, hi):
        return grad1[i * cols + lo : i * cols + hi, 0:channels]

    write_strips(place, outs, [(take, 2 * h, rows, cols)])


def clear_outside(place, flat, dims):
    h, frame_rows, ext_cols = (dims.h, dims.rows + 2 * dims.h, dims.ext_cols)
    margin = (ext_cols - dims.cols) // 2

    @pl.when(jnp.logical_not(place.has["above"]))
    def _():
        flat[0 : h * ext_cols, :] = jnp.zeros((h * ext_cols, LANES), f32)

    @pl.when(jnp.logical_not(place.has["below"]))
    def _():
        last = (frame_rows - h) * ext_cols
        flat[last:, :] = jnp.zeros((flat.shape[0] - last, LANES), f32)

    @pl.when(jnp.logical_not(place.has["left"]))
    def _():
        for r in range(frame_rows):
            flat[r * ext_cols : r * ext_cols + margin, :] = jnp.zeros((margin, LANES), f32)

    @pl.when(jnp.logical_not(place.has["right"]))
    def _():
        for r in range(frame_rows):
            flat[(r + 1) * ext_cols - margin : (r + 1) * ext_cols, :] = jnp.zeros((margin, LANES), f32)


def sums_kernel(dims, x1, grad1, normed1, pre_grad1, hidden1, cot, gain_part, taps_sum, up_sum, down_sum, sums):
    kernel_sums(x1, 1, dims.ext_cols, grad1, 0, dims.cols, dims.rows, dims.cols, dims.size, sums)
    store_sums(dims, sums, gain_part[...], taps_sum)
    upstream = pad_lanes(cot[...].reshape(dims.rows * dims.cols, dims.channels))
    up_sum[...] = dot_leading(normed1[...], pre_grad1[...]).T
    down_sum[...] = dot_leading(upstream, hidden1[...]).T


def store_sums(dims, sums, gain_part, target):
    taps = dims.size * dims.size
    target[...] = jnp.zeros(target.shape, f32)
    for t in range(taps):
        target[t : t + 1, :] = jnp.sum(sums[t * 8 : t * 8 + 8, :], axis=0, keepdims=True)
    target[taps : taps + 1, :] = jnp.sum(gain_part, axis=0, keepdims=True)


def third_kernel(dims, *refs):
    count = len(combos(dims.row_count))
    (grad1, cot, taps1, gains, up_t, down_t, x0, unit0, inv0, hidden0, slope0) = refs[:11]
    (taps_sum1, up_sum1, down_sum1) = refs[11:14]
    strips = refs[14 : 14 + count]
    cot_strips = refs[14 + count : 14 + 2 * count]
    (grad0, middle, keep, small_keep, send) = refs[14 + 2 * count : 19 + 2 * count]
    (wide_grad, cot_frame, upstream, own, sums, up_acc, down_acc, gain_sum, small, tall, slabs) = refs[19 + 2 * count :]
    place = Place(dims.row_count, dims.col_count)
    rows, cols, channels, h, size = (dims.rows, dims.cols, dims.channels, dims.h, dims.size)
    ext_rows, ext_cols, wide = (dims.ext_rows, dims.ext_cols, dims.wide)
    skip = dims.skipped_rows(place)
    read = received(place, strips, (0, 0))
    assemble(
        place, wide_grad, lambda i: grad1[i * cols : (i + 1) * cols, 0:channels], read, 2 * h, rows, cols, channels
    )
    read_cot = received(place, cot_strips, (rows, 2 * h))
    margin = (ext_cols - cols) // 2
    cot_frame[...] = jnp.zeros(cot_frame.shape, f32)
    for vertical, start, n in (("above", 0, h), (None, h, rows), ("below", h + rows, h)):
        for i in range(n):
            base = (start + i) * ext_cols
            line = cot[i].astype(f32) if vertical is None else read_cot(vertical, None, i)
            cot_frame[base + margin : base + margin + cols, 0:channels] = line
            cot_frame[base : base + margin, 0:channels] = read_cot(vertical, "left", i)[SIDE - margin :]
            cot_frame[base + margin + cols : base + ext_cols, 0:channels] = read_cot(vertical, "right", i)[:margin]

    used = ext_rows * ext_cols
    if dims.ext_pad > used:
        upstream[used:, :] = jnp.zeros((dims.ext_pad - used, LANES), f32)
        own[used:, :] = jnp.zeros((dims.ext_pad - used, LANES), f32)
    grad0[...] = jnp.zeros(grad0.shape, f32)
    frame = pl.multiple_of(skip * ext_cols, 8)

    def conv1(g, carry):
        at = pl.multiple_of(g * 8, 8)
        total = conv_group(wide_grad, pl.multiple_of(skip * wide, 8) + at + 1, wide, ext_rows, taps1, size, True)
        col = lax.broadcasted_iota(jnp.int32, (8, LANES), 0) + (at - margin)
        inside = jnp.where(jnp.logical_and(col >= 0, col < cols), 1.0, 0.0)
        for r in range(ext_rows):
            px = pl.ds(r * ext_cols + at, 8)
            upstream[px, :] = cot_frame[pl.ds(frame + r * ext_cols + at, 8), :] + total[r]
            mine = jnp.logical_and(r + skip >= h, r + skip < h + rows)
            own[px, :] = jnp.where(mine, inside, 0.0)
        return carry

    lax.fori_loop(0, ext_cols // 8, conv1, 0)
    for i in range(rows):
        line = upstream[pl.ds((i + h - skip) * ext_cols + margin, cols), :]
        middle[i * cols : (i + 1) * cols, :] = round16(line)

    gain = pad_lanes(gains[0:1, :])
    gain_sum[...] = jnp.zeros(gain_sum.shape, f32)
    up_acc[...] = jnp.zeros(up_acc.shape, f32)
    down_acc[...] = jnp.zeros(down_acc.shape, f32)
    step = dims.ext_step

    def mix0(k, carry):
        px = pl.ds(pl.multiple_of(k * step, 16), step)
        flow = upstream[px, :].astype(bf16)
        mine = own[px, :]
        unit = unit0[px, :].astype(f32)
        pre_grad = (dot(flow, down_t[0]) * slope0[px, :].astype(f32)).astype(bf16)
        normed_grad = dot(pre_grad, up_t[0])
        normed = (unit * gain * mine).astype(bf16)
        up_acc[...] += dot_leading(normed, pre_grad)
        down_acc[...] += dot_leading(flow * mine.astype(bf16), hidden0[px, :])
        product = normed_grad * unit * mine
        gain_sum[...] += jnp.sum(product.reshape(step // 8, 8, LANES), axis=0)
        px_frame = pl.ds(frame + pl.multiple_of(k * step, 16), step)
        grad0[px_frame, :] = round16(norm_backward(normed_grad, unit, inv0[px, :], gain, channels))
        return carry

    lax.fori_loop(0, dims.ext_pad // step, mix0, 0)
    clear_outside(place, grad0, dims)
    kernel_sums(
        x0, h * wide + SIDE - h, wide, grad0, h * ext_cols + margin, ext_cols, rows, cols, size, sums
    )
    store_sums(dims, sums, gain_sum[...], small)

    taps_rows = size * size + 1
    merged = jnp.concatenate([small[0:taps_rows, :], taps_sum1[0:taps_rows, :]], axis=0) * dims.factor
    merged = jnp.concatenate([merged, jnp.zeros((dims.small_rows - 2 * taps_rows, LANES), f32)], axis=0)
    merged = merged.astype(bf16)
    small_keep[...] = merged.astype(f32)

    layer_rows, part, half = (dims.layer_rows, dims.part, dims.half)
    units = up_acc.shape[1]
    up0 = up_acc[...].T * dims.factor
    down0 = down_acc[...].T * dims.factor
    up1 = up_sum1[...] * dims.factor
    down1 = down_sum1[...] * dims.factor
    lane = lax.broadcasted_iota(jnp.int32, (units, LANES), 1)
    slab_rows = 2 * layer_rows
    for r in range(dims.row_count):
        for layer, (u, d) in enumerate(((up0, down0), (up1, down1))):
            first = pltpu.roll(u, LANES - r * half, 1) if r else u
            shift = (half - r * half) % LANES
            second = pltpu.roll(d, shift, 1) if shift else d
            joined = jnp.where(lane < half, first, jnp.where(lane < 2 * half, second, 0.0))
            tall[layer * (units + 8) : layer * (units + 8) + units, :] = joined

        def slab(c, carry, r=r):
            index = 0
            for j, (axis, bit) in enumerate(dims.stages):
                value = (r >> bit) & 1 if axis == "row" else lax.rem(lax.div(c, 1 << bit), 2)
                index = index + value * (1 << (len(dims.stages) - 1 - j))
            for layer in range(2):
                to = pl.multiple_of(index * slab_rows + layer * layer_rows, 8)
                slabs[pl.ds(to, layer_rows), :] = tall[pl.ds(layer * (units + 8) + c * part, layer_rows), :]
            return carry

        lax.fori_loop(0, dims.col_count, slab, 0)

    split(dims, place, 0, slabs, merged, keep, send)


def split(dims, place, stage, slabs, merged, keep, send):
    count = slabs.shape[0] // 2
    axis, bit = dims.stages[stage]
    mine = lax.rem(lax.div(lax.axis_index(axis), 1 << bit), 2)
    keep[...] = slabs[pl.ds(pl.multiple_of(mine * count, 16), count), :]
    send[0:count, :] = slabs[pl.ds(pl.multiple_of((1 - mine) * count, 16), count), :].astype(bf16)
    send[count:, :] = merged


def stage_kernel(dims, stage, keep, small, got, keep_out, small_out, send, total):
    place = Place(dims.row_count, dims.col_count)
    count = keep.shape[0]
    total[...] = keep[...] + got[0:count, :].astype(f32)
    merged = (small[...] + got[count:, :].astype(f32)).astype(bf16)
    small_out[...] = merged.astype(f32)
    split(dims, place, stage, total, merged, keep_out, send)


def last_kernel(dims, keep, small, got, kernel_out, gain_out, up_out, down_out):
    count = keep.shape[0]
    total = keep[...] + got[0:count, :].astype(f32)
    merged = small[...] + got[count:, :].astype(f32)
    size, channels, half, part = (dims.size, dims.channels, dims.half, dims.part)
    for layer in range(2):
        block = total[layer * dims.layer_rows : layer * dims.layer_rows + part]
        up_out[layer] = block[:, :half]
        down_out[layer] = block[:, half : 2 * half]
        for t in range(size * size + 1):
            at = layer * (size * size + 1) + t
            row = merged[at : at + 1, 0:channels]
            if t < size * size:
                kernel_out[t // size, t % size, layer : layer + 1, :] = row
            else:
                gain_out[layer : layer + 1, :] = row


def image_kernel(dims, grad0, middle, taps0, out, work):
    rows, cols, size = (dims.rows, dims.cols, dims.size)

    def conv0(g, carry):
        at = pl.multiple_of(g * 8, 8)
        total = conv_group(grad0, at + 1, dims.ext_cols, rows, taps0, size, True)
        for r in range(rows):
            work[pl.ds(r * cols + at, 8), :] = middle[pl.ds(r * cols + at, 8), :] + total[r]
        return carry

    lax.fori_loop(0, cols // 8, conv0, 0)
    for r in range(rows):
        out[r] = work[r * cols : (r + 1) * cols, 0 : dims.channels].astype(bf16)


class Dims:
    def skipped_rows(self, place):
        if self.row_count > 2:
            return 0
        return jnp.where(place.has["above"], 0, self.h)


def dims_of(image, kernels, up_weights):
    d = Dims()
    d.row_count, d.col_count = (lax.axis_size("row"), lax.axis_size("col"))
    d.rows, d.cols, d.channels = image.shape
    d.size = kernels.shape[1]
    d.h = d.size // 2
    d.ext_rows, d.ext_cols = (d.rows + (d.h if d.row_count == 2 else 2 * d.h), d.cols + 8)
    d.wide = d.cols + 2 * SIDE
    d.ext_pad = -(-d.ext_rows * d.ext_cols // 16) * 16
    d.ext_step = max(s for s in range(16, 700, 16) if d.ext_pad % s == 0)
    d.line_step = 4
    d.half = d.channels // d.row_count
    d.part = up_weights.shape[2] // d.col_count
    d.layer_rows = ceil8(d.part)
    d.count = d.row_count * d.col_count
    d.small_rows = -(-2 * (d.size * d.size + 1) // 16) * 16
    d.factor = 1.0 / math.sqrt(d.rows * d.cols * d.count)
    row_bits, col_bits = (d.row_count.bit_length() - 1, d.col_count.bit_length() - 1)
    d.stages = [("col", 0)] + [("row", b) for b in range(row_bits)] + [("col", b) for b in range(1, col_bits)]
    return d


def halving_pairs(d, stage):
    axis, bit = d.stages[stage]
    pairs = []
    for r in range(d.row_count):
        for c in range(d.col_count):
            pr, pc = (r ^ (1 << bit), c) if axis == "row" else (r, c ^ (1 << bit))
            pairs.append((r * d.col_count + c, pr * d.col_count + pc))
    return pairs


def run(kernel, outs, scratch, *args, in_hbm=0, sems=0, busy_us=1):
    shapes = [jax.ShapeDtypeStruct(shape, kind) for shape, kind in outs]
    space = pl.BlockSpec(memory_space=pltpu.VMEM)
    far = pl.BlockSpec(memory_space=pltpu.HBM)
    held = [pltpu.VMEM(shape, kind) for shape, kind in scratch]
    if sems:
        held.append(pltpu.SemaphoreType.DMA((sems,)))
    return pl.pallas_call(
        kernel,
        out_shape=shapes,
        in_specs=[far] * in_hbm + [space] * (len(args) - in_hbm),
        out_specs=[space] * len(shapes),
        scratch_shapes=held,
        compiler_params=pltpu.CompilerParams(vmem_limit_bytes=32 * 1024 * 1024),
        cost_estimate=pl.CostEstimate(flops=int(busy_us * 1e9), bytes_accessed=1 << 18, transcendentals=0),
    )(*args)


def per_device(image, kernels, gains, up_weights, down_weights, cotangent):
    d = dims_of(image, kernels, up_weights)
    bind = functools.partial
    rows, cols, channels = image.shape
    units = up_weights.shape[2]
    tile, ext, wide = (rows * cols, d.ext_pad, (rows + 4 * d.h) * d.wide)
    frame = (rows + 2 * d.h) * d.ext_cols + 16
    taps = ((d.size * d.size * 8, LANES), f32)
    sums_rows = ceil8(d.size * d.size + 1)

    shapes = strip_shapes(d.row_count, rows, cols, channels, (2 * d.h, d.h))
    image, cot, *strips = run(
        bind(strips_kernel, d),
        [(image.shape, bf16), (image.shape, bf16)] + [(s, bf16) for s in shapes],
        [],
        image,
        cotangent,
        in_hbm=2,
        sems=2,
    )
    strips = exchange(strips, d.row_count, d.col_count)
    up, down, up_t, down_t, taps0, taps1, gains = run(
        weights_kernel,
        [
            ((2, LANES, units), bf16),
            ((2, units, LANES), bf16),
            ((2, units, LANES), bf16),
            ((2, LANES, units), bf16),
            taps,
            taps,
            (gains.shape, f32),
        ],
        [((2, channels, units), bf16), ((2, channels, units), bf16), ((d.size, d.size, 2, channels), f32)],
        up_weights,
        jnp.swapaxes(down_weights, 1, 2),
        jnp.transpose(kernels, (1, 2, 0, 3)),
        gains,
        in_hbm=4,
        sems=4,
        busy_us=2,
    )

    grad_shapes = strip_shapes(d.row_count, rows, cols, channels, (2 * d.h,))
    first = run(
        bind(first_kernel, d),
        [
            (image.shape, bf16),
            ((wide, LANES), f32),
            ((frame, LANES), f32),
            ((ext, LANES), bf16),
            ((ext, LANES), f32),
            ((ext, units), bf16),
            ((ext, units), bf16),
            ((tile, LANES), f32),
            ((tile, LANES), bf16),
            ((tile, units), bf16),
            ((tile, units), bf16),
            ((8, LANES), f32),
        ]
        + [(s, bf16) for s in grad_shapes],
        [((ext, LANES), f32)],
        image,
        cot,
        taps0,
        taps1,
        gains,
        up,
        down,
        up_t,
        down_t,
        *strips,
        busy_us=15,
    )
    (output, x0, x1, unit0, inv0, hidden0, slope0, grad1, normed1, pre_grad1, hidden1, gain_part) = first[:12]
    grad_strips = exchange(first[12:], d.row_count, d.col_count)

    taps_sum1, up_sum1, down_sum1 = run(
        bind(sums_kernel, d),
        [((sums_rows, LANES), f32), ((units, LANES), f32), ((units, LANES), f32)],
        [taps],
        x1,
        grad1,
        normed1,
        pre_grad1,
        hidden1,
        cot,
        gain_part,
        busy_us=3,
    )

    held = d.count // 2 * 2 * d.layer_rows
    small = ((d.small_rows, LANES), f32)
    grad0, middle, keep, sums, send = run(
        bind(third_kernel, d),
        [((frame, LANES), f32), ((tile, LANES), f32), ((held, LANES), f32), small, ((held + d.small_rows, LANES), bf16)],
        [
            ((wide, LANES), f32),
            ((frame, LANES), f32),
            ((ext, LANES), f32),
            ((ext, LANES), f32),
            taps,
            ((LANES, units), f32),
            ((LANES, units), f32),
            ((8, LANES), f32),
            ((sums_rows, LANES), f32),
            ((2 * (units + 8), LANES), f32),
            ((2 * held, LANES), f32),
        ],
        grad1,
        cot,
        taps1,
        gains,
        up_t,
        down_t,
        x0,
        unit0,
        inv0,
        hidden0,
        slope0,
        taps_sum1,
        up_sum1,
        down_sum1,
        *grad_strips,
        *strips,
        busy_us=12,
    )
    (gradient,) = run(
        bind(image_kernel, d), [(image.shape, bf16)], [((tile, LANES), f32)], grad0, middle, taps0, busy_us=3
    )
    axes = ("row", "col")
    for stage in range(len(d.stages)):
        got = lax.ppermute(send, axes, halving_pairs(d, stage))
        if stage + 1 < len(d.stages):
            held //= 2
            keep, sums, send = run(
                bind(stage_kernel, d, stage + 1),
                [((held, LANES), f32), small, ((held + d.small_rows, LANES), bf16)],
                [((2 * held, LANES), f32)],
                keep,
                sums,
                got,
            )
    kernel_out, gain_out, up_out, down_out = run(
        bind(last_kernel, d),
        [
            ((d.size, d.size, 2, channels), f32),
            (gains.shape, f32),
            ((2, d.part, d.half), f32),
            ((2, d.part, d.half), f32),
        ],
        [],
        keep,
        sums,
        got,
    )
    kernel_out = jnp.transpose(kernel_out, (2, 0, 1, 3))
    return (output, gradient, kernel_out, gain_out, jnp.swapaxes(up_out, 1, 2), down_out)


def solution(mesh):
    placed = (P("row", "col", None), P(), P(), P(), P(), P("row", "col", None))
    return jax.shard_map(
        per_device,
        mesh=mesh,
        in_specs=placed,
        out_specs=(
            P("row", "col", None),
            P("row", "col", None),
            P(),
            P(),
            P(None, "row", "col"),
            P(None, "col", "row"),
        ),
        check_vma=False,
    )
```

```python
import functools
import math

import jax
import jax.numpy as jnp
from jax import lax
from jax.experimental import pallas as pl
from jax.experimental.pallas import tpu as pltpu
from jax.sharding import PartitionSpec as P

epsilon = 1e-06
inv_sqrt_two = 0.7071067811865476
inv_sqrt_two_pi = 0.3989422804014327
log2_e = 1.4426950408889634
LANES = 128
SIDE = 8
f32, bf16 = (jnp.float32, jnp.bfloat16)


def ceil8(n):
    return -(-n // 8) * 8


def combos(row_count):
    listed = [(None, 0), (None, 1), (0, None), (0, 0), (0, 1)]
    if row_count > 2:
        listed += [(1, None), (1, 0), (1, 1)]
    return listed


def partner(index, start, count):
    if start is None:
        return index
    other = index + 1 if (index - start) % 2 == 0 else index - 1
    return other if 0 <= other < count else None


def swap_pairs(row_count, col_count, row_start, col_start):
    pairs = []
    for r in range(row_count):
        for c in range(col_count):
            pr, pc = (partner(r, row_start, row_count), partner(c, col_start, col_count))
            if pr is None:
                pr, pc = (r, c ^ 1)
            elif pc is None:
                pr, pc = (r ^ 1 if row_start is None else pr, c)
            pairs.append((r * col_count + c, pr * col_count + pc))
    return pairs


def exchange(bands, others, row_count, col_count):
    got = {}
    for strips, pairs in ((bands, band_combos(row_count)), (others, other_combos(row_count))):
        for strip, (rs, cs) in zip(strips, pairs):
            got[rs, cs] = lax.ppermute(strip, ("row", "col"), swap_pairs(row_count, col_count, rs, cs))
    return [got[pair] for pair in combos(row_count)]


class Place:
    def __init__(self, row_count, col_count):
        row, col = (lax.axis_index("row"), lax.axis_index("col"))
        self.even_row, self.even_col = (lax.rem(row, 2) == 0, lax.rem(col, 2) == 0)
        self.has = {
            "above": row > 0,
            "below": row < row_count - 1,
            "left": col > 0,
            "right": col < col_count - 1,
        }
        self.row_count = row_count


def band_combos(row_count):
    return [pair for pair in combos(row_count) if pair[1] is None]


def other_combos(row_count):
    return [pair for pair in combos(row_count) if pair[1] is not None]


def write_strips(place, outs, takes, pairs):
    for out, (rs, cs) in zip(outs, pairs):
        at = 0
        for take, radius, rows, cols in takes:
            row_sets = [slice(0, rows)] * 2
            col_sets = [slice(0, cols)] * 2
            if rs is not None:
                row_sets = [slice(rows - radius, rows), slice(0, radius)]
                if rs == 1:
                    row_sets = row_sets[::-1]
            if cs is not None:
                col_sets = [slice(cols - SIDE, cols), slice(0, SIDE)]
                if cs == 1:
                    col_sets = col_sets[::-1]
            count = row_sets[0].stop - row_sets[0].start
            for i in range(count):
                parts = {}
                for er in (0, 1):
                    for ec in (0, 1):
                        key = (row_sets[er].start + i, col_sets[ec].start, col_sets[ec].stop)
                        if key not in parts:
                            parts[key] = take(*key)
                        parts[er, ec] = parts[key]
                if cs is None:
                    pick = [parts[0, 0], parts[1, 0]]
                else:
                    pick = [jnp.where(place.even_col, parts[e, 0], parts[e, 1]) for e in (0, 1)]
                value = pick[0] if rs is None else jnp.where(place.even_row, pick[0], pick[1])
                out[at + i] = value.astype(out.dtype)
            at += count


def strip_shapes(pairs, rows, cols, channels, radii):
    shapes = []
    for rs, cs in pairs:
        height = sum(rows if rs is None else radius for radius in radii)
        shapes.append((height, cols if cs is None else SIDE, channels))
    return shapes


def received(place, strips, row_sections):
    table = dict(zip(combos(place.row_count), strips))
    full_start, band_start = row_sections

    def along(rs, cs, i):
        return table[rs, cs][(full_start if rs is None else band_start) + i].astype(f32)

    def column(rs, side, i):
        if side is None:
            return along(rs, None, i)
        near, far = (along(rs, 0, i), along(rs, 1, i))
        if side == "left":
            return jnp.where(place.even_col, far, near)
        return jnp.where(place.even_col, near, far)

    def read(vertical, side, i):
        if vertical is None:
            value = column(None, side, i)
        elif place.row_count == 2:
            value = column(0, side, i)
        else:
            near, far = (column(0, side, i), column(1, side, i))
            if vertical == "above":
                value = jnp.where(place.even_row, far, near)
            else:
                value = jnp.where(place.even_row, near, far)
        if vertical is not None:
            value = jnp.where(place.has[vertical], value, 0.0)
        if side is not None:
            value = jnp.where(place.has[side], value, 0.0)
        return value

    return read


def assemble(place, target, own, read, radius, rows, cols, channels):
    width = cols + 2 * SIDE
    target[...] = jnp.zeros(target.shape, f32)
    for vertical, start, count in (("above", 0, radius), (None, radius, rows), ("below", radius + rows, radius)):
        for i in range(count):
            base = (start + i) * width
            middle = own(i) if vertical is None else read(vertical, None, i)
            target[base + SIDE : base + SIDE + cols, 0:channels] = middle
            target[base : base + SIDE, 0:channels] = read(vertical, "left", i)
            target[base + SIDE + cols : base + width, 0:channels] = read(vertical, "right", i)


def spread_taps(kernel_ref, layer, target):
    size, channels = (kernel_ref.shape[0], kernel_ref.shape[3])
    for a in range(size):
        for b in range(size):
            t = a * size + b
            row = pad_lanes(kernel_ref[a, b, layer : layer + 1, :])
            target[t * 16 : t * 16 + 16, :] = jnp.broadcast_to(row, (16, LANES)).astype(bf16)


def tree_sum(terms):
    while len(terms) > 1:
        pairs = [terms[i] + terms[i + 1] for i in range(0, len(terms) - 1, 2)]
        terms = pairs + ([terms[-1]] if len(terms) % 2 else [])
    return terms[0]


def conv_group(src, base, stride, rows_out, taps, size, flipped=False):
    total = [None] * rows_out
    for b in range(size):
        order = [a * size + b for a in range(size)]
        if flipped:
            order = [size * size - 1 - t for t in order]
        weights = [taps[t * 16 : t * 16 + 16, :] for t in order]
        window = []
        for i in range(rows_out + size - 1):
            window.append(src[pl.ds(base + i * stride + b, 16), :].astype(bf16))
            r = i - size + 1
            if r >= 0:
                term = tree_sum([window[r + a] * weights[a] for a in range(size)]).astype(f32)
                total[r] = term if total[r] is None else total[r] + term
    return total


def group_start(g, cols):
    return pl.multiple_of(jnp.minimum(g * 16, cols - 16), 8)


def kernel_sums(src, src_base, src_stride, grad, grad_base, grad_stride, rows, cols, size, sums):
    sums[...] = jnp.zeros(sums.shape, f32)

    def group(g, carry):
        at = pl.multiple_of(g * 16, 16)
        grads = [grad[pl.ds(grad_base + i * grad_stride + at, 16), :].astype(bf16) for i in range(rows)]
        for b in range(size):
            lines = [
                src[pl.ds(src_base + i * src_stride + at + b, 16), :].astype(bf16) for i in range(rows + size - 1)
            ]
            for a in range(size):
                term = tree_sum([lines[r + a] * grads[r] for r in range(rows)]).astype(f32)
                t = (a * size + b) * 8
                sums[t : t + 8, :] += term[0:8] + term[8:16]
        return carry

    lax.fori_loop(0, cols // 16, group, 0)


def lane_total(x):
    high = x.astype(bf16)
    low = (x - high.astype(f32)).astype(bf16)
    both = jnp.concatenate([high, low], axis=1)
    ones = jnp.ones((2 * LANES, LANES), bf16)
    return jnp.dot(both, ones, preferred_element_type=f32)


def layer_norm(conv, channels):
    lane = lax.broadcasted_iota(jnp.int32, conv.shape, 1)
    centred = jnp.where(lane < channels, conv - lane_total(conv) * (1.0 / channels), 0.0)
    variance = lane_total(centred * centred) * (1.0 / channels)
    inverse = lax.rsqrt(variance + epsilon)
    return (centred * inverse, inverse)


def norm_backward(normed_grad, unit, inverse, gain, channels):
    m = normed_grad * gain
    mean = lane_total(m) * (1.0 / channels)
    along = lane_total(m * unit) * (1.0 / channels)
    lane = lax.broadcasted_iota(jnp.int32, m.shape, 1)
    return jnp.where(lane < channels, inverse * (m - mean - unit * along), 0.0)


def gelu_parts(v):
    d = 1.0 + (0.3275911 * inv_sqrt_two) * jnp.abs(v)
    t = pl.reciprocal(d, approx=True)
    t = t * (2.0 - d * t)
    bell = jnp.exp2(v * v * (-0.5 * log2_e))
    series = 0.5 * 1.061405429 * t + 0.5 * -1.453152027
    series = series * t + 0.5 * 1.421413741
    series = series * t + 0.5 * -0.284496736
    series = series * t + 0.5 * 0.254829592
    tail = series * t * bell
    cdf = jnp.where(v >= 0.0, 1.0 - tail, tail)
    return (v * cdf, cdf + v * (bell * inv_sqrt_two_pi))


def dot(x, w):
    return jnp.dot(x, w, preferred_element_type=f32)


def dot_leading(x, y):
    return lax.dot_general(x, y, (((0,), (0,)), ((), ())), preferred_element_type=f32)


def pad_lanes(x):
    rows, channels = x.shape
    return jnp.concatenate([x, jnp.zeros((rows, LANES - channels), x.dtype)], axis=1)


def load_weights(up_ref, down_t_ref, layer, up, down, up_t, down_t):
    channels, units = up_ref.shape[1:]
    blank = jnp.zeros((LANES - channels, units), f32)
    up_f = jnp.concatenate([up_ref[layer].astype(f32), blank], axis=0)
    down_f = jnp.concatenate([down_t_ref[layer].astype(f32), blank], axis=0)
    up[layer] = up_f.astype(bf16)
    down_t[layer] = down_f.astype(bf16)
    up_t[layer] = up_f.T.astype(bf16)
    down[layer] = down_f.T.astype(bf16)


def round16(x):
    return x.astype(bf16).astype(f32)


def fetch(sources, targets, sems):
    copies = [pltpu.make_async_copy(a, b, sems.at[i]) for i, (a, b) in enumerate(zip(sources, targets))]
    for copy in copies:
        copy.start()
    for copy in copies:
        copy.wait()


def image_take(ref):
    return lambda i, lo, hi: ref[i].astype(f32)[lo:hi]


def flat_take(ref, cols, channels):
    return lambda i, lo, hi: ref[i * cols + lo : i * cols + hi, 0:channels]


def bands_kernel(dims, image_in, image, *refs):
    outs, sems = (refs[:-1], refs[-1])
    place = Place(dims.row_count, dims.col_count)
    fetch((image_in,), (image,), sems)
    takes = [(image_take(image), 2 * dims.h, dims.rows, dims.cols)]
    write_strips(place, outs, takes, band_combos(dims.row_count))


def others_kernel(dims, image, *refs):
    outs = refs[len(band_combos(dims.row_count)) :]
    place = Place(dims.row_count, dims.col_count)
    takes = [(image_take(image), 2 * dims.h, dims.rows, dims.cols)]
    write_strips(place, outs, takes, other_combos(dims.row_count))


def grad_others_kernel(dims, grad1, cot, *refs):
    outs = refs[len(band_combos(dims.row_count)) :]
    place = Place(dims.row_count, dims.col_count)
    takes = [
        (flat_take(grad1, dims.cols, dims.channels), 2 * dims.h, dims.rows, dims.cols),
        (image_take(cot), dims.h, dims.rows, dims.cols),
    ]
    write_strips(place, outs, takes, other_combos(dims.row_count))


def weights_kernel(up_in, down_t_in, kernels_in, gains_in, up, down, up_t, down_t, taps0, taps1, gains, *refs):
    up_w, down_w, kernels, sems = refs
    fetch((up_in, down_t_in, kernels_in, gains_in), (up_w, down_w, kernels, gains), sems)
    spread_taps(kernels, 0, taps0)
    spread_taps(kernels, 1, taps1)
    for layer in range(2):
        load_weights(up_w, down_w, layer, up, down, up_t, down_t)


def first_kernel(dims, *refs):
    count = len(combos(dims.row_count))
    image, cot, taps0, taps1, gains, up, down, up_t, down_t = refs[:9]
    strips = refs[9 : 9 + count]
    refs = refs[9 + count :]
    (output, x0, x1, unit0, inv0, hidden0, slope0, grad1, normed1, pre_grad1, hidden1, gain_sum) = refs[:12]
    outs, conv = (refs[12:-1], refs[-1])
    place = Place(dims.row_count, dims.col_count)
    rows, cols, channels, h, size = (dims.rows, dims.cols, dims.channels, dims.h, dims.size)
    ext_rows, ext_cols, wide = (dims.ext_rows, dims.ext_cols, dims.wide)
    skip = dims.skipped_rows(place)
    read = received(place, strips, (0, 0))
    assemble(place, x0, lambda i: image[i].astype(f32), read, 2 * h, rows, cols, channels)

    x1[...] = jnp.zeros(x1.shape, f32)
    if dims.ext_pad > ext_rows * ext_cols:
        conv[ext_rows * ext_cols :, :] = jnp.zeros((dims.ext_pad - ext_rows * ext_cols, LANES), f32)
    frame = pl.multiple_of(skip * ext_cols, 8)

    def conv0(g, carry):
        at = group_start(g, ext_cols)
        base = pl.multiple_of(skip * wide, 8) + at
        total = conv_group(x0, base + 1, wide, ext_rows, taps0, size)
        for r in range(ext_rows):
            conv[pl.ds(r * ext_cols + at, 16), :] = total[r]
            x1[pl.ds(frame + r * ext_cols + at, 16), :] = x0[pl.ds(base + (r + h) * wide + 4, 16), :]
        return carry

    lax.fori_loop(0, -(-ext_cols // 16), conv0, 0)
    gain = pad_lanes(gains[0:1, :])
    step = dims.ext_step

    def mix0(k, carry):
        px = pl.ds(pl.multiple_of(k * step, 16), step)
        px_frame = pl.ds(frame + pl.multiple_of(k * step, 16), step)
        unit, inverse = layer_norm(conv[px, :], channels)
        unit0[px, :] = unit.astype(bf16)
        inv0[px, :] = inverse
        pre = dot((unit * gain).astype(bf16), up[0])
        value, slope = gelu_parts(pre)
        hidden = value.astype(bf16)
        hidden0[px, :] = hidden
        slope0[px, :] = slope.astype(bf16)
        x1[px_frame, :] = round16(x1[px_frame, :] + dot(hidden, down[0]))
        return carry

    lax.fori_loop(0, dims.ext_pad // step, mix0, 0)
    clear_outside(place, x1, dims)

    def conv1(g, carry):
        at = group_start(g, cols)
        total = conv_group(x1, at + 1, ext_cols, rows, taps1, size)
        for r in range(rows):
            conv[pl.ds(r * cols + at, 16), :] = total[r]
        return carry

    lax.fori_loop(0, -(-cols // 16), conv1, 0)
    gain1 = pad_lanes(gains[1:2, :])
    gain_sum[...] = jnp.zeros(gain_sum.shape, f32)
    lines = dims.line_step
    step1 = lines * cols

    def mix1(k, carry):
        px = pl.ds(pl.multiple_of(k * step1, step1), step1)
        unit, inverse = layer_norm(conv[px, :], channels)
        normed = (unit * gain1).astype(bf16)
        normed1[px, :] = normed
        value, slope = gelu_parts(dot(normed, up[1]))
        hidden = value.astype(bf16)
        hidden1[px, :] = hidden
        branch = dot(hidden, down[1])
        for i in range(lines):
            start = (k * lines + i + h) * ext_cols + 4
            line = x1[pl.ds(start, cols), :] + branch[i * cols : (i + 1) * cols]
            output[k * lines + i] = line[:, :channels].astype(bf16)
        upstream = pad_lanes(cot[pl.ds(k * lines, lines)].reshape(step1, channels))
        pre_grad = (dot(upstream, down_t[1]) * slope).astype(bf16)
        pre_grad1[px, :] = pre_grad
        normed_grad = dot(pre_grad, up_t[1])
        product = normed_grad * unit
        gain_sum[...] += jnp.sum(product.reshape(step1 // 8, 8, LANES), axis=0)
        grad1[px, :] = round16(norm_backward(normed_grad, unit, inverse, gain1, channels))
        return carry

    lax.fori_loop(0, rows // lines, mix1, 0)

    takes = [(flat_take(grad1, cols, channels), 2 * h, rows, cols), (image_take(cot), h, rows, cols)]
    write_strips(place, outs, takes, band_combos(dims.row_count))


def clear_outside(place, flat, dims):
    h, frame_rows, ext_cols = (dims.h, dims.rows + 2 * dims.h, dims.ext_cols)
    margin = (ext_cols - dims.cols) // 2

    @pl.when(jnp.logical_not(place.has["above"]))
    def _():
        flat[0 : h * ext_cols, :] = jnp.zeros((h * ext_cols, LANES), f32)

    @pl.when(jnp.logical_not(place.has["below"]))
    def _():
        last = (frame_rows - h) * ext_cols
        flat[last:, :] = jnp.zeros((flat.shape[0] - last, LANES), f32)

    @pl.when(jnp.logical_not(place.has["left"]))
    def _():
        for r in range(frame_rows):
            flat[r * ext_cols : r * ext_cols + margin, :] = jnp.zeros((margin, LANES), f32)

    @pl.when(jnp.logical_not(place.has["right"]))
    def _():
        for r in range(frame_rows):
            flat[(r + 1) * ext_cols - margin : (r + 1) * ext_cols, :] = jnp.zeros((margin, LANES), f32)


def sums_kernel(dims, x1, grad1, normed1, pre_grad1, hidden1, cot, gain_part, taps_sum, up_sum, down_sum, sums):
    kernel_sums(x1, 1, dims.ext_cols, grad1, 0, dims.cols, dims.rows, dims.cols, dims.size, sums)
    store_sums(dims, sums, gain_part[...], taps_sum)
    upstream = pad_lanes(cot[...].reshape(dims.rows * dims.cols, dims.channels))
    up_sum[...] = dot_leading(normed1[...], pre_grad1[...]).T
    down_sum[...] = dot_leading(upstream, hidden1[...]).T


def store_sums(dims, sums, gain_part, target):
    taps = dims.size * dims.size
    target[...] = jnp.zeros(target.shape, f32)
    for t in range(taps):
        target[t : t + 1, :] = jnp.sum(sums[t * 8 : t * 8 + 8, :], axis=0, keepdims=True)
    target[taps : taps + 1, :] = jnp.sum(gain_part, axis=0, keepdims=True)


def third_kernel(dims, *refs):
    count = len(combos(dims.row_count))
    (grad1, cot, taps1, gains, up_t, down_t, x0, unit0, inv0, hidden0, slope0) = refs[:11]
    (taps_sum1, up_sum1, down_sum1) = refs[11:14]
    strips = refs[14 : 14 + count]
    (grad0, middle, keep, small_keep, send) = refs[14 + count : 19 + count]
    (wide_grad, cot_frame, upstream, own, sums, up_acc, down_acc, gain_sum, small, tall, slabs) = refs[19 + count :]
    place = Place(dims.row_count, dims.col_count)
    rows, cols, channels, h, size = (dims.rows, dims.cols, dims.channels, dims.h, dims.size)
    ext_rows, ext_cols, wide = (dims.ext_rows, dims.ext_cols, dims.wide)
    skip = dims.skipped_rows(place)
    read = received(place, strips, (0, 0))
    assemble(
        place, wide_grad, lambda i: grad1[i * cols : (i + 1) * cols, 0:channels], read, 2 * h, rows, cols, channels
    )
    read_cot = received(place, strips, (rows, 2 * h))
    margin = (ext_cols - cols) // 2
    cot_frame[...] = jnp.zeros(cot_frame.shape, f32)
    for vertical, start, n in (("above", 0, h), (None, h, rows), ("below", h + rows, h)):
        for i in range(n):
            base = (start + i) * ext_cols
            line = cot[i].astype(f32) if vertical is None else read_cot(vertical, None, i)
            cot_frame[base + margin : base + margin + cols, 0:channels] = line
            cot_frame[base : base + margin, 0:channels] = read_cot(vertical, "left", i)[SIDE - margin :]
            cot_frame[base + margin + cols : base + ext_cols, 0:channels] = read_cot(vertical, "right", i)[:margin]

    used = ext_rows * ext_cols
    if dims.ext_pad > used:
        upstream[used:, :] = jnp.zeros((dims.ext_pad - used, LANES), f32)
        own[used:, :] = jnp.zeros((dims.ext_pad - used, LANES), f32)
    grad0[...] = jnp.zeros(grad0.shape, f32)
    frame = pl.multiple_of(skip * ext_cols, 8)

    def conv1(g, carry):
        at = group_start(g, ext_cols)
        total = conv_group(wide_grad, pl.multiple_of(skip * wide, 8) + at + 1, wide, ext_rows, taps1, size, True)
        col = lax.broadcasted_iota(jnp.int32, (16, LANES), 0) + (at - margin)
        inside = jnp.where(jnp.logical_and(col >= 0, col < cols), 1.0, 0.0)
        for r in range(ext_rows):
            px = pl.ds(r * ext_cols + at, 16)
            upstream[px, :] = cot_frame[pl.ds(frame + r * ext_cols + at, 16), :] + total[r]
            mine = jnp.logical_and(r + skip >= h, r + skip < h + rows)
            own[px, :] = jnp.where(mine, inside, 0.0)
        return carry

    lax.fori_loop(0, -(-ext_cols // 16), conv1, 0)
    for i in range(rows):
        line = upstream[pl.ds((i + h - skip) * ext_cols + margin, cols), :]
        middle[i * cols : (i + 1) * cols, :] = round16(line)

    gain = pad_lanes(gains[0:1, :])
    gain_sum[...] = jnp.zeros(gain_sum.shape, f32)
    up_acc[...] = jnp.zeros(up_acc.shape, f32)
    down_acc[...] = jnp.zeros(down_acc.shape, f32)
    step = dims.ext_step

    def mix0(k, carry):
        px = pl.ds(pl.multiple_of(k * step, 16), step)
        flow = upstream[px, :].astype(bf16)
        mine = own[px, :]
        unit = unit0[px, :].astype(f32)
        pre_grad = (dot(flow, down_t[0]) * slope0[px, :].astype(f32)).astype(bf16)
        normed_grad = dot(pre_grad, up_t[0])
        normed = (unit * gain * mine).astype(bf16)
        up_acc[...] += dot_leading(normed, pre_grad)
        down_acc[...] += dot_leading(flow * mine.astype(bf16), hidden0[px, :])
        product = normed_grad * unit * mine
        gain_sum[...] += jnp.sum(product.reshape(step // 8, 8, LANES), axis=0)
        px_frame = pl.ds(frame + pl.multiple_of(k * step, 16), step)
        grad0[px_frame, :] = round16(norm_backward(normed_grad, unit, inv0[px, :], gain, channels))
        return carry

    lax.fori_loop(0, dims.ext_pad // step, mix0, 0)
    clear_outside(place, grad0, dims)
    kernel_sums(
        x0, h * wide + SIDE - h, wide, grad0, h * ext_cols + margin, ext_cols, rows, cols, size, sums
    )
    store_sums(dims, sums, gain_sum[...], small)

    taps_rows = size * size + 1
    merged = jnp.concatenate([small[0:taps_rows, :], taps_sum1[0:taps_rows, :]], axis=0) * dims.factor
    merged = jnp.concatenate([merged, jnp.zeros((dims.small_rows - 2 * taps_rows, LANES), f32)], axis=0)
    merged = merged.astype(bf16)
    small_keep[...] = merged.astype(f32)

    layer_rows, part, half = (dims.layer_rows, dims.part, dims.half)
    units = up_acc.shape[1]
    up0 = up_acc[...].T * dims.factor
    down0 = down_acc[...].T * dims.factor
    up1 = up_sum1[...] * dims.factor
    down1 = down_sum1[...] * dims.factor
    lane = lax.broadcasted_iota(jnp.int32, (units, LANES), 1)
    slab_rows = 2 * layer_rows
    for r in range(dims.row_count):
        for layer, (u, d) in enumerate(((up0, down0), (up1, down1))):
            first = pltpu.roll(u, LANES - r * half, 1) if r else u
            shift = (half - r * half) % LANES
            second = pltpu.roll(d, shift, 1) if shift else d
            joined = jnp.where(lane < half, first, jnp.where(lane < 2 * half, second, 0.0))
            tall[layer * (units + 8) : layer * (units + 8) + units, :] = joined

        def slab(c, carry, r=r):
            index = 0
            for j, (axis, bit) in enumerate(dims.stages):
                value = (r >> bit) & 1 if axis == "row" else lax.rem(lax.div(c, 1 << bit), 2)
                index = index + value * (1 << (len(dims.stages) - 1 - j))
            for layer in range(2):
                to = pl.multiple_of(index * slab_rows + layer * layer_rows, 8)
                slabs[pl.ds(to, layer_rows), :] = tall[pl.ds(layer * (units + 8) + c * part, layer_rows), :]
            return carry

        lax.fori_loop(0, dims.col_count, slab, 0)

    split(dims, place, 0, slabs, merged, keep, send)


def split(dims, place, stage, slabs, merged, keep, send):
    count = slabs.shape[0] // 2
    axis, bit = dims.stages[stage]
    mine = lax.rem(lax.div(lax.axis_index(axis), 1 << bit), 2)
    keep[...] = slabs[pl.ds(pl.multiple_of(mine * count, 16), count), :]
    send[0:count, :] = slabs[pl.ds(pl.multiple_of((1 - mine) * count, 16), count), :].astype(bf16)
    send[count:, :] = merged


def stage_kernel(dims, stage, keep, small, got, *refs):
    keep_out, small_out, send, total = refs[-4:]
    place = Place(dims.row_count, dims.col_count)
    count = keep.shape[0]
    total[...] = keep[...] + got[0:count, :].astype(f32)
    merged = (small[...] + got[count:, :].astype(f32)).astype(bf16)
    small_out[...] = merged.astype(f32)
    split(dims, place, stage, total, merged, keep_out, send)


def last_kernel(dims, keep, small, got, kernel_out, gain_out, up_out, down_out):
    count = keep.shape[0]
    total = keep[...] + got[0:count, :].astype(f32)
    merged = small[...] + got[count:, :].astype(f32)
    size, channels, half, part = (dims.size, dims.channels, dims.half, dims.part)
    for layer in range(2):
        block = total[layer * dims.layer_rows : layer * dims.layer_rows + part]
        up_out[layer] = block[:, :half]
        down_out[layer] = block[:, half : 2 * half]
        for t in range(size * size + 1):
            at = layer * (size * size + 1) + t
            row = merged[at : at + 1, 0:channels]
            if t < size * size:
                kernel_out[t // size, t % size, layer : layer + 1, :] = row
            else:
                gain_out[layer : layer + 1, :] = row


def image_kernel(dims, grad0, middle, taps0, after, out, ready, work):
    rows, cols, size = (dims.rows, dims.cols, dims.size)

    def conv0(g, carry):
        at = group_start(g, cols)
        total = conv_group(grad0, at + 1, dims.ext_cols, rows, taps0, size, True)
        for r in range(rows):
            work[pl.ds(r * cols + at, 16), :] = middle[pl.ds(r * cols + at, 16), :] + total[r]
        return carry

    lax.fori_loop(0, -(-cols // 16), conv0, 0)
    for r in range(rows):
        out[r] = work[r * cols : (r + 1) * cols, 0 : dims.channels].astype(bf16)
    ready[...] = jnp.zeros(ready.shape, f32)


class Dims:
    def skipped_rows(self, place):
        if self.row_count > 2:
            return 0
        return jnp.where(place.has["above"], 0, self.h)


def dims_of(image, kernels, up_weights):
    d = Dims()
    d.row_count, d.col_count = (lax.axis_size("row"), lax.axis_size("col"))
    d.rows, d.cols, d.channels = image.shape
    d.size = kernels.shape[1]
    d.h = d.size // 2
    d.ext_rows, d.ext_cols = (d.rows + (d.h if d.row_count == 2 else 2 * d.h), d.cols + 8)
    d.wide = d.cols + 2 * SIDE
    d.ext_pad = -(-d.ext_rows * d.ext_cols // 16) * 16
    d.ext_step = max(s for s in range(16, 700, 16) if d.ext_pad % s == 0)
    d.line_step = 4
    d.half = d.channels // d.row_count
    d.part = up_weights.shape[2] // d.col_count
    d.layer_rows = ceil8(d.part)
    d.count = d.row_count * d.col_count
    d.small_rows = -(-2 * (d.size * d.size + 1) // 16) * 16
    d.factor = 1.0 / math.sqrt(d.rows * d.cols * d.count)
    row_bits, col_bits = (d.row_count.bit_length() - 1, d.col_count.bit_length() - 1)
    d.stages = [("col", 0)] + [("row", b) for b in range(row_bits)] + [("col", b) for b in range(1, col_bits)]
    return d


def halving_pairs(d, stage):
    axis, bit = d.stages[stage]
    pairs = []
    for r in range(d.row_count):
        for c in range(d.col_count):
            pr, pc = (r ^ (1 << bit), c) if axis == "row" else (r, c ^ (1 << bit))
            pairs.append((r * d.col_count + c, pr * d.col_count + pc))
    return pairs


def run(kernel, outs, scratch, *args, in_hbm=0, sems=0, busy_us=1):
    shapes = [jax.ShapeDtypeStruct(shape, kind) for shape, kind in outs]
    space = pl.BlockSpec(memory_space=pltpu.VMEM)
    far = pl.BlockSpec(memory_space=pltpu.HBM)
    held = [pltpu.VMEM(shape, kind) for shape, kind in scratch]
    if sems:
        held.append(pltpu.SemaphoreType.DMA((sems,)))
    return pl.pallas_call(
        kernel,
        out_shape=shapes,
        in_specs=[far] * in_hbm + [space] * (len(args) - in_hbm),
        out_specs=[space] * len(shapes),
        scratch_shapes=held,
        compiler_params=pltpu.CompilerParams(vmem_limit_bytes=32 * 1024 * 1024),
        cost_estimate=pl.CostEstimate(flops=int(busy_us * 1e9), bytes_accessed=1 << 18, transcendentals=0),
    )(*args)


def per_device(image, kernels, gains, up_weights, down_weights, cotangent):
    d = dims_of(image, kernels, up_weights)
    bind = functools.partial
    rows, cols, channels = image.shape
    units = up_weights.shape[2]
    tile, ext, wide = (rows * cols, d.ext_pad, (rows + 4 * d.h) * d.wide)
    frame = (rows + 2 * d.h) * d.ext_cols + 16
    taps = ((d.size * d.size * 16, LANES), bf16)
    tap_sums = ((d.size * d.size * 8, LANES), f32)
    sums_rows = ceil8(d.size * d.size + 1)

    bands, others = (band_combos(d.row_count), other_combos(d.row_count))

    def strips_of(pairs, radii):
        return [(shape, bf16) for shape in strip_shapes(pairs, rows, cols, channels, radii)]

    image, *band_strips = run(
        bind(bands_kernel, d), [(image.shape, bf16)] + strips_of(bands, (2 * d.h,)), [], image, in_hbm=1, sems=1
    )
    other_strips = run(bind(others_kernel, d), strips_of(others, (2 * d.h,)), [], image, *band_strips)
    strips = exchange(band_strips, other_strips, d.row_count, d.col_count)
    up, down, up_t, down_t, taps0, taps1, gains = run(
        weights_kernel,
        [
            ((2, LANES, units), bf16),
            ((2, units, LANES), bf16),
            ((2, units, LANES), bf16),
            ((2, LANES, units), bf16),
            taps,
            taps,
            (gains.shape, f32),
        ],
        [((2, channels, units), bf16), ((2, channels, units), bf16), ((d.size, d.size, 2, channels), f32)],
        up_weights,
        jnp.swapaxes(down_weights, 1, 2),
        jnp.transpose(kernels, (1, 2, 0, 3)),
        gains,
        in_hbm=4,
        sems=4,
        busy_us=2,
    )

    first = run(
        bind(first_kernel, d),
        [
            (image.shape, bf16),
            ((wide, LANES), f32),
            ((frame, LANES), f32),
            ((ext, LANES), bf16),
            ((ext, LANES), f32),
            ((ext, units), bf16),
            ((ext, units), bf16),
            ((tile, LANES), f32),
            ((tile, LANES), bf16),
            ((tile, units), bf16),
            ((tile, units), bf16),
            ((8, LANES), f32),
        ]
        + strips_of(bands, (2 * d.h, d.h)),
        [((ext, LANES), f32)],
        image,
        cotangent,
        taps0,
        taps1,
        gains,
        up,
        down,
        up_t,
        down_t,
        *strips,
        busy_us=15,
    )
    (output, x0, x1, unit0, inv0, hidden0, slope0, grad1, normed1, pre_grad1, hidden1, gain_part) = first[:12]
    band_strips = first[12:]
    other_strips = run(
        bind(grad_others_kernel, d), strips_of(others, (2 * d.h, d.h)), [], grad1, cotangent, *band_strips
    )
    strips = exchange(band_strips, other_strips, d.row_count, d.col_count)

    taps_sum1, up_sum1, down_sum1 = run(
        bind(sums_kernel, d),
        [((sums_rows, LANES), f32), ((units, LANES), f32), ((units, LANES), f32)],
        [tap_sums],
        x1,
        grad1,
        normed1,
        pre_grad1,
        hidden1,
        cotangent,
        gain_part,
        busy_us=3,
    )

    held = d.count // 2 * 2 * d.layer_rows
    small = ((d.small_rows, LANES), f32)
    grad0, middle, keep, sums, send = run(
        bind(third_kernel, d),
        [((frame, LANES), f32), ((tile, LANES), f32), ((held, LANES), f32), small, ((held + d.small_rows, LANES), bf16)],
        [
            ((wide, LANES), f32),
            ((frame, LANES), f32),
            ((ext, LANES), f32),
            ((ext, LANES), f32),
            tap_sums,
            ((LANES, units), f32),
            ((LANES, units), f32),
            ((8, LANES), f32),
            ((sums_rows, LANES), f32),
            ((2 * (units + 8), LANES), f32),
            ((2 * held, LANES), f32),
        ],
        grad1,
        cotangent,
        taps1,
        gains,
        up_t,
        down_t,
        x0,
        unit0,
        inv0,
        hidden0,
        slope0,
        taps_sum1,
        up_sum1,
        down_sum1,
        *strips,
        busy_us=12,
    )
    axes = ("row", "col")
    for stage in range(len(d.stages)):
        got = lax.ppermute(send, axes, halving_pairs(d, stage))
        if stage == 1:
            gradient, *ready = run(
                bind(image_kernel, d),
                [(image.shape, bf16), ((8, LANES), f32)],
                [((tile, LANES), f32)],
                grad0,
                middle,
                taps0,
                sums,
                busy_us=3,
            )
        else:
            ready = []
        if stage + 1 < len(d.stages):
            held //= 2
            keep, sums, send = run(
                bind(stage_kernel, d, stage + 1),
                [((held, LANES), f32), small, ((held + d.small_rows, LANES), bf16)],
                [((2 * held, LANES), f32)],
                keep,
                sums,
                got,
                *ready,
            )
    kernel_out, gain_out, up_out, down_out = run(
        bind(last_kernel, d),
        [
            ((d.size, d.size, 2, channels), f32),
            (gains.shape, f32),
            ((2, d.part, d.half), f32),
            ((2, d.part, d.half), f32),
        ],
        [],
        keep,
        sums,
        got,
    )
    kernel_out = jnp.transpose(kernel_out, (2, 0, 1, 3))
    return (output, gradient, kernel_out, gain_out, jnp.swapaxes(up_out, 1, 2), down_out)


def solution(mesh):
    placed = (P("row", "col", None), P(), P(), P(), P(), P("row", "col", None))
    return jax.shard_map(
        per_device,
        mesh=mesh,
        in_specs=placed,
        out_specs=(
            P("row", "col", None),
            P("row", "col", None),
            P(),
            P(),
            P(None, "row", "col"),
            P(None, "col", "row"),
        ),
        check_vma=False,
    )
```

```python
import functools
import math

import jax
import jax.numpy as jnp
from jax import lax
from jax.experimental import pallas as pl
from jax.experimental.pallas import tpu as pltpu
from jax.sharding import PartitionSpec as P

epsilon = 1e-06
inv_sqrt_two = 0.7071067811865476
inv_sqrt_two_pi = 0.3989422804014327
log2_e = 1.4426950408889634
LANES = 128
SIDE = 8
f32, bf16 = (jnp.float32, jnp.bfloat16)


def ceil8(n):
    return -(-n // 8) * 8


def combos(row_count):
    listed = [(None, 0), (None, 1), (0, None), (0, 0), (0, 1)]
    if row_count > 2:
        listed += [(1, None), (1, 0), (1, 1)]
    return listed


def partner(index, start, count):
    if start is None:
        return index
    other = index + 1 if (index - start) % 2 == 0 else index - 1
    return other if 0 <= other < count else None


def swap_pairs(row_count, col_count, row_start, col_start):
    pairs = []
    for r in range(row_count):
        for c in range(col_count):
            pr, pc = (partner(r, row_start, row_count), partner(c, col_start, col_count))
            if pr is None:
                pr, pc = (r, c ^ 1)
            elif pc is None:
                pr, pc = (r ^ 1 if row_start is None else pr, c)
            pairs.append((r * col_count + c, pr * col_count + pc))
    return pairs


def exchange(bands, others, row_count, col_count):
    got = {}
    for strips, pairs in ((bands, band_combos(row_count)), (others, other_combos(row_count))):
        for strip, (rs, cs) in zip(strips, pairs):
            got[rs, cs] = lax.ppermute(strip, ("row", "col"), swap_pairs(row_count, col_count, rs, cs))
    return [got[pair] for pair in combos(row_count)]


class Place:
    def __init__(self, row_count, col_count):
        row, col = (lax.axis_index("row"), lax.axis_index("col"))
        self.even_row, self.even_col = (lax.rem(row, 2) == 0, lax.rem(col, 2) == 0)
        self.has = {
            "above": row > 0,
            "below": row < row_count - 1,
            "left": col > 0,
            "right": col < col_count - 1,
        }
        self.row_count = row_count


def band_combos(row_count):
    return [pair for pair in combos(row_count) if pair[1] is None]


def other_combos(row_count):
    return [pair for pair in combos(row_count) if pair[1] is not None]


def write_strips(place, outs, takes, pairs):
    for out, (rs, cs) in zip(outs, pairs):
        at = 0
        for take, radius, rows, cols in takes:
            row_sets = [slice(0, rows)] * 2
            col_sets = [slice(0, cols)] * 2
            if rs is not None:
                row_sets = [slice(rows - radius, rows), slice(0, radius)]
                if rs == 1:
                    row_sets = row_sets[::-1]
            if cs is not None:
                col_sets = [slice(cols - SIDE, cols), slice(0, SIDE)]
                if cs == 1:
                    col_sets = col_sets[::-1]
            count = row_sets[0].stop - row_sets[0].start
            for i in range(count):
                parts = {}
                for er in (0, 1):
                    for ec in (0, 1):
                        key = (row_sets[er].start + i, col_sets[ec].start, col_sets[ec].stop)
                        if key not in parts:
                            parts[key] = take(*key)
                        parts[er, ec] = parts[key]
                if cs is None:
                    pick = [parts[0, 0], parts[1, 0]]
                else:
                    pick = [jnp.where(place.even_col, parts[e, 0], parts[e, 1]) for e in (0, 1)]
                value = pick[0] if rs is None else jnp.where(place.even_row, pick[0], pick[1])
                out[at + i] = value.astype(out.dtype)
            at += count


def strip_shapes(pairs, rows, cols, channels, radii):
    shapes = []
    for rs, cs in pairs:
        height = sum(rows if rs is None else radius for radius in radii)
        shapes.append((height, cols if cs is None else SIDE, channels))
    return shapes


def received(place, strips, row_sections):
    table = dict(zip(combos(place.row_count), strips))
    full_start, band_start = row_sections

    def along(rs, cs, i):
        return table[rs, cs][(full_start if rs is None else band_start) + i].astype(f32)

    def column(rs, side, i):
        if side is None:
            return along(rs, None, i)
        near, far = (along(rs, 0, i), along(rs, 1, i))
        if side == "left":
            return jnp.where(place.even_col, far, near)
        return jnp.where(place.even_col, near, far)

    def read(vertical, side, i):
        if vertical is None:
            value = column(None, side, i)
        elif place.row_count == 2:
            value = column(0, side, i)
        else:
            near, far = (column(0, side, i), column(1, side, i))
            if vertical == "above":
                value = jnp.where(place.even_row, far, near)
            else:
                value = jnp.where(place.even_row, near, far)
        if vertical is not None:
            value = jnp.where(place.has[vertical], value, 0.0)
        if side is not None:
            value = jnp.where(place.has[side], value, 0.0)
        return value

    return read


def assemble(place, target, own, read, radius, rows, cols, channels):
    width = cols + 2 * SIDE
    target[...] = jnp.zeros(target.shape, f32)
    for vertical, start, count in (("above", 0, radius), (None, radius, rows), ("below", radius + rows, radius)):
        for i in range(count):
            base = (start + i) * width
            middle = own(i) if vertical is None else read(vertical, None, i)
            target[base + SIDE : base + SIDE + cols, 0:channels] = middle
            target[base : base + SIDE, 0:channels] = read(vertical, "left", i)
            target[base + SIDE + cols : base + width, 0:channels] = read(vertical, "right", i)


def spread_taps(kernel_ref, layer, target):
    size, channels = (kernel_ref.shape[0], kernel_ref.shape[3])
    for a in range(size):
        for b in range(size):
            t = a * size + b
            row = pad_lanes(kernel_ref[a, b, layer : layer + 1, :])
            target[t * 16 : t * 16 + 16, :] = jnp.broadcast_to(row, (16, LANES)).astype(bf16)


def tree_sum(terms):
    while len(terms) > 1:
        pairs = [terms[i] + terms[i + 1] for i in range(0, len(terms) - 1, 2)]
        terms = pairs + ([terms[-1]] if len(terms) % 2 else [])
    return terms[0]


def conv_group(src, base, stride, rows_out, taps, size, flipped=False):
    total = [None] * rows_out
    for b in range(size):
        order = [a * size + b for a in range(size)]
        if flipped:
            order = [size * size - 1 - t for t in order]
        weights = [taps[t * 16 : t * 16 + 16, :] for t in order]
        window = []
        for i in range(rows_out + size - 1):
            window.append(src[pl.ds(base + i * stride + b, 16), :].astype(bf16))
            r = i - size + 1
            if r >= 0:
                term = tree_sum([window[r + a] * weights[a] for a in range(size)]).astype(f32)
                total[r] = term if total[r] is None else total[r] + term
    return total


def group_start(g, cols):
    return pl.multiple_of(jnp.minimum(g * 16, cols - 16), 8)


def kernel_sums(src, src_base, src_stride, grad, grad_base, grad_stride, rows, cols, size, sums):
    sums[...] = jnp.zeros(sums.shape, f32)

    def group(g, carry):
        at = pl.multiple_of(g * 16, 16)
        grads = [grad[pl.ds(grad_base + i * grad_stride + at, 16), :].astype(bf16) for i in range(rows)]
        for b in range(size):
            lines = [
                src[pl.ds(src_base + i * src_stride + at + b, 16), :].astype(bf16) for i in range(rows + size - 1)
            ]
            for a in range(size):
                term = tree_sum([lines[r + a] * grads[r] for r in range(rows)]).astype(f32)
                t = (a * size + b) * 8
                sums[t : t + 8, :] += term[0:8] + term[8:16]
        return carry

    lax.fori_loop(0, cols // 16, group, 0)


def diagonal(first, second):
    top = jnp.concatenate([first, jnp.zeros((first.shape[0], second.shape[1]), first.dtype)], axis=1)
    bottom = jnp.concatenate([jnp.zeros((second.shape[0], first.shape[1]), first.dtype), second], axis=1)
    return jnp.concatenate([top, bottom], axis=0)


def lane_total(x):
    high = x.astype(bf16)
    low = (x - high.astype(f32)).astype(bf16)
    both = jnp.concatenate([high, low], axis=1)
    return dot(both, jnp.ones((2 * LANES, LANES), bf16))


def paired_dot(x, y, weights):
    total = dot(jnp.concatenate([x.astype(bf16), y.astype(bf16)], axis=1), weights)
    half = weights.shape[1] // 2
    return (total[:, :half], total[:, half:])


def layer_norm(parts, channels, ones):
    lane = lax.broadcasted_iota(jnp.int32, parts[0].shape, 1)
    centred = [jnp.where(lane < channels, x - lane_total(x) * (1.0 / channels), 0.0) for x in parts]
    variances = paired_dot(centred[0] * centred[0], centred[1] * centred[1], ones)
    inverses = [lax.rsqrt(v * (1.0 / channels) + epsilon) for v in variances]
    return ([c * i for c, i in zip(centred, inverses)], inverses)


def norm_backward(normed_grad, unit, inverse, gain, channels, ones):
    m = normed_grad * gain
    mean, along = paired_dot(m, m * unit, ones)
    lane = lax.broadcasted_iota(jnp.int32, m.shape, 1)
    centred = m - (mean + unit * along) * (1.0 / channels)
    return jnp.where(lane < channels, inverse * centred, 0.0)


def gelu_parts(v):
    d = 1.0 + (0.3275911 * inv_sqrt_two) * jnp.abs(v)
    t = pl.reciprocal(d, approx=True)
    t = t * (2.0 - d * t)
    bell = jnp.exp2(v * v * (-0.5 * log2_e))
    series = 0.5 * 1.061405429 * t + 0.5 * -1.453152027
    series = series * t + 0.5 * 1.421413741
    series = series * t + 0.5 * -0.284496736
    series = series * t + 0.5 * 0.254829592
    tail = series * t * bell
    cdf = jnp.where(v >= 0.0, 1.0 - tail, tail)
    return (v * cdf, cdf + v * (bell * inv_sqrt_two_pi))


def dot(x, w):
    return jnp.dot(x, w, preferred_element_type=f32)


def dot_leading(x, y):
    return lax.dot_general(x, y, (((0,), (0,)), ((), ())), preferred_element_type=f32)


def pad_lanes(x):
    rows, channels = x.shape
    return jnp.concatenate([x, jnp.zeros((rows, LANES - channels), x.dtype)], axis=1)


def pieces(total, size):
    return [(start, min(size, total - start)) for start in range(0, total, size)]


def round16(x):
    return x.astype(bf16).astype(f32)


def fetch(sources, targets, sems):
    copies = [pltpu.make_async_copy(a, b, sems.at[i]) for i, (a, b) in enumerate(zip(sources, targets))]
    for copy in copies:
        copy.start()
    for copy in copies:
        copy.wait()


def image_take(ref):
    return lambda i, lo, hi: ref[i].astype(f32)[lo:hi]


def flat_take(ref, cols, channels):
    return lambda i, lo, hi: ref[i * cols + lo : i * cols + hi, 0:channels]


def bands_kernel(dims, image_in, image, *refs):
    outs, sems = (refs[:-1], refs[-1])
    place = Place(dims.row_count, dims.col_count)
    fetch((image_in,), (image,), sems)
    takes = [(image_take(image), 2 * dims.h, dims.rows, dims.cols)]
    write_strips(place, outs, takes, band_combos(dims.row_count))


def others_kernel(dims, image, *refs):
    outs = refs[len(band_combos(dims.row_count)) :]
    place = Place(dims.row_count, dims.col_count)
    takes = [(image_take(image), 2 * dims.h, dims.rows, dims.cols)]
    write_strips(place, outs, takes, other_combos(dims.row_count))


def grad_others_kernel(dims, grad1, cot, *refs):
    outs = refs[len(band_combos(dims.row_count)) :]
    place = Place(dims.row_count, dims.col_count)
    takes = [
        (flat_take(grad1, dims.cols, dims.channels), 2 * dims.h, dims.rows, dims.cols),
        (image_take(cot), dims.h, dims.rows, dims.cols),
    ]
    write_strips(place, outs, takes, other_combos(dims.row_count))


def weights_kernel(up_in, down_t_in, kernels_in, gains_in, *refs):
    forward0, back0, forward1, back1, grad_in0, grad_out0, taps0, taps1, gains, up_w, down_w, kernels, sems = refs
    fetch((up_in, down_t_in, kernels_in, gains_in), (up_w, down_w, kernels, gains), sems)
    spread_taps(kernels, 0, taps0)
    spread_taps(kernels, 1, taps1)
    channels, units = up_w.shape[1:]
    blank = jnp.zeros((LANES - channels, units), f32)
    wide, tall = ([], [])
    for layer in range(2):
        for ref in (up_w, down_w):
            full = jnp.concatenate([ref[layer].astype(f32), blank], axis=0)
            wide.append(full.astype(bf16))
            tall.append(full.T.astype(bf16))
    (up0, down_t0, up1, down_t1), (up_t0, down0, up_t1, down1) = (wide, tall)
    forward0[...] = diagonal(up0, up0)
    back0[...] = diagonal(down0, down0)
    forward1[...] = diagonal(up1, down_t1)
    back1[...] = diagonal(down1, up_t1)
    grad_in0[...] = diagonal(down_t0, down_t0)
    grad_out0[...] = diagonal(up_t0, up_t0)


def first_kernel(dims, *refs):
    count = len(combos(dims.row_count))
    image, cot, taps0, taps1, gains, forward0, back0, forward1, back1 = refs[:9]
    strips = refs[9 : 9 + count]
    refs = refs[9 + count :]
    (output, x0, x1, unit0, inv0, hidden0, slope0, grad1, normed1, pre_grad1, hidden1, gain_sum) = refs[:12]
    outs, conv = (refs[12:-1], refs[-1])
    place = Place(dims.row_count, dims.col_count)
    rows, cols, channels, h, size = (dims.rows, dims.cols, dims.channels, dims.h, dims.size)
    ext_rows, ext_cols, wide = (dims.ext_rows, dims.ext_cols, dims.wide)
    skip = dims.skipped_rows(place)
    read = received(place, strips, (0, 0))
    assemble(place, x0, lambda i: image[i].astype(f32), read, 2 * h, rows, cols, channels)

    x1[...] = jnp.zeros(x1.shape, f32)
    if dims.ext_pad > ext_rows * ext_cols:
        conv[ext_rows * ext_cols :, :] = jnp.zeros((dims.ext_pad - ext_rows * ext_cols, LANES), f32)
    frame = pl.multiple_of(skip * ext_cols, 8)

    def conv0(g, carry):
        at = group_start(g, ext_cols)
        base = pl.multiple_of(skip * wide, 8) + at
        total = conv_group(x0, base + 1, wide, ext_rows, taps0, size)
        for r in range(ext_rows):
            conv[pl.ds(r * ext_cols + at, 16), :] = total[r]
            x1[pl.ds(frame + r * ext_cols + at, 16), :] = x0[pl.ds(base + (r + h) * wide + 4, 16), :]
        return carry

    lax.fori_loop(0, -(-ext_cols // 16), conv0, 0)
    gain = pad_lanes(gains[0:1, :])
    ones = diagonal(jnp.ones((LANES, LANES), bf16), jnp.ones((LANES, LANES), bf16))
    half = dims.ext_pad // 2
    for start, n in pieces(half, dims.piece):
        spans = [(start, n), (half + start, n)]
        units, inverses = layer_norm([conv[at : at + n, :] for at, n in spans], channels, ones)
        pres = paired_dot(units[0] * gain, units[1] * gain, forward0[...])
        hiddens = []
        for (at, n), unit, inverse, pre in zip(spans, units, inverses, pres):
            unit0[at : at + n, :] = unit.astype(bf16)
            inv0[at : at + n, :] = inverse
            value, slope = gelu_parts(pre)
            hiddens.append(value.astype(bf16))
            hidden0[at : at + n, :] = hiddens[-1]
            slope0[at : at + n, :] = slope.astype(bf16)
        branches = paired_dot(hiddens[0], hiddens[1], back0[...])
        for (at, n), branch in zip(spans, branches):
            px = pl.ds(frame + at, n)
            x1[px, :] = round16(x1[px, :] + branch)
    clear_outside(place, x1, dims)

    def conv1(g, carry):
        at = group_start(g, cols)
        total = conv_group(x1, at + 1, ext_cols, rows, taps1, size)
        for r in range(rows):
            conv[pl.ds(r * cols + at, 16), :] = total[r]
        return carry

    lax.fori_loop(0, -(-cols // 16), conv1, 0)
    gain1 = pad_lanes(gains[1:2, :])
    gain_sum[...] = jnp.zeros(gain_sum.shape, f32)
    lines = dims.line_step
    step = lines * cols
    for k in range(rows // lines):
        px = slice(k * step, (k + 1) * step)
        middle = k * step + step // 2
        units, inverses = layer_norm([conv[k * step : middle, :], conv[middle : (k + 1) * step, :]], channels, ones)
        unit, inverse = (jnp.concatenate(units, axis=0), jnp.concatenate(inverses, axis=0))
        normed = (unit * gain1).astype(bf16)
        normed1[px, :] = normed
        upstream = pad_lanes(cot[k * lines : (k + 1) * lines].reshape(step, channels))
        pre, hidden_grad = paired_dot(normed, upstream, forward1[...])
        value, slope = gelu_parts(pre)
        hidden = value.astype(bf16)
        hidden1[px, :] = hidden
        pre_grad = (hidden_grad * slope).astype(bf16)
        pre_grad1[px, :] = pre_grad
        branch, normed_grad = paired_dot(hidden, pre_grad, back1[...])
        for i in range(lines):
            start = (k * lines + i + h) * ext_cols + 4
            line = x1[start : start + cols, :] + branch[i * cols : (i + 1) * cols]
            output[k * lines + i] = line[:, :channels].astype(bf16)
        product = normed_grad * unit
        gain_sum[...] += jnp.sum(product.reshape(step // 8, 8, LANES), axis=0)
        grad1[px, :] = round16(norm_backward(normed_grad, unit, inverse, gain1, channels, ones))

    takes = [(flat_take(grad1, cols, channels), 2 * h, rows, cols), (image_take(cot), h, rows, cols)]
    write_strips(place, outs, takes, band_combos(dims.row_count))


def clear_outside(place, flat, dims):
    h, frame_rows, ext_cols = (dims.h, dims.rows + 2 * dims.h, dims.ext_cols)
    margin = (ext_cols - dims.cols) // 2

    @pl.when(jnp.logical_not(place.has["above"]))
    def _():
        flat[0 : h * ext_cols, :] = jnp.zeros((h * ext_cols, LANES), f32)

    @pl.when(jnp.logical_not(place.has["below"]))
    def _():
        last = (frame_rows - h) * ext_cols
        flat[last:, :] = jnp.zeros((flat.shape[0] - last, LANES), f32)

    @pl.when(jnp.logical_not(place.has["left"]))
    def _():
        for r in range(frame_rows):
            flat[r * ext_cols : r * ext_cols + margin, :] = jnp.zeros((margin, LANES), f32)

    @pl.when(jnp.logical_not(place.has["right"]))
    def _():
        for r in range(frame_rows):
            flat[(r + 1) * ext_cols - margin : (r + 1) * ext_cols, :] = jnp.zeros((margin, LANES), f32)


def sums_kernel(dims, x1, grad1, normed1, pre_grad1, hidden1, cot, gain_part, taps_sum, up_sum, down_sum, sums):
    kernel_sums(x1, 1, dims.ext_cols, grad1, 0, dims.cols, dims.rows, dims.cols, dims.size, sums)
    store_sums(dims, sums, gain_part[...], taps_sum)
    upstream = pad_lanes(cot[...].reshape(dims.rows * dims.cols, dims.channels))
    up_sum[...] = dot_leading(normed1[...], pre_grad1[...]).T
    down_sum[...] = dot_leading(upstream, hidden1[...]).T


def store_sums(dims, sums, gain_part, target):
    taps = dims.size * dims.size
    target[...] = jnp.zeros(target.shape, f32)
    for t in range(taps):
        target[t : t + 1, :] = jnp.sum(sums[t * 8 : t * 8 + 8, :], axis=0, keepdims=True)
    target[taps : taps + 1, :] = jnp.sum(gain_part, axis=0, keepdims=True)


def third_kernel(dims, *refs):
    count = len(combos(dims.row_count))
    (grad1, cot, taps1, gains, grad_in0, grad_out0, x0, unit0, inv0, hidden0, slope0) = refs[:11]
    (taps_sum1, up_sum1, down_sum1) = refs[11:14]
    strips = refs[14 : 14 + count]
    (grad0, middle, keep, small_keep, send) = refs[14 + count : 19 + count]
    (wide_grad, cot_frame, upstream, own, sums, up_acc, down_acc, gain_sum, small, tall, slabs) = refs[19 + count :]
    place = Place(dims.row_count, dims.col_count)
    rows, cols, channels, h, size = (dims.rows, dims.cols, dims.channels, dims.h, dims.size)
    ext_rows, ext_cols, wide = (dims.ext_rows, dims.ext_cols, dims.wide)
    skip = dims.skipped_rows(place)
    read = received(place, strips, (0, 0))
    assemble(
        place, wide_grad, lambda i: grad1[i * cols : (i + 1) * cols, 0:channels], read, 2 * h, rows, cols, channels
    )
    read_cot = received(place, strips, (rows, 2 * h))
    margin = (ext_cols - cols) // 2
    cot_frame[...] = jnp.zeros(cot_frame.shape, f32)
    for vertical, start, n in (("above", 0, h), (None, h, rows), ("below", h + rows, h)):
        for i in range(n):
            base = (start + i) * ext_cols
            line = cot[i].astype(f32) if vertical is None else read_cot(vertical, None, i)
            cot_frame[base + margin : base + margin + cols, 0:channels] = line
            cot_frame[base : base + margin, 0:channels] = read_cot(vertical, "left", i)[SIDE - margin :]
            cot_frame[base + margin + cols : base + ext_cols, 0:channels] = read_cot(vertical, "right", i)[:margin]

    used = ext_rows * ext_cols
    if dims.ext_pad > used:
        upstream[used:, :] = jnp.zeros((dims.ext_pad - used, LANES), f32)
        own[used:, :] = jnp.zeros((dims.ext_pad - used, LANES), f32)
    grad0[...] = jnp.zeros(grad0.shape, f32)
    frame = pl.multiple_of(skip * ext_cols, 8)

    def conv1(g, carry):
        at = group_start(g, ext_cols)
        total = conv_group(wide_grad, pl.multiple_of(skip * wide, 8) + at + 1, wide, ext_rows, taps1, size, True)
        col = lax.broadcasted_iota(jnp.int32, (16, LANES), 0) + (at - margin)
        inside = jnp.where(jnp.logical_and(col >= 0, col < cols), 1.0, 0.0)
        for r in range(ext_rows):
            px = pl.ds(r * ext_cols + at, 16)
            upstream[px, :] = cot_frame[pl.ds(frame + r * ext_cols + at, 16), :] + total[r]
            mine = jnp.logical_and(r + skip >= h, r + skip < h + rows)
            own[px, :] = jnp.where(mine, inside, 0.0)
        return carry

    lax.fori_loop(0, -(-ext_cols // 16), conv1, 0)
    for i in range(rows):
        line = upstream[pl.ds((i + h - skip) * ext_cols + margin, cols), :]
        middle[i * cols : (i + 1) * cols, :] = round16(line)

    gain = pad_lanes(gains[0:1, :])
    gain_sum[...] = jnp.zeros(gain_sum.shape, f32)
    up_acc[...] = jnp.zeros(up_acc.shape, f32)
    down_acc[...] = jnp.zeros(down_acc.shape, f32)
    ones = diagonal(jnp.ones((LANES, LANES), bf16), jnp.ones((LANES, LANES), bf16))
    half_px = dims.ext_pad // 2
    for start, n in pieces(half_px, dims.piece):
        spans = [(start, n), (half_px + start, n)]
        flows = [upstream[at : at + n, :].astype(bf16) for at, n in spans]
        hidden_grads = paired_dot(flows[0], flows[1], grad_in0[...])
        pre_grads = [
            (grad * slope0[at : at + n, :].astype(f32)).astype(bf16) for grad, (at, n) in zip(hidden_grads, spans)
        ]
        normed_grads = paired_dot(pre_grads[0], pre_grads[1], grad_out0[...])
        for (at, n), flow, pre_grad, normed_grad in zip(spans, flows, pre_grads, normed_grads):
            mine = own[at : at + n, :]
            unit = unit0[at : at + n, :].astype(f32)
            normed = (unit * gain * mine).astype(bf16)
            up_acc[...] += dot_leading(normed, pre_grad)
            down_acc[...] += dot_leading(flow * mine.astype(bf16), hidden0[at : at + n, :])
            product = normed_grad * unit * mine
            gain_sum[...] += jnp.sum(product.reshape(n // 8, 8, LANES), axis=0)
            grad = norm_backward(normed_grad, unit, inv0[at : at + n, :], gain, channels, ones)
            grad0[pl.ds(frame + at, n), :] = round16(grad)
    clear_outside(place, grad0, dims)
    kernel_sums(
        x0, h * wide + SIDE - h, wide, grad0, h * ext_cols + margin, ext_cols, rows, cols, size, sums
    )
    store_sums(dims, sums, gain_sum[...], small)

    taps_rows = size * size + 1
    merged = jnp.concatenate([small[0:taps_rows, :], taps_sum1[0:taps_rows, :]], axis=0) * dims.factor
    merged = jnp.concatenate([merged, jnp.zeros((dims.small_rows - 2 * taps_rows, LANES), f32)], axis=0)
    merged = merged.astype(bf16)
    small_keep[...] = merged.astype(f32)

    layer_rows, part, half = (dims.layer_rows, dims.part, dims.half)
    units = up_acc.shape[1]
    up0 = up_acc[...].T * dims.factor
    down0 = down_acc[...].T * dims.factor
    up1 = up_sum1[...] * dims.factor
    down1 = down_sum1[...] * dims.factor
    lane = lax.broadcasted_iota(jnp.int32, (units, LANES), 1)
    slab_rows = 2 * layer_rows
    for r in range(dims.row_count):
        for layer, (u, d) in enumerate(((up0, down0), (up1, down1))):
            first = pltpu.roll(u, LANES - r * half, 1) if r else u
            shift = (half - r * half) % LANES
            second = pltpu.roll(d, shift, 1) if shift else d
            joined = jnp.where(lane < half, first, jnp.where(lane < 2 * half, second, 0.0))
            tall[layer * (units + 8) : layer * (units + 8) + units, :] = joined

        def slab(c, carry, r=r):
            index = 0
            for j, (axis, bit) in enumerate(dims.stages):
                value = (r >> bit) & 1 if axis == "row" else lax.rem(lax.div(c, 1 << bit), 2)
                index = index + value * (1 << (len(dims.stages) - 1 - j))
            for layer in range(2):
                to = pl.multiple_of(index * slab_rows + layer * layer_rows, 8)
                slabs[pl.ds(to, layer_rows), :] = tall[pl.ds(layer * (units + 8) + c * part, layer_rows), :]
            return carry

        lax.fori_loop(0, dims.col_count, slab, 0)

    split(dims, place, 0, slabs, merged, keep, send)


def split(dims, place, stage, slabs, merged, keep, send):
    count = slabs.shape[0] // 2
    axis, bit = dims.stages[stage]
    mine = lax.rem(lax.div(lax.axis_index(axis), 1 << bit), 2)
    keep[...] = slabs[pl.ds(pl.multiple_of(mine * count, 16), count), :]
    send[0:count, :] = slabs[pl.ds(pl.multiple_of((1 - mine) * count, 16), count), :].astype(bf16)
    send[count:, :] = merged


def stage_kernel(dims, stage, keep, small, got, *refs):
    keep_out, small_out, send, total = refs[-4:]
    place = Place(dims.row_count, dims.col_count)
    count = keep.shape[0]
    total[...] = keep[...] + got[0:count, :].astype(f32)
    merged = (small[...] + got[count:, :].astype(f32)).astype(bf16)
    small_out[...] = merged.astype(f32)
    split(dims, place, stage, total, merged, keep_out, send)


def group_kernel(dims, keep, small, got, packed):
    count = keep.shape[0]
    total = (keep[...] + got[0:count, :].astype(f32)).astype(bf16)
    merged = (small[...] + got[count:, :].astype(f32)).astype(bf16)
    slab = count // 4
    for k in range(4):
        packed[k, 0:slab, :] = total[k * slab : (k + 1) * slab]
        packed[k, slab:, :] = merged


def last_kernel(dims, got, kernel_out, gain_out, up_out, down_out):
    every = (got[0].astype(f32) + got[1].astype(f32)) + (got[2].astype(f32) + got[3].astype(f32))
    count = 2 * dims.layer_rows
    total, merged = (every[0:count], every[count:])
    size, channels, half, part = (dims.size, dims.channels, dims.half, dims.part)
    for layer in range(2):
        block = total[layer * dims.layer_rows : layer * dims.layer_rows + part]
        up_out[layer] = block[:, :half]
        down_out[layer] = block[:, half : 2 * half]
        for t in range(size * size + 1):
            at = layer * (size * size + 1) + t
            row = merged[at : at + 1, 0:channels]
            if t < size * size:
                kernel_out[t // size, t % size, layer : layer + 1, :] = row
            else:
                gain_out[layer : layer + 1, :] = row


def image_kernel(dims, grad0, middle, taps0, after, out, ready, work):
    rows, cols, size = (dims.rows, dims.cols, dims.size)

    def conv0(g, carry):
        at = group_start(g, cols)
        total = conv_group(grad0, at + 1, dims.ext_cols, rows, taps0, size, True)
        for r in range(rows):
            work[pl.ds(r * cols + at, 16), :] = middle[pl.ds(r * cols + at, 16), :] + total[r]
        return carry

    lax.fori_loop(0, -(-cols // 16), conv0, 0)
    for r in range(rows):
        out[r] = work[r * cols : (r + 1) * cols, 0 : dims.channels].astype(bf16)
    ready[...] = jnp.zeros(ready.shape, f32)


class Dims:
    def skipped_rows(self, place):
        if self.row_count > 2:
            return 0
        return jnp.where(place.has["above"], 0, self.h)


def dims_of(image, kernels, up_weights):
    d = Dims()
    d.row_count, d.col_count = (lax.axis_size("row"), lax.axis_size("col"))
    d.rows, d.cols, d.channels = image.shape
    d.size = kernels.shape[1]
    d.h = d.size // 2
    d.ext_rows, d.ext_cols = (d.rows + (d.h if d.row_count == 2 else 2 * d.h), d.cols + 8)
    d.wide = d.cols + 2 * SIDE
    d.ext_pad = -(-d.ext_rows * d.ext_cols // 32) * 32
    d.piece = 176
    d.line_step = 4
    d.half = d.channels // d.row_count
    d.part = up_weights.shape[2] // d.col_count
    d.layer_rows = ceil8(d.part)
    d.count = d.row_count * d.col_count
    d.small_rows = -(-2 * (d.size * d.size + 1) // 16) * 16
    d.factor = 1.0 / math.sqrt(d.rows * d.cols * d.count)
    row_bits, col_bits = (d.row_count.bit_length() - 1, d.col_count.bit_length() - 1)
    d.stages = [("col", 0)] + [("row", b) for b in range(row_bits)] + [("col", b) for b in range(1, col_bits - 2)]
    d.stages += [("col", col_bits - 1), ("col", col_bits - 2)]
    d.swaps = len(d.stages) - 2
    return d


def halving_pairs(d, stage):
    axis, bit = d.stages[stage]
    pairs = []
    for r in range(d.row_count):
        for c in range(d.col_count):
            pr, pc = (r ^ (1 << bit), c) if axis == "row" else (r, c ^ (1 << bit))
            pairs.append((r * d.col_count + c, pr * d.col_count + pc))
    return pairs


def run(kernel, outs, scratch, *args, in_hbm=0, sems=0, busy_us=1):
    shapes = [jax.ShapeDtypeStruct(shape, kind) for shape, kind in outs]
    space = pl.BlockSpec(memory_space=pltpu.VMEM)
    far = pl.BlockSpec(memory_space=pltpu.HBM)
    held = [pltpu.VMEM(shape, kind) for shape, kind in scratch]
    if sems:
        held.append(pltpu.SemaphoreType.DMA((sems,)))
    return pl.pallas_call(
        kernel,
        out_shape=shapes,
        in_specs=[far] * in_hbm + [space] * (len(args) - in_hbm),
        out_specs=[space] * len(shapes),
        scratch_shapes=held,
        compiler_params=pltpu.CompilerParams(vmem_limit_bytes=32 * 1024 * 1024),
        cost_estimate=pl.CostEstimate(flops=int(busy_us * 1e9), bytes_accessed=1 << 18, transcendentals=0),
    )(*args)


def per_device(image, kernels, gains, up_weights, down_weights, cotangent):
    d = dims_of(image, kernels, up_weights)
    bind = functools.partial
    rows, cols, channels = image.shape
    units = up_weights.shape[2]
    tile, ext, wide = (rows * cols, d.ext_pad, (rows + 4 * d.h) * d.wide)
    frame = (rows + 2 * d.h) * d.ext_cols + 16
    taps = ((d.size * d.size * 16, LANES), bf16)
    tap_sums = ((d.size * d.size * 8, LANES), f32)
    sums_rows = ceil8(d.size * d.size + 1)

    bands, others = (band_combos(d.row_count), other_combos(d.row_count))

    def strips_of(pairs, radii):
        return [(shape, bf16) for shape in strip_shapes(pairs, rows, cols, channels, radii)]

    image, *band_strips = run(
        bind(bands_kernel, d), [(image.shape, bf16)] + strips_of(bands, (2 * d.h,)), [], image, in_hbm=1, sems=1
    )
    other_strips = run(bind(others_kernel, d), strips_of(others, (2 * d.h,)), [], image, *band_strips)
    strips = exchange(band_strips, other_strips, d.row_count, d.col_count)
    mixing = [((2 * LANES, 2 * units), bf16), ((2 * units, 2 * LANES), bf16)]
    forward0, back0, forward1, back1, grad_in0, grad_out0, taps0, taps1, gains = run(
        weights_kernel,
        mixing * 3 + [taps, taps, (gains.shape, f32)],
        [((2, channels, units), bf16), ((2, channels, units), bf16), ((d.size, d.size, 2, channels), f32)],
        up_weights,
        jnp.swapaxes(down_weights, 1, 2),
        jnp.transpose(kernels, (1, 2, 0, 3)),
        gains,
        in_hbm=4,
        sems=4,
        busy_us=2,
    )

    first = run(
        bind(first_kernel, d),
        [
            (image.shape, bf16),
            ((wide, LANES), f32),
            ((frame, LANES), f32),
            ((ext, LANES), bf16),
            ((ext, LANES), f32),
            ((ext, units), bf16),
            ((ext, units), bf16),
            ((tile, LANES), f32),
            ((tile, LANES), bf16),
            ((tile, units), bf16),
            ((tile, units), bf16),
            ((8, LANES), f32),
        ]
        + strips_of(bands, (2 * d.h, d.h)),
        [((ext, LANES), f32)],
        image,
        cotangent,
        taps0,
        taps1,
        gains,
        forward0,
        back0,
        forward1,
        back1,
        *strips,
        busy_us=15,
    )
    (output, x0, x1, unit0, inv0, hidden0, slope0, grad1, normed1, pre_grad1, hidden1, gain_part) = first[:12]
    band_strips = first[12:]
    other_strips = run(
        bind(grad_others_kernel, d), strips_of(others, (2 * d.h, d.h)), [], grad1, cotangent, *band_strips
    )
    strips = exchange(band_strips, other_strips, d.row_count, d.col_count)

    taps_sum1, up_sum1, down_sum1 = run(
        bind(sums_kernel, d),
        [((sums_rows, LANES), f32), ((units, LANES), f32), ((units, LANES), f32)],
        [tap_sums],
        x1,
        grad1,
        normed1,
        pre_grad1,
        hidden1,
        cotangent,
        gain_part,
        busy_us=3,
    )

    held = d.count // 2 * 2 * d.layer_rows
    small = ((d.small_rows, LANES), f32)
    grad0, middle, keep, sums, send = run(
        bind(third_kernel, d),
        [((frame, LANES), f32), ((tile, LANES), f32), ((held, LANES), f32), small, ((held + d.small_rows, LANES), bf16)],
        [
            ((wide, LANES), f32),
            ((frame, LANES), f32),
            ((ext, LANES), f32),
            ((ext, LANES), f32),
            tap_sums,
            ((LANES, units), f32),
            ((LANES, units), f32),
            ((8, LANES), f32),
            ((sums_rows, LANES), f32),
            ((2 * (units + 8), LANES), f32),
            ((2 * held, LANES), f32),
        ],
        grad1,
        cotangent,
        taps1,
        gains,
        grad_in0,
        grad_out0,
        x0,
        unit0,
        inv0,
        hidden0,
        slope0,
        taps_sum1,
        up_sum1,
        down_sum1,
        *strips,
        busy_us=12,
    )
    axes = ("row", "col")
    for stage in range(d.swaps):
        got = lax.ppermute(send, axes, halving_pairs(d, stage))
        if stage == 1:
            gradient, *ready = run(
                bind(image_kernel, d),
                [(image.shape, bf16), ((8, LANES), f32)],
                [((tile, LANES), f32)],
                grad0,
                middle,
                taps0,
                sums,
                busy_us=3,
            )
        else:
            ready = []
        if stage + 1 < d.swaps:
            held //= 2
            keep, sums, send = run(
                bind(stage_kernel, d, stage + 1),
                [((held, LANES), f32), small, ((held + d.small_rows, LANES), bf16)],
                [((2 * held, LANES), f32)],
                keep,
                sums,
                got,
                *ready,
            )
    (packed,) = run(
        bind(group_kernel, d), [((4, held // 4 + d.small_rows, LANES), bf16)], [], keep, sums, got
    )
    stride = d.col_count // 4
    groups = [[first + stride * k for k in range(4)] for first in range(stride)]
    got = lax.all_to_all(packed, "col", 0, 0, axis_index_groups=groups, tiled=True)
    kernel_out, gain_out, up_out, down_out = run(
        bind(last_kernel, d),
        [
            ((d.size, d.size, 2, channels), f32),
            (gains.shape, f32),
            ((2, d.part, d.half), f32),
            ((2, d.part, d.half), f32),
        ],
        [],
        got,
    )
    kernel_out = jnp.transpose(kernel_out, (2, 0, 1, 3))
    return (output, gradient, kernel_out, gain_out, jnp.swapaxes(up_out, 1, 2), down_out)


def solution(mesh):
    placed = (P("row", "col", None), P(), P(), P(), P(), P("row", "col", None))
    return jax.shard_map(
        per_device,
        mesh=mesh,
        in_specs=placed,
        out_specs=(
            P("row", "col", None),
            P("row", "col", None),
            P(),
            P(),
            P(None, "row", "col"),
            P(None, "col", "row"),
        ),
        check_vma=False,
    )
```

```python
import functools
import math

import jax
import jax.numpy as jnp
from jax import lax
from jax.experimental import pallas as pl
from jax.experimental.pallas import tpu as pltpu
from jax.sharding import PartitionSpec as P

epsilon = 1e-06
inv_sqrt_two = 0.7071067811865476
inv_sqrt_two_pi = 0.3989422804014327
log2_e = 1.4426950408889634
LANES = 128
SIDE = 8
f32, bf16 = (jnp.float32, jnp.bfloat16)


def ceil8(n):
    return -(-n // 8) * 8


def combos(row_count):
    listed = [(None, 0), (None, 1), (0, None), (0, 0), (0, 1)]
    if row_count > 2:
        listed += [(1, None), (1, 0), (1, 1)]
    return listed


def partner(index, start, count):
    if start is None:
        return index
    other = index + 1 if (index - start) % 2 == 0 else index - 1
    return other if 0 <= other < count else None


def swap_pairs(row_count, col_count, row_start, col_start):
    pairs = []
    for r in range(row_count):
        for c in range(col_count):
            pr, pc = (partner(r, row_start, row_count), partner(c, col_start, col_count))
            if pr is None:
                pr, pc = (r, c ^ 1)
            elif pc is None:
                pr, pc = (r ^ 1 if row_start is None else pr, c)
            pairs.append((r * col_count + c, pr * col_count + pc))
    return pairs


def exchange(bands, others, row_count, col_count):
    got = {}
    for strips, pairs in ((bands, band_combos(row_count)), (others, other_combos(row_count))):
        for strip, (rs, cs) in zip(strips, pairs):
            got[rs, cs] = lax.ppermute(strip, ("row", "col"), swap_pairs(row_count, col_count, rs, cs))
    return [got[pair] for pair in combos(row_count)]


class Place:
    def __init__(self, row_count, col_count):
        row, col = (lax.axis_index("row"), lax.axis_index("col"))
        self.even_row, self.even_col = (lax.rem(row, 2) == 0, lax.rem(col, 2) == 0)
        self.has = {
            "above": row > 0,
            "below": row < row_count - 1,
            "left": col > 0,
            "right": col < col_count - 1,
        }
        self.row_count = row_count


def band_combos(row_count):
    return [pair for pair in combos(row_count) if pair[1] is None]


def other_combos(row_count):
    return [pair for pair in combos(row_count) if pair[1] is not None]


def write_strips(place, outs, takes, pairs):
    for out, (rs, cs) in zip(outs, pairs):
        at = 0
        for take, radius, rows, cols in takes:
            row_sets = [slice(0, rows)] * 2
            col_sets = [slice(0, cols)] * 2
            if rs is not None:
                row_sets = [slice(rows - radius, rows), slice(0, radius)]
                if rs == 1:
                    row_sets = row_sets[::-1]
            if cs is not None:
                col_sets = [slice(cols - SIDE, cols), slice(0, SIDE)]
                if cs == 1:
                    col_sets = col_sets[::-1]
            count = row_sets[0].stop - row_sets[0].start
            for i in range(count):
                parts = {}
                for er in (0, 1):
                    for ec in (0, 1):
                        key = (row_sets[er].start + i, col_sets[ec].start, col_sets[ec].stop)
                        if key not in parts:
                            parts[key] = take(*key)
                        parts[er, ec] = parts[key]
                if cs is None:
                    pick = [parts[0, 0], parts[1, 0]]
                else:
                    pick = [jnp.where(place.even_col, parts[e, 0], parts[e, 1]) for e in (0, 1)]
                value = pick[0] if rs is None else jnp.where(place.even_row, pick[0], pick[1])
                out[at + i] = value.astype(out.dtype)
            at += count


def strip_shapes(pairs, rows, cols, channels, radii):
    shapes = []
    for rs, cs in pairs:
        height = sum(rows if rs is None else radius for radius in radii)
        shapes.append((height, cols if cs is None else SIDE, channels))
    return shapes


def received(place, strips, row_sections):
    table = dict(zip(combos(place.row_count), strips))
    full_start, band_start = row_sections

    def along(rs, cs, i):
        return table[rs, cs][(full_start if rs is None else band_start) + i].astype(f32)

    def column(rs, side, i):
        if side is None:
            return along(rs, None, i)
        near, far = (along(rs, 0, i), along(rs, 1, i))
        if side == "left":
            return jnp.where(place.even_col, far, near)
        return jnp.where(place.even_col, near, far)

    def read(vertical, side, i):
        if vertical is None:
            value = column(None, side, i)
        elif place.row_count == 2:
            value = column(0, side, i)
        else:
            near, far = (column(0, side, i), column(1, side, i))
            if vertical == "above":
                value = jnp.where(place.even_row, far, near)
            else:
                value = jnp.where(place.even_row, near, far)
        if vertical is not None:
            value = jnp.where(place.has[vertical], value, 0.0)
        if side is not None:
            value = jnp.where(place.has[side], value, 0.0)
        return value

    return read


def assemble(place, target, own, read, radius, rows, cols, channels):
    width = cols + 2 * SIDE
    target[...] = jnp.zeros(target.shape, f32)
    for vertical, start, count in (("above", 0, radius), (None, radius, rows), ("below", radius + rows, radius)):
        for i in range(count):
            base = (start + i) * width
            middle = own(i) if vertical is None else read(vertical, None, i)
            target[base + SIDE : base + SIDE + cols, 0:channels] = middle
            target[base : base + SIDE, 0:channels] = read(vertical, "left", i)
            target[base + SIDE + cols : base + width, 0:channels] = read(vertical, "right", i)


def spread_taps(kernel_ref, layer, target):
    size, channels = (kernel_ref.shape[0], kernel_ref.shape[3])
    for a in range(size):
        for b in range(size):
            t = a * size + b
            row = pad_lanes(kernel_ref[a, b, layer : layer + 1, :])
            target[t * 16 : t * 16 + 16, :] = jnp.broadcast_to(row, (16, LANES)).astype(bf16)


def tree_sum(terms):
    while len(terms) > 1:
        pairs = [terms[i] + terms[i + 1] for i in range(0, len(terms) - 1, 2)]
        terms = pairs + ([terms[-1]] if len(terms) % 2 else [])
    return terms[0]


def conv_group(src, base, stride, rows_out, taps, size, flipped=False):
    total = [None] * rows_out
    for b in range(size):
        order = [a * size + b for a in range(size)]
        if flipped:
            order = [size * size - 1 - t for t in order]
        weights = [taps[t * 16 : t * 16 + 16, :] for t in order]
        window = []
        for i in range(rows_out + size - 1):
            window.append(src[pl.ds(base + i * stride + b, 16), :].astype(bf16))
            r = i - size + 1
            if r >= 0:
                term = tree_sum([window[r + a] * weights[a] for a in range(size)]).astype(f32)
                total[r] = term if total[r] is None else total[r] + term
    return total


def group_start(g, cols):
    return pl.multiple_of(jnp.minimum(g * 16, cols - 16), 8)


def kernel_sums(src, src_base, src_stride, grad, grad_base, grad_stride, rows, cols, size, sums):
    sums[...] = jnp.zeros(sums.shape, f32)

    def group(g, carry):
        at = pl.multiple_of(g * 16, 16)
        grads = [grad[pl.ds(grad_base + i * grad_stride + at, 16), :].astype(bf16) for i in range(rows)]
        for b in range(size):
            lines = [
                src[pl.ds(src_base + i * src_stride + at + b, 16), :].astype(bf16) for i in range(rows + size - 1)
            ]
            for a in range(size):
                term = tree_sum([lines[r + a] * grads[r] for r in range(rows)]).astype(f32)
                t = (a * size + b) * 8
                sums[t : t + 8, :] += term[0:8] + term[8:16]
        return carry

    lax.fori_loop(0, cols // 16, group, 0)


def diagonal(first, second):
    top = jnp.concatenate([first, jnp.zeros((first.shape[0], second.shape[1]), first.dtype)], axis=1)
    bottom = jnp.concatenate([jnp.zeros((second.shape[0], first.shape[1]), first.dtype), second], axis=1)
    return jnp.concatenate([top, bottom], axis=0)


def lane_total(x):
    high = x.astype(bf16)
    low = (x - high.astype(f32)).astype(bf16)
    both = jnp.concatenate([high, low], axis=1)
    return dot(both, jnp.ones((2 * LANES, LANES), bf16))


def paired_dot(x, y, weights):
    total = dot(jnp.concatenate([x.astype(bf16), y.astype(bf16)], axis=1), weights)
    half = weights.shape[1] // 2
    return (total[:, :half], total[:, half:])


def layer_norm(parts, channels, ones):
    lane = lax.broadcasted_iota(jnp.int32, parts[0].shape, 1)
    centred = [jnp.where(lane < channels, x - lane_total(x) * (1.0 / channels), 0.0) for x in parts]
    variances = paired_dot(centred[0] * centred[0], centred[1] * centred[1], ones)
    inverses = [lax.rsqrt(v * (1.0 / channels) + epsilon) for v in variances]
    return ([c * i for c, i in zip(centred, inverses)], inverses)


def norm_backward(normed_grad, unit, inverse, gain, channels, ones):
    m = normed_grad * gain
    mean, along = paired_dot(m, m * unit, ones)
    lane = lax.broadcasted_iota(jnp.int32, m.shape, 1)
    centred = m - (mean + unit * along) * (1.0 / channels)
    return jnp.where(lane < channels, inverse * centred, 0.0)


def gelu_parts(v):
    d = 1.0 + (0.3275911 * inv_sqrt_two) * jnp.abs(v)
    t = pl.reciprocal(d, approx=True)
    t = t * (2.0 - d * t)
    bell = jnp.exp2(v * v * (-0.5 * log2_e))
    series = 0.5 * 1.061405429 * t + 0.5 * -1.453152027
    series = series * t + 0.5 * 1.421413741
    series = series * t + 0.5 * -0.284496736
    series = series * t + 0.5 * 0.254829592
    tail = series * t * bell
    cdf = jnp.where(v >= 0.0, 1.0 - tail, tail)
    return (v * cdf, cdf + v * (bell * inv_sqrt_two_pi))


def dot(x, w):
    return jnp.dot(x, w, preferred_element_type=f32)


def dot_leading(x, y):
    return lax.dot_general(x, y, (((0,), (0,)), ((), ())), preferred_element_type=f32)


def pad_lanes(x):
    rows, channels = x.shape
    return jnp.concatenate([x, jnp.zeros((rows, LANES - channels), x.dtype)], axis=1)


def pieces(total, size):
    return [(start, min(size, total - start)) for start in range(0, total, size)]


def round16(x):
    return x.astype(bf16).astype(f32)


def fetch(sources, targets, sems):
    copies = [pltpu.make_async_copy(a, b, sems.at[i]) for i, (a, b) in enumerate(zip(sources, targets))]
    for copy in copies:
        copy.start()
    for copy in copies:
        copy.wait()


def image_take(ref):
    return lambda i, lo, hi: ref[i].astype(f32)[lo:hi]


def flat_take(ref, cols, channels):
    return lambda i, lo, hi: ref[i * cols + lo : i * cols + hi, 0:channels]


def bands_kernel(dims, image_in, image, *refs):
    outs, sems = (refs[:-1], refs[-1])
    place = Place(dims.row_count, dims.col_count)
    fetch((image_in,), (image,), sems)
    takes = [(image_take(image), 2 * dims.h, dims.rows, dims.cols)]
    write_strips(place, outs, takes, band_combos(dims.row_count))


def others_kernel(dims, image, *refs):
    outs = refs[len(band_combos(dims.row_count)) :]
    place = Place(dims.row_count, dims.col_count)
    takes = [(image_take(image), 2 * dims.h, dims.rows, dims.cols)]
    write_strips(place, outs, takes, other_combos(dims.row_count))


def grad_others_kernel(dims, grad1, cot, *refs):
    outs = refs[len(band_combos(dims.row_count)) :]
    place = Place(dims.row_count, dims.col_count)
    takes = [
        (flat_take(grad1, dims.cols, dims.channels), 2 * dims.h, dims.rows, dims.cols),
        (image_take(cot), dims.h, dims.rows, dims.cols),
    ]
    write_strips(place, outs, takes, other_combos(dims.row_count))


def weights_kernel(up_in, down_t_in, kernels_in, gains_in, *refs):
    forward0, back0, forward1, back1, grad_in0, grad_out0, taps0, taps1, gains, up_w, down_w, kernels, sems = refs
    fetch((up_in, down_t_in, kernels_in, gains_in), (up_w, down_w, kernels, gains), sems)
    spread_taps(kernels, 0, taps0)
    spread_taps(kernels, 1, taps1)
    channels, units = up_w.shape[1:]
    blank = jnp.zeros((LANES - channels, units), f32)
    wide, tall = ([], [])
    for layer in range(2):
        for ref in (up_w, down_w):
            full = jnp.concatenate([ref[layer].astype(f32), blank], axis=0)
            wide.append(full.astype(bf16))
            tall.append(full.T.astype(bf16))
    (up0, down_t0, up1, down_t1), (up_t0, down0, up_t1, down1) = (wide, tall)
    forward0[...] = diagonal(up0, up0)
    back0[...] = diagonal(down0, down0)
    forward1[...] = diagonal(up1, down_t1)
    back1[...] = diagonal(down1, up_t1)
    grad_in0[...] = diagonal(down_t0, down_t0)
    grad_out0[...] = diagonal(up_t0, up_t0)


def first_kernel(dims, *refs):
    count = len(combos(dims.row_count))
    image, cot, taps0, taps1, gains, forward0, back0, forward1, back1 = refs[:9]
    strips = refs[9 : 9 + count]
    refs = refs[9 + count :]
    (output, x0, x1, unit0, inv0, hidden0, slope0, grad1, normed1, pre_grad1, hidden1, gain_sum) = refs[:12]
    outs, conv = (refs[12:-1], refs[-1])
    place = Place(dims.row_count, dims.col_count)
    rows, cols, channels, h, size = (dims.rows, dims.cols, dims.channels, dims.h, dims.size)
    ext_rows, ext_cols, wide = (dims.ext_rows, dims.ext_cols, dims.wide)
    skip = dims.skipped_rows(place)
    read = received(place, strips, (0, 0))
    assemble(place, x0, lambda i: image[i].astype(f32), read, 2 * h, rows, cols, channels)

    x1[...] = jnp.zeros(x1.shape, f32)
    if dims.ext_pad > ext_rows * ext_cols:
        conv[ext_rows * ext_cols :, :] = jnp.zeros((dims.ext_pad - ext_rows * ext_cols, LANES), f32)
    frame = pl.multiple_of(skip * ext_cols, 8)

    def conv0(g, carry):
        at = group_start(g, ext_cols)
        base = pl.multiple_of(skip * wide, 8) + at
        total = conv_group(x0, base + 1, wide, ext_rows, taps0, size)
        for r in range(ext_rows):
            conv[pl.ds(r * ext_cols + at, 16), :] = total[r]
            x1[pl.ds(frame + r * ext_cols + at, 16), :] = x0[pl.ds(base + (r + h) * wide + 4, 16), :]
        return carry

    lax.fori_loop(0, -(-ext_cols // 16), conv0, 0)
    gain = pad_lanes(gains[0:1, :])
    ones = diagonal(jnp.ones((LANES, LANES), bf16), jnp.ones((LANES, LANES), bf16))
    half = dims.ext_pad // 2
    for start, n in pieces(half, dims.piece):
        spans = [(start, n), (half + start, n)]
        units, inverses = layer_norm([conv[at : at + n, :] for at, n in spans], channels, ones)
        pres = paired_dot(units[0] * gain, units[1] * gain, forward0[...])
        hiddens = []
        for (at, n), unit, inverse, pre in zip(spans, units, inverses, pres):
            unit0[at : at + n, :] = unit.astype(bf16)
            inv0[at : at + n, :] = inverse
            value, slope = gelu_parts(pre)
            hiddens.append(value.astype(bf16))
            hidden0[at : at + n, :] = hiddens[-1]
            slope0[at : at + n, :] = slope.astype(bf16)
        branches = paired_dot(hiddens[0], hiddens[1], back0[...])
        for (at, n), branch in zip(spans, branches):
            px = pl.ds(frame + at, n)
            x1[px, :] = round16(x1[px, :] + branch)
    clear_outside(place, x1, dims)

    def conv1(g, carry):
        at = group_start(g, cols)
        total = conv_group(x1, at + 1, ext_cols, rows, taps1, size)
        for r in range(rows):
            conv[pl.ds(r * cols + at, 16), :] = total[r]
        return carry

    lax.fori_loop(0, -(-cols // 16), conv1, 0)
    gain1 = pad_lanes(gains[1:2, :])
    gain_sum[...] = jnp.zeros(gain_sum.shape, f32)
    lines = dims.line_step
    step = lines * cols
    for k in range(rows // lines):
        px = slice(k * step, (k + 1) * step)
        middle = k * step + step // 2
        units, inverses = layer_norm([conv[k * step : middle, :], conv[middle : (k + 1) * step, :]], channels, ones)
        unit, inverse = (jnp.concatenate(units, axis=0), jnp.concatenate(inverses, axis=0))
        normed = (unit * gain1).astype(bf16)
        normed1[px, :] = normed
        upstream = pad_lanes(cot[k * lines : (k + 1) * lines].reshape(step, channels))
        pre, hidden_grad = paired_dot(normed, upstream, forward1[...])
        value, slope = gelu_parts(pre)
        hidden = value.astype(bf16)
        hidden1[px, :] = hidden
        pre_grad = (hidden_grad * slope).astype(bf16)
        pre_grad1[px, :] = pre_grad
        branch, normed_grad = paired_dot(hidden, pre_grad, back1[...])
        for i in range(lines):
            start = (k * lines + i + h) * ext_cols + 4
            line = x1[start : start + cols, :] + branch[i * cols : (i + 1) * cols]
            output[k * lines + i] = line[:, :channels].astype(bf16)
        product = normed_grad * unit
        gain_sum[...] += jnp.sum(product.reshape(step // 8, 8, LANES), axis=0)
        grad1[px, :] = round16(norm_backward(normed_grad, unit, inverse, gain1, channels, ones))

    takes = [(flat_take(grad1, cols, channels), 2 * h, rows, cols), (image_take(cot), h, rows, cols)]
    write_strips(place, outs, takes, band_combos(dims.row_count))


def clear_outside(place, flat, dims):
    h, frame_rows, ext_cols = (dims.h, dims.rows + 2 * dims.h, dims.ext_cols)
    margin = (ext_cols - dims.cols) // 2

    @pl.when(jnp.logical_not(place.has["above"]))
    def _():
        flat[0 : h * ext_cols, :] = jnp.zeros((h * ext_cols, LANES), f32)

    @pl.when(jnp.logical_not(place.has["below"]))
    def _():
        last = (frame_rows - h) * ext_cols
        flat[last:, :] = jnp.zeros((flat.shape[0] - last, LANES), f32)

    @pl.when(jnp.logical_not(place.has["left"]))
    def _():
        for r in range(frame_rows):
            flat[r * ext_cols : r * ext_cols + margin, :] = jnp.zeros((margin, LANES), f32)

    @pl.when(jnp.logical_not(place.has["right"]))
    def _():
        for r in range(frame_rows):
            flat[(r + 1) * ext_cols - margin : (r + 1) * ext_cols, :] = jnp.zeros((margin, LANES), f32)


def sums_kernel(
    dims, x1, grad1, normed1, pre_grad1, hidden1, cot, gain_part, final, taps_sum, up_sum, down_sum, output, sums
):
    output[...] = final[...]
    kernel_sums(x1, 1, dims.ext_cols, grad1, 0, dims.cols, dims.rows, dims.cols, dims.size, sums)
    store_sums(dims, sums, gain_part[...], taps_sum)
    upstream = pad_lanes(cot[...].reshape(dims.rows * dims.cols, dims.channels))
    up_sum[...] = dot_leading(normed1[...], pre_grad1[...]).T
    down_sum[...] = dot_leading(upstream, hidden1[...]).T


def store_sums(dims, sums, gain_part, target):
    taps = dims.size * dims.size
    target[...] = jnp.zeros(target.shape, f32)
    for t in range(taps):
        target[t : t + 1, :] = jnp.sum(sums[t * 8 : t * 8 + 8, :], axis=0, keepdims=True)
    target[taps : taps + 1, :] = jnp.sum(gain_part, axis=0, keepdims=True)


def third_kernel(dims, *refs):
    count = len(combos(dims.row_count))
    (grad1, cot, taps1, gains, grad_in0, grad_out0, x0, unit0, inv0, hidden0, slope0) = refs[:11]
    (taps_sum1, up_sum1, down_sum1) = refs[11:14]
    strips = refs[14 : 14 + count]
    (grad0, middle, keep, small_keep, send) = refs[14 + count : 19 + count]
    (wide_grad, cot_frame, upstream, own, sums, up_acc, down_acc, gain_sum, small, tall, slabs) = refs[19 + count :]
    place = Place(dims.row_count, dims.col_count)
    rows, cols, channels, h, size = (dims.rows, dims.cols, dims.channels, dims.h, dims.size)
    ext_rows, ext_cols, wide = (dims.ext_rows, dims.ext_cols, dims.wide)
    skip = dims.skipped_rows(place)
    read = received(place, strips, (0, 0))
    assemble(
        place, wide_grad, lambda i: grad1[i * cols : (i + 1) * cols, 0:channels], read, 2 * h, rows, cols, channels
    )
    read_cot = received(place, strips, (rows, 2 * h))
    margin = (ext_cols - cols) // 2
    cot_frame[...] = jnp.zeros(cot_frame.shape, f32)
    for vertical, start, n in (("above", 0, h), (None, h, rows), ("below", h + rows, h)):
        for i in range(n):
            base = (start + i) * ext_cols
            line = cot[i].astype(f32) if vertical is None else read_cot(vertical, None, i)
            cot_frame[base + margin : base + margin + cols, 0:channels] = line
            cot_frame[base : base + margin, 0:channels] = read_cot(vertical, "left", i)[SIDE - margin :]
            cot_frame[base + margin + cols : base + ext_cols, 0:channels] = read_cot(vertical, "right", i)[:margin]

    used = ext_rows * ext_cols
    if dims.ext_pad > used:
        upstream[used:, :] = jnp.zeros((dims.ext_pad - used, LANES), f32)
        own[used:, :] = jnp.zeros((dims.ext_pad - used, LANES), f32)
    grad0[...] = jnp.zeros(grad0.shape, f32)
    frame = pl.multiple_of(skip * ext_cols, 8)

    def conv1(g, carry):
        at = group_start(g, ext_cols)
        total = conv_group(wide_grad, pl.multiple_of(skip * wide, 8) + at + 1, wide, ext_rows, taps1, size, True)
        col = lax.broadcasted_iota(jnp.int32, (16, LANES), 0) + (at - margin)
        inside = jnp.where(jnp.logical_and(col >= 0, col < cols), 1.0, 0.0)
        for r in range(ext_rows):
            px = pl.ds(r * ext_cols + at, 16)
            upstream[px, :] = cot_frame[pl.ds(frame + r * ext_cols + at, 16), :] + total[r]
            mine = jnp.logical_and(r + skip >= h, r + skip < h + rows)
            own[px, :] = jnp.where(mine, inside, 0.0)
        return carry

    lax.fori_loop(0, -(-ext_cols // 16), conv1, 0)
    for i in range(rows):
        line = upstream[pl.ds((i + h - skip) * ext_cols + margin, cols), :]
        middle[i * cols : (i + 1) * cols, :] = round16(line)

    gain = pad_lanes(gains[0:1, :])
    gain_sum[...] = jnp.zeros(gain_sum.shape, f32)
    up_acc[...] = jnp.zeros(up_acc.shape, f32)
    down_acc[...] = jnp.zeros(down_acc.shape, f32)
    ones = diagonal(jnp.ones((LANES, LANES), bf16), jnp.ones((LANES, LANES), bf16))
    half_px = dims.ext_pad // 2
    for start, n in pieces(half_px, dims.piece):
        spans = [(start, n), (half_px + start, n)]
        flows = [upstream[at : at + n, :].astype(bf16) for at, n in spans]
        hidden_grads = paired_dot(flows[0], flows[1], grad_in0[...])
        pre_grads = [
            (grad * slope0[at : at + n, :].astype(f32)).astype(bf16) for grad, (at, n) in zip(hidden_grads, spans)
        ]
        normed_grads = paired_dot(pre_grads[0], pre_grads[1], grad_out0[...])
        for (at, n), flow, pre_grad, normed_grad in zip(spans, flows, pre_grads, normed_grads):
            mine = own[at : at + n, :]
            unit = unit0[at : at + n, :].astype(f32)
            normed = (unit * gain * mine).astype(bf16)
            up_acc[...] += dot_leading(normed, pre_grad)
            down_acc[...] += dot_leading(flow * mine.astype(bf16), hidden0[at : at + n, :])
            product = normed_grad * unit * mine
            gain_sum[...] += jnp.sum(product.reshape(n // 8, 8, LANES), axis=0)
            grad = norm_backward(normed_grad, unit, inv0[at : at + n, :], gain, channels, ones)
            grad0[pl.ds(frame + at, n), :] = round16(grad)
    clear_outside(place, grad0, dims)
    kernel_sums(
        x0, h * wide + SIDE - h, wide, grad0, h * ext_cols + margin, ext_cols, rows, cols, size, sums
    )
    store_sums(dims, sums, gain_sum[...], small)

    taps_rows = size * size + 1
    merged = jnp.concatenate([small[0:taps_rows, :], taps_sum1[0:taps_rows, :]], axis=0) * dims.factor
    merged = jnp.concatenate([merged, jnp.zeros((dims.small_rows - 2 * taps_rows, LANES), f32)], axis=0)
    merged = merged.astype(bf16)
    small_keep[...] = merged.astype(f32)

    layer_rows, part, half = (dims.layer_rows, dims.part, dims.half)
    units = up_acc.shape[1]
    up0 = up_acc[...].T * dims.factor
    down0 = down_acc[...].T * dims.factor
    up1 = up_sum1[...] * dims.factor
    down1 = down_sum1[...] * dims.factor
    lane = lax.broadcasted_iota(jnp.int32, (units, LANES), 1)
    slab_rows = 2 * layer_rows
    for r in range(dims.row_count):
        for layer, (u, d) in enumerate(((up0, down0), (up1, down1))):
            first = pltpu.roll(u, LANES - r * half, 1) if r else u
            shift = (half - r * half) % LANES
            second = pltpu.roll(d, shift, 1) if shift else d
            joined = jnp.where(lane < half, first, jnp.where(lane < 2 * half, second, 0.0))
            tall[layer * (units + 8) : layer * (units + 8) + units, :] = joined

        def slab(c, carry, r=r):
            index = 0
            for j, (axis, bit) in enumerate(dims.stages):
                value = (r >> bit) & 1 if axis == "row" else lax.rem(lax.div(c, 1 << bit), 2)
                index = index + value * (1 << (len(dims.stages) - 1 - j))
            for layer in range(2):
                to = pl.multiple_of(index * slab_rows + layer * layer_rows, 8)
                slabs[pl.ds(to, layer_rows), :] = tall[pl.ds(layer * (units + 8) + c * part, layer_rows), :]
            return carry

        lax.fori_loop(0, dims.col_count, slab, 0)

    split(dims, 0, slabs, merged, keep, (send,))


def split(dims, stage, slabs, merged, keep, sends):
    group = dims.groups[stage]
    count = slabs.shape[0] >> len(group)
    mine = 0
    for axis, bit in group:
        mine = mine * 2 + lax.rem(lax.div(lax.axis_index(axis), 1 << bit), 2)
    keep[...] = slabs[pl.ds(pl.multiple_of(mine * count, 16), count), :]
    for mask, send in enumerate(sends, 1):
        other = 0
        for j in range(len(group)):
            weight = 1 << j
            digit = lax.rem(lax.div(mine, weight), 2)
            other = other + weight * (1 - digit if mask & weight else digit)
        send[0:count, :] = slabs[pl.ds(pl.multiple_of(other * count, 16), count), :].astype(bf16)
        send[count:, :] = merged


def gather_up(keep, small, gots):
    count = keep.shape[0]
    slabs = [keep[...]] + [got[0:count, :].astype(f32) for got in gots]
    sums = [small[...]] + [got[count:, :].astype(f32) for got in gots]
    if len(gots) == 1:
        return (slabs[0] + slabs[1], sums[0] + sums[1])
    return tuple((x[0] + x[1]) + (x[2] + x[3]) for x in (slabs, sums))


def stage_kernel(dims, stage, keep, small, *refs):
    before, after = (len_sends(dims.groups[stage - 1]), len_sends(dims.groups[stage]))
    gots = refs[:before]
    keep_out, small_out = refs[-3 - after : -1 - after]
    sends, total = (refs[-1 - after : -1], refs[-1])
    slabs, merged = gather_up(keep, small, gots)
    total[...] = slabs
    merged = merged.astype(bf16)
    small_out[...] = merged.astype(f32)
    split(dims, stage, total, merged, keep_out, sends)


def len_sends(group):
    return (1 << len(group)) - 1


def last_kernel(dims, keep, small, *refs):
    gots, (kernel_out, gain_out, up_out, down_out) = (refs[:-4], refs[-4:])
    total, merged = gather_up(keep, small, gots)
    size, channels, half, part = (dims.size, dims.channels, dims.half, dims.part)
    for layer in range(2):
        block = total[layer * dims.layer_rows : layer * dims.layer_rows + part]
        up_out[layer] = block[:, :half]
        down_out[layer] = block[:, half : 2 * half]
        for t in range(size * size + 1):
            at = layer * (size * size + 1) + t
            row = merged[at : at + 1, 0:channels]
            if t < size * size:
                kernel_out[t // size, t % size, layer : layer + 1, :] = row
            else:
                gain_out[layer : layer + 1, :] = row


def image_kernel(dims, grad0, middle, taps0, after, out, ready, work):
    rows, cols, size = (dims.rows, dims.cols, dims.size)

    def conv0(g, carry):
        at = group_start(g, cols)
        total = conv_group(grad0, at + 1, dims.ext_cols, rows, taps0, size, True)
        for r in range(rows):
            work[pl.ds(r * cols + at, 16), :] = middle[pl.ds(r * cols + at, 16), :] + total[r]
        return carry

    lax.fori_loop(0, -(-cols // 16), conv0, 0)
    for r in range(rows):
        out[r] = work[r * cols : (r + 1) * cols, 0 : dims.channels].astype(bf16)
    ready[...] = jnp.zeros(ready.shape, f32)


class Dims:
    def skipped_rows(self, place):
        if self.row_count > 2:
            return 0
        return jnp.where(place.has["above"], 0, self.h)


def dims_of(image, kernels, up_weights):
    d = Dims()
    d.row_count, d.col_count = (lax.axis_size("row"), lax.axis_size("col"))
    d.rows, d.cols, d.channels = image.shape
    d.size = kernels.shape[1]
    d.h = d.size // 2
    d.ext_rows, d.ext_cols = (d.rows + (d.h if d.row_count == 2 else 2 * d.h), d.cols + 8)
    d.wide = d.cols + 2 * SIDE
    d.ext_pad = -(-d.ext_rows * d.ext_cols // 32) * 32
    d.piece = 176
    d.line_step = 4
    d.half = d.channels // d.row_count
    d.part = up_weights.shape[2] // d.col_count
    d.layer_rows = ceil8(d.part)
    d.count = d.row_count * d.col_count
    d.small_rows = -(-2 * (d.size * d.size + 1) // 16) * 16
    d.factor = 1.0 / math.sqrt(d.rows * d.cols * d.count)
    row_bits, col_bits = (d.row_count.bit_length() - 1, d.col_count.bit_length() - 1)
    bits = [("row", b) for b in range(row_bits)] + [("col", b) for b in range(1, col_bits)]
    d.groups = [[("col", 0)]] + [bits[i : i + 2] for i in range(0, len(bits), 2)]
    d.stages = [bit for group in d.groups for bit in group]
    return d


def swap_by(d, group, mask):
    flip = {"row": 0, "col": 0}
    for j, (axis, bit) in enumerate(group):
        if mask >> (len(group) - 1 - j) & 1:
            flip[axis] |= 1 << bit
    pairs = []
    for r in range(d.row_count):
        for c in range(d.col_count):
            pairs.append((r * d.col_count + c, (r ^ flip["row"]) * d.col_count + (c ^ flip["col"])))
    return pairs


def run(kernel, outs, scratch, *args, in_hbm=0, sems=0, busy_us=1):
    shapes = [jax.ShapeDtypeStruct(shape, kind) for shape, kind in outs]
    space = pl.BlockSpec(memory_space=pltpu.VMEM)
    far = pl.BlockSpec(memory_space=pltpu.HBM)
    held = [pltpu.VMEM(shape, kind) for shape, kind in scratch]
    if sems:
        held.append(pltpu.SemaphoreType.DMA((sems,)))
    return pl.pallas_call(
        kernel,
        out_shape=shapes,
        in_specs=[far] * in_hbm + [space] * (len(args) - in_hbm),
        out_specs=[space] * len(shapes),
        scratch_shapes=held,
        compiler_params=pltpu.CompilerParams(vmem_limit_bytes=32 * 1024 * 1024),
        cost_estimate=pl.CostEstimate(flops=int(busy_us * 1e9), bytes_accessed=1 << 18, transcendentals=0),
    )(*args)


def per_device(image, kernels, gains, up_weights, down_weights, cotangent):
    d = dims_of(image, kernels, up_weights)
    bind = functools.partial
    rows, cols, channels = image.shape
    units = up_weights.shape[2]
    tile, ext, wide = (rows * cols, d.ext_pad, (rows + 4 * d.h) * d.wide)
    frame = (rows + 2 * d.h) * d.ext_cols + 16
    taps = ((d.size * d.size * 16, LANES), bf16)
    tap_sums = ((d.size * d.size * 8, LANES), f32)
    sums_rows = ceil8(d.size * d.size + 1)

    bands, others = (band_combos(d.row_count), other_combos(d.row_count))

    def strips_of(pairs, radii):
        return [(shape, bf16) for shape in strip_shapes(pairs, rows, cols, channels, radii)]

    image, *band_strips = run(
        bind(bands_kernel, d), [(image.shape, bf16)] + strips_of(bands, (2 * d.h,)), [], image, in_hbm=1, sems=1
    )
    other_strips = run(bind(others_kernel, d), strips_of(others, (2 * d.h,)), [], image, *band_strips)
    strips = exchange(band_strips, other_strips, d.row_count, d.col_count)
    mixing = [((2 * LANES, 2 * units), bf16), ((2 * units, 2 * LANES), bf16)]
    forward0, back0, forward1, back1, grad_in0, grad_out0, taps0, taps1, gains = run(
        weights_kernel,
        mixing * 3 + [taps, taps, (gains.shape, f32)],
        [((2, channels, units), bf16), ((2, channels, units), bf16), ((d.size, d.size, 2, channels), f32)],
        up_weights,
        jnp.swapaxes(down_weights, 1, 2),
        jnp.transpose(kernels, (1, 2, 0, 3)),
        gains,
        in_hbm=4,
        sems=4,
        busy_us=2,
    )

    first = run(
        bind(first_kernel, d),
        [
            (image.shape, bf16),
            ((wide, LANES), f32),
            ((frame, LANES), f32),
            ((ext, LANES), bf16),
            ((ext, LANES), f32),
            ((ext, units), bf16),
            ((ext, units), bf16),
            ((tile, LANES), f32),
            ((tile, LANES), bf16),
            ((tile, units), bf16),
            ((tile, units), bf16),
            ((8, LANES), f32),
        ]
        + strips_of(bands, (2 * d.h, d.h)),
        [((ext, LANES), f32)],
        image,
        cotangent,
        taps0,
        taps1,
        gains,
        forward0,
        back0,
        forward1,
        back1,
        *strips,
        busy_us=15,
    )
    (final, x0, x1, unit0, inv0, hidden0, slope0, grad1, normed1, pre_grad1, hidden1, gain_part) = first[:12]
    band_strips = first[12:]
    other_strips = run(
        bind(grad_others_kernel, d), strips_of(others, (2 * d.h, d.h)), [], grad1, cotangent, *band_strips
    )
    strips = exchange(band_strips, other_strips, d.row_count, d.col_count)

    taps_sum1, up_sum1, down_sum1, output = run(
        bind(sums_kernel, d),
        [((sums_rows, LANES), f32), ((units, LANES), f32), ((units, LANES), f32), (image.shape, bf16)],
        [tap_sums],
        x1,
        grad1,
        normed1,
        pre_grad1,
        hidden1,
        cotangent,
        gain_part,
        final,
        busy_us=3,
    )

    held = d.count // 2 * 2 * d.layer_rows
    small = ((d.small_rows, LANES), f32)
    grad0, middle, keep, sums, send = run(
        bind(third_kernel, d),
        [((frame, LANES), f32), ((tile, LANES), f32), ((held, LANES), f32), small, ((held + d.small_rows, LANES), bf16)],
        [
            ((wide, LANES), f32),
            ((frame, LANES), f32),
            ((ext, LANES), f32),
            ((ext, LANES), f32),
            tap_sums,
            ((LANES, units), f32),
            ((LANES, units), f32),
            ((8, LANES), f32),
            ((sums_rows, LANES), f32),
            ((2 * (units + 8), LANES), f32),
            ((2 * held, LANES), f32),
        ],
        grad1,
        cotangent,
        taps1,
        gains,
        grad_in0,
        grad_out0,
        x0,
        unit0,
        inv0,
        hidden0,
        slope0,
        taps_sum1,
        up_sum1,
        down_sum1,
        *strips,
        busy_us=12,
    )
    axes = ("row", "col")
    sends = [send]
    for stage, group in enumerate(d.groups):
        gots = [lax.ppermute(x, axes, swap_by(d, group, mask)) for mask, x in enumerate(sends, 1)]
        ready = []
        if stage == 1:
            gradient, *ready = run(
                bind(image_kernel, d),
                [(image.shape, bf16), ((8, LANES), f32)],
                [((tile, LANES), f32)],
                grad0,
                middle,
                taps0,
                sums,
                busy_us=3,
            )
        if stage + 1 < len(d.groups):
            after = d.groups[stage + 1]
            whole, held = (held, held >> len(after))
            keep, sums, *sends = run(
                bind(stage_kernel, d, stage + 1),
                [((held, LANES), f32), small] + [((held + d.small_rows, LANES), bf16)] * len_sends(after),
                [((whole, LANES), f32)],
                keep,
                sums,
                *gots,
                *ready,
            )
    kernel_out, gain_out, up_out, down_out = run(
        bind(last_kernel, d),
        [
            ((d.size, d.size, 2, channels), f32),
            (gains.shape, f32),
            ((2, d.part, d.half), f32),
            ((2, d.part, d.half), f32),
        ],
        [],
        keep,
        sums,
        *gots,
    )
    kernel_out = jnp.transpose(kernel_out, (2, 0, 1, 3))
    return (output, gradient, kernel_out, gain_out, jnp.swapaxes(up_out, 1, 2), down_out)


def solution(mesh):
    placed = (P("row", "col", None), P(), P(), P(), P(), P("row", "col", None))
    return jax.shard_map(
        per_device,
        mesh=mesh,
        in_specs=placed,
        out_specs=(
            P("row", "col", None),
            P("row", "col", None),
            P(),
            P(),
            P(None, "row", "col"),
            P(None, "col", "row"),
        ),
        check_vma=False,
    )
```

```python
import functools
import math

import jax
import jax.numpy as jnp
from jax import lax
from jax.experimental import pallas as pl
from jax.experimental.pallas import tpu as pltpu
from jax.sharding import PartitionSpec as P

epsilon = 1e-06
inv_sqrt_two = 0.7071067811865476
inv_sqrt_two_pi = 0.3989422804014327
log2_e = 1.4426950408889634
LANES = 128
SIDE = 8
f32, bf16 = (jnp.float32, jnp.bfloat16)


def ceil8(n):
    return -(-n // 8) * 8


def band_starts(row_count):
    return [0] if row_count == 2 else [0, 1]


def partner(index, start, count):
    if start is None:
        return index
    other = index + 1 if (index - start) % 2 == 0 else index - 1
    return other if 0 <= other < count else None


def swap_pairs(row_count, col_count, row_start, col_start):
    pairs = []
    for r in range(row_count):
        for c in range(col_count):
            pr, pc = (partner(r, row_start, row_count), partner(c, col_start, col_count))
            if pr is None:
                pr, pc = (r, c ^ 1)
            elif pc is None:
                pr, pc = (r ^ 1 if row_start is None else pr, c)
            pairs.append((r * col_count + c, pr * col_count + pc))
    return pairs


def swap_bands(bands, row_count, col_count):
    axes = ("row", "col")
    starts = band_starts(row_count)
    return [lax.ppermute(x, axes, swap_pairs(row_count, col_count, s, None)) for x, s in zip(bands, starts)]


def swap_columns(strips, row_count, col_count):
    axes = ("row", "col")
    return [lax.ppermute(x, axes, swap_pairs(row_count, col_count, None, s)) for s, x in enumerate(strips)]


class Place:
    def __init__(self, row_count, col_count):
        row, col = (lax.axis_index("row"), lax.axis_index("col"))
        self.even_row, self.even_col = (lax.rem(row, 2) == 0, lax.rem(col, 2) == 0)
        self.has = {
            "above": row > 0,
            "below": row < row_count - 1,
            "left": col > 0,
            "right": col < col_count - 1,
        }
        self.row_count = row_count

    def pick_band(self, bands, vertical):
        if self.row_count == 2:
            return lambda i: bands[0][i]
        near, far = ((0, 1) if vertical == "below" else (1, 0))
        return lambda i: jnp.where(self.even_row, bands[near][i].astype(f32), bands[far][i].astype(f32))


def write_bands(place, outs, takes):
    for out, start in zip(outs, band_starts(place.row_count)):
        at = 0
        for take, radius, rows in takes:
            for i in range(radius):
                low, high = (take(i), take(rows - radius + i))
                value = jnp.where(place.even_row, high, low) if start == 0 else jnp.where(place.even_row, low, high)
                out[at + i] = value.astype(out.dtype)
            at += radius


def tall_rows(place, bands, at, own, radius, rows):
    listed = []
    for i in range(radius):
        listed.append((place.pick_band(bands, "above"), at + i, "above"))
    for i in range(rows):
        listed.append((own, i, None))
    for i in range(radius):
        listed.append((place.pick_band(bands, "below"), at + i, "below"))
    for take, i, vertical in listed:
        value = take(i).astype(f32)
        yield value if vertical is None else jnp.where(place.has[vertical], value, 0.0)


def write_columns(place, outs, row, value):
    cols = value.shape[0]
    first, last = (value[0:SIDE], value[cols - SIDE : cols])
    outs[0][row] = jnp.where(place.even_col, last, first).astype(bf16)
    outs[1][row] = jnp.where(place.even_col, first, last).astype(bf16)


def side_columns(place, strips, row, side):
    near, far = (strips[0][row].astype(f32), strips[1][row].astype(f32))
    if side == "left":
        value = jnp.where(place.even_col, far, near)
    else:
        value = jnp.where(place.even_col, near, far)
    return jnp.where(place.has[side], value, 0.0)


def frame_rows(place, target, tall, strips, at, rows, cols, margin, channels):
    width = cols + 2 * margin
    target[...] = jnp.zeros(target.shape, f32)
    for i in range(rows):
        base = i * width
        target[base + margin : base + margin + cols, :] = tall[i * cols : (i + 1) * cols, :]
        target[base : base + margin, 0:channels] = side_columns(place, strips, at + i, "left")[SIDE - margin :]
        target[base + margin + cols : base + width, 0:channels] = side_columns(place, strips, at + i, "right")[:margin]


def spread_taps(kernel_ref, layer, target):
    size, channels = (kernel_ref.shape[0], kernel_ref.shape[3])
    for a in range(size):
        for b in range(size):
            t = a * size + b
            row = pad_lanes(kernel_ref[a, b, layer : layer + 1, :])
            target[t * 16 : t * 16 + 16, :] = jnp.broadcast_to(row, (16, LANES)).astype(bf16)


def tree_sum(terms):
    while len(terms) > 1:
        pairs = [terms[i] + terms[i + 1] for i in range(0, len(terms) - 1, 2)]
        terms = pairs + ([terms[-1]] if len(terms) % 2 else [])
    return terms[0]


def conv_group(src, base, stride, rows_out, taps, size, flipped=False):
    total = [None] * rows_out
    for b in range(size):
        order = [a * size + b for a in range(size)]
        if flipped:
            order = [size * size - 1 - t for t in order]
        weights = [taps[t * 16 : t * 16 + 16, :] for t in order]
        window = []
        for i in range(rows_out + size - 1):
            window.append(src[pl.ds(base + i * stride + b, 16), :].astype(bf16))
            r = i - size + 1
            if r >= 0:
                term = tree_sum([window[r + a] * weights[a] for a in range(size)]).astype(f32)
                total[r] = term if total[r] is None else total[r] + term
    return total


def group_start(g, cols):
    return pl.multiple_of(jnp.minimum(g * 16, cols - 16), 8)


def kernel_sums(src, src_base, src_stride, grad, grad_base, grad_stride, rows, cols, size, sums):
    sums[...] = jnp.zeros(sums.shape, f32)

    def group(g, carry):
        at = pl.multiple_of(g * 16, 16)
        grads = [grad[pl.ds(grad_base + i * grad_stride + at, 16), :].astype(bf16) for i in range(rows)]
        for b in range(size):
            lines = [
                src[pl.ds(src_base + i * src_stride + at + b, 16), :].astype(bf16) for i in range(rows + size - 1)
            ]
            for a in range(size):
                term = tree_sum([lines[r + a] * grads[r] for r in range(rows)]).astype(f32)
                t = (a * size + b) * 8
                sums[t : t + 8, :] += term[0:8] + term[8:16]
        return carry

    lax.fori_loop(0, cols // 16, group, 0)


def diagonal(first, second):
    top = jnp.concatenate([first, jnp.zeros((first.shape[0], second.shape[1]), first.dtype)], axis=1)
    bottom = jnp.concatenate([jnp.zeros((second.shape[0], first.shape[1]), first.dtype), second], axis=1)
    return jnp.concatenate([top, bottom], axis=0)


def lane_total(x):
    high = x.astype(bf16)
    low = (x - high.astype(f32)).astype(bf16)
    both = jnp.concatenate([high, low], axis=1)
    return dot(both, jnp.ones((2 * LANES, LANES), bf16))


def paired_dot(x, y, weights):
    total = dot(jnp.concatenate([x.astype(bf16), y.astype(bf16)], axis=1), weights)
    half = weights.shape[1] // 2
    return (total[:, :half], total[:, half:])


def layer_norm(parts, channels, ones):
    lane = lax.broadcasted_iota(jnp.int32, parts[0].shape, 1)
    centred = [jnp.where(lane < channels, x - lane_total(x) * (1.0 / channels), 0.0) for x in parts]
    variances = paired_dot(centred[0] * centred[0], centred[1] * centred[1], ones)
    inverses = [lax.rsqrt(v * (1.0 / channels) + epsilon) for v in variances]
    return ([c * i for c, i in zip(centred, inverses)], inverses)


def norm_backward(normed_grad, unit, inverse, gain, channels, ones):
    m = normed_grad * gain
    mean, along = paired_dot(m, m * unit, ones)
    lane = lax.broadcasted_iota(jnp.int32, m.shape, 1)
    centred = m - (mean + unit * along) * (1.0 / channels)
    return jnp.where(lane < channels, inverse * centred, 0.0)


def gelu_parts(v):
    p = 0.3275911 * inv_sqrt_two
    c1, c2, c3, c4, c5 = (
        0.5 * c / p ** (k + 1)
        for k, c in enumerate((0.254829592, -0.284496736, 1.421413741, -1.453152027, 1.061405429))
    )
    t = pl.reciprocal(jnp.abs(v) + 1.0 / p, approx=True)
    bell = jnp.exp2(v * v * (-0.5 * log2_e))
    tail = ((((c5 * t + c4) * t + c3) * t + c2) * t + c1) * t * bell
    cdf = jnp.where(v >= 0.0, 1.0 - tail, tail)
    return (v * cdf, cdf + v * (bell * inv_sqrt_two_pi))


def dot(x, w):
    return jnp.dot(x, w, preferred_element_type=f32)


def dot_leading(x, y):
    return lax.dot_general(x, y, (((0,), (0,)), ((), ())), preferred_element_type=f32)


def pad_lanes(x):
    rows, channels = x.shape
    return jnp.concatenate([x, jnp.zeros((rows, LANES - channels), x.dtype)], axis=1)


def pieces(total, size):
    return [(start, min(size, total - start)) for start in range(0, total, size)]


def round16(x):
    return x.astype(bf16).astype(f32)


def fetch(sources, targets, sems):
    copies = [pltpu.make_async_copy(a, b, sems.at[i]) for i, (a, b) in enumerate(zip(sources, targets))]
    for copy in copies:
        copy.start()
    for copy in copies:
        copy.wait()


def bands_kernel(dims, image_in, image, *refs):
    outs, sems = (refs[:-1], refs[-1])
    place = Place(dims.row_count, dims.col_count)
    fetch((image_in,), (image,), sems)
    write_bands(place, outs, [(lambda i: image[i].astype(f32), 2 * dims.h, dims.rows)])


def columns_kernel(dims, image, *refs):
    bands, (tall, first, second) = (refs[:-3], refs[-3:])
    place = Place(dims.row_count, dims.col_count)
    cols, channels = (dims.cols, dims.channels)
    tall[...] = jnp.zeros(tall.shape, f32)
    for i, value in enumerate(tall_rows(place, bands, 0, lambda i: image[i], 2 * dims.h, dims.rows)):
        tall[i * cols : (i + 1) * cols, 0:channels] = value
        write_columns(place, (first, second), i, value)


def grad_columns_kernel(dims, grad1, cot, *refs):
    bands, (tall, tall_cot, first, second) = (refs[:-4], refs[-4:])
    place = Place(dims.row_count, dims.col_count)
    cols, channels, h, rows = (dims.cols, dims.channels, dims.h, dims.rows)
    tall[...] = jnp.zeros(tall.shape, f32)
    tall_cot[...] = jnp.zeros(tall_cot.shape, f32)

    def own(i):
        return grad1[i * cols : (i + 1) * cols, 0:channels]

    for i, value in enumerate(tall_rows(place, bands, 0, own, 2 * h, rows)):
        tall[i * cols : (i + 1) * cols, 0:channels] = value
        write_columns(place, (first, second), i, value)
    for i, value in enumerate(tall_rows(place, bands, 2 * h, lambda i: cot[i], h, rows)):
        tall_cot[i * cols : (i + 1) * cols, 0:channels] = value
        write_columns(place, (first, second), rows + 4 * h + i, value)


def middle_groups(ext_cols):
    starts = list(range(16, ext_cols - 16 - 8 + 1, 16))
    return (starts, [0, ext_cols - 16])


def middle_kernel(dims, flipped, tall, taps, out):
    cols, ext_rows, margin = (dims.cols, dims.ext_rows, (dims.ext_cols - dims.cols) // 2)
    skip = dims.skipped_rows(Place(dims.row_count, dims.col_count))
    width = dims.middle_cols

    def group(g, carry):
        at = pl.multiple_of(g * 16, 16)
        base = pl.multiple_of(skip * cols, 8) + at + 16 - margin - dims.h
        total = conv_group(tall, base, cols, ext_rows, taps, dims.size, flipped)
        for r in range(ext_rows):
            out[pl.ds(r * width + at, 16), :] = total[r]
        return carry

    lax.fori_loop(0, width // 16, group, 0)


def weights_kernel(up_in, down_t_in, kernels_in, gains_in, *refs):
    forward0, back0, forward1, back1, grad_in0, grad_out0, taps0, taps1, gains, up_w, down_w, kernels, sems = refs
    fetch((up_in, down_t_in, kernels_in, gains_in), (up_w, down_w, kernels, gains), sems)
    spread_taps(kernels, 0, taps0)
    spread_taps(kernels, 1, taps1)
    channels, units = up_w.shape[1:]
    blank = jnp.zeros((LANES - channels, units), f32)
    wide, tall = ([], [])
    for layer in range(2):
        for ref in (up_w, down_w):
            full = jnp.concatenate([ref[layer].astype(f32), blank], axis=0)
            wide.append(full.astype(bf16))
            tall.append(full.T.astype(bf16))
    (up0, down_t0, up1, down_t1), (up_t0, down0, up_t1, down1) = (wide, tall)
    forward0[...] = diagonal(up0, up0)
    back0[...] = diagonal(down0, down0)
    forward1[...] = diagonal(up1, down_t1)
    back1[...] = diagonal(down1, up_t1)
    grad_in0[...] = diagonal(down_t0, down_t0)
    grad_out0[...] = diagonal(up_t0, up_t0)


def first_kernel(dims, *refs):
    tall, done, cot, taps0, taps1, gains, forward0, back0, forward1, back1 = refs[:10]
    strips = refs[10:12]
    refs = refs[12:]
    (output, x0, x1, unit0, inv0, hidden0, slope0, grad1, normed1, pre_grad1, hidden1, gain_sum) = refs[:12]
    outs, conv = (refs[12:-1], refs[-1])
    place = Place(dims.row_count, dims.col_count)
    rows, cols, channels, h, size = (dims.rows, dims.cols, dims.channels, dims.h, dims.size)
    ext_rows, ext_cols, wide = (dims.ext_rows, dims.ext_cols, dims.wide)
    skip = dims.skipped_rows(place)
    frame_rows(place, x0, tall, strips, 0, rows + 4 * h, cols, SIDE, channels)

    x1[...] = jnp.zeros(x1.shape, f32)
    if dims.ext_pad > ext_rows * ext_cols:
        conv[ext_rows * ext_cols :, :] = jnp.zeros((dims.ext_pad - ext_rows * ext_cols, LANES), f32)
    frame = pl.multiple_of(skip * ext_cols, 8)

    def conv0(g, carry):
        at = pl.multiple_of(g * (ext_cols - 16), 8)
        base = pl.multiple_of(skip * wide, 8) + at
        total = conv_group(x0, base + 1, wide, ext_rows, taps0, size)
        for r in range(ext_rows):
            conv[pl.ds(r * ext_cols + at, 16), :] = total[r]
        return carry

    lax.fori_loop(0, 2, conv0, 0)
    for r in range(ext_rows):
        width = dims.middle_cols
        conv[r * ext_cols + 16 : r * ext_cols + 16 + width, :] = done[r * width : (r + 1) * width, :]
        line = x0[pl.ds(skip * wide + (r + h) * wide + 4, ext_cols), :]
        x1[pl.ds(frame + r * ext_cols, ext_cols), :] = line
    gain = pad_lanes(gains[0:1, :])
    ones = diagonal(jnp.ones((LANES, LANES), bf16), jnp.ones((LANES, LANES), bf16))
    half = dims.ext_pad // 2
    for start, n in pieces(half, dims.piece):
        spans = [(start, n), (half + start, n)]
        units, inverses = layer_norm([conv[at : at + n, :] for at, n in spans], channels, ones)
        pres = paired_dot(units[0] * gain, units[1] * gain, forward0[...])
        hiddens = []
        for (at, n), unit, inverse, pre in zip(spans, units, inverses, pres):
            unit0[at : at + n, :] = unit.astype(bf16)
            inv0[at : at + n, :] = inverse
            value, slope = gelu_parts(pre)
            hiddens.append(value.astype(bf16))
            hidden0[at : at + n, :] = hiddens[-1]
            slope0[at : at + n, :] = slope.astype(bf16)
        branches = paired_dot(hiddens[0], hiddens[1], back0[...])
        for (at, n), branch in zip(spans, branches):
            px = pl.ds(frame + at, n)
            x1[px, :] = round16(x1[px, :] + branch)
    clear_outside(place, x1, dims)

    def conv1(g, carry):
        at = group_start(g, cols)
        total = conv_group(x1, at + 1, ext_cols, rows, taps1, size)
        for r in range(rows):
            conv[pl.ds(r * cols + at, 16), :] = total[r]
        return carry

    lax.fori_loop(0, -(-cols // 16), conv1, 0)
    gain1 = pad_lanes(gains[1:2, :])
    gain_sum[...] = jnp.zeros(gain_sum.shape, f32)
    lines = dims.line_step
    step = lines * cols
    for k in range(rows // lines):
        px = slice(k * step, (k + 1) * step)
        middle = k * step + step // 2
        units, inverses = layer_norm([conv[k * step : middle, :], conv[middle : (k + 1) * step, :]], channels, ones)
        unit, inverse = (jnp.concatenate(units, axis=0), jnp.concatenate(inverses, axis=0))
        normed = (unit * gain1).astype(bf16)
        normed1[px, :] = normed
        upstream = pad_lanes(cot[k * lines : (k + 1) * lines].reshape(step, channels))
        pre, hidden_grad = paired_dot(normed, upstream, forward1[...])
        value, slope = gelu_parts(pre)
        hidden = value.astype(bf16)
        hidden1[px, :] = hidden
        pre_grad = (hidden_grad * slope).astype(bf16)
        pre_grad1[px, :] = pre_grad
        branch, normed_grad = paired_dot(hidden, pre_grad, back1[...])
        for i in range(lines):
            start = (k * lines + i + h) * ext_cols + 4
            line = x1[start : start + cols, :] + branch[i * cols : (i + 1) * cols]
            output[k * lines + i] = line[:, :channels].astype(bf16)
        product = normed_grad * unit
        gain_sum[...] += jnp.sum(product.reshape(step // 8, 8, LANES), axis=0)
        grad1[px, :] = round16(norm_backward(normed_grad, unit, inverse, gain1, channels, ones))

    def own(i):
        return grad1[i * cols : (i + 1) * cols, 0:channels]

    write_bands(place, outs, [(own, 2 * h, rows), (lambda i: cot[i].astype(f32), h, rows)])


def clear_outside(place, flat, dims):
    h, frame_rows, ext_cols = (dims.h, dims.rows + 2 * dims.h, dims.ext_cols)
    margin = (ext_cols - dims.cols) // 2

    @pl.when(jnp.logical_not(place.has["above"]))
    def _():
        flat[0 : h * ext_cols, :] = jnp.zeros((h * ext_cols, LANES), f32)

    @pl.when(jnp.logical_not(place.has["below"]))
    def _():
        last = (frame_rows - h) * ext_cols
        flat[last:, :] = jnp.zeros((flat.shape[0] - last, LANES), f32)

    @pl.when(jnp.logical_not(place.has["left"]))
    def _():
        for r in range(frame_rows):
            flat[r * ext_cols : r * ext_cols + margin, :] = jnp.zeros((margin, LANES), f32)

    @pl.when(jnp.logical_not(place.has["right"]))
    def _():
        for r in range(frame_rows):
            flat[(r + 1) * ext_cols - margin : (r + 1) * ext_cols, :] = jnp.zeros((margin, LANES), f32)


def sums_kernel(
    dims, x1, grad1, normed1, pre_grad1, hidden1, cot, gain_part, final, taps_sum, up_sum, down_sum, output, sums
):
    output[...] = final[...]
    kernel_sums(x1, 1, dims.ext_cols, grad1, 0, dims.cols, dims.rows, dims.cols, dims.size, sums)
    store_sums(dims, sums, gain_part[...], taps_sum)
    upstream = pad_lanes(cot[...].reshape(dims.rows * dims.cols, dims.channels))
    up_sum[...] = dot_leading(normed1[...], pre_grad1[...]).T
    down_sum[...] = dot_leading(upstream, hidden1[...]).T


def store_sums(dims, sums, gain_part, target):
    taps = dims.size * dims.size
    target[...] = jnp.zeros(target.shape, f32)
    for t in range(taps):
        target[t : t + 1, :] = jnp.sum(sums[t * 8 : t * 8 + 8, :], axis=0, keepdims=True)
    target[taps : taps + 1, :] = jnp.sum(gain_part, axis=0, keepdims=True)


def third_kernel(dims, *refs):
    (tall, tall_cot, done, taps1, gains, grad_in0, grad_out0, x0, unit0, inv0, hidden0, slope0) = refs[:12]
    (taps_sum1, up_sum1, down_sum1) = refs[12:15]
    strips = refs[15:17]
    (grad0, middle, keep, small_keep, send) = refs[17:22]
    (wide_grad, cot_frame, upstream, own, sums, up_acc, down_acc, gain_sum, small, table, slabs) = refs[22:]
    place = Place(dims.row_count, dims.col_count)
    rows, cols, channels, h, size = (dims.rows, dims.cols, dims.channels, dims.h, dims.size)
    ext_rows, ext_cols, wide = (dims.ext_rows, dims.ext_cols, dims.wide)
    skip = dims.skipped_rows(place)
    margin = (ext_cols - cols) // 2
    frame_rows(place, wide_grad, tall, strips, 0, rows + 4 * h, cols, SIDE, channels)
    frame_rows(place, cot_frame, tall_cot, strips, rows + 4 * h, rows + 2 * h, cols, margin, channels)

    used = ext_rows * ext_cols
    if dims.ext_pad > used:
        upstream[used:, :] = jnp.zeros((dims.ext_pad - used, LANES), f32)
        own[used:, :] = jnp.zeros((dims.ext_pad - used, LANES), f32)
    grad0[...] = jnp.zeros(grad0.shape, f32)
    frame = pl.multiple_of(skip * ext_cols, 8)

    def conv1(g, carry):
        at = pl.multiple_of(g * (ext_cols - 16), 8)
        total = conv_group(wide_grad, pl.multiple_of(skip * wide, 8) + at + 1, wide, ext_rows, taps1, size, True)
        for r in range(ext_rows):
            upstream[pl.ds(r * ext_cols + at, 16), :] = total[r]
        return carry

    lax.fori_loop(0, 2, conv1, 0)
    col = lax.broadcasted_iota(jnp.int32, (ext_cols, LANES), 0) - margin
    inside = jnp.where(jnp.logical_and(col >= 0, col < cols), 1.0, 0.0)
    for r in range(ext_rows):
        px, width = (slice(r * ext_cols, (r + 1) * ext_cols), dims.middle_cols)
        upstream[r * ext_cols + 16 : r * ext_cols + 16 + width, :] = done[r * width : (r + 1) * width, :]
        upstream[px, :] = upstream[px, :] + cot_frame[pl.ds(frame + r * ext_cols, ext_cols), :]
        mine = jnp.logical_and(r + skip >= h, r + skip < h + rows)
        own[px, :] = jnp.where(mine, inside, 0.0)
    for i in range(rows):
        line = upstream[pl.ds((i + h - skip) * ext_cols + margin, cols), :]
        middle[i * cols : (i + 1) * cols, :] = round16(line)

    gain = pad_lanes(gains[0:1, :])
    gain_sum[...] = jnp.zeros(gain_sum.shape, f32)
    up_acc[...] = jnp.zeros(up_acc.shape, f32)
    down_acc[...] = jnp.zeros(down_acc.shape, f32)
    ones = diagonal(jnp.ones((LANES, LANES), bf16), jnp.ones((LANES, LANES), bf16))
    half_px = dims.ext_pad // 2
    for start, n in pieces(half_px, dims.piece):
        spans = [(start, n), (half_px + start, n)]
        flows = [upstream[at : at + n, :].astype(bf16) for at, n in spans]
        hidden_grads = paired_dot(flows[0], flows[1], grad_in0[...])
        pre_grads = [
            (grad * slope0[at : at + n, :].astype(f32)).astype(bf16) for grad, (at, n) in zip(hidden_grads, spans)
        ]
        normed_grads = paired_dot(pre_grads[0], pre_grads[1], grad_out0[...])
        for (at, n), flow, pre_grad, normed_grad in zip(spans, flows, pre_grads, normed_grads):
            mine = own[at : at + n, :]
            unit = unit0[at : at + n, :].astype(f32)
            normed = (unit * gain * mine).astype(bf16)
            up_acc[...] += dot_leading(normed, pre_grad)
            down_acc[...] += dot_leading(flow * mine.astype(bf16), hidden0[at : at + n, :])
            product = normed_grad * unit * mine
            gain_sum[...] += jnp.sum(product.reshape(n // 8, 8, LANES), axis=0)
            grad = norm_backward(normed_grad, unit, inv0[at : at + n, :], gain, channels, ones)
            grad0[pl.ds(frame + at, n), :] = round16(grad)
    clear_outside(place, grad0, dims)
    kernel_sums(
        x0, h * wide + SIDE - h, wide, grad0, h * ext_cols + margin, ext_cols, rows, cols, size, sums
    )
    store_sums(dims, sums, gain_sum[...], small)

    taps_rows = size * size + 1
    merged = jnp.concatenate([small[0:taps_rows, :], taps_sum1[0:taps_rows, :]], axis=0) * dims.factor
    merged = fold_rows(merged, dims.small_rows, 3 * 32).astype(bf16)
    small_keep[...] = merged.astype(f32)

    layer_rows, part, half = (dims.layer_rows, dims.part, dims.half)
    units = up_acc.shape[1]
    up0 = up_acc[...].T * dims.factor
    down0 = down_acc[...].T * dims.factor
    up1 = up_sum1[...] * dims.factor
    down1 = down_sum1[...] * dims.factor
    lane = lax.broadcasted_iota(jnp.int32, (units, LANES), 1)
    for r in range(dims.row_count):
        for layer, (u, d) in enumerate(((up0, down0), (up1, down1))):
            first = pltpu.roll(u, LANES - r * half, 1) if r else u
            shift = (half - r * half) % LANES
            second = pltpu.roll(d, shift, 1) if shift else d
            joined = jnp.where(lane < half, first, jnp.where(lane < 2 * half, second, 0.0))
            table[layer * (units + 8) : layer * (units + 8) + units, :] = joined

        def slab(c, carry, r=r):
            index = 0
            for j, (axis, bit) in enumerate(dims.stages):
                value = (r >> bit) & 1 if axis == "row" else lax.rem(lax.div(c, 1 << bit), 2)
                index = index + value * (1 << (len(dims.stages) - 1 - j))
            blocks = [table[pl.ds(layer * (units + 8) + c * part, layer_rows), :] for layer in range(2)]
            whole = fold_rows(jnp.concatenate(blocks, axis=0), dims.slab_rows, 2 * half)
            slabs[pl.ds(pl.multiple_of(index * dims.slab_rows, 8), dims.slab_rows), :] = whole
            return carry

        lax.fori_loop(0, dims.col_count, slab, 0)

    split(dims, 0, slabs, merged, keep, (send,))


def fold_rows(x, rows, used):
    n = x.shape[0]
    if rows >= n:
        return pad_rows(x, rows)
    assert used <= 96
    stride = ceil8(n - rows)
    rest = pad_rows(x[rows:], stride)
    pieces_of = pad_rows(jnp.concatenate([pltpu.roll(rest, 96 - 32 * k, 1) for k in range(3)], axis=0), rows)
    lane = lax.broadcasted_iota(jnp.int32, (rows, LANES), 1)
    return jnp.where(lane < 96, x[:rows], pieces_of)


def pad_rows(x, rows):
    if rows == x.shape[0]:
        return x
    return jnp.concatenate([x, jnp.zeros((rows - x.shape[0], LANES), x.dtype)], axis=0)


def unfold_rows(x, n):
    rows = x.shape[0]
    if rows >= n:
        return x[:n]
    stride = ceil8(n - rows)
    lane = lax.broadcasted_iota(jnp.int32, (stride, LANES), 1)
    rest = jnp.zeros((stride, LANES), x.dtype)
    for k in range(3):
        moved = pltpu.roll(x[k * stride : (k + 1) * stride], 32 + 32 * k, 1)
        rest = jnp.where(jnp.logical_and(lane >= 32 * k, lane < 32 * k + 32), moved, rest)
    return jnp.concatenate([x, rest[: n - rows]], axis=0)


def split(dims, stage, slabs, merged, keep, sends):
    group = dims.groups[stage]
    count = slabs.shape[0] >> len(group)
    mine = 0
    for axis, bit in group:
        mine = mine * 2 + lax.rem(lax.div(lax.axis_index(axis), 1 << bit), 2)
    keep[...] = slabs[pl.ds(pl.multiple_of(mine * count, 8), count), :]
    sums_rows = merged.shape[0]
    for mask, send in enumerate(sends, 1):
        other = 0
        for j in range(len(group)):
            weight = 1 << j
            digit = lax.rem(lax.div(mine, weight), 2)
            other = other + weight * (1 - digit if mask & weight else digit)
        send[0:sums_rows, :] = merged
        send[sums_rows:, :] = slabs[pl.ds(pl.multiple_of(other * count, 8), count), :].astype(bf16)


def gather_up(keep, small, gots):
    count = small.shape[0]
    slabs = [keep[...]] + [got[count:, :].astype(f32) for got in gots]
    sums = [small[...]] + [got[0:count, :].astype(f32) for got in gots]
    if len(gots) == 1:
        return (slabs[0] + slabs[1], sums[0] + sums[1])
    return tuple((x[0] + x[1]) + (x[2] + x[3]) for x in (slabs, sums))


def stage_kernel(dims, stage, keep, small, *refs):
    before, after = (len_sends(dims.groups[stage - 1]), len_sends(dims.groups[stage]))
    gots = refs[:before]
    keep_out, small_out = refs[-3 - after : -1 - after]
    sends, total = (refs[-1 - after : -1], refs[-1])
    slabs, merged = gather_up(keep, small, gots)
    total[...] = slabs
    merged = merged.astype(bf16)
    small_out[...] = merged.astype(f32)
    split(dims, stage, total, merged, keep_out, sends)


def len_sends(group):
    return (1 << len(group)) - 1


def last_kernel(dims, keep, small, *refs):
    gots, (kernel_out, gain_out, up_out, down_out) = (refs[:-4], refs[-4:])
    total, merged = gather_up(keep, small, gots)
    total = unfold_rows(total, 2 * dims.layer_rows)
    merged = unfold_rows(merged, 2 * (dims.size * dims.size + 1))
    size, channels, half, part = (dims.size, dims.channels, dims.half, dims.part)
    for layer in range(2):
        block = total[layer * dims.layer_rows : layer * dims.layer_rows + part]
        up_out[layer] = block[:, :half]
        down_out[layer] = block[:, half : 2 * half]
        for t in range(size * size + 1):
            at = layer * (size * size + 1) + t
            row = merged[at : at + 1, 0:channels]
            if t < size * size:
                kernel_out[t // size, t % size, layer : layer + 1, :] = row
            else:
                gain_out[layer : layer + 1, :] = row


def image_kernel(dims, grad0, middle, taps0, after, out, ready, work):
    rows, cols, size = (dims.rows, dims.cols, dims.size)

    def conv0(g, carry):
        at = group_start(g, cols)
        total = conv_group(grad0, at + 1, dims.ext_cols, rows, taps0, size, True)
        for r in range(rows):
            work[pl.ds(r * cols + at, 16), :] = middle[pl.ds(r * cols + at, 16), :] + total[r]
        return carry

    lax.fori_loop(0, -(-cols // 16), conv0, 0)
    for r in range(rows):
        out[r] = work[r * cols : (r + 1) * cols, 0 : dims.channels].astype(bf16)
    ready[...] = jnp.zeros(ready.shape, f32)


class Dims:
    def skipped_rows(self, place):
        if self.row_count > 2:
            return 0
        return jnp.where(place.has["above"], 0, self.h)


def dims_of(image, kernels, up_weights):
    d = Dims()
    d.row_count, d.col_count = (lax.axis_size("row"), lax.axis_size("col"))
    d.rows, d.cols, d.channels = image.shape
    d.size = kernels.shape[1]
    d.h = d.size // 2
    d.ext_rows, d.ext_cols = (d.rows + (d.h if d.row_count == 2 else 2 * d.h), d.cols + 8)
    d.wide = d.cols + 2 * SIDE
    d.ext_pad = -(-d.ext_rows * d.ext_cols // 32) * 32
    d.piece = 176
    d.line_step = 4
    d.half = d.channels // d.row_count
    d.part = up_weights.shape[2] // d.col_count
    d.layer_rows = ceil8(d.part)
    d.count = d.row_count * d.col_count
    d.small_rows = 80 if d.size == 7 and d.channels <= 96 else -(-2 * (d.size * d.size + 1) // 16) * 16
    d.slab_rows = 40 if d.layer_rows == 24 and 2 * d.half <= 96 else 2 * d.layer_rows
    d.middle_cols = (d.cols - 16) // 16 * 16
    d.factor = 1.0 / math.sqrt(d.rows * d.cols * d.count)
    row_bits, col_bits = (d.row_count.bit_length() - 1, d.col_count.bit_length() - 1)
    bits = [("row", b) for b in range(row_bits)] + [("col", b) for b in range(1, col_bits)]
    d.groups = [[("col", 0)]] + [bits[i : i + 2] for i in range(0, len(bits), 2)]
    d.stages = [bit for group in d.groups for bit in group]
    return d


def swap_by(d, group, mask):
    flip = {"row": 0, "col": 0}
    for j, (axis, bit) in enumerate(group):
        if mask >> (len(group) - 1 - j) & 1:
            flip[axis] |= 1 << bit
    pairs = []
    for r in range(d.row_count):
        for c in range(d.col_count):
            pairs.append((r * d.col_count + c, (r ^ flip["row"]) * d.col_count + (c ^ flip["col"])))
    return pairs


def run(kernel, outs, scratch, *args, in_hbm=0, sems=0, busy_us=1):
    shapes = [jax.ShapeDtypeStruct(shape, kind) for shape, kind in outs]
    space = pl.BlockSpec(memory_space=pltpu.VMEM)
    far = pl.BlockSpec(memory_space=pltpu.HBM)
    held = [pltpu.VMEM(shape, kind) for shape, kind in scratch]
    if sems:
        held.append(pltpu.SemaphoreType.DMA((sems,)))
    return pl.pallas_call(
        kernel,
        out_shape=shapes,
        in_specs=[far] * in_hbm + [space] * (len(args) - in_hbm),
        out_specs=[space] * len(shapes),
        scratch_shapes=held,
        compiler_params=pltpu.CompilerParams(vmem_limit_bytes=32 * 1024 * 1024),
        cost_estimate=pl.CostEstimate(flops=int(busy_us * 1e9), bytes_accessed=1 << 18, transcendentals=0),
    )(*args)


def per_device(image, kernels, gains, up_weights, down_weights, cotangent):
    d = dims_of(image, kernels, up_weights)
    bind = functools.partial
    rows, cols, channels = image.shape
    units = up_weights.shape[2]
    tile, ext, wide = (rows * cols, d.ext_pad, (rows + 4 * d.h) * d.wide)
    frame = (rows + 2 * d.h) * d.ext_cols + 16
    taps = ((d.size * d.size * 16, LANES), bf16)
    tap_sums = ((d.size * d.size * 8, LANES), f32)
    sums_rows = ceil8(d.size * d.size + 1)

    counts = (d.row_count, d.col_count)
    band_count, tall_rows_count = (len(band_starts(d.row_count)), rows + 4 * d.h)
    tall = ((tall_rows_count * cols, LANES), f32)
    done = ((d.ext_rows * d.middle_cols, LANES), f32)

    def bands_of(height):
        return [((height, cols, channels), bf16)] * band_count

    def columns_of(height):
        return [((height, SIDE, channels), bf16)] * 2

    image, *bands = run(
        bind(bands_kernel, d), [(image.shape, bf16)] + bands_of(2 * d.h), [], image, in_hbm=1, sems=1
    )
    bands = swap_bands(bands, *counts)
    mixing = [((2 * LANES, 2 * units), bf16), ((2 * units, 2 * LANES), bf16)]
    forward0, back0, forward1, back1, grad_in0, grad_out0, taps0, taps1, gains = run(
        weights_kernel,
        mixing * 3 + [taps, taps, (gains.shape, f32)],
        [((2, channels, units), bf16), ((2, channels, units), bf16), ((d.size, d.size, 2, channels), f32)],
        up_weights,
        jnp.swapaxes(down_weights, 1, 2),
        jnp.transpose(kernels, (1, 2, 0, 3)),
        gains,
        in_hbm=4,
        sems=4,
        busy_us=2,
    )

    tall_image, *strips = run(
        bind(columns_kernel, d), [tall] + columns_of(tall_rows_count), [], image, *bands
    )
    strips = swap_columns(strips, *counts)
    (done0,) = run(bind(middle_kernel, d, False), [done], [], tall_image, taps0, busy_us=2)
    first = run(
        bind(first_kernel, d),
        [
            (image.shape, bf16),
            ((wide, LANES), f32),
            ((frame, LANES), f32),
            ((ext, LANES), bf16),
            ((ext, LANES), f32),
            ((ext, units), bf16),
            ((ext, units), bf16),
            ((tile, LANES), f32),
            ((tile, LANES), bf16),
            ((tile, units), bf16),
            ((tile, units), bf16),
            ((8, LANES), f32),
        ]
        + bands_of(3 * d.h),
        [((ext, LANES), f32)],
        tall_image,
        done0,
        cotangent,
        taps0,
        taps1,
        gains,
        forward0,
        back0,
        forward1,
        back1,
        *strips,
        busy_us=15,
    )
    (final, x0, x1, unit0, inv0, hidden0, slope0, grad1, normed1, pre_grad1, hidden1, gain_part) = first[:12]
    bands = swap_bands(first[12:], *counts)

    taps_sum1, up_sum1, down_sum1, output = run(
        bind(sums_kernel, d),
        [((sums_rows, LANES), f32), ((units, LANES), f32), ((units, LANES), f32), (image.shape, bf16)],
        [tap_sums],
        x1,
        grad1,
        normed1,
        pre_grad1,
        hidden1,
        cotangent,
        gain_part,
        final,
        busy_us=3,
    )

    tall_grad, tall_cot, *strips = run(
        bind(grad_columns_kernel, d),
        [tall, (((rows + 2 * d.h) * cols, LANES), f32)] + columns_of(2 * rows + 6 * d.h),
        [],
        grad1,
        cotangent,
        *bands,
    )
    strips = swap_columns(strips, *counts)
    (done1,) = run(bind(middle_kernel, d, True), [done], [], tall_grad, taps1, busy_us=2)
    held = d.count // 2 * d.slab_rows
    small = ((d.small_rows, LANES), f32)
    grad0, middle, keep, sums, send = run(
        bind(third_kernel, d),
        [((frame, LANES), f32), ((tile, LANES), f32), ((held, LANES), f32), small, ((held + d.small_rows, LANES), bf16)],
        [
            ((wide, LANES), f32),
            ((frame, LANES), f32),
            ((ext, LANES), f32),
            ((ext, LANES), f32),
            tap_sums,
            ((LANES, units), f32),
            ((LANES, units), f32),
            ((8, LANES), f32),
            ((sums_rows, LANES), f32),
            ((2 * (units + 8), LANES), f32),
            ((2 * held, LANES), f32),
        ],
        tall_grad,
        tall_cot,
        done1,
        taps1,
        gains,
        grad_in0,
        grad_out0,
        x0,
        unit0,
        inv0,
        hidden0,
        slope0,
        taps_sum1,
        up_sum1,
        down_sum1,
        *strips,
        busy_us=12,
    )
    axes = ("row", "col")
    sends = [send]
    for stage, group in enumerate(d.groups):
        gots = [lax.ppermute(x, axes, swap_by(d, group, mask)) for mask, x in enumerate(sends, 1)]
        ready = []
        if stage == 1:
            gradient, *ready = run(
                bind(image_kernel, d),
                [(image.shape, bf16), ((8, LANES), f32)],
                [((tile, LANES), f32)],
                grad0,
                middle,
                taps0,
                sums,
                busy_us=3,
            )
        if stage + 1 < len(d.groups):
            after = d.groups[stage + 1]
            whole, held = (held, held >> len(after))
            keep, sums, *sends = run(
                bind(stage_kernel, d, stage + 1),
                [((held, LANES), f32), small] + [((held + d.small_rows, LANES), bf16)] * len_sends(after),
                [((whole, LANES), f32)],
                keep,
                sums,
                *gots,
                *ready,
            )
    kernel_out, gain_out, up_out, down_out = run(
        bind(last_kernel, d),
        [
            ((d.size, d.size, 2, channels), f32),
            (gains.shape, f32),
            ((2, d.part, d.half), f32),
            ((2, d.part, d.half), f32),
        ],
        [],
        keep,
        sums,
        *gots,
    )
    kernel_out = jnp.transpose(kernel_out, (2, 0, 1, 3))
    return (output, gradient, kernel_out, gain_out, jnp.swapaxes(up_out, 1, 2), down_out)


def solution(mesh):
    placed = (P("row", "col", None), P(), P(), P(), P(), P("row", "col", None))
    return jax.shard_map(
        per_device,
        mesh=mesh,
        in_specs=placed,
        out_specs=(
            P("row", "col", None),
            P("row", "col", None),
            P(),
            P(),
            P(None, "row", "col"),
            P(None, "col", "row"),
        ),
        check_vma=False,
    )
```

```python
import functools
import math

import jax
import jax.numpy as jnp
from jax import lax
from jax.experimental import pallas as pl
from jax.experimental.pallas import tpu as pltpu
from jax.sharding import PartitionSpec as P

epsilon = 1e-06
inv_sqrt_two = 0.7071067811865476
inv_sqrt_two_pi = 0.3989422804014327
log2_e = 1.4426950408889634
LANES = 128
SIDE = 8
f32, bf16 = (jnp.float32, jnp.bfloat16)


def ceil8(n):
    return -(-n // 8) * 8


def combos(row_count):
    listed = [(None, 0), (None, 1), (0, None), (0, 0), (0, 1)]
    if row_count > 2:
        listed += [(1, None), (1, 0), (1, 1)]
    return listed


def partner(index, start, count):
    if start is None:
        return index
    other = index + 1 if (index - start) % 2 == 0 else index - 1
    return other if 0 <= other < count else None


def swap_pairs(row_count, col_count, row_start, col_start):
    pairs = []
    for r in range(row_count):
        for c in range(col_count):
            pr, pc = (partner(r, row_start, row_count), partner(c, col_start, col_count))
            if pr is None:
                pr, pc = (r, c ^ 1)
            elif pc is None:
                pr, pc = (r ^ 1 if row_start is None else pr, c)
            pairs.append((r * col_count + c, pr * col_count + pc))
    return pairs


def exchange(bands, others, row_count, col_count):
    got = {}
    for strips, pairs in ((bands, band_combos(row_count)), (others, other_combos(row_count))):
        for strip, (rs, cs) in zip(strips, pairs):
            got[rs, cs] = lax.ppermute(strip, ("row", "col"), swap_pairs(row_count, col_count, rs, cs))
    return [got[pair] for pair in combos(row_count)]


class Place:
    def __init__(self, row_count, col_count):
        row, col = (lax.axis_index("row"), lax.axis_index("col"))
        self.even_row, self.even_col = (lax.rem(row, 2) == 0, lax.rem(col, 2) == 0)
        self.has = {
            "above": row > 0,
            "below": row < row_count - 1,
            "left": col > 0,
            "right": col < col_count - 1,
        }
        self.row_count = row_count


def band_combos(row_count):
    return [pair for pair in combos(row_count) if pair[1] is None]


def other_combos(row_count):
    return [pair for pair in combos(row_count) if pair[1] is not None]


def write_strips(place, outs, takes, pairs):
    for out, (rs, cs) in zip(outs, pairs):
        at = 0
        for take, radius, rows, cols in takes:
            row_sets = [slice(0, rows)] * 2
            col_sets = [slice(0, cols)] * 2
            if rs is not None:
                row_sets = [slice(rows - radius, rows), slice(0, radius)]
                if rs == 1:
                    row_sets = row_sets[::-1]
            if cs is not None:
                col_sets = [slice(cols - SIDE, cols), slice(0, SIDE)]
                if cs == 1:
                    col_sets = col_sets[::-1]
            count = row_sets[0].stop - row_sets[0].start
            for i in range(count):
                parts = {}
                for er in (0, 1):
                    for ec in (0, 1):
                        key = (row_sets[er].start + i, col_sets[ec].start, col_sets[ec].stop)
                        if key not in parts:
                            parts[key] = take(*key)
                        parts[er, ec] = parts[key]
                if cs is None:
                    pick = [parts[0, 0], parts[1, 0]]
                else:
                    pick = [jnp.where(place.even_col, parts[e, 0], parts[e, 1]) for e in (0, 1)]
                value = pick[0] if rs is None else jnp.where(place.even_row, pick[0], pick[1])
                out[at + i] = value.astype(out.dtype)
            at += count


def strip_shapes(pairs, rows, cols, channels, radii):
    shapes = []
    for rs, cs in pairs:
        height = sum(rows if rs is None else radius for radius in radii)
        shapes.append((height, cols if cs is None else SIDE, channels))
    return shapes


def received(place, strips, row_sections):
    table = dict(zip(combos(place.row_count), strips))
    full_start, band_start = row_sections

    def along(rs, cs, i):
        return table[rs, cs][(full_start if rs is None else band_start) + i].astype(f32)

    def column(rs, side, i):
        if side is None:
            return along(rs, None, i)
        near, far = (along(rs, 0, i), along(rs, 1, i))
        if side == "left":
            return jnp.where(place.even_col, far, near)
        return jnp.where(place.even_col, near, far)

    def read(vertical, side, i):
        if vertical is None:
            value = column(None, side, i)
        elif place.row_count == 2:
            value = column(0, side, i)
        else:
            near, far = (column(0, side, i), column(1, side, i))
            if vertical == "above":
                value = jnp.where(place.even_row, far, near)
            else:
                value = jnp.where(place.even_row, near, far)
        if vertical is not None:
            value = jnp.where(place.has[vertical], value, 0.0)
        if side is not None:
            value = jnp.where(place.has[side], value, 0.0)
        return value

    return read


def assemble(place, target, own, read, radius, rows, cols, channels):
    width = cols + 2 * SIDE
    target[...] = jnp.zeros(target.shape, f32)
    for vertical, start, count in (("above", 0, radius), (None, radius, rows), ("below", radius + rows, radius)):
        for i in range(count):
            base = (start + i) * width
            middle = own(i) if vertical is None else read(vertical, None, i)
            target[base + SIDE : base + SIDE + cols, 0:channels] = middle
            target[base : base + SIDE, 0:channels] = read(vertical, "left", i)
            target[base + SIDE + cols : base + width, 0:channels] = read(vertical, "right", i)


def spread_taps(kernel_ref, layer, target):
    size, channels = (kernel_ref.shape[0], kernel_ref.shape[3])
    for a in range(size):
        for b in range(size):
            t = a * size + b
            row = pad_lanes(kernel_ref[a, b, layer : layer + 1, :])
            target[t * 16 : t * 16 + 16, :] = jnp.broadcast_to(row, (16, LANES)).astype(bf16)


def tree_sum(terms):
    while len(terms) > 1:
        pairs = [terms[i] + terms[i + 1] for i in range(0, len(terms) - 1, 2)]
        terms = pairs + ([terms[-1]] if len(terms) % 2 else [])
    return terms[0]


def conv_group(src, base, stride, rows_out, taps, size, flipped=False):
    total = [None] * rows_out
    for b in range(size):
        order = [a * size + b for a in range(size)]
        if flipped:
            order = [size * size - 1 - t for t in order]
        weights = [taps[t * 16 : t * 16 + 16, :] for t in order]
        window = []
        for i in range(rows_out + size - 1):
            window.append(src[pl.ds(base + i * stride + b, 16), :].astype(bf16))
            r = i - size + 1
            if r >= 0:
                term = tree_sum([window[r + a] * weights[a] for a in range(size)]).astype(f32)
                total[r] = term if total[r] is None else total[r] + term
    return total


def group_start(g, cols):
    return pl.multiple_of(jnp.minimum(g * 16, cols - 16), 8)


def kernel_sums(src, src_base, src_stride, grad, grad_base, grad_stride, rows, cols, size, sums):
    sums[...] = jnp.zeros(sums.shape, f32)

    def group(g, carry):
        at = pl.multiple_of(g * 16, 16)
        grads = [grad[pl.ds(grad_base + i * grad_stride + at, 16), :].astype(bf16) for i in range(rows)]
        for b in range(size):
            lines = [
                src[pl.ds(src_base + i * src_stride + at + b, 16), :].astype(bf16) for i in range(rows + size - 1)
            ]
            for a in range(size):
                term = tree_sum([lines[r + a] * grads[r] for r in range(rows)]).astype(f32)
                t = (a * size + b) * 8
                sums[t : t + 8, :] += term[0:8] + term[8:16]
        return carry

    lax.fori_loop(0, cols // 16, group, 0)


def diagonal(first, second):
    top = jnp.concatenate([first, jnp.zeros((first.shape[0], second.shape[1]), first.dtype)], axis=1)
    bottom = jnp.concatenate([jnp.zeros((second.shape[0], first.shape[1]), first.dtype), second], axis=1)
    return jnp.concatenate([top, bottom], axis=0)


def lane_total(x):
    high = x.astype(bf16)
    low = (x - high.astype(f32)).astype(bf16)
    both = jnp.concatenate([high, low], axis=1)
    return dot(both, jnp.ones((2 * LANES, LANES), bf16))


def paired_dot(x, y, weights):
    total = dot(jnp.concatenate([x.astype(bf16), y.astype(bf16)], axis=1), weights)
    half = weights.shape[1] // 2
    return (total[:, :half], total[:, half:])


def layer_norm(parts, channels, ones):
    lane = lax.broadcasted_iota(jnp.int32, parts[0].shape, 1)
    centred = [jnp.where(lane < channels, x - lane_total(x) * (1.0 / channels), 0.0) for x in parts]
    variances = paired_dot(centred[0] * centred[0], centred[1] * centred[1], ones)
    inverses = [lax.rsqrt(v * (1.0 / channels) + epsilon) for v in variances]
    return ([c * i for c, i in zip(centred, inverses)], inverses)


def norm_backward(normed_grad, unit, inverse, gain, channels, ones):
    m = normed_grad * gain
    mean, along = paired_dot(m, m * unit, ones)
    lane = lax.broadcasted_iota(jnp.int32, m.shape, 1)
    centred = m - (mean + unit * along) * (1.0 / channels)
    return jnp.where(lane < channels, inverse * centred, 0.0)


def gelu_parts(v):
    p = 0.3275911 * inv_sqrt_two
    c1, c2, c3, c4, c5 = (
        0.5 * c / p ** (k + 1)
        for k, c in enumerate((0.254829592, -0.284496736, 1.421413741, -1.453152027, 1.061405429))
    )
    t = pl.reciprocal(jnp.abs(v) + 1.0 / p, approx=True)
    bell = jnp.exp2(v * v * (-0.5 * log2_e))
    tail = ((((c5 * t + c4) * t + c3) * t + c2) * t + c1) * t * bell
    cdf = jnp.where(v >= 0.0, 1.0 - tail, tail)
    return (v * cdf, cdf + v * (bell * inv_sqrt_two_pi))


def dot(x, w):
    return jnp.dot(x, w, preferred_element_type=f32)


def dot_leading(x, y):
    return lax.dot_general(x, y, (((0,), (0,)), ((), ())), preferred_element_type=f32)


def pad_lanes(x):
    rows, channels = x.shape
    return jnp.concatenate([x, jnp.zeros((rows, LANES - channels), x.dtype)], axis=1)


def pieces(total, size):
    return [(start, min(size, total - start)) for start in range(0, total, size)]


def round16(x):
    return x.astype(bf16).astype(f32)


def fetch(sources, targets, sems):
    copies = [pltpu.make_async_copy(a, b, sems.at[i]) for i, (a, b) in enumerate(zip(sources, targets))]
    for copy in copies:
        copy.start()
    for copy in copies:
        copy.wait()


def image_take(ref):
    return lambda i, lo, hi: ref[i].astype(f32)[lo:hi]


def flat_take(ref, cols, channels):
    return lambda i, lo, hi: ref[i * cols + lo : i * cols + hi, 0:channels]


def bands_kernel(dims, image_in, image, *refs):
    outs, sems = (refs[:-1], refs[-1])
    place = Place(dims.row_count, dims.col_count)
    fetch((image_in,), (image,), sems)
    takes = [(image_take(image), 2 * dims.h, dims.rows, dims.cols)]
    write_strips(place, outs, takes, band_combos(dims.row_count))


def others_kernel(dims, image, *refs):
    outs = refs[len(band_combos(dims.row_count)) :]
    place = Place(dims.row_count, dims.col_count)
    takes = [(image_take(image), 2 * dims.h, dims.rows, dims.cols)]
    write_strips(place, outs, takes, other_combos(dims.row_count))


def grad_others_kernel(dims, grad1, cot, *refs):
    outs = refs[len(band_combos(dims.row_count)) :]
    place = Place(dims.row_count, dims.col_count)
    takes = [
        (flat_take(grad1, dims.cols, dims.channels), 2 * dims.h, dims.rows, dims.cols),
        (image_take(cot), dims.h, dims.rows, dims.cols),
    ]
    write_strips(place, outs, takes, other_combos(dims.row_count))


def weights_kernel(up_in, down_t_in, kernels_in, gains_in, *refs):
    forward0, back0, forward1, back1, grad_in0, grad_out0, taps0, taps1, gains, up_w, down_w, kernels, sems = refs
    fetch((up_in, down_t_in, kernels_in, gains_in), (up_w, down_w, kernels, gains), sems)
    spread_taps(kernels, 0, taps0)
    spread_taps(kernels, 1, taps1)
    channels, units = up_w.shape[1:]
    blank = jnp.zeros((LANES - channels, units), f32)
    wide, tall = ([], [])
    for layer in range(2):
        for ref in (up_w, down_w):
            full = jnp.concatenate([ref[layer].astype(f32), blank], axis=0)
            wide.append(full.astype(bf16))
            tall.append(full.T.astype(bf16))
    (up0, down_t0, up1, down_t1), (up_t0, down0, up_t1, down1) = (wide, tall)
    forward0[...] = diagonal(up0, up0)
    back0[...] = diagonal(down0, down0)
    forward1[...] = diagonal(up1, down_t1)
    back1[...] = diagonal(down1, up_t1)
    grad_in0[...] = diagonal(down_t0, down_t0)
    grad_out0[...] = diagonal(up_t0, up_t0)


def first_kernel(dims, *refs):
    count = len(combos(dims.row_count))
    image, cot, taps0, taps1, gains, forward0, back0, forward1, back1 = refs[:9]
    strips = refs[9 : 9 + count]
    refs = refs[9 + count :]
    (output, x0, x1, unit0, inv0, hidden0, slope0, grad1, normed1, pre_grad1, hidden1, gain_sum) = refs[:12]
    outs, conv = (refs[12:-1], refs[-1])
    place = Place(dims.row_count, dims.col_count)
    rows, cols, channels, h, size = (dims.rows, dims.cols, dims.channels, dims.h, dims.size)
    ext_rows, ext_cols, wide = (dims.ext_rows, dims.ext_cols, dims.wide)
    skip = dims.skipped_rows(place)
    read = received(place, strips, (0, 0))
    assemble(place, x0, lambda i: image[i].astype(f32), read, 2 * h, rows, cols, channels)

    x1[...] = jnp.zeros(x1.shape, f32)
    if dims.ext_pad > ext_rows * ext_cols:
        conv[ext_rows * ext_cols :, :] = jnp.zeros((dims.ext_pad - ext_rows * ext_cols, LANES), f32)
    frame = pl.multiple_of(skip * ext_cols, 8)

    def conv0(g, carry):
        at = group_start(g, ext_cols)
        base = pl.multiple_of(skip * wide, 8) + at
        total = conv_group(x0, base + 1, wide, ext_rows, taps0, size)
        for r in range(ext_rows):
            conv[pl.ds(r * ext_cols + at, 16), :] = total[r]
            x1[pl.ds(frame + r * ext_cols + at, 16), :] = x0[pl.ds(base + (r + h) * wide + 4, 16), :]
        return carry

    lax.fori_loop(0, -(-ext_cols // 16), conv0, 0)
    gain = pad_lanes(gains[0:1, :])
    ones = diagonal(jnp.ones((LANES, LANES), bf16), jnp.ones((LANES, LANES), bf16))
    half = dims.ext_pad // 2
    for start, n in pieces(half, dims.piece):
        spans = [(start, n), (half + start, n)]
        units, inverses = layer_norm([conv[at : at + n, :] for at, n in spans], channels, ones)
        pres = paired_dot(units[0] * gain, units[1] * gain, forward0[...])
        hiddens = []
        for (at, n), unit, inverse, pre in zip(spans, units, inverses, pres):
            unit0[at : at + n, :] = unit.astype(bf16)
            inv0[at : at + n, :] = inverse
            value, slope = gelu_parts(pre)
            hiddens.append(value.astype(bf16))
            hidden0[at : at + n, :] = hiddens[-1]
            slope0[at : at + n, :] = slope.astype(bf16)
        branches = paired_dot(hiddens[0], hiddens[1], back0[...])
        for (at, n), branch in zip(spans, branches):
            px = pl.ds(frame + at, n)
            x1[px, :] = round16(x1[px, :] + branch)
    clear_outside(place, x1, dims)

    def conv1(g, carry):
        at = group_start(g, cols)
        total = conv_group(x1, at + 1, ext_cols, rows, taps1, size)
        for r in range(rows):
            conv[pl.ds(r * cols + at, 16), :] = total[r]
        return carry

    lax.fori_loop(0, -(-cols // 16), conv1, 0)
    gain1 = pad_lanes(gains[1:2, :])
    gain_sum[...] = jnp.zeros(gain_sum.shape, f32)
    lines = dims.line_step
    step = lines * cols
    for k in range(rows // lines):
        px = slice(k * step, (k + 1) * step)
        middle = k * step + step // 2
        units, inverses = layer_norm([conv[k * step : middle, :], conv[middle : (k + 1) * step, :]], channels, ones)
        unit, inverse = (jnp.concatenate(units, axis=0), jnp.concatenate(inverses, axis=0))
        normed = (unit * gain1).astype(bf16)
        normed1[px, :] = normed
        upstream = pad_lanes(cot[k * lines : (k + 1) * lines].reshape(step, channels))
        pre, hidden_grad = paired_dot(normed, upstream, forward1[...])
        value, slope = gelu_parts(pre)
        hidden = value.astype(bf16)
        hidden1[px, :] = hidden
        pre_grad = (hidden_grad * slope).astype(bf16)
        pre_grad1[px, :] = pre_grad
        branch, normed_grad = paired_dot(hidden, pre_grad, back1[...])
        for i in range(lines):
            start = (k * lines + i + h) * ext_cols + 4
            line = x1[start : start + cols, :] + branch[i * cols : (i + 1) * cols]
            output[k * lines + i] = line[:, :channels].astype(bf16)
        product = normed_grad * unit
        gain_sum[...] += jnp.sum(product.reshape(step // 8, 8, LANES), axis=0)
        grad1[px, :] = round16(norm_backward(normed_grad, unit, inverse, gain1, channels, ones))

    takes = [(flat_take(grad1, cols, channels), 2 * h, rows, cols), (image_take(cot), h, rows, cols)]
    write_strips(place, outs, takes, band_combos(dims.row_count))


def clear_outside(place, flat, dims):
    h, frame_rows, ext_cols = (dims.h, dims.rows + 2 * dims.h, dims.ext_cols)
    margin = (ext_cols - dims.cols) // 2

    @pl.when(jnp.logical_not(place.has["above"]))
    def _():
        flat[0 : h * ext_cols, :] = jnp.zeros((h * ext_cols, LANES), f32)

    @pl.when(jnp.logical_not(place.has["below"]))
    def _():
        last = (frame_rows - h) * ext_cols
        flat[last:, :] = jnp.zeros((flat.shape[0] - last, LANES), f32)

    @pl.when(jnp.logical_not(place.has["left"]))
    def _():
        for r in range(frame_rows):
            flat[r * ext_cols : r * ext_cols + margin, :] = jnp.zeros((margin, LANES), f32)

    @pl.when(jnp.logical_not(place.has["right"]))
    def _():
        for r in range(frame_rows):
            flat[(r + 1) * ext_cols - margin : (r + 1) * ext_cols, :] = jnp.zeros((margin, LANES), f32)


def sums_kernel(
    dims, x1, grad1, normed1, pre_grad1, hidden1, cot, gain_part, final, taps_sum, up_sum, down_sum, output, sums
):
    output[...] = final[...]
    kernel_sums(x1, 1, dims.ext_cols, grad1, 0, dims.cols, dims.rows, dims.cols, dims.size, sums)
    store_sums(dims, sums, gain_part[...], taps_sum)
    upstream = pad_lanes(cot[...].reshape(dims.rows * dims.cols, dims.channels))
    up_sum[...] = dot_leading(normed1[...], pre_grad1[...]).T
    down_sum[...] = dot_leading(upstream, hidden1[...]).T


def store_sums(dims, sums, gain_part, target):
    taps = dims.size * dims.size
    target[...] = jnp.zeros(target.shape, f32)
    for t in range(taps):
        target[t : t + 1, :] = jnp.sum(sums[t * 8 : t * 8 + 8, :], axis=0, keepdims=True)
    target[taps : taps + 1, :] = jnp.sum(gain_part, axis=0, keepdims=True)


def third_kernel(dims, *refs):
    count = len(combos(dims.row_count))
    (grad1, cot, taps1, gains, grad_in0, grad_out0, x0, unit0, inv0, hidden0, slope0) = refs[:11]
    (taps_sum1, up_sum1, down_sum1) = refs[11:14]
    strips = refs[14 : 14 + count]
    (grad0, middle, keep, small_keep, send) = refs[14 + count : 19 + count]
    (wide_grad, cot_frame, upstream, own, sums, up_acc, down_acc, gain_sum, small, tall, slabs) = refs[19 + count :]
    place = Place(dims.row_count, dims.col_count)
    rows, cols, channels, h, size = (dims.rows, dims.cols, dims.channels, dims.h, dims.size)
    ext_rows, ext_cols, wide = (dims.ext_rows, dims.ext_cols, dims.wide)
    skip = dims.skipped_rows(place)
    read = received(place, strips, (0, 0))
    assemble(
        place, wide_grad, lambda i: grad1[i * cols : (i + 1) * cols, 0:channels], read, 2 * h, rows, cols, channels
    )
    read_cot = received(place, strips, (rows, 2 * h))
    margin = (ext_cols - cols) // 2
    cot_frame[...] = jnp.zeros(cot_frame.shape, f32)
    for vertical, start, n in (("above", 0, h), (None, h, rows), ("below", h + rows, h)):
        for i in range(n):
            base = (start + i) * ext_cols
            line = cot[i].astype(f32) if vertical is None else read_cot(vertical, None, i)
            cot_frame[base + margin : base + margin + cols, 0:channels] = line
            cot_frame[base : base + margin, 0:channels] = read_cot(vertical, "left", i)[SIDE - margin :]
            cot_frame[base + margin + cols : base + ext_cols, 0:channels] = read_cot(vertical, "right", i)[:margin]

    used = ext_rows * ext_cols
    if dims.ext_pad > used:
        upstream[used:, :] = jnp.zeros((dims.ext_pad - used, LANES), f32)
        own[used:, :] = jnp.zeros((dims.ext_pad - used, LANES), f32)
    grad0[...] = jnp.zeros(grad0.shape, f32)
    frame = pl.multiple_of(skip * ext_cols, 8)

    def conv1(g, carry):
        at = group_start(g, ext_cols)
        total = conv_group(wide_grad, pl.multiple_of(skip * wide, 8) + at + 1, wide, ext_rows, taps1, size, True)
        col = lax.broadcasted_iota(jnp.int32, (16, LANES), 0) + (at - margin)
        inside = jnp.where(jnp.logical_and(col >= 0, col < cols), 1.0, 0.0)
        for r in range(ext_rows):
            px = pl.ds(r * ext_cols + at, 16)
            upstream[px, :] = cot_frame[pl.ds(frame + r * ext_cols + at, 16), :] + total[r]
            mine = jnp.logical_and(r + skip >= h, r + skip < h + rows)
            own[px, :] = jnp.where(mine, inside, 0.0)
        return carry

    lax.fori_loop(0, -(-ext_cols // 16), conv1, 0)
    for i in range(rows):
        line = upstream[pl.ds((i + h - skip) * ext_cols + margin, cols), :]
        middle[i * cols : (i + 1) * cols, :] = round16(line)

    gain = pad_lanes(gains[0:1, :])
    gain_sum[...] = jnp.zeros(gain_sum.shape, f32)
    up_acc[...] = jnp.zeros(up_acc.shape, f32)
    down_acc[...] = jnp.zeros(down_acc.shape, f32)
    ones = diagonal(jnp.ones((LANES, LANES), bf16), jnp.ones((LANES, LANES), bf16))
    half_px = dims.ext_pad // 2
    for start, n in pieces(half_px, dims.piece):
        spans = [(start, n), (half_px + start, n)]
        flows = [upstream[at : at + n, :].astype(bf16) for at, n in spans]
        hidden_grads = paired_dot(flows[0], flows[1], grad_in0[...])
        pre_grads = [
            (grad * slope0[at : at + n, :].astype(f32)).astype(bf16) for grad, (at, n) in zip(hidden_grads, spans)
        ]
        normed_grads = paired_dot(pre_grads[0], pre_grads[1], grad_out0[...])
        for (at, n), flow, pre_grad, normed_grad in zip(spans, flows, pre_grads, normed_grads):
            mine = own[at : at + n, :]
            unit = unit0[at : at + n, :].astype(f32)
            normed = (unit * gain * mine).astype(bf16)
            up_acc[...] += dot_leading(normed, pre_grad)
            down_acc[...] += dot_leading(flow * mine.astype(bf16), hidden0[at : at + n, :])
            product = normed_grad * unit * mine
            gain_sum[...] += jnp.sum(product.reshape(n // 8, 8, LANES), axis=0)
            grad = norm_backward(normed_grad, unit, inv0[at : at + n, :], gain, channels, ones)
            grad0[pl.ds(frame + at, n), :] = round16(grad)
    clear_outside(place, grad0, dims)
    kernel_sums(
        x0, h * wide + SIDE - h, wide, grad0, h * ext_cols + margin, ext_cols, rows, cols, size, sums
    )
    store_sums(dims, sums, gain_sum[...], small)

    taps_rows = size * size + 1
    merged = jnp.concatenate([small[0:taps_rows, :], taps_sum1[0:taps_rows, :]], axis=0) * dims.factor
    merged = fold_rows(merged, dims.small_rows, channels).astype(bf16)
    small_keep[...] = merged.astype(f32)

    layer_rows, part, half = (dims.layer_rows, dims.part, dims.half)
    units = up_acc.shape[1]
    up0 = up_acc[...].T * dims.factor
    down0 = down_acc[...].T * dims.factor
    up1 = up_sum1[...] * dims.factor
    down1 = down_sum1[...] * dims.factor
    lane = lax.broadcasted_iota(jnp.int32, (units, LANES), 1)
    slab_rows = 2 * layer_rows
    for r in range(dims.row_count):
        for layer, (u, d) in enumerate(((up0, down0), (up1, down1))):
            first = pltpu.roll(u, LANES - r * half, 1) if r else u
            shift = (half - r * half) % LANES
            second = pltpu.roll(d, shift, 1) if shift else d
            joined = jnp.where(lane < half, first, jnp.where(lane < 2 * half, second, 0.0))
            tall[layer * (units + 8) : layer * (units + 8) + units, :] = joined

        def slab(c, carry, r=r):
            index = 0
            for j, (axis, bit) in enumerate(dims.stages):
                value = (r >> bit) & 1 if axis == "row" else lax.rem(lax.div(c, 1 << bit), 2)
                index = index + value * (1 << (len(dims.stages) - 1 - j))
            for layer in range(2):
                to = pl.multiple_of(index * slab_rows + layer * layer_rows, 8)
                slabs[pl.ds(to, layer_rows), :] = tall[pl.ds(layer * (units + 8) + c * part, layer_rows), :]
            return carry

        lax.fori_loop(0, dims.col_count, slab, 0)

    split(dims, 0, slabs, merged, keep, (send,))


def fold_rows(x, rows, used):
    n = x.shape[0]
    if rows >= n:
        return pad_rows(x, rows)
    assert used <= 96
    stride = ceil8(n - rows)
    rest = pad_rows(x[rows:], stride)
    pieces_of = pad_rows(jnp.concatenate([pltpu.roll(rest, 96 - 32 * k, 1) for k in range(3)], axis=0), rows)
    lane = lax.broadcasted_iota(jnp.int32, (rows, LANES), 1)
    return jnp.where(lane < 96, x[:rows], pieces_of)


def pad_rows(x, rows):
    if rows == x.shape[0]:
        return x
    return jnp.concatenate([x, jnp.zeros((rows - x.shape[0], LANES), x.dtype)], axis=0)


def unfold_rows(x, n):
    rows = x.shape[0]
    if rows >= n:
        return x[:n]
    stride = ceil8(n - rows)
    lane = lax.broadcasted_iota(jnp.int32, (stride, LANES), 1)
    rest = jnp.zeros((stride, LANES), x.dtype)
    for k in range(3):
        moved = pltpu.roll(x[k * stride : (k + 1) * stride], 32 + 32 * k, 1)
        rest = jnp.where(jnp.logical_and(lane >= 32 * k, lane < 32 * k + 32), moved, rest)
    return jnp.concatenate([x, rest[: n - rows]], axis=0)


def split(dims, stage, slabs, merged, keep, sends):
    group = dims.groups[stage]
    count = slabs.shape[0] >> len(group)
    mine = 0
    for axis, bit in group:
        mine = mine * 2 + lax.rem(lax.div(lax.axis_index(axis), 1 << bit), 2)
    keep[...] = slabs[pl.ds(pl.multiple_of(mine * count, 16), count), :]
    for mask, send in enumerate(sends, 1):
        other = 0
        for j in range(len(group)):
            weight = 1 << j
            digit = lax.rem(lax.div(mine, weight), 2)
            other = other + weight * (1 - digit if mask & weight else digit)
        send[0:count, :] = slabs[pl.ds(pl.multiple_of(other * count, 16), count), :].astype(bf16)
        send[count:, :] = merged


def gather_up(keep, small, gots):
    count = keep.shape[0]
    slabs = [keep[...]] + [got[0:count, :].astype(f32) for got in gots]
    sums = [small[...]] + [got[count:, :].astype(f32) for got in gots]
    if len(gots) == 1:
        return (slabs[0] + slabs[1], sums[0] + sums[1])
    return tuple((x[0] + x[1]) + (x[2] + x[3]) for x in (slabs, sums))


def stage_kernel(dims, stage, keep, small, *refs):
    before, after = (len_sends(dims.groups[stage - 1]), len_sends(dims.groups[stage]))
    gots = refs[:before]
    keep_out, small_out = refs[-3 - after : -1 - after]
    sends, total = (refs[-1 - after : -1], refs[-1])
    slabs, merged = gather_up(keep, small, gots)
    total[...] = slabs
    merged = merged.astype(bf16)
    small_out[...] = merged.astype(f32)
    split(dims, stage, total, merged, keep_out, sends)


def len_sends(group):
    return (1 << len(group)) - 1


def last_kernel(dims, keep, small, *refs):
    gots, (kernel_out, gain_out, up_out, down_out) = (refs[:-4], refs[-4:])
    total, merged = gather_up(keep, small, gots)
    merged = unfold_rows(merged, 2 * (dims.size * dims.size + 1))
    size, channels, half, part = (dims.size, dims.channels, dims.half, dims.part)
    for layer in range(2):
        block = total[layer * dims.layer_rows : layer * dims.layer_rows + part]
        up_out[layer] = block[:, :half]
        down_out[layer] = block[:, half : 2 * half]
        for t in range(size * size + 1):
            at = layer * (size * size + 1) + t
            row = merged[at : at + 1, 0:channels]
            if t < size * size:
                kernel_out[t // size, t % size, layer : layer + 1, :] = row
            else:
                gain_out[layer : layer + 1, :] = row


def image_kernel(dims, grad0, middle, taps0, after, out, ready, work):
    rows, cols, size = (dims.rows, dims.cols, dims.size)

    def conv0(g, carry):
        at = group_start(g, cols)
        total = conv_group(grad0, at + 1, dims.ext_cols, rows, taps0, size, True)
        for r in range(rows):
            work[pl.ds(r * cols + at, 16), :] = middle[pl.ds(r * cols + at, 16), :] + total[r]
        return carry

    lax.fori_loop(0, -(-cols // 16), conv0, 0)
    for r in range(rows):
        out[r] = work[r * cols : (r + 1) * cols, 0 : dims.channels].astype(bf16)
    ready[...] = jnp.zeros(ready.shape, f32)


class Dims:
    def skipped_rows(self, place):
        if self.row_count > 2:
            return 0
        return jnp.where(place.has["above"], 0, self.h)


def dims_of(image, kernels, up_weights):
    d = Dims()
    d.row_count, d.col_count = (lax.axis_size("row"), lax.axis_size("col"))
    d.rows, d.cols, d.channels = image.shape
    d.size = kernels.shape[1]
    d.h = d.size // 2
    d.ext_rows, d.ext_cols = (d.rows + (d.h if d.row_count == 2 else 2 * d.h), d.cols + 8)
    d.wide = d.cols + 2 * SIDE
    d.ext_pad = -(-d.ext_rows * d.ext_cols // 32) * 32
    d.piece = 176
    d.line_step = 4
    d.half = d.channels // d.row_count
    d.part = up_weights.shape[2] // d.col_count
    d.layer_rows = ceil8(d.part)
    d.count = d.row_count * d.col_count
    d.small_rows = 80 if d.size == 7 and d.channels <= 96 else -(-2 * (d.size * d.size + 1) // 16) * 16
    d.factor = 1.0 / math.sqrt(d.rows * d.cols * d.count)
    row_bits, col_bits = (d.row_count.bit_length() - 1, d.col_count.bit_length() - 1)
    bits = [("row", b) for b in range(row_bits)] + [("col", b) for b in range(1, col_bits)]
    d.groups = [[("col", 0)]] + [bits[i : i + 2] for i in range(0, len(bits), 2)]
    d.stages = [bit for group in d.groups for bit in group]
    return d


def swap_by(d, group, mask):
    flip = {"row": 0, "col": 0}
    for j, (axis, bit) in enumerate(group):
        if mask >> (len(group) - 1 - j) & 1:
            flip[axis] |= 1 << bit
    pairs = []
    for r in range(d.row_count):
        for c in range(d.col_count):
            pairs.append((r * d.col_count + c, (r ^ flip["row"]) * d.col_count + (c ^ flip["col"])))
    return pairs


def run(kernel, outs, scratch, *args, in_hbm=0, sems=0, busy_us=1):
    shapes = [jax.ShapeDtypeStruct(shape, kind) for shape, kind in outs]
    space = pl.BlockSpec(memory_space=pltpu.VMEM)
    far = pl.BlockSpec(memory_space=pltpu.HBM)
    held = [pltpu.VMEM(shape, kind) for shape, kind in scratch]
    if sems:
        held.append(pltpu.SemaphoreType.DMA((sems,)))
    return pl.pallas_call(
        kernel,
        out_shape=shapes,
        in_specs=[far] * in_hbm + [space] * (len(args) - in_hbm),
        out_specs=[space] * len(shapes),
        scratch_shapes=held,
        compiler_params=pltpu.CompilerParams(vmem_limit_bytes=32 * 1024 * 1024),
        cost_estimate=pl.CostEstimate(flops=int(busy_us * 1e9), bytes_accessed=1 << 18, transcendentals=0),
    )(*args)


def per_device(image, kernels, gains, up_weights, down_weights, cotangent):
    d = dims_of(image, kernels, up_weights)
    bind = functools.partial
    rows, cols, channels = image.shape
    units = up_weights.shape[2]
    tile, ext, wide = (rows * cols, d.ext_pad, (rows + 4 * d.h) * d.wide)
    frame = (rows + 2 * d.h) * d.ext_cols + 16
    taps = ((d.size * d.size * 16, LANES), bf16)
    tap_sums = ((d.size * d.size * 8, LANES), f32)
    sums_rows = ceil8(d.size * d.size + 1)

    bands, others = (band_combos(d.row_count), other_combos(d.row_count))

    def strips_of(pairs, radii):
        return [(shape, bf16) for shape in strip_shapes(pairs, rows, cols, channels, radii)]

    image, *band_strips = run(
        bind(bands_kernel, d), [(image.shape, bf16)] + strips_of(bands, (2 * d.h,)), [], image, in_hbm=1, sems=1
    )
    other_strips = run(bind(others_kernel, d), strips_of(others, (2 * d.h,)), [], image, *band_strips)
    strips = exchange(band_strips, other_strips, d.row_count, d.col_count)
    mixing = [((2 * LANES, 2 * units), bf16), ((2 * units, 2 * LANES), bf16)]
    forward0, back0, forward1, back1, grad_in0, grad_out0, taps0, taps1, gains = run(
        weights_kernel,
        mixing * 3 + [taps, taps, (gains.shape, f32)],
        [((2, channels, units), bf16), ((2, channels, units), bf16), ((d.size, d.size, 2, channels), f32)],
        up_weights,
        jnp.swapaxes(down_weights, 1, 2),
        jnp.transpose(kernels, (1, 2, 0, 3)),
        gains,
        in_hbm=4,
        sems=4,
        busy_us=2,
    )

    first = run(
        bind(first_kernel, d),
        [
            (image.shape, bf16),
            ((wide, LANES), f32),
            ((frame, LANES), f32),
            ((ext, LANES), bf16),
            ((ext, LANES), f32),
            ((ext, units), bf16),
            ((ext, units), bf16),
            ((tile, LANES), f32),
            ((tile, LANES), bf16),
            ((tile, units), bf16),
            ((tile, units), bf16),
            ((8, LANES), f32),
        ]
        + strips_of(bands, (2 * d.h, d.h)),
        [((ext, LANES), f32)],
        image,
        cotangent,
        taps0,
        taps1,
        gains,
        forward0,
        back0,
        forward1,
        back1,
        *strips,
        busy_us=15,
    )
    (final, x0, x1, unit0, inv0, hidden0, slope0, grad1, normed1, pre_grad1, hidden1, gain_part) = first[:12]
    band_strips = first[12:]
    other_strips = run(
        bind(grad_others_kernel, d), strips_of(others, (2 * d.h, d.h)), [], grad1, cotangent, *band_strips
    )
    strips = exchange(band_strips, other_strips, d.row_count, d.col_count)

    taps_sum1, up_sum1, down_sum1, output = run(
        bind(sums_kernel, d),
        [((sums_rows, LANES), f32), ((units, LANES), f32), ((units, LANES), f32), (image.shape, bf16)],
        [tap_sums],
        x1,
        grad1,
        normed1,
        pre_grad1,
        hidden1,
        cotangent,
        gain_part,
        final,
        busy_us=3,
    )

    held = d.count // 2 * 2 * d.layer_rows
    small = ((d.small_rows, LANES), f32)
    grad0, middle, keep, sums, send = run(
        bind(third_kernel, d),
        [((frame, LANES), f32), ((tile, LANES), f32), ((held, LANES), f32), small, ((held + d.small_rows, LANES), bf16)],
        [
            ((wide, LANES), f32),
            ((frame, LANES), f32),
            ((ext, LANES), f32),
            ((ext, LANES), f32),
            tap_sums,
            ((LANES, units), f32),
            ((LANES, units), f32),
            ((8, LANES), f32),
            ((sums_rows, LANES), f32),
            ((2 * (units + 8), LANES), f32),
            ((2 * held, LANES), f32),
        ],
        grad1,
        cotangent,
        taps1,
        gains,
        grad_in0,
        grad_out0,
        x0,
        unit0,
        inv0,
        hidden0,
        slope0,
        taps_sum1,
        up_sum1,
        down_sum1,
        *strips,
        busy_us=12,
    )
    axes = ("row", "col")
    sends = [send]
    for stage, group in enumerate(d.groups):
        gots = [lax.ppermute(x, axes, swap_by(d, group, mask)) for mask, x in enumerate(sends, 1)]
        ready = []
        if stage == 1:
            gradient, *ready = run(
                bind(image_kernel, d),
                [(image.shape, bf16), ((8, LANES), f32)],
                [((tile, LANES), f32)],
                grad0,
                middle,
                taps0,
                sums,
                busy_us=3,
            )
        if stage + 1 < len(d.groups):
            after = d.groups[stage + 1]
            whole, held = (held, held >> len(after))
            keep, sums, *sends = run(
                bind(stage_kernel, d, stage + 1),
                [((held, LANES), f32), small] + [((held + d.small_rows, LANES), bf16)] * len_sends(after),
                [((whole, LANES), f32)],
                keep,
                sums,
                *gots,
                *ready,
            )
    kernel_out, gain_out, up_out, down_out = run(
        bind(last_kernel, d),
        [
            ((d.size, d.size, 2, channels), f32),
            (gains.shape, f32),
            ((2, d.part, d.half), f32),
            ((2, d.part, d.half), f32),
        ],
        [],
        keep,
        sums,
        *gots,
    )
    kernel_out = jnp.transpose(kernel_out, (2, 0, 1, 3))
    return (output, gradient, kernel_out, gain_out, jnp.swapaxes(up_out, 1, 2), down_out)


def solution(mesh):
    placed = (P("row", "col", None), P(), P(), P(), P(), P("row", "col", None))
    return jax.shard_map(
        per_device,
        mesh=mesh,
        in_specs=placed,
        out_specs=(
            P("row", "col", None),
            P("row", "col", None),
            P(),
            P(),
            P(None, "row", "col"),
            P(None, "col", "row"),
        ),
        check_vma=False,
    )
```

```python
import functools
import math

import jax
import jax.numpy as jnp
from jax import lax
from jax.experimental import pallas as pl
from jax.experimental.pallas import tpu as pltpu
from jax.sharding import PartitionSpec as P

epsilon = 1e-06
inv_sqrt_two = 0.7071067811865476
inv_sqrt_two_pi = 0.3989422804014327
log2_e = 1.4426950408889634
LANES = 128
SIDE = 8
f32, bf16 = (jnp.float32, jnp.bfloat16)


def ceil8(n):
    return -(-n // 8) * 8


def combos(row_count):
    listed = [(None, 0), (None, 1), (0, None), (0, 0), (0, 1)]
    if row_count > 2:
        listed += [(1, None), (1, 0), (1, 1)]
    return listed


def partner(index, start, count):
    if start is None:
        return index
    other = index + 1 if (index - start) % 2 == 0 else index - 1
    return other if 0 <= other < count else None


def swap_pairs(row_count, col_count, row_start, col_start):
    pairs = []
    for r in range(row_count):
        for c in range(col_count):
            pr, pc = (partner(r, row_start, row_count), partner(c, col_start, col_count))
            if pr is None:
                pr, pc = (r, c ^ 1)
            elif pc is None:
                pr, pc = (r ^ 1 if row_start is None else pr, c)
            pairs.append((r * col_count + c, pr * col_count + pc))
    return pairs


def exchange(bands, others, row_count, col_count):
    got = {}
    for strips, pairs in ((bands, band_combos(row_count)), (others, other_combos(row_count))):
        for strip, (rs, cs) in zip(strips, pairs):
            got[rs, cs] = lax.ppermute(strip, ("row", "col"), swap_pairs(row_count, col_count, rs, cs))
    return [got[pair] for pair in combos(row_count)]


class Place:
    def __init__(self, row_count, col_count):
        row, col = (lax.axis_index("row"), lax.axis_index("col"))
        self.even_row, self.even_col = (lax.rem(row, 2) == 0, lax.rem(col, 2) == 0)
        self.has = {
            "above": row > 0,
            "below": row < row_count - 1,
            "left": col > 0,
            "right": col < col_count - 1,
        }
        self.row_count = row_count


def band_combos(row_count):
    return [pair for pair in combos(row_count) if pair[1] is None]


def other_combos(row_count):
    return [pair for pair in combos(row_count) if pair[1] is not None]


def write_strips(place, outs, takes, pairs):
    for out, (rs, cs) in zip(outs, pairs):
        at = 0
        for take, radius, rows, cols in takes:
            row_sets = [slice(0, rows)] * 2
            col_sets = [slice(0, cols)] * 2
            if rs is not None:
                row_sets = [slice(rows - radius, rows), slice(0, radius)]
                if rs == 1:
                    row_sets = row_sets[::-1]
            if cs is not None:
                col_sets = [slice(cols - SIDE, cols), slice(0, SIDE)]
                if cs == 1:
                    col_sets = col_sets[::-1]
            count = row_sets[0].stop - row_sets[0].start
            for i in range(count):
                parts = {}
                for er in (0, 1):
                    for ec in (0, 1):
                        key = (row_sets[er].start + i, col_sets[ec].start, col_sets[ec].stop)
                        if key not in parts:
                            parts[key] = take(*key)
                        parts[er, ec] = parts[key]
                if cs is None:
                    pick = [parts[0, 0], parts[1, 0]]
                else:
                    pick = [jnp.where(place.even_col, parts[e, 0], parts[e, 1]) for e in (0, 1)]
                value = pick[0] if rs is None else jnp.where(place.even_row, pick[0], pick[1])
                out[at + i] = value.astype(out.dtype)
            at += count


def strip_shapes(pairs, rows, cols, channels, radii):
    shapes = []
    for rs, cs in pairs:
        height = sum(rows if rs is None else radius for radius in radii)
        shapes.append((height, cols if cs is None else SIDE, channels))
    return shapes


def received(place, strips, row_sections):
    table = dict(zip(combos(place.row_count), strips))
    full_start, band_start = row_sections

    def along(rs, cs, i):
        return table[rs, cs][(full_start if rs is None else band_start) + i].astype(f32)

    def column(rs, side, i):
        if side is None:
            return along(rs, None, i)
        near, far = (along(rs, 0, i), along(rs, 1, i))
        if side == "left":
            return jnp.where(place.even_col, far, near)
        return jnp.where(place.even_col, near, far)

    def read(vertical, side, i):
        if vertical is None:
            value = column(None, side, i)
        elif place.row_count == 2:
            value = column(0, side, i)
        else:
            near, far = (column(0, side, i), column(1, side, i))
            if vertical == "above":
                value = jnp.where(place.even_row, far, near)
            else:
                value = jnp.where(place.even_row, near, far)
        if vertical is not None:
            value = jnp.where(place.has[vertical], value, 0.0)
        if side is not None:
            value = jnp.where(place.has[side], value, 0.0)
        return value

    return read


def assemble(place, target, own, read, radius, rows, cols, channels):
    width = cols + 2 * SIDE
    target[...] = jnp.zeros(target.shape, f32)
    for vertical, start, count in (("above", 0, radius), (None, radius, rows), ("below", radius + rows, radius)):
        for i in range(count):
            base = (start + i) * width
            middle = own(i) if vertical is None else read(vertical, None, i)
            target[base + SIDE : base + SIDE + cols, 0:channels] = middle
            target[base : base + SIDE, 0:channels] = read(vertical, "left", i)
            target[base + SIDE + cols : base + width, 0:channels] = read(vertical, "right", i)


def spread_taps(kernel_ref, layer, target):
    size, channels = (kernel_ref.shape[0], kernel_ref.shape[3])
    for a in range(size):
        for b in range(size):
            t = a * size + b
            row = pad_lanes(kernel_ref[a, b, layer : layer + 1, :])
            target[t * 16 : t * 16 + 16, :] = jnp.broadcast_to(row, (16, LANES)).astype(bf16)


def tree_sum(terms):
    while len(terms) > 1:
        pairs = [terms[i] + terms[i + 1] for i in range(0, len(terms) - 1, 2)]
        terms = pairs + ([terms[-1]] if len(terms) % 2 else [])
    return terms[0]


def conv_group(src, base, stride, rows_out, taps, size, flipped=False):
    total = [None] * rows_out
    for b in range(size):
        order = [a * size + b for a in range(size)]
        if flipped:
            order = [size * size - 1 - t for t in order]
        weights = [taps[t * 16 : t * 16 + 16, :] for t in order]
        window = []
        for i in range(rows_out + size - 1):
            window.append(src[pl.ds(base + i * stride + b, 16), :].astype(bf16))
            r = i - size + 1
            if r >= 0:
                term = tree_sum([window[r + a] * weights[a] for a in range(size)]).astype(f32)
                total[r] = term if total[r] is None else total[r] + term
    return total


def group_start(g, cols):
    return pl.multiple_of(jnp.minimum(g * 16, cols - 16), 8)


def kernel_sums(src, src_base, src_stride, grad, grad_base, grad_stride, rows, cols, size, sums):
    sums[...] = jnp.zeros(sums.shape, f32)

    def group(g, carry):
        at = pl.multiple_of(g * 16, 16)
        grads = [grad[pl.ds(grad_base + i * grad_stride + at, 16), :].astype(bf16) for i in range(rows)]
        for b in range(size):
            lines = [
                src[pl.ds(src_base + i * src_stride + at + b, 16), :].astype(bf16) for i in range(rows + size - 1)
            ]
            for a in range(size):
                term = tree_sum([lines[r + a] * grads[r] for r in range(rows)]).astype(f32)
                t = (a * size + b) * 8
                sums[t : t + 8, :] += term[0:8] + term[8:16]
        return carry

    lax.fori_loop(0, cols // 16, group, 0)


def diagonal(first, second):
    top = jnp.concatenate([first, jnp.zeros((first.shape[0], second.shape[1]), first.dtype)], axis=1)
    bottom = jnp.concatenate([jnp.zeros((second.shape[0], first.shape[1]), first.dtype), second], axis=1)
    return jnp.concatenate([top, bottom], axis=0)


def lane_total(x):
    high = x.astype(bf16)
    low = (x - high.astype(f32)).astype(bf16)
    both = jnp.concatenate([high, low], axis=1)
    return dot(both, jnp.ones((2 * LANES, LANES), bf16))


def paired_dot(x, y, weights):
    total = dot(jnp.concatenate([x.astype(bf16), y.astype(bf16)], axis=1), weights)
    half = weights.shape[1] // 2
    return (total[:, :half], total[:, half:])


def layer_norm(parts, channels, ones):
    lane = lax.broadcasted_iota(jnp.int32, parts[0].shape, 1)
    centred = [jnp.where(lane < channels, x - lane_total(x) * (1.0 / channels), 0.0) for x in parts]
    variances = paired_dot(centred[0] * centred[0], centred[1] * centred[1], ones)
    inverses = [lax.rsqrt(v * (1.0 / channels) + epsilon) for v in variances]
    return ([c * i for c, i in zip(centred, inverses)], inverses)


def norm_backward(normed_grad, unit, inverse, gain, channels, ones):
    m = normed_grad * gain
    mean, along = paired_dot(m, m * unit, ones)
    lane = lax.broadcasted_iota(jnp.int32, m.shape, 1)
    centred = m - (mean + unit * along) * (1.0 / channels)
    return jnp.where(lane < channels, inverse * centred, 0.0)


def gelu_parts(v):
    p = 0.3275911 * inv_sqrt_two
    c1, c2, c3, c4, c5 = (
        0.5 * c / p ** (k + 1)
        for k, c in enumerate((0.254829592, -0.284496736, 1.421413741, -1.453152027, 1.061405429))
    )
    t = pl.reciprocal(jnp.abs(v) + 1.0 / p, approx=True)
    bell = jnp.exp2(v * v * (-0.5 * log2_e))
    tail = ((((c5 * t + c4) * t + c3) * t + c2) * t + c1) * t * bell
    cdf = jnp.where(v >= 0.0, 1.0 - tail, tail)
    return (v * cdf, cdf + v * (bell * inv_sqrt_two_pi))


def dot(x, w):
    return jnp.dot(x, w, preferred_element_type=f32)


def dot_leading(x, y):
    return lax.dot_general(x, y, (((0,), (0,)), ((), ())), preferred_element_type=f32)


def pad_lanes(x):
    rows, channels = x.shape
    return jnp.concatenate([x, jnp.zeros((rows, LANES - channels), x.dtype)], axis=1)


def pieces(total, size):
    return [(start, min(size, total - start)) for start in range(0, total, size)]


def round16(x):
    return x.astype(bf16).astype(f32)


def fetch(sources, targets, sems):
    copies = [pltpu.make_async_copy(a, b, sems.at[i]) for i, (a, b) in enumerate(zip(sources, targets))]
    for copy in copies:
        copy.start()
    for copy in copies:
        copy.wait()


def image_take(ref):
    return lambda i, lo, hi: ref[i].astype(f32)[lo:hi]


def flat_take(ref, cols, channels):
    return lambda i, lo, hi: ref[i * cols + lo : i * cols + hi, 0:channels]


def bands_kernel(dims, image_in, image, *refs):
    outs, sems = (refs[:-1], refs[-1])
    place = Place(dims.row_count, dims.col_count)
    fetch((image_in,), (image,), sems)
    takes = [(image_take(image), 2 * dims.h, dims.rows, dims.cols)]
    write_strips(place, outs, takes, band_combos(dims.row_count))


def others_kernel(dims, image, *refs):
    outs = refs[len(band_combos(dims.row_count)) :]
    place = Place(dims.row_count, dims.col_count)
    takes = [(image_take(image), 2 * dims.h, dims.rows, dims.cols)]
    write_strips(place, outs, takes, other_combos(dims.row_count))


def grad_others_kernel(dims, grad1, cot, *refs):
    outs = refs[len(band_combos(dims.row_count)) :]
    place = Place(dims.row_count, dims.col_count)
    takes = [
        (flat_take(grad1, dims.cols, dims.channels), 2 * dims.h, dims.rows, dims.cols),
        (image_take(cot), dims.h, dims.rows, dims.cols),
    ]
    write_strips(place, outs, takes, other_combos(dims.row_count))


def weights_kernel(up_in, down_t_in, kernels_in, gains_in, *refs):
    forward0, back0, forward1, back1, grad_in0, grad_out0, taps0, taps1, gains, up_w, down_w, kernels, sems = refs
    fetch((up_in, down_t_in, kernels_in, gains_in), (up_w, down_w, kernels, gains), sems)
    spread_taps(kernels, 0, taps0)
    spread_taps(kernels, 1, taps1)
    channels, units = up_w.shape[1:]
    blank = jnp.zeros((LANES - channels, units), f32)
    wide, tall = ([], [])
    for layer in range(2):
        for ref in (up_w, down_w):
            full = jnp.concatenate([ref[layer].astype(f32), blank], axis=0)
            wide.append(full.astype(bf16))
            tall.append(full.T.astype(bf16))
    (up0, down_t0, up1, down_t1), (up_t0, down0, up_t1, down1) = (wide, tall)
    forward0[...] = diagonal(up0, up0)
    back0[...] = diagonal(down0, down0)
    forward1[...] = diagonal(up1, down_t1)
    back1[...] = diagonal(down1, up_t1)
    grad_in0[...] = diagonal(down_t0, down_t0)
    grad_out0[...] = diagonal(up_t0, up_t0)


def first_kernel(dims, *refs):
    count = len(combos(dims.row_count))
    image, cot, taps0, taps1, gains, forward0, back0, forward1, back1 = refs[:9]
    strips = refs[9 : 9 + count]
    refs = refs[9 + count :]
    (output, x0, x1, unit0, inv0, hidden0, slope0, grad1, normed1, pre_grad1, hidden1, gain_sum) = refs[:12]
    outs, conv = (refs[12:-1], refs[-1])
    place = Place(dims.row_count, dims.col_count)
    rows, cols, channels, h, size = (dims.rows, dims.cols, dims.channels, dims.h, dims.size)
    ext_rows, ext_cols, wide = (dims.ext_rows, dims.ext_cols, dims.wide)
    skip = dims.skipped_rows(place)
    read = received(place, strips, (0, 0))
    assemble(place, x0, lambda i: image[i].astype(f32), read, 2 * h, rows, cols, channels)

    x1[...] = jnp.zeros(x1.shape, f32)
    if dims.ext_pad > ext_rows * ext_cols:
        conv[ext_rows * ext_cols :, :] = jnp.zeros((dims.ext_pad - ext_rows * ext_cols, LANES), f32)
    frame = pl.multiple_of(skip * ext_cols, 8)

    def conv0(g, carry):
        at = group_start(g, ext_cols)
        base = pl.multiple_of(skip * wide, 8) + at
        total = conv_group(x0, base + 1, wide, ext_rows, taps0, size)
        for r in range(ext_rows):
            conv[pl.ds(r * ext_cols + at, 16), :] = total[r]
            x1[pl.ds(frame + r * ext_cols + at, 16), :] = x0[pl.ds(base + (r + h) * wide + 4, 16), :]
        return carry

    lax.fori_loop(0, -(-ext_cols // 16), conv0, 0)
    gain = pad_lanes(gains[0:1, :])
    ones = diagonal(jnp.ones((LANES, LANES), bf16), jnp.ones((LANES, LANES), bf16))
    half = dims.ext_pad // 2
    for start, n in pieces(half, dims.piece):
        spans = [(start, n), (half + start, n)]
        units, inverses = layer_norm([conv[at : at + n, :] for at, n in spans], channels, ones)
        pres = paired_dot(units[0] * gain, units[1] * gain, forward0[...])
        hiddens = []
        for (at, n), unit, inverse, pre in zip(spans, units, inverses, pres):
            unit0[at : at + n, :] = unit.astype(bf16)
            inv0[at : at + n, :] = inverse
            value, slope = gelu_parts(pre)
            hiddens.append(value.astype(bf16))
            hidden0[at : at + n, :] = hiddens[-1]
            slope0[at : at + n, :] = slope.astype(bf16)
        branches = paired_dot(hiddens[0], hiddens[1], back0[...])
        for (at, n), branch in zip(spans, branches):
            px = pl.ds(frame + at, n)
            x1[px, :] = round16(x1[px, :] + branch)
    clear_outside(place, x1, dims)

    def conv1(g, carry):
        at = group_start(g, cols)
        total = conv_group(x1, at + 1, ext_cols, rows, taps1, size)
        for r in range(rows):
            conv[pl.ds(r * cols + at, 16), :] = total[r]
        return carry

    lax.fori_loop(0, -(-cols // 16), conv1, 0)
    gain1 = pad_lanes(gains[1:2, :])
    gain_sum[...] = jnp.zeros(gain_sum.shape, f32)
    lines = dims.line_step
    step = lines * cols
    for k in range(rows // lines):
        px = slice(k * step, (k + 1) * step)
        middle = k * step + step // 2
        units, inverses = layer_norm([conv[k * step : middle, :], conv[middle : (k + 1) * step, :]], channels, ones)
        unit, inverse = (jnp.concatenate(units, axis=0), jnp.concatenate(inverses, axis=0))
        normed = (unit * gain1).astype(bf16)
        normed1[px, :] = normed
        upstream = pad_lanes(cot[k * lines : (k + 1) * lines].reshape(step, channels))
        pre, hidden_grad = paired_dot(normed, upstream, forward1[...])
        value, slope = gelu_parts(pre)
        hidden = value.astype(bf16)
        hidden1[px, :] = hidden
        pre_grad = (hidden_grad * slope).astype(bf16)
        pre_grad1[px, :] = pre_grad
        branch, normed_grad = paired_dot(hidden, pre_grad, back1[...])
        for i in range(lines):
            start = (k * lines + i + h) * ext_cols + 4
            line = x1[start : start + cols, :] + branch[i * cols : (i + 1) * cols]
            output[k * lines + i] = line[:, :channels].astype(bf16)
        product = normed_grad * unit
        gain_sum[...] += jnp.sum(product.reshape(step // 8, 8, LANES), axis=0)
        grad1[px, :] = round16(norm_backward(normed_grad, unit, inverse, gain1, channels, ones))

    takes = [(flat_take(grad1, cols, channels), 2 * h, rows, cols), (image_take(cot), h, rows, cols)]
    write_strips(place, outs, takes, band_combos(dims.row_count))


def clear_outside(place, flat, dims):
    h, frame_rows, ext_cols = (dims.h, dims.rows + 2 * dims.h, dims.ext_cols)
    margin = (ext_cols - dims.cols) // 2

    @pl.when(jnp.logical_not(place.has["above"]))
    def _():
        flat[0 : h * ext_cols, :] = jnp.zeros((h * ext_cols, LANES), f32)

    @pl.when(jnp.logical_not(place.has["below"]))
    def _():
        last = (frame_rows - h) * ext_cols
        flat[last:, :] = jnp.zeros((flat.shape[0] - last, LANES), f32)

    @pl.when(jnp.logical_not(place.has["left"]))
    def _():
        for r in range(frame_rows):
            flat[r * ext_cols : r * ext_cols + margin, :] = jnp.zeros((margin, LANES), f32)

    @pl.when(jnp.logical_not(place.has["right"]))
    def _():
        for r in range(frame_rows):
            flat[(r + 1) * ext_cols - margin : (r + 1) * ext_cols, :] = jnp.zeros((margin, LANES), f32)


def sums_kernel(
    dims, x1, grad1, normed1, pre_grad1, hidden1, cot, gain_part, final, taps_sum, up_sum, down_sum, output, sums
):
    output[...] = final[...]
    kernel_sums(x1, 1, dims.ext_cols, grad1, 0, dims.cols, dims.rows, dims.cols, dims.size, sums)
    store_sums(dims, sums, gain_part[...], taps_sum)
    upstream = pad_lanes(cot[...].reshape(dims.rows * dims.cols, dims.channels))
    up_sum[...] = dot_leading(normed1[...], pre_grad1[...]).T
    down_sum[...] = dot_leading(upstream, hidden1[...]).T


def store_sums(dims, sums, gain_part, target):
    taps = dims.size * dims.size
    target[...] = jnp.zeros(target.shape, f32)
    for t in range(taps):
        target[t : t + 1, :] = jnp.sum(sums[t * 8 : t * 8 + 8, :], axis=0, keepdims=True)
    target[taps : taps + 1, :] = jnp.sum(gain_part, axis=0, keepdims=True)


def third_kernel(dims, *refs):
    count = len(combos(dims.row_count))
    (grad1, cot, taps1, gains, grad_in0, grad_out0, x0, unit0, inv0, hidden0, slope0) = refs[:11]
    (taps_sum1, up_sum1, down_sum1) = refs[11:14]
    strips = refs[14 : 14 + count]
    (grad0, middle, keep, small_keep, send) = refs[14 + count : 19 + count]
    (wide_grad, cot_frame, upstream, own, sums, normed0, flow0, pre_grad0, gain_sum, small, tall, slabs) = refs[19 + count :]
    place = Place(dims.row_count, dims.col_count)
    rows, cols, channels, h, size = (dims.rows, dims.cols, dims.channels, dims.h, dims.size)
    ext_rows, ext_cols, wide = (dims.ext_rows, dims.ext_cols, dims.wide)
    skip = dims.skipped_rows(place)
    read = received(place, strips, (0, 0))
    assemble(
        place, wide_grad, lambda i: grad1[i * cols : (i + 1) * cols, 0:channels], read, 2 * h, rows, cols, channels
    )
    read_cot = received(place, strips, (rows, 2 * h))
    margin = (ext_cols - cols) // 2
    cot_frame[...] = jnp.zeros(cot_frame.shape, f32)
    for vertical, start, n in (("above", 0, h), (None, h, rows), ("below", h + rows, h)):
        for i in range(n):
            base = (start + i) * ext_cols
            line = cot[i].astype(f32) if vertical is None else read_cot(vertical, None, i)
            cot_frame[base + margin : base + margin + cols, 0:channels] = line
            cot_frame[base : base + margin, 0:channels] = read_cot(vertical, "left", i)[SIDE - margin :]
            cot_frame[base + margin + cols : base + ext_cols, 0:channels] = read_cot(vertical, "right", i)[:margin]

    used = ext_rows * ext_cols
    if dims.ext_pad > used:
        upstream[used:, :] = jnp.zeros((dims.ext_pad - used, LANES), f32)
        own[used:, :] = jnp.zeros((dims.ext_pad - used, LANES), f32)
    grad0[...] = jnp.zeros(grad0.shape, f32)
    frame = pl.multiple_of(skip * ext_cols, 8)

    def conv1(g, carry):
        at = group_start(g, ext_cols)
        total = conv_group(wide_grad, pl.multiple_of(skip * wide, 8) + at + 1, wide, ext_rows, taps1, size, True)
        col = lax.broadcasted_iota(jnp.int32, (16, LANES), 0) + (at - margin)
        inside = jnp.where(jnp.logical_and(col >= 0, col < cols), 1.0, 0.0)
        for r in range(ext_rows):
            px = pl.ds(r * ext_cols + at, 16)
            upstream[px, :] = cot_frame[pl.ds(frame + r * ext_cols + at, 16), :] + total[r]
            mine = jnp.logical_and(r + skip >= h, r + skip < h + rows)
            own[px, :] = jnp.where(mine, inside, 0.0)
        return carry

    lax.fori_loop(0, -(-ext_cols // 16), conv1, 0)
    for i in range(rows):
        line = upstream[pl.ds((i + h - skip) * ext_cols + margin, cols), :]
        middle[i * cols : (i + 1) * cols, :] = round16(line)

    gain = pad_lanes(gains[0:1, :])
    gain_sum[...] = jnp.zeros(gain_sum.shape, f32)
    ones = diagonal(jnp.ones((LANES, LANES), bf16), jnp.ones((LANES, LANES), bf16))
    half_px = dims.ext_pad // 2
    for start, n in pieces(half_px, dims.piece):
        spans = [(start, n), (half_px + start, n)]
        flows = [upstream[at : at + n, :].astype(bf16) for at, n in spans]
        hidden_grads = paired_dot(flows[0], flows[1], grad_in0[...])
        pre_grads = [
            (grad * slope0[at : at + n, :].astype(f32)).astype(bf16) for grad, (at, n) in zip(hidden_grads, spans)
        ]
        normed_grads = paired_dot(pre_grads[0], pre_grads[1], grad_out0[...])
        for (at, n), flow, pre_grad, normed_grad in zip(spans, flows, pre_grads, normed_grads):
            mine = own[at : at + n, :]
            unit = unit0[at : at + n, :].astype(f32)
            normed0[at : at + n, :] = (unit * gain * mine).astype(bf16)
            flow0[at : at + n, :] = flow * mine.astype(bf16)
            pre_grad0[at : at + n, :] = pre_grad
            product = normed_grad * unit * mine
            gain_sum[...] += jnp.sum(product.reshape(n // 8, 8, LANES), axis=0)
            grad = norm_backward(normed_grad, unit, inv0[at : at + n, :], gain, channels, ones)
            grad0[pl.ds(frame + at, n), :] = round16(grad)
    clear_outside(place, grad0, dims)
    kernel_sums(
        x0, h * wide + SIDE - h, wide, grad0, h * ext_cols + margin, ext_cols, rows, cols, size, sums
    )
    store_sums(dims, sums, gain_sum[...], small)

    taps_rows = size * size + 1
    merged = jnp.concatenate([small[0:taps_rows, :], taps_sum1[0:taps_rows, :]], axis=0) * dims.factor
    merged = fold_rows(merged, dims.small_rows, channels).astype(bf16)
    small_keep[...] = merged.astype(f32)

    layer_rows, part, half = (dims.layer_rows, dims.part, dims.half)
    units = hidden0.shape[1]
    up0 = dot_leading(normed0[...], pre_grad0[...]).T * dims.factor
    down0 = dot_leading(flow0[...], hidden0[...]).T * dims.factor
    up1 = up_sum1[...] * dims.factor
    down1 = down_sum1[...] * dims.factor
    lane = lax.broadcasted_iota(jnp.int32, (units, LANES), 1)
    slab_rows = 2 * layer_rows
    for r in range(dims.row_count):
        for layer, (u, d) in enumerate(((up0, down0), (up1, down1))):
            first = pltpu.roll(u, LANES - r * half, 1) if r else u
            shift = (half - r * half) % LANES
            second = pltpu.roll(d, shift, 1) if shift else d
            joined = jnp.where(lane < half, first, jnp.where(lane < 2 * half, second, 0.0))
            tall[layer * (units + 8) : layer * (units + 8) + units, :] = joined

        for c in range(dims.col_count):
            index = 0
            for axis, bit in dims.stages:
                index = 2 * index + ((r if axis == "row" else c) >> bit & 1)
            for layer in range(2):
                to, at = (index * slab_rows + layer * layer_rows, layer * (units + 8) + c * part)
                slabs[to : to + layer_rows, :] = tall[at : at + layer_rows, :]

    split(dims, 0, slabs, merged, keep, (send,))


def fold_rows(x, rows, used):
    n = x.shape[0]
    if rows >= n:
        return pad_rows(x, rows)
    assert used <= 96
    stride = ceil8(n - rows)
    rest = pad_rows(x[rows:], stride)
    pieces_of = pad_rows(jnp.concatenate([pltpu.roll(rest, 96 - 32 * k, 1) for k in range(3)], axis=0), rows)
    lane = lax.broadcasted_iota(jnp.int32, (rows, LANES), 1)
    return jnp.where(lane < 96, x[:rows], pieces_of)


def pad_rows(x, rows):
    if rows == x.shape[0]:
        return x
    return jnp.concatenate([x, jnp.zeros((rows - x.shape[0], LANES), x.dtype)], axis=0)


def unfold_rows(x, n):
    rows = x.shape[0]
    if rows >= n:
        return x[:n]
    stride = ceil8(n - rows)
    lane = lax.broadcasted_iota(jnp.int32, (stride, LANES), 1)
    rest = jnp.zeros((stride, LANES), x.dtype)
    for k in range(3):
        moved = pltpu.roll(x[k * stride : (k + 1) * stride], 32 + 32 * k, 1)
        rest = jnp.where(jnp.logical_and(lane >= 32 * k, lane < 32 * k + 32), moved, rest)
    return jnp.concatenate([x, rest[: n - rows]], axis=0)


def split(dims, stage, slabs, merged, keep, sends):
    group = dims.groups[stage]
    count = slabs.shape[0] >> len(group)
    mine = 0
    for axis, bit in group:
        mine = mine * 2 + lax.rem(lax.div(lax.axis_index(axis), 1 << bit), 2)
    keep[...] = slabs[pl.ds(pl.multiple_of(mine * count, 16), count), :]
    for mask, send in enumerate(sends, 1):
        other = 0
        for j in range(len(group)):
            weight = 1 << j
            digit = lax.rem(lax.div(mine, weight), 2)
            other = other + weight * (1 - digit if mask & weight else digit)
        send[0:count, :] = slabs[pl.ds(pl.multiple_of(other * count, 16), count), :].astype(bf16)
        send[count:, :] = merged


def gather_up(keep, small, gots):
    count = keep.shape[0]
    slabs = [keep[...]] + [got[0:count, :].astype(f32) for got in gots]
    sums = [small[...]] + [got[count:, :].astype(f32) for got in gots]
    if len(gots) == 1:
        return (slabs[0] + slabs[1], sums[0] + sums[1])
    return tuple((x[0] + x[1]) + (x[2] + x[3]) for x in (slabs, sums))


def stage_kernel(dims, stage, keep, small, *refs):
    before, after = (len_sends(dims.groups[stage - 1]), len_sends(dims.groups[stage]))
    gots = refs[:before]
    keep_out, small_out = refs[-3 - after : -1 - after]
    sends, total = (refs[-1 - after : -1], refs[-1])
    slabs, merged = gather_up(keep, small, gots)
    total[...] = slabs
    merged = merged.astype(bf16)
    small_out[...] = merged.astype(f32)
    split(dims, stage, total, merged, keep_out, sends)


def len_sends(group):
    return (1 << len(group)) - 1


def last_kernel(dims, keep, small, *refs):
    gots, (kernel_out, gain_out, up_out, down_out) = (refs[:-4], refs[-4:])
    total, merged = gather_up(keep, small, gots)
    merged = unfold_rows(merged, 2 * (dims.size * dims.size + 1))
    size, channels, half, part = (dims.size, dims.channels, dims.half, dims.part)
    for layer in range(2):
        block = total[layer * dims.layer_rows : layer * dims.layer_rows + part]
        up_out[layer] = block[:, :half]
        down_out[layer] = block[:, half : 2 * half]
        for t in range(size * size + 1):
            at = layer * (size * size + 1) + t
            row = merged[at : at + 1, 0:channels]
            if t < size * size:
                kernel_out[t // size, t % size, layer : layer + 1, :] = row
            else:
                gain_out[layer : layer + 1, :] = row


def image_kernel(dims, grad0, middle, taps0, after, out, ready, work):
    rows, cols, size = (dims.rows, dims.cols, dims.size)

    def conv0(g, carry):
        at = group_start(g, cols)
        total = conv_group(grad0, at + 1, dims.ext_cols, rows, taps0, size, True)
        for r in range(rows):
            work[pl.ds(r * cols + at, 16), :] = middle[pl.ds(r * cols + at, 16), :] + total[r]
        return carry

    lax.fori_loop(0, -(-cols // 16), conv0, 0)
    for r in range(rows):
        out[r] = work[r * cols : (r + 1) * cols, 0 : dims.channels].astype(bf16)
    ready[...] = jnp.zeros(ready.shape, f32)


class Dims:
    def skipped_rows(self, place):
        if self.row_count > 2:
            return 0
        return jnp.where(place.has["above"], 0, self.h)


def dims_of(image, kernels, up_weights):
    d = Dims()
    d.row_count, d.col_count = (lax.axis_size("row"), lax.axis_size("col"))
    d.rows, d.cols, d.channels = image.shape
    d.size = kernels.shape[1]
    d.h = d.size // 2
    d.ext_rows, d.ext_cols = (d.rows + (d.h if d.row_count == 2 else 2 * d.h), d.cols + 8)
    d.wide = d.cols + 2 * SIDE
    d.ext_pad = -(-d.ext_rows * d.ext_cols // 32) * 32
    d.piece = 176
    d.line_step = 4
    d.half = d.channels // d.row_count
    d.part = up_weights.shape[2] // d.col_count
    d.layer_rows = ceil8(d.part)
    d.count = d.row_count * d.col_count
    d.small_rows = 80 if d.size == 7 and d.channels <= 96 else -(-2 * (d.size * d.size + 1) // 16) * 16
    d.factor = 1.0 / math.sqrt(d.rows * d.cols * d.count)
    row_bits, col_bits = (d.row_count.bit_length() - 1, d.col_count.bit_length() - 1)
    bits = [("row", b) for b in range(row_bits)] + [("col", b) for b in range(1, col_bits)]
    d.groups = [[("col", 0)]] + [bits[i : i + 2] for i in range(0, len(bits), 2)]
    d.stages = [bit for group in d.groups for bit in group]
    return d


def swap_by(d, group, mask):
    flip = {"row": 0, "col": 0}
    for j, (axis, bit) in enumerate(group):
        if mask >> (len(group) - 1 - j) & 1:
            flip[axis] |= 1 << bit
    pairs = []
    for r in range(d.row_count):
        for c in range(d.col_count):
            pairs.append((r * d.col_count + c, (r ^ flip["row"]) * d.col_count + (c ^ flip["col"])))
    return pairs


def run(kernel, outs, scratch, *args, in_hbm=0, sems=0, busy_us=1):
    shapes = [jax.ShapeDtypeStruct(shape, kind) for shape, kind in outs]
    space = pl.BlockSpec(memory_space=pltpu.VMEM)
    far = pl.BlockSpec(memory_space=pltpu.HBM)
    held = [pltpu.VMEM(shape, kind) for shape, kind in scratch]
    if sems:
        held.append(pltpu.SemaphoreType.DMA((sems,)))
    return pl.pallas_call(
        kernel,
        out_shape=shapes,
        in_specs=[far] * in_hbm + [space] * (len(args) - in_hbm),
        out_specs=[space] * len(shapes),
        scratch_shapes=held,
        compiler_params=pltpu.CompilerParams(vmem_limit_bytes=32 * 1024 * 1024),
        cost_estimate=pl.CostEstimate(flops=int(busy_us * 1e9), bytes_accessed=1 << 18, transcendentals=0),
    )(*args)


def per_device(image, kernels, gains, up_weights, down_weights, cotangent):
    d = dims_of(image, kernels, up_weights)
    bind = functools.partial
    rows, cols, channels = image.shape
    units = up_weights.shape[2]
    tile, ext, wide = (rows * cols, d.ext_pad, (rows + 4 * d.h) * d.wide)
    frame = (rows + 2 * d.h) * d.ext_cols + 16
    taps = ((d.size * d.size * 16, LANES), bf16)
    tap_sums = ((d.size * d.size * 8, LANES), f32)
    sums_rows = ceil8(d.size * d.size + 1)

    bands, others = (band_combos(d.row_count), other_combos(d.row_count))

    def strips_of(pairs, radii):
        return [(shape, bf16) for shape in strip_shapes(pairs, rows, cols, channels, radii)]

    image, *band_strips = run(
        bind(bands_kernel, d), [(image.shape, bf16)] + strips_of(bands, (2 * d.h,)), [], image, in_hbm=1, sems=1
    )
    other_strips = run(bind(others_kernel, d), strips_of(others, (2 * d.h,)), [], image, *band_strips)
    strips = exchange(band_strips, other_strips, d.row_count, d.col_count)
    mixing = [((2 * LANES, 2 * units), bf16), ((2 * units, 2 * LANES), bf16)]
    forward0, back0, forward1, back1, grad_in0, grad_out0, taps0, taps1, gains = run(
        weights_kernel,
        mixing * 3 + [taps, taps, (gains.shape, f32)],
        [((2, channels, units), bf16), ((2, channels, units), bf16), ((d.size, d.size, 2, channels), f32)],
        up_weights,
        jnp.swapaxes(down_weights, 1, 2),
        jnp.transpose(kernels, (1, 2, 0, 3)),
        gains,
        in_hbm=4,
        sems=4,
        busy_us=2,
    )

    first = run(
        bind(first_kernel, d),
        [
            (image.shape, bf16),
            ((wide, LANES), f32),
            ((frame, LANES), f32),
            ((ext, LANES), bf16),
            ((ext, LANES), f32),
            ((ext, units), bf16),
            ((ext, units), bf16),
            ((tile, LANES), f32),
            ((tile, LANES), bf16),
            ((tile, units), bf16),
            ((tile, units), bf16),
            ((8, LANES), f32),
        ]
        + strips_of(bands, (2 * d.h, d.h)),
        [((ext, LANES), f32)],
        image,
        cotangent,
        taps0,
        taps1,
        gains,
        forward0,
        back0,
        forward1,
        back1,
        *strips,
        busy_us=15,
    )
    (final, x0, x1, unit0, inv0, hidden0, slope0, grad1, normed1, pre_grad1, hidden1, gain_part) = first[:12]
    band_strips = first[12:]
    other_strips = run(
        bind(grad_others_kernel, d), strips_of(others, (2 * d.h, d.h)), [], grad1, cotangent, *band_strips
    )
    strips = exchange(band_strips, other_strips, d.row_count, d.col_count)

    taps_sum1, up_sum1, down_sum1, output = run(
        bind(sums_kernel, d),
        [((sums_rows, LANES), f32), ((units, LANES), f32), ((units, LANES), f32), (image.shape, bf16)],
        [tap_sums],
        x1,
        grad1,
        normed1,
        pre_grad1,
        hidden1,
        cotangent,
        gain_part,
        final,
        busy_us=3,
    )

    held = d.count // 2 * 2 * d.layer_rows
    small = ((d.small_rows, LANES), f32)
    grad0, middle, keep, sums, send = run(
        bind(third_kernel, d),
        [((frame, LANES), f32), ((tile, LANES), f32), ((held, LANES), f32), small, ((held + d.small_rows, LANES), bf16)],
        [
            ((wide, LANES), f32),
            ((frame, LANES), f32),
            ((ext, LANES), f32),
            ((ext, LANES), f32),
            tap_sums,
            ((ext, LANES), bf16),
            ((ext, LANES), bf16),
            ((ext, units), bf16),
            ((8, LANES), f32),
            ((sums_rows, LANES), f32),
            ((2 * (units + 8), LANES), f32),
            ((2 * held, LANES), f32),
        ],
        grad1,
        cotangent,
        taps1,
        gains,
        grad_in0,
        grad_out0,
        x0,
        unit0,
        inv0,
        hidden0,
        slope0,
        taps_sum1,
        up_sum1,
        down_sum1,
        *strips,
        busy_us=12,
    )
    axes = ("row", "col")
    sends = [send]
    for stage, group in enumerate(d.groups):
        gots = [lax.ppermute(x, axes, swap_by(d, group, mask)) for mask, x in enumerate(sends, 1)]
        ready = []
        if stage == 1:
            gradient, *ready = run(
                bind(image_kernel, d),
                [(image.shape, bf16), ((8, LANES), f32)],
                [((tile, LANES), f32)],
                grad0,
                middle,
                taps0,
                sums,
                busy_us=3,
            )
        if stage + 1 < len(d.groups):
            after = d.groups[stage + 1]
            whole, held = (held, held >> len(after))
            keep, sums, *sends = run(
                bind(stage_kernel, d, stage + 1),
                [((held, LANES), f32), small] + [((held + d.small_rows, LANES), bf16)] * len_sends(after),
                [((whole, LANES), f32)],
                keep,
                sums,
                *gots,
                *ready,
            )
    kernel_out, gain_out, up_out, down_out = run(
        bind(last_kernel, d),
        [
            ((d.size, d.size, 2, channels), f32),
            (gains.shape, f32),
            ((2, d.part, d.half), f32),
            ((2, d.part, d.half), f32),
        ],
        [],
        keep,
        sums,
        *gots,
    )
    kernel_out = jnp.transpose(kernel_out, (2, 0, 1, 3))
    return (output, gradient, kernel_out, gain_out, jnp.swapaxes(up_out, 1, 2), down_out)


def solution(mesh):
    placed = (P("row", "col", None), P(), P(), P(), P(), P("row", "col", None))
    return jax.shard_map(
        per_device,
        mesh=mesh,
        in_specs=placed,
        out_specs=(
            P("row", "col", None),
            P("row", "col", None),
            P(),
            P(),
            P(None, "row", "col"),
            P(None, "col", "row"),
        ),
        check_vma=False,
    )
```

```python
import functools
import math

import jax
import jax.numpy as jnp
from jax import lax
from jax.experimental import pallas as pl
from jax.experimental.pallas import tpu as pltpu
from jax.sharding import PartitionSpec as P

epsilon = 1e-06
inv_sqrt_two = 0.7071067811865476
inv_sqrt_two_pi = 0.3989422804014327
log2_e = 1.4426950408889634
LANES = 128
SIDE = 8
f32, bf16 = (jnp.float32, jnp.bfloat16)


def ceil8(n):
    return -(-n // 8) * 8


def combos(row_count):
    listed = [(None, 0), (None, 1), (0, None), (0, 0), (0, 1)]
    if row_count > 2:
        listed += [(1, None), (1, 0), (1, 1)]
    return listed


def partner(index, start, count):
    if start is None:
        return index
    other = index + 1 if (index - start) % 2 == 0 else index - 1
    return other if 0 <= other < count else None


def swap_pairs(row_count, col_count, row_start, col_start):
    pairs = []
    for r in range(row_count):
        for c in range(col_count):
            pr, pc = (partner(r, row_start, row_count), partner(c, col_start, col_count))
            if pr is None:
                pr, pc = (r, c ^ 1)
            elif pc is None:
                pr, pc = (r ^ 1 if row_start is None else pr, c)
            pairs.append((r * col_count + c, pr * col_count + pc))
    return pairs


def exchange(bands, others, row_count, col_count):
    got = {}
    for strips, pairs in ((bands, band_combos(row_count)), (others, other_combos(row_count))):
        for strip, (rs, cs) in zip(strips, pairs):
            got[rs, cs] = lax.ppermute(strip, ("row", "col"), swap_pairs(row_count, col_count, rs, cs))
    return [got[pair] for pair in combos(row_count)]


class Place:
    def __init__(self, row_count, col_count):
        row, col = (lax.axis_index("row"), lax.axis_index("col"))
        self.even_row, self.even_col = (lax.rem(row, 2) == 0, lax.rem(col, 2) == 0)
        self.has = {
            "above": row > 0,
            "below": row < row_count - 1,
            "left": col > 0,
            "right": col < col_count - 1,
        }
        self.row_count = row_count


def band_combos(row_count):
    return [pair for pair in combos(row_count) if pair[1] is None]


def other_combos(row_count):
    return [pair for pair in combos(row_count) if pair[1] is not None]


def write_strips(place, outs, takes, pairs):
    for out, (rs, cs) in zip(outs, pairs):
        at = 0
        for take, radius, rows, cols in takes:
            row_sets = [slice(0, rows)] * 2
            col_sets = [slice(0, cols)] * 2
            if rs is not None:
                row_sets = [slice(rows - radius, rows), slice(0, radius)]
                if rs == 1:
                    row_sets = row_sets[::-1]
            if cs is not None:
                col_sets = [slice(cols - SIDE, cols), slice(0, SIDE)]
                if cs == 1:
                    col_sets = col_sets[::-1]
            count = row_sets[0].stop - row_sets[0].start
            for i in range(count):
                parts = {}
                for er in (0, 1):
                    for ec in (0, 1):
                        key = (row_sets[er].start + i, col_sets[ec].start, col_sets[ec].stop)
                        if key not in parts:
                            parts[key] = take(*key)
                        parts[er, ec] = parts[key]
                if cs is None:
                    pick = [parts[0, 0], parts[1, 0]]
                else:
                    pick = [jnp.where(place.even_col, parts[e, 0], parts[e, 1]) for e in (0, 1)]
                value = pick[0] if rs is None else jnp.where(place.even_row, pick[0], pick[1])
                out[at + i] = value.astype(out.dtype)
            at += count


def strip_shapes(pairs, rows, cols, channels, radii):
    shapes = []
    for rs, cs in pairs:
        height = sum(rows if rs is None else radius for radius in radii)
        shapes.append((height, cols if cs is None else SIDE, channels))
    return shapes


def received(place, strips, row_sections):
    table = dict(zip(combos(place.row_count), strips))
    full_start, band_start = row_sections

    def along(rs, cs, i):
        return table[rs, cs][(full_start if rs is None else band_start) + i].astype(f32)

    def column(rs, side, i):
        if side is None:
            return along(rs, None, i)
        near, far = (along(rs, 0, i), along(rs, 1, i))
        if side == "left":
            return jnp.where(place.even_col, far, near)
        return jnp.where(place.even_col, near, far)

    def read(vertical, side, i):
        if vertical is None:
            value = column(None, side, i)
        elif place.row_count == 2:
            value = column(0, side, i)
        else:
            near, far = (column(0, side, i), column(1, side, i))
            if vertical == "above":
                value = jnp.where(place.even_row, far, near)
            else:
                value = jnp.where(place.even_row, near, far)
        if vertical is not None:
            value = jnp.where(place.has[vertical], value, 0.0)
        if side is not None:
            value = jnp.where(place.has[side], value, 0.0)
        return value

    return read


def assemble(place, target, own, read, radius, rows, cols, channels):
    width = cols + 2 * SIDE
    target[...] = jnp.zeros(target.shape, f32)
    for vertical, start, count in (("above", 0, radius), (None, radius, rows), ("below", radius + rows, radius)):
        for i in range(count):
            base = (start + i) * width
            middle = own(i) if vertical is None else read(vertical, None, i)
            target[base + SIDE : base + SIDE + cols, 0:channels] = middle
            target[base : base + SIDE, 0:channels] = read(vertical, "left", i)
            target[base + SIDE + cols : base + width, 0:channels] = read(vertical, "right", i)


def spread_taps(kernel_ref, layer, target):
    size, channels = (kernel_ref.shape[0], kernel_ref.shape[3])
    for a in range(size):
        for b in range(size):
            t = a * size + b
            row = pad_lanes(kernel_ref[a, b, layer : layer + 1, :])
            target[t * 16 : t * 16 + 16, :] = jnp.broadcast_to(row, (16, LANES)).astype(bf16)


def tree_sum(terms):
    while len(terms) > 1:
        pairs = [terms[i] + terms[i + 1] for i in range(0, len(terms) - 1, 2)]
        terms = pairs + ([terms[-1]] if len(terms) % 2 else [])
    return terms[0]


def conv_group(src, base, stride, rows_out, taps, size, flipped=False):
    total = [None] * rows_out
    for b in range(size):
        order = [a * size + b for a in range(size)]
        if flipped:
            order = [size * size - 1 - t for t in order]
        weights = [taps[t * 16 : t * 16 + 16, :] for t in order]
        window = []
        for i in range(rows_out + size - 1):
            window.append(src[pl.ds(base + i * stride + b, 16), :].astype(bf16))
            r = i - size + 1
            if r >= 0:
                term = tree_sum([window[r + a] * weights[a] for a in range(size)]).astype(f32)
                total[r] = term if total[r] is None else total[r] + term
    return total


def group_start(g, cols):
    return pl.multiple_of(jnp.minimum(g * 16, cols - 16), 8)


def kernel_sums(src, src_base, src_stride, grad, grad_base, grad_stride, rows, cols, size, sums):
    sums[...] = jnp.zeros(sums.shape, f32)

    def group(g, carry):
        at = pl.multiple_of(g * 16, 16)
        grads = [grad[pl.ds(grad_base + i * grad_stride + at, 16), :].astype(bf16) for i in range(rows)]
        for b in range(size):
            lines = [
                src[pl.ds(src_base + i * src_stride + at + b, 16), :].astype(bf16) for i in range(rows + size - 1)
            ]
            for a in range(size):
                term = tree_sum([lines[r + a] * grads[r] for r in range(rows)]).astype(f32)
                t = (a * size + b) * 8
                sums[t : t + 8, :] += term[0:8] + term[8:16]
        return carry

    lax.fori_loop(0, cols // 16, group, 0)


def diagonal(first, second):
    top = jnp.concatenate([first, jnp.zeros((first.shape[0], second.shape[1]), first.dtype)], axis=1)
    bottom = jnp.concatenate([jnp.zeros((second.shape[0], first.shape[1]), first.dtype), second], axis=1)
    return jnp.concatenate([top, bottom], axis=0)


def by_blocks(function, *arrays, size=16):
    count = arrays[0].shape[0]
    results = [function(*(x[i : i + size] for x in arrays)) for i in range(0, count, size)]
    return tuple(jnp.concatenate(parts, axis=0) for parts in zip(*results))


def in_channels(shape, channels):
    return lax.broadcasted_iota(jnp.int32, shape, 1) < channels


def high_low(x):
    high = x.astype(bf16)
    return (jnp.concatenate([high, (x - high.astype(f32)).astype(bf16)], axis=1),)


def side_by_side(x, y):
    return jnp.concatenate([x, y], axis=1)


def layer_norm(parts, gain, channels, ones):
    def centre(x, total):
        centred = jnp.where(in_channels(x.shape, channels), x - total * (1.0 / channels), 0.0)
        return (centred, (centred * centred).astype(bf16))

    def finish(centred, total):
        inverse = lax.rsqrt(total * (1.0 / channels) + epsilon)
        unit = centred * inverse
        return (unit, inverse, (unit * gain).astype(bf16))

    totals = [dot(by_blocks(high_low, x)[0], jnp.ones((2 * LANES, LANES), bf16)) for x in parts]
    centred, squares = zip(*(by_blocks(centre, x, total) for x, total in zip(parts, totals)))
    variances = dot(side_by_side(*squares), ones)
    return [by_blocks(finish, c, variances[:, k * LANES : (k + 1) * LANES]) for k, c in enumerate(centred)]


def norm_backward(normed_grad, unit, inverse, gain, channels, ones):
    def products(normed_grad, unit):
        m = normed_grad * gain
        return (side_by_side(m.astype(bf16), (m * unit).astype(bf16)),)

    def finish(normed_grad, unit, inverse, sums):
        along = sums[:, :LANES] + unit * sums[:, LANES:]
        grad = inverse * (normed_grad * gain - along * (1.0 / channels))
        return (round16(jnp.where(in_channels(grad.shape, channels), grad, 0.0)),)

    sums = dot(by_blocks(products, normed_grad, unit)[0], ones)
    return by_blocks(finish, normed_grad, unit, inverse, sums)[0]


def gelu_parts(v):
    p = 0.3275911 * inv_sqrt_two
    c1, c2, c3, c4, c5 = (
        0.5 * c / p ** (k + 1)
        for k, c in enumerate((0.254829592, -0.284496736, 1.421413741, -1.453152027, 1.061405429))
    )
    t = pl.reciprocal(jnp.abs(v) + 1.0 / p, approx=True)
    bell = jnp.exp2(v * v * (-0.5 * log2_e))
    tail = ((((c5 * t + c4) * t + c3) * t + c2) * t + c1) * t * bell
    cdf = jnp.where(v >= 0.0, 1.0 - tail, tail)
    return (v * cdf, cdf + v * (bell * inv_sqrt_two_pi))


def dot(x, w):
    return jnp.dot(x, w, preferred_element_type=f32)


def dot_leading(x, y):
    return lax.dot_general(x, y, (((0,), (0,)), ((), ())), preferred_element_type=f32)


def pad_lanes(x):
    rows, channels = x.shape
    return jnp.concatenate([x, jnp.zeros((rows, LANES - channels), x.dtype)], axis=1)


def pieces(total, size):
    return [(start, min(size, total - start)) for start in range(0, total, size)]


def round16(x):
    return x.astype(bf16).astype(f32)


def fetch(sources, targets, sems):
    copies = [pltpu.make_async_copy(a, b, sems.at[i]) for i, (a, b) in enumerate(zip(sources, targets))]
    for copy in copies:
        copy.start()
    for copy in copies:
        copy.wait()


def image_take(ref):
    return lambda i, lo, hi: ref[i].astype(f32)[lo:hi]


def flat_take(ref, cols, channels):
    return lambda i, lo, hi: ref[i * cols + lo : i * cols + hi, 0:channels]


def bands_kernel(dims, image_in, image, *refs):
    outs, sems = (refs[:-1], refs[-1])
    place = Place(dims.row_count, dims.col_count)
    fetch((image_in,), (image,), sems)
    takes = [(image_take(image), 2 * dims.h, dims.rows, dims.cols)]
    write_strips(place, outs, takes, band_combos(dims.row_count))


def others_kernel(dims, image, *refs):
    outs = refs[len(band_combos(dims.row_count)) :]
    place = Place(dims.row_count, dims.col_count)
    takes = [(image_take(image), 2 * dims.h, dims.rows, dims.cols)]
    write_strips(place, outs, takes, other_combos(dims.row_count))


def grad_others_kernel(dims, grad1, cot, *refs):
    outs = refs[len(band_combos(dims.row_count)) :]
    place = Place(dims.row_count, dims.col_count)
    takes = [
        (flat_take(grad1, dims.cols, dims.channels), 2 * dims.h, dims.rows, dims.cols),
        (image_take(cot), dims.h, dims.rows, dims.cols),
    ]
    write_strips(place, outs, takes, other_combos(dims.row_count))


def weights_kernel(up_in, down_t_in, kernels_in, gains_in, *refs):
    forward0, back0, forward1, back1, grad_in0, grad_out0, taps0, taps1, gains, up_w, down_w, kernels, sems = refs
    fetch((up_in, down_t_in, kernels_in, gains_in), (up_w, down_w, kernels, gains), sems)
    spread_taps(kernels, 0, taps0)
    spread_taps(kernels, 1, taps1)
    channels, units = up_w.shape[1:]
    blank = jnp.zeros((LANES - channels, units), f32)
    wide, tall = ([], [])
    for layer in range(2):
        for ref in (up_w, down_w):
            full = jnp.concatenate([ref[layer].astype(f32), blank], axis=0)
            wide.append(full.astype(bf16))
            tall.append(full.T.astype(bf16))
    (up0, down_t0, up1, down_t1), (up_t0, down0, up_t1, down1) = (wide, tall)
    forward0[...] = diagonal(up0, up0)
    back0[...] = diagonal(down0, down0)
    forward1[...] = diagonal(up1, down_t1)
    back1[...] = diagonal(down1, up_t1)
    grad_in0[...] = diagonal(down_t0, down_t0)
    grad_out0[...] = diagonal(up_t0, up_t0)


def first_kernel(dims, *refs):
    count = len(combos(dims.row_count))
    image, cot, taps0, taps1, gains, forward0, back0, forward1, back1 = refs[:9]
    strips = refs[9 : 9 + count]
    refs = refs[9 + count :]
    (output, x0, x1, unit0, inv0, hidden0, slope0, grad1, normed1, pre_grad1, hidden1, gain_sum) = refs[:12]
    outs, conv = (refs[12:-1], refs[-1])
    place = Place(dims.row_count, dims.col_count)
    rows, cols, channels, h, size = (dims.rows, dims.cols, dims.channels, dims.h, dims.size)
    ext_rows, ext_cols, wide = (dims.ext_rows, dims.ext_cols, dims.wide)
    skip = dims.skipped_rows(place)
    read = received(place, strips, (0, 0))
    assemble(place, x0, lambda i: image[i].astype(f32), read, 2 * h, rows, cols, channels)

    x1[...] = jnp.zeros(x1.shape, f32)
    if dims.ext_pad > ext_rows * ext_cols:
        conv[ext_rows * ext_cols :, :] = jnp.zeros((dims.ext_pad - ext_rows * ext_cols, LANES), f32)
    frame = pl.multiple_of(skip * ext_cols, 8)

    def conv0(g, carry):
        at = group_start(g, ext_cols)
        base = pl.multiple_of(skip * wide, 8) + at
        total = conv_group(x0, base + 1, wide, ext_rows, taps0, size)
        for r in range(ext_rows):
            conv[pl.ds(r * ext_cols + at, 16), :] = total[r]
            x1[pl.ds(frame + r * ext_cols + at, 16), :] = x0[pl.ds(base + (r + h) * wide + 4, 16), :]
        return carry

    lax.fori_loop(0, -(-ext_cols // 16), conv0, 0)
    gain = pad_lanes(gains[0:1, :])
    ones = diagonal(jnp.ones((LANES, LANES), bf16), jnp.ones((LANES, LANES), bf16))
    half = dims.ext_pad // 2
    for start, n in pieces(half, dims.piece):
        spans = [(start, n), (half + start, n)]
        parts = layer_norm([conv[at : at + n, :] for at, n in spans], gain, channels, ones)
        pres = dot(side_by_side(parts[0][2], parts[1][2]), forward0[...])
        count = pres.shape[1] // 2
        hiddens = []
        for k, ((at, n), (unit, inverse, _)) in enumerate(zip(spans, parts)):
            unit0[at : at + n, :] = unit.astype(bf16)
            inv0[at : at + n, :] = inverse

            def activate(pre):
                value, slope = gelu_parts(pre)
                return (value.astype(bf16), slope.astype(bf16))

            hidden, slope = by_blocks(activate, pres[:, k * count : (k + 1) * count])
            hidden0[at : at + n, :] = hidden
            slope0[at : at + n, :] = slope
            hiddens.append(hidden)
        branches = dot(side_by_side(*hiddens), back0[...])
        for k, (at, n) in enumerate(spans):
            px = pl.ds(frame + at, n)
            x1[px, :] = round16(x1[px, :] + branches[:, k * LANES : (k + 1) * LANES])
    clear_outside(place, x1, dims)

    def conv1(g, carry):
        at = group_start(g, cols)
        total = conv_group(x1, at + 1, ext_cols, rows, taps1, size)
        for r in range(rows):
            conv[pl.ds(r * cols + at, 16), :] = total[r]
        return carry

    lax.fori_loop(0, -(-cols // 16), conv1, 0)
    gain1 = pad_lanes(gains[1:2, :])
    gain_sum[...] = jnp.zeros(gain_sum.shape, f32)
    lines = dims.line_step
    step = lines * cols
    for k in range(rows // lines):
        px = slice(k * step, (k + 1) * step)
        middle = k * step + step // 2
        parts = layer_norm(
            [conv[k * step : middle, :], conv[middle : (k + 1) * step, :]], gain1, channels, ones
        )
        unit, inverse, normed = (jnp.concatenate(pair, axis=0) for pair in zip(*parts))
        normed1[px, :] = normed
        upstream = pad_lanes(cot[k * lines : (k + 1) * lines].reshape(step, channels))
        both = dot(side_by_side(normed, upstream), forward1[...])

        def activate(pre, hidden_grad):
            value, slope = gelu_parts(pre)
            return (value.astype(bf16), (hidden_grad * slope).astype(bf16))

        count = both.shape[1] // 2
        hidden, pre_grad = by_blocks(activate, both[:, :count], both[:, count:])
        hidden1[px, :] = hidden
        pre_grad1[px, :] = pre_grad
        both = dot(side_by_side(hidden, pre_grad), back1[...])
        branch, normed_grad = (both[:, :LANES], both[:, LANES:])
        for i in range(lines):
            start = (k * lines + i + h) * ext_cols + 4
            line = x1[start : start + cols, :] + branch[i * cols : (i + 1) * cols]
            output[k * lines + i] = line[:, :channels].astype(bf16)
        product = normed_grad * unit
        gain_sum[...] += jnp.sum(product.reshape(step // 8, 8, LANES), axis=0)
        grad1[px, :] = norm_backward(normed_grad, unit, inverse, gain1, channels, ones)

    takes = [(flat_take(grad1, cols, channels), 2 * h, rows, cols), (image_take(cot), h, rows, cols)]
    write_strips(place, outs, takes, band_combos(dims.row_count))


def clear_outside(place, flat, dims):
    h, frame_rows, ext_cols = (dims.h, dims.rows + 2 * dims.h, dims.ext_cols)
    margin = (ext_cols - dims.cols) // 2

    @pl.when(jnp.logical_not(place.has["above"]))
    def _():
        flat[0 : h * ext_cols, :] = jnp.zeros((h * ext_cols, LANES), f32)

    @pl.when(jnp.logical_not(place.has["below"]))
    def _():
        last = (frame_rows - h) * ext_cols
        flat[last:, :] = jnp.zeros((flat.shape[0] - last, LANES), f32)

    @pl.when(jnp.logical_not(place.has["left"]))
    def _():
        for r in range(frame_rows):
            flat[r * ext_cols : r * ext_cols + margin, :] = jnp.zeros((margin, LANES), f32)

    @pl.when(jnp.logical_not(place.has["right"]))
    def _():
        for r in range(frame_rows):
            flat[(r + 1) * ext_cols - margin : (r + 1) * ext_cols, :] = jnp.zeros((margin, LANES), f32)


def sums_kernel(
    dims, x1, grad1, normed1, pre_grad1, hidden1, cot, gain_part, final, taps_sum, up_sum, down_sum, output, sums
):
    output[...] = final[...]
    kernel_sums(x1, 1, dims.ext_cols, grad1, 0, dims.cols, dims.rows, dims.cols, dims.size, sums)
    store_sums(dims, sums, gain_part[...], taps_sum)
    upstream = pad_lanes(cot[...].reshape(dims.rows * dims.cols, dims.channels))
    up_sum[...] = dot_leading(normed1[...], pre_grad1[...]).T
    down_sum[...] = dot_leading(upstream, hidden1[...]).T


def store_sums(dims, sums, gain_part, target):
    taps = dims.size * dims.size
    target[...] = jnp.zeros(target.shape, f32)
    for t in range(taps):
        target[t : t + 1, :] = jnp.sum(sums[t * 8 : t * 8 + 8, :], axis=0, keepdims=True)
    target[taps : taps + 1, :] = jnp.sum(gain_part, axis=0, keepdims=True)


def third_kernel(dims, *refs):
    count = len(combos(dims.row_count))
    (grad1, cot, taps1, gains, grad_in0, grad_out0, x0, unit0, inv0, hidden0, slope0) = refs[:11]
    (taps_sum1, up_sum1, down_sum1) = refs[11:14]
    strips = refs[14 : 14 + count]
    (grad0, middle, keep, small_keep, send) = refs[14 + count : 19 + count]
    (wide_grad, cot_frame, upstream, own, sums, normed0, flow0, pre_grad0, gain_sum, small, tall, slabs) = refs[19 + count :]
    place = Place(dims.row_count, dims.col_count)
    rows, cols, channels, h, size = (dims.rows, dims.cols, dims.channels, dims.h, dims.size)
    ext_rows, ext_cols, wide = (dims.ext_rows, dims.ext_cols, dims.wide)
    skip = dims.skipped_rows(place)
    read = received(place, strips, (0, 0))
    assemble(
        place, wide_grad, lambda i: grad1[i * cols : (i + 1) * cols, 0:channels], read, 2 * h, rows, cols, channels
    )
    read_cot = received(place, strips, (rows, 2 * h))
    margin = (ext_cols - cols) // 2
    cot_frame[...] = jnp.zeros(cot_frame.shape, f32)
    for vertical, start, n in (("above", 0, h), (None, h, rows), ("below", h + rows, h)):
        for i in range(n):
            base = (start + i) * ext_cols
            line = cot[i].astype(f32) if vertical is None else read_cot(vertical, None, i)
            cot_frame[base + margin : base + margin + cols, 0:channels] = line
            cot_frame[base : base + margin, 0:channels] = read_cot(vertical, "left", i)[SIDE - margin :]
            cot_frame[base + margin + cols : base + ext_cols, 0:channels] = read_cot(vertical, "right", i)[:margin]

    used = ext_rows * ext_cols
    if dims.ext_pad > used:
        upstream[used:, :] = jnp.zeros((dims.ext_pad - used, LANES), f32)
        own[used:, :] = jnp.zeros((dims.ext_pad - used, LANES), f32)
    grad0[...] = jnp.zeros(grad0.shape, f32)
    frame = pl.multiple_of(skip * ext_cols, 8)

    def conv1(g, carry):
        at = group_start(g, ext_cols)
        total = conv_group(wide_grad, pl.multiple_of(skip * wide, 8) + at + 1, wide, ext_rows, taps1, size, True)
        col = lax.broadcasted_iota(jnp.int32, (16, LANES), 0) + (at - margin)
        inside = jnp.where(jnp.logical_and(col >= 0, col < cols), 1.0, 0.0)
        for r in range(ext_rows):
            px = pl.ds(r * ext_cols + at, 16)
            upstream[px, :] = cot_frame[pl.ds(frame + r * ext_cols + at, 16), :] + total[r]
            mine = jnp.logical_and(r + skip >= h, r + skip < h + rows)
            own[px, :] = jnp.where(mine, inside, 0.0)
        return carry

    lax.fori_loop(0, -(-ext_cols // 16), conv1, 0)
    for i in range(rows):
        line = upstream[pl.ds((i + h - skip) * ext_cols + margin, cols), :]
        middle[i * cols : (i + 1) * cols, :] = round16(line)

    gain = pad_lanes(gains[0:1, :])
    gain_sum[...] = jnp.zeros(gain_sum.shape, f32)
    ones = diagonal(jnp.ones((LANES, LANES), bf16), jnp.ones((LANES, LANES), bf16))
    half_px = dims.ext_pad // 2
    for start, n in pieces(half_px, dims.piece):
        spans = [(start, n), (half_px + start, n)]
        flows = [upstream[at : at + n, :].astype(bf16) for at, n in spans]
        hidden_grads = dot(side_by_side(*flows), grad_in0[...])
        count = hidden_grads.shape[1] // 2

        def slope_times(grad, slope):
            return ((grad * slope.astype(f32)).astype(bf16),)

        pre_grads = [
            by_blocks(slope_times, hidden_grads[:, k * count : (k + 1) * count], slope0[at : at + n, :])[0]
            for k, (at, n) in enumerate(spans)
        ]
        both = dot(side_by_side(*pre_grads), grad_out0[...])
        normed_grads = (both[:, :LANES], both[:, LANES:])
        for (at, n), flow, pre_grad, normed_grad in zip(spans, flows, pre_grads, normed_grads):
            mine = own[at : at + n, :]
            unit = unit0[at : at + n, :].astype(f32)
            normed0[at : at + n, :] = (unit * gain * mine).astype(bf16)
            flow0[at : at + n, :] = flow * mine.astype(bf16)
            pre_grad0[at : at + n, :] = pre_grad
            product = normed_grad * unit * mine
            gain_sum[...] += jnp.sum(product.reshape(n // 8, 8, LANES), axis=0)
            grad = norm_backward(normed_grad, unit, inv0[at : at + n, :], gain, channels, ones)
            grad0[pl.ds(frame + at, n), :] = grad
    clear_outside(place, grad0, dims)
    kernel_sums(
        x0, h * wide + SIDE - h, wide, grad0, h * ext_cols + margin, ext_cols, rows, cols, size, sums
    )
    store_sums(dims, sums, gain_sum[...], small)

    taps_rows = size * size + 1
    merged = jnp.concatenate([small[0:taps_rows, :], taps_sum1[0:taps_rows, :]], axis=0) * dims.factor
    merged = fold_rows(merged, dims.small_rows, channels).astype(bf16)
    small_keep[...] = merged.astype(f32)

    layer_rows, part, half = (dims.layer_rows, dims.part, dims.half)
    units = hidden0.shape[1]
    up0 = dot_leading(normed0[...], pre_grad0[...]).T * dims.factor
    down0 = dot_leading(flow0[...], hidden0[...]).T * dims.factor
    up1 = up_sum1[...] * dims.factor
    down1 = down_sum1[...] * dims.factor
    lane = lax.broadcasted_iota(jnp.int32, (units, LANES), 1)
    slab_rows = 2 * layer_rows
    for r in range(dims.row_count):
        for layer, (u, d) in enumerate(((up0, down0), (up1, down1))):
            first = pltpu.roll(u, LANES - r * half, 1) if r else u
            shift = (half - r * half) % LANES
            second = pltpu.roll(d, shift, 1) if shift else d
            joined = jnp.where(lane < half, first, jnp.where(lane < 2 * half, second, 0.0))
            tall[layer * (units + 8) : layer * (units + 8) + units, :] = joined

        for c in range(dims.col_count):
            index = 0
            for axis, bit in dims.stages:
                index = 2 * index + ((r if axis == "row" else c) >> bit & 1)
            for layer in range(2):
                to, at = (index * slab_rows + layer * layer_rows, layer * (units + 8) + c * part)
                slabs[to : to + layer_rows, :] = tall[at : at + layer_rows, :]

    split(dims, 0, slabs, merged, keep, (send,))


def fold_rows(x, rows, used):
    n = x.shape[0]
    if rows >= n:
        return pad_rows(x, rows)
    assert used <= 96
    stride = ceil8(n - rows)
    rest = pad_rows(x[rows:], stride)
    pieces_of = pad_rows(jnp.concatenate([pltpu.roll(rest, 96 - 32 * k, 1) for k in range(3)], axis=0), rows)
    lane = lax.broadcasted_iota(jnp.int32, (rows, LANES), 1)
    return jnp.where(lane < 96, x[:rows], pieces_of)


def pad_rows(x, rows):
    if rows == x.shape[0]:
        return x
    return jnp.concatenate([x, jnp.zeros((rows - x.shape[0], LANES), x.dtype)], axis=0)


def unfold_rows(x, n):
    rows = x.shape[0]
    if rows >= n:
        return x[:n]
    stride = ceil8(n - rows)
    lane = lax.broadcasted_iota(jnp.int32, (stride, LANES), 1)
    rest = jnp.zeros((stride, LANES), x.dtype)
    for k in range(3):
        moved = pltpu.roll(x[k * stride : (k + 1) * stride], 32 + 32 * k, 1)
        rest = jnp.where(jnp.logical_and(lane >= 32 * k, lane < 32 * k + 32), moved, rest)
    return jnp.concatenate([x, rest[: n - rows]], axis=0)


def split(dims, stage, slabs, merged, keep, sends):
    group = dims.groups[stage]
    count = slabs.shape[0] >> len(group)
    mine = 0
    for axis, bit in group:
        mine = mine * 2 + lax.rem(lax.div(lax.axis_index(axis), 1 << bit), 2)
    keep[...] = slabs[pl.ds(pl.multiple_of(mine * count, 16), count), :]
    for mask, send in enumerate(sends, 1):
        other = 0
        for j in range(len(group)):
            weight = 1 << j
            digit = lax.rem(lax.div(mine, weight), 2)
            other = other + weight * (1 - digit if mask & weight else digit)
        send[0:count, :] = slabs[pl.ds(pl.multiple_of(other * count, 16), count), :].astype(bf16)
        send[count:, :] = merged


def gather_up(keep, small, gots):
    count = keep.shape[0]
    slabs = [keep[...]] + [got[0:count, :].astype(f32) for got in gots]
    sums = [small[...]] + [got[count:, :].astype(f32) for got in gots]
    if len(gots) == 1:
        return (slabs[0] + slabs[1], sums[0] + sums[1])
    return tuple((x[0] + x[1]) + (x[2] + x[3]) for x in (slabs, sums))


def stage_kernel(dims, stage, keep, small, *refs):
    before, after = (len_sends(dims.groups[stage - 1]), len_sends(dims.groups[stage]))
    gots = refs[:before]
    keep_out, small_out = refs[-3 - after : -1 - after]
    sends, total = (refs[-1 - after : -1], refs[-1])
    slabs, merged = gather_up(keep, small, gots)
    total[...] = slabs
    merged = merged.astype(bf16)
    small_out[...] = merged.astype(f32)
    split(dims, stage, total, merged, keep_out, sends)


def len_sends(group):
    return (1 << len(group)) - 1


def last_kernel(dims, keep, small, *refs):
    gots, (kernel_out, gain_out, up_out, down_out) = (refs[:-4], refs[-4:])
    total, merged = gather_up(keep, small, gots)
    merged = unfold_rows(merged, 2 * (dims.size * dims.size + 1))
    size, channels, half, part = (dims.size, dims.channels, dims.half, dims.part)
    for layer in range(2):
        block = total[layer * dims.layer_rows : layer * dims.layer_rows + part]
        up_out[layer] = block[:, :half]
        down_out[layer] = block[:, half : 2 * half]
        for t in range(size * size + 1):
            at = layer * (size * size + 1) + t
            row = merged[at : at + 1, 0:channels]
            if t < size * size:
                kernel_out[t // size, t % size, layer : layer + 1, :] = row
            else:
                gain_out[layer : layer + 1, :] = row


def image_kernel(dims, grad0, middle, taps0, after, out, ready, work):
    rows, cols, size = (dims.rows, dims.cols, dims.size)

    def conv0(g, carry):
        at = group_start(g, cols)
        total = conv_group(grad0, at + 1, dims.ext_cols, rows, taps0, size, True)
        for r in range(rows):
            work[pl.ds(r * cols + at, 16), :] = middle[pl.ds(r * cols + at, 16), :] + total[r]
        return carry

    lax.fori_loop(0, -(-cols // 16), conv0, 0)
    for r in range(rows):
        out[r] = work[r * cols : (r + 1) * cols, 0 : dims.channels].astype(bf16)
    ready[...] = jnp.zeros(ready.shape, f32)


class Dims:
    def skipped_rows(self, place):
        if self.row_count > 2:
            return 0
        return jnp.where(place.has["above"], 0, self.h)


def dims_of(image, kernels, up_weights):
    d = Dims()
    d.row_count, d.col_count = (lax.axis_size("row"), lax.axis_size("col"))
    d.rows, d.cols, d.channels = image.shape
    d.size = kernels.shape[1]
    d.h = d.size // 2
    d.ext_rows, d.ext_cols = (d.rows + (d.h if d.row_count == 2 else 2 * d.h), d.cols + 8)
    d.wide = d.cols + 2 * SIDE
    d.ext_pad = -(-d.ext_rows * d.ext_cols // 32) * 32
    d.piece = 176
    d.line_step = 4
    d.half = d.channels // d.row_count
    d.part = up_weights.shape[2] // d.col_count
    d.layer_rows = ceil8(d.part)
    d.count = d.row_count * d.col_count
    d.small_rows = 80 if d.size == 7 and d.channels <= 96 else -(-2 * (d.size * d.size + 1) // 16) * 16
    d.factor = 1.0 / math.sqrt(d.rows * d.cols * d.count)
    row_bits, col_bits = (d.row_count.bit_length() - 1, d.col_count.bit_length() - 1)
    bits = [("row", b) for b in range(row_bits)] + [("col", b) for b in range(1, col_bits)]
    d.groups = [[("col", 0)]] + [bits[i : i + 2] for i in range(0, len(bits), 2)]
    d.stages = [bit for group in d.groups for bit in group]
    return d


def swap_by(d, group, mask):
    flip = {"row": 0, "col": 0}
    for j, (axis, bit) in enumerate(group):
        if mask >> (len(group) - 1 - j) & 1:
            flip[axis] |= 1 << bit
    pairs = []
    for r in range(d.row_count):
        for c in range(d.col_count):
            pairs.append((r * d.col_count + c, (r ^ flip["row"]) * d.col_count + (c ^ flip["col"])))
    return pairs


def run(kernel, outs, scratch, *args, in_hbm=0, sems=0, busy_us=1):
    shapes = [jax.ShapeDtypeStruct(shape, kind) for shape, kind in outs]
    space = pl.BlockSpec(memory_space=pltpu.VMEM)
    far = pl.BlockSpec(memory_space=pltpu.HBM)
    held = [pltpu.VMEM(shape, kind) for shape, kind in scratch]
    if sems:
        held.append(pltpu.SemaphoreType.DMA((sems,)))
    return pl.pallas_call(
        kernel,
        out_shape=shapes,
        in_specs=[far] * in_hbm + [space] * (len(args) - in_hbm),
        out_specs=[space] * len(shapes),
        scratch_shapes=held,
        compiler_params=pltpu.CompilerParams(vmem_limit_bytes=32 * 1024 * 1024),
        cost_estimate=pl.CostEstimate(flops=int(busy_us * 1e9), bytes_accessed=1 << 18, transcendentals=0),
    )(*args)


def per_device(image, kernels, gains, up_weights, down_weights, cotangent):
    d = dims_of(image, kernels, up_weights)
    bind = functools.partial
    rows, cols, channels = image.shape
    units = up_weights.shape[2]
    tile, ext, wide = (rows * cols, d.ext_pad, (rows + 4 * d.h) * d.wide)
    frame = (rows + 2 * d.h) * d.ext_cols + 16
    taps = ((d.size * d.size * 16, LANES), bf16)
    tap_sums = ((d.size * d.size * 8, LANES), f32)
    sums_rows = ceil8(d.size * d.size + 1)

    bands, others = (band_combos(d.row_count), other_combos(d.row_count))

    def strips_of(pairs, radii):
        return [(shape, bf16) for shape in strip_shapes(pairs, rows, cols, channels, radii)]

    image, *band_strips = run(
        bind(bands_kernel, d), [(image.shape, bf16)] + strips_of(bands, (2 * d.h,)), [], image, in_hbm=1, sems=1
    )
    other_strips = run(bind(others_kernel, d), strips_of(others, (2 * d.h,)), [], image, *band_strips)
    strips = exchange(band_strips, other_strips, d.row_count, d.col_count)
    mixing = [((2 * LANES, 2 * units), bf16), ((2 * units, 2 * LANES), bf16)]
    forward0, back0, forward1, back1, grad_in0, grad_out0, taps0, taps1, gains = run(
        weights_kernel,
        mixing * 3 + [taps, taps, (gains.shape, f32)],
        [((2, channels, units), bf16), ((2, channels, units), bf16), ((d.size, d.size, 2, channels), f32)],
        up_weights,
        jnp.swapaxes(down_weights, 1, 2),
        jnp.transpose(kernels, (1, 2, 0, 3)),
        gains,
        in_hbm=4,
        sems=4,
        busy_us=2,
    )

    first = run(
        bind(first_kernel, d),
        [
            (image.shape, bf16),
            ((wide, LANES), f32),
            ((frame, LANES), f32),
            ((ext, LANES), bf16),
            ((ext, LANES), f32),
            ((ext, units), bf16),
            ((ext, units), bf16),
            ((tile, LANES), f32),
            ((tile, LANES), bf16),
            ((tile, units), bf16),
            ((tile, units), bf16),
            ((8, LANES), f32),
        ]
        + strips_of(bands, (2 * d.h, d.h)),
        [((ext, LANES), f32)],
        image,
        cotangent,
        taps0,
        taps1,
        gains,
        forward0,
        back0,
        forward1,
        back1,
        *strips,
        busy_us=15,
    )
    (final, x0, x1, unit0, inv0, hidden0, slope0, grad1, normed1, pre_grad1, hidden1, gain_part) = first[:12]
    band_strips = first[12:]
    other_strips = run(
        bind(grad_others_kernel, d), strips_of(others, (2 * d.h, d.h)), [], grad1, cotangent, *band_strips
    )
    strips = exchange(band_strips, other_strips, d.row_count, d.col_count)

    taps_sum1, up_sum1, down_sum1, output = run(
        bind(sums_kernel, d),
        [((sums_rows, LANES), f32), ((units, LANES), f32), ((units, LANES), f32), (image.shape, bf16)],
        [tap_sums],
        x1,
        grad1,
        normed1,
        pre_grad1,
        hidden1,
        cotangent,
        gain_part,
        final,
        busy_us=3,
    )

    held = d.count // 2 * 2 * d.layer_rows
    small = ((d.small_rows, LANES), f32)
    grad0, middle, keep, sums, send = run(
        bind(third_kernel, d),
        [((frame, LANES), f32), ((tile, LANES), f32), ((held, LANES), f32), small, ((held + d.small_rows, LANES), bf16)],
        [
            ((wide, LANES), f32),
            ((frame, LANES), f32),
            ((ext, LANES), f32),
            ((ext, LANES), f32),
            tap_sums,
            ((ext, LANES), bf16),
            ((ext, LANES), bf16),
            ((ext, units), bf16),
            ((8, LANES), f32),
            ((sums_rows, LANES), f32),
            ((2 * (units + 8), LANES), f32),
            ((2 * held, LANES), f32),
        ],
        grad1,
        cotangent,
        taps1,
        gains,
        grad_in0,
        grad_out0,
        x0,
        unit0,
        inv0,
        hidden0,
        slope0,
        taps_sum1,
        up_sum1,
        down_sum1,
        *strips,
        busy_us=12,
    )
    axes = ("row", "col")
    sends = [send]
    for stage, group in enumerate(d.groups):
        gots = [lax.ppermute(x, axes, swap_by(d, group, mask)) for mask, x in enumerate(sends, 1)]
        ready = []
        if stage == 1:
            gradient, *ready = run(
                bind(image_kernel, d),
                [(image.shape, bf16), ((8, LANES), f32)],
                [((tile, LANES), f32)],
                grad0,
                middle,
                taps0,
                sums,
                busy_us=3,
            )
        if stage + 1 < len(d.groups):
            after = d.groups[stage + 1]
            whole, held = (held, held >> len(after))
            keep, sums, *sends = run(
                bind(stage_kernel, d, stage + 1),
                [((held, LANES), f32), small] + [((held + d.small_rows, LANES), bf16)] * len_sends(after),
                [((whole, LANES), f32)],
                keep,
                sums,
                *gots,
                *ready,
            )
    kernel_out, gain_out, up_out, down_out = run(
        bind(last_kernel, d),
        [
            ((d.size, d.size, 2, channels), f32),
            (gains.shape, f32),
            ((2, d.part, d.half), f32),
            ((2, d.part, d.half), f32),
        ],
        [],
        keep,
        sums,
        *gots,
    )
    kernel_out = jnp.transpose(kernel_out, (2, 0, 1, 3))
    return (output, gradient, kernel_out, gain_out, jnp.swapaxes(up_out, 1, 2), down_out)


def solution(mesh):
    placed = (P("row", "col", None), P(), P(), P(), P(), P("row", "col", None))
    return jax.shard_map(
        per_device,
        mesh=mesh,
        in_specs=placed,
        out_specs=(
            P("row", "col", None),
            P("row", "col", None),
            P(),
            P(),
            P(None, "row", "col"),
            P(None, "col", "row"),
        ),
        check_vma=False,
    )
```

```python
import functools
import math

import jax
import jax.numpy as jnp
from jax import lax
from jax.experimental import pallas as pl
from jax.experimental.pallas import tpu as pltpu
from jax.sharding import PartitionSpec as P

epsilon = 1e-06
inv_sqrt_two = 0.7071067811865476
inv_sqrt_two_pi = 0.3989422804014327
log2_e = 1.4426950408889634
LANES = 128
SIDE = 8
f32, bf16 = (jnp.float32, jnp.bfloat16)


def ceil8(n):
    return -(-n // 8) * 8


def combos(row_count):
    listed = [(None, 0), (None, 1), (0, None), (0, 0), (0, 1)]
    if row_count > 2:
        listed += [(1, None), (1, 0), (1, 1)]
    return listed


def partner(index, start, count):
    if start is None:
        return index
    other = index + 1 if (index - start) % 2 == 0 else index - 1
    return other if 0 <= other < count else None


def swap_pairs(row_count, col_count, row_start, col_start):
    pairs = []
    for r in range(row_count):
        for c in range(col_count):
            pr, pc = (partner(r, row_start, row_count), partner(c, col_start, col_count))
            if pr is None:
                pr, pc = (r, c ^ 1)
            elif pc is None:
                pr, pc = (r ^ 1 if row_start is None else pr, c)
            pairs.append((r * col_count + c, pr * col_count + pc))
    return pairs


def exchange(bands, others, row_count, col_count):
    got = {}
    for strips, pairs in ((bands, band_combos(row_count)), (others, other_combos(row_count))):
        for strip, (rs, cs) in zip(strips, pairs):
            got[rs, cs] = lax.ppermute(strip, ("row", "col"), swap_pairs(row_count, col_count, rs, cs))
    return [got[pair] for pair in combos(row_count)]


class Place:
    def __init__(self, row_count, col_count):
        row, col = (lax.axis_index("row"), lax.axis_index("col"))
        self.even_row, self.even_col = (lax.rem(row, 2) == 0, lax.rem(col, 2) == 0)
        self.has = {
            "above": row > 0,
            "below": row < row_count - 1,
            "left": col > 0,
            "right": col < col_count - 1,
        }
        self.row_count = row_count


def band_combos(row_count):
    return [pair for pair in combos(row_count) if pair[1] is None]


def other_combos(row_count):
    return [pair for pair in combos(row_count) if pair[1] is not None]


def write_strips(place, outs, takes, pairs):
    for out, (rs, cs) in zip(outs, pairs):
        at = 0
        for take, radius, rows, cols in takes:
            row_sets = [slice(0, rows)] * 2
            col_sets = [slice(0, cols)] * 2
            if rs is not None:
                row_sets = [slice(rows - radius, rows), slice(0, radius)]
                if rs == 1:
                    row_sets = row_sets[::-1]
            if cs is not None:
                col_sets = [slice(cols - SIDE, cols), slice(0, SIDE)]
                if cs == 1:
                    col_sets = col_sets[::-1]
            count = row_sets[0].stop - row_sets[0].start
            for i in range(count):
                parts = {}
                for er in (0, 1):
                    for ec in (0, 1):
                        key = (row_sets[er].start + i, col_sets[ec].start, col_sets[ec].stop)
                        if key not in parts:
                            parts[key] = take(*key)
                        parts[er, ec] = parts[key]
                if cs is None:
                    pick = [parts[0, 0], parts[1, 0]]
                else:
                    pick = [jnp.where(place.even_col, parts[e, 0], parts[e, 1]) for e in (0, 1)]
                value = pick[0] if rs is None else jnp.where(place.even_row, pick[0], pick[1])
                out[at + i] = value.astype(out.dtype)
            at += count


def strip_shapes(pairs, rows, cols, channels, radii):
    shapes = []
    for rs, cs in pairs:
        height = sum(rows if rs is None else radius for radius in radii)
        shapes.append((height, cols if cs is None else SIDE, channels))
    return shapes


def received(place, strips, row_sections):
    table = dict(zip(combos(place.row_count), strips))
    full_start, band_start = row_sections

    def along(rs, cs, i):
        return table[rs, cs][(full_start if rs is None else band_start) + i].astype(f32)

    def column(rs, side, i):
        if side is None:
            return along(rs, None, i)
        near, far = (along(rs, 0, i), along(rs, 1, i))
        if side == "left":
            return jnp.where(place.even_col, far, near)
        return jnp.where(place.even_col, near, far)

    def read(vertical, side, i):
        if vertical is None:
            value = column(None, side, i)
        elif place.row_count == 2:
            value = column(0, side, i)
        else:
            near, far = (column(0, side, i), column(1, side, i))
            if vertical == "above":
                value = jnp.where(place.even_row, far, near)
            else:
                value = jnp.where(place.even_row, near, far)
        if vertical is not None:
            value = jnp.where(place.has[vertical], value, 0.0)
        if side is not None:
            value = jnp.where(place.has[side], value, 0.0)
        return value

    return read


def assemble(place, target, own, read, radius, rows, cols, channels):
    width = cols + 2 * SIDE
    target[...] = jnp.zeros(target.shape, f32)
    for vertical, start, count in (("above", 0, radius), (None, radius, rows), ("below", radius + rows, radius)):
        for i in range(count):
            base = (start + i) * width
            middle = own(i) if vertical is None else read(vertical, None, i)
            target[base + SIDE : base + SIDE + cols, 0:channels] = middle
            target[base : base + SIDE, 0:channels] = read(vertical, "left", i)
            target[base + SIDE + cols : base + width, 0:channels] = read(vertical, "right", i)


def spread_taps(kernel_ref, layer, target):
    size, channels = (kernel_ref.shape[0], kernel_ref.shape[3])
    for a in range(size):
        for b in range(size):
            t = a * size + b
            row = pad_lanes(kernel_ref[a, b, layer : layer + 1, :])
            target[t * 16 : t * 16 + 16, :] = jnp.broadcast_to(row, (16, LANES)).astype(bf16)


def tree_sum(terms):
    while len(terms) > 1:
        pairs = [terms[i] + terms[i + 1] for i in range(0, len(terms) - 1, 2)]
        terms = pairs + ([terms[-1]] if len(terms) % 2 else [])
    return terms[0]


def conv_group(src, base, stride, rows_out, taps, size, flipped=False):
    total = [None] * rows_out
    for b in range(size):
        order = [a * size + b for a in range(size)]
        if flipped:
            order = [size * size - 1 - t for t in order]
        weights = [taps[t * 16 : t * 16 + 16, :] for t in order]
        window = []
        for i in range(rows_out + size - 1):
            window.append(src[pl.ds(base + i * stride + b, 16), :].astype(bf16))
            r = i - size + 1
            if r >= 0:
                term = tree_sum([window[r + a] * weights[a] for a in range(size)]).astype(f32)
                total[r] = term if total[r] is None else total[r] + term
    return total


def group_start(g, cols):
    return pl.multiple_of(jnp.minimum(g * 16, cols - 16), 8)


def kernel_sums(src, src_base, src_stride, grad, grad_base, grad_stride, rows, cols, size, sums):
    sums[...] = jnp.zeros(sums.shape, f32)

    def group(g, carry):
        at = pl.multiple_of(g * 16, 16)
        grads = [grad[pl.ds(grad_base + i * grad_stride + at, 16), :].astype(bf16) for i in range(rows)]
        for b in range(size):
            lines = [
                src[pl.ds(src_base + i * src_stride + at + b, 16), :].astype(bf16) for i in range(rows + size - 1)
            ]
            for a in range(size):
                term = tree_sum([lines[r + a] * grads[r] for r in range(rows)]).astype(f32)
                t = (a * size + b) * 8
                sums[t : t + 8, :] += term[0:8] + term[8:16]
        return carry

    lax.fori_loop(0, cols // 16, group, 0)


def diagonal(first, second):
    top = jnp.concatenate([first, jnp.zeros((first.shape[0], second.shape[1]), first.dtype)], axis=1)
    bottom = jnp.concatenate([jnp.zeros((second.shape[0], first.shape[1]), first.dtype), second], axis=1)
    return jnp.concatenate([top, bottom], axis=0)


def together(steps):
    steps = list(steps)
    while steps:
        steps = [step for step in steps if next(step, steps) is not steps]


def by_blocks(function, *arrays, size=16):
    count = arrays[0].shape[0]
    results = [function(*(x[i : i + size] for x in arrays)) for i in range(0, count, size)]
    return tuple(jnp.concatenate(parts, axis=0) for parts in zip(*results))


def in_channels(shape, channels):
    return lax.broadcasted_iota(jnp.int32, shape, 1) < channels


def high_low(x):
    high = x.astype(bf16)
    return (jnp.concatenate([high, (x - high.astype(f32)).astype(bf16)], axis=1),)


def side_by_side(x, y):
    return jnp.concatenate([x, y], axis=1)


def layer_norm(parts, gain, channels, ones):
    def centre(x, total):
        centred = jnp.where(in_channels(x.shape, channels), x - total * (1.0 / channels), 0.0)
        return (centred, (centred * centred).astype(bf16))

    def finish(centred, total):
        inverse = lax.rsqrt(total * (1.0 / channels) + epsilon)
        unit = centred * inverse
        return (unit, inverse, (unit * gain).astype(bf16))

    totals = [dot(by_blocks(high_low, x)[0], jnp.ones((2 * LANES, LANES), bf16)) for x in parts]
    yield
    centred, squares = zip(*(by_blocks(centre, x, total) for x, total in zip(parts, totals)))
    variances = dot(side_by_side(*squares), ones)
    yield
    return [by_blocks(finish, c, variances[:, k * LANES : (k + 1) * LANES]) for k, c in enumerate(centred)]


def norm_backward(normed_grad, unit, inverse, gain, channels, ones):
    def products(normed_grad, unit):
        m = normed_grad * gain
        return (side_by_side(m.astype(bf16), (m * unit).astype(bf16)),)

    def finish(normed_grad, unit, inverse, sums):
        along = sums[:, :LANES] + unit * sums[:, LANES:]
        grad = inverse * (normed_grad * gain - along * (1.0 / channels))
        return (round16(jnp.where(in_channels(grad.shape, channels), grad, 0.0)),)

    sums = dot(by_blocks(products, normed_grad, unit)[0], ones)
    yield
    return by_blocks(finish, normed_grad, unit, inverse, sums)[0]


def gelu_parts(v):
    p = 0.3275911 * inv_sqrt_two
    c1, c2, c3, c4, c5 = (
        0.5 * c / p ** (k + 1)
        for k, c in enumerate((0.254829592, -0.284496736, 1.421413741, -1.453152027, 1.061405429))
    )
    t = pl.reciprocal(jnp.abs(v) + 1.0 / p, approx=True)
    bell = jnp.exp2(v * v * (-0.5 * log2_e))
    tail = ((((c5 * t + c4) * t + c3) * t + c2) * t + c1) * t * bell
    cdf = jnp.where(v >= 0.0, 1.0 - tail, tail)
    return (v * cdf, cdf + v * (bell * inv_sqrt_two_pi))


def dot(x, w):
    return jnp.dot(x, w, preferred_element_type=f32)


def dot_leading(x, y):
    return lax.dot_general(x, y, (((0,), (0,)), ((), ())), preferred_element_type=f32)


def pad_lanes(x):
    rows, channels = x.shape
    return jnp.concatenate([x, jnp.zeros((rows, LANES - channels), x.dtype)], axis=1)


def pieces(total, size):
    return [(start, min(size, total - start)) for start in range(0, total, size)]


def round16(x):
    return x.astype(bf16).astype(f32)


def fetch(sources, targets, sems):
    copies = [pltpu.make_async_copy(a, b, sems.at[i]) for i, (a, b) in enumerate(zip(sources, targets))]
    for copy in copies:
        copy.start()
    for copy in copies:
        copy.wait()


def image_take(ref):
    return lambda i, lo, hi: ref[i].astype(f32)[lo:hi]


def flat_take(ref, cols, channels):
    return lambda i, lo, hi: ref[i * cols + lo : i * cols + hi, 0:channels]


def bands_kernel(dims, image_in, image, *refs):
    outs, sems = (refs[:-1], refs[-1])
    place = Place(dims.row_count, dims.col_count)
    fetch((image_in,), (image,), sems)
    takes = [(image_take(image), 2 * dims.h, dims.rows, dims.cols)]
    write_strips(place, outs, takes, band_combos(dims.row_count))


def others_kernel(dims, image, *refs):
    outs = refs[len(band_combos(dims.row_count)) :]
    place = Place(dims.row_count, dims.col_count)
    takes = [(image_take(image), 2 * dims.h, dims.rows, dims.cols)]
    write_strips(place, outs, takes, other_combos(dims.row_count))


def grad_others_kernel(dims, grad1, cot, *refs):
    outs = refs[len(band_combos(dims.row_count)) :]
    place = Place(dims.row_count, dims.col_count)
    takes = [
        (flat_take(grad1, dims.cols, dims.channels), 2 * dims.h, dims.rows, dims.cols),
        (image_take(cot), dims.h, dims.rows, dims.cols),
    ]
    write_strips(place, outs, takes, other_combos(dims.row_count))


def weights_kernel(up_in, down_t_in, kernels_in, gains_in, *refs):
    forward0, back0, forward1, back1, grad_in0, grad_out0, taps0, taps1, gains, up_w, down_w, kernels, sems = refs
    fetch((up_in, down_t_in, kernels_in, gains_in), (up_w, down_w, kernels, gains), sems)
    spread_taps(kernels, 0, taps0)
    spread_taps(kernels, 1, taps1)
    channels, units = up_w.shape[1:]
    blank = jnp.zeros((LANES - channels, units), f32)
    wide, tall = ([], [])
    for layer in range(2):
        for ref in (up_w, down_w):
            full = jnp.concatenate([ref[layer].astype(f32), blank], axis=0)
            wide.append(full.astype(bf16))
            tall.append(full.T.astype(bf16))
    (up0, down_t0, up1, down_t1), (up_t0, down0, up_t1, down1) = (wide, tall)
    forward0[...] = diagonal(up0, up0)
    back0[...] = diagonal(down0, down0)
    forward1[...] = diagonal(up1, down_t1)
    back1[...] = diagonal(down1, up_t1)
    grad_in0[...] = diagonal(down_t0, down_t0)
    grad_out0[...] = diagonal(up_t0, up_t0)


def first_kernel(dims, *refs):
    count = len(combos(dims.row_count))
    image, cot, taps0, taps1, gains, forward0, back0, forward1, back1 = refs[:9]
    strips = refs[9 : 9 + count]
    refs = refs[9 + count :]
    (output, x0, x1, unit0, inv0, hidden0, slope0, grad1, normed1, pre_grad1, hidden1, gain_sum) = refs[:12]
    outs, conv = (refs[12:-1], refs[-1])
    place = Place(dims.row_count, dims.col_count)
    rows, cols, channels, h, size = (dims.rows, dims.cols, dims.channels, dims.h, dims.size)
    ext_rows, ext_cols, wide = (dims.ext_rows, dims.ext_cols, dims.wide)
    skip = dims.skipped_rows(place)
    read = received(place, strips, (0, 0))
    assemble(place, x0, lambda i: image[i].astype(f32), read, 2 * h, rows, cols, channels)

    x1[...] = jnp.zeros(x1.shape, f32)
    if dims.ext_pad > ext_rows * ext_cols:
        conv[ext_rows * ext_cols :, :] = jnp.zeros((dims.ext_pad - ext_rows * ext_cols, LANES), f32)
    frame = pl.multiple_of(skip * ext_cols, 8)

    def conv0(g, carry):
        at = group_start(g, ext_cols)
        base = pl.multiple_of(skip * wide, 8) + at
        total = conv_group(x0, base + 1, wide, ext_rows, taps0, size)
        for r in range(ext_rows):
            conv[pl.ds(r * ext_cols + at, 16), :] = total[r]
            x1[pl.ds(frame + r * ext_cols + at, 16), :] = x0[pl.ds(base + (r + h) * wide + 4, 16), :]
        return carry

    lax.fori_loop(0, -(-ext_cols // 16), conv0, 0)
    gain = pad_lanes(gains[0:1, :])
    ones = diagonal(jnp.ones((LANES, LANES), bf16), jnp.ones((LANES, LANES), bf16))
    half = dims.ext_pad // 2

    def mix0(start, n):
        spans = [(start, n), (half + start, n)]
        parts = yield from layer_norm([conv[at : at + n, :] for at, n in spans], gain, channels, ones)
        pres = dot(side_by_side(parts[0][2], parts[1][2]), forward0[...])
        yield
        count = pres.shape[1] // 2
        hiddens = []
        for k, ((at, n), (unit, inverse, _)) in enumerate(zip(spans, parts)):
            unit0[at : at + n, :] = unit.astype(bf16)
            inv0[at : at + n, :] = inverse

            def activate(pre):
                value, slope = gelu_parts(pre)
                return (value.astype(bf16), slope.astype(bf16))

            hidden, slope = by_blocks(activate, pres[:, k * count : (k + 1) * count])
            hidden0[at : at + n, :] = hidden
            slope0[at : at + n, :] = slope
            hiddens.append(hidden)
        branches = dot(side_by_side(*hiddens), back0[...])
        yield
        for k, (at, n) in enumerate(spans):
            px = pl.ds(frame + at, n)
            x1[px, :] = round16(x1[px, :] + branches[:, k * LANES : (k + 1) * LANES])
    together([mix0(start, n) for start, n in pieces(half, dims.piece)])
    clear_outside(place, x1, dims)

    def conv1(g, carry):
        at = group_start(g, cols)
        total = conv_group(x1, at + 1, ext_cols, rows, taps1, size)
        for r in range(rows):
            conv[pl.ds(r * cols + at, 16), :] = total[r]
        return carry

    lax.fori_loop(0, -(-cols // 16), conv1, 0)
    gain1 = pad_lanes(gains[1:2, :])
    gain_sum[...] = jnp.zeros(gain_sum.shape, f32)
    lines = dims.line_step
    step = lines * cols

    def mix1(k):
        px = slice(k * step, (k + 1) * step)
        middle = k * step + step // 2
        parts = yield from layer_norm(
            [conv[k * step : middle, :], conv[middle : (k + 1) * step, :]], gain1, channels, ones
        )
        unit, inverse, normed = (jnp.concatenate(pair, axis=0) for pair in zip(*parts))
        normed1[px, :] = normed
        upstream = pad_lanes(cot[k * lines : (k + 1) * lines].reshape(step, channels))
        both = dot(side_by_side(normed, upstream), forward1[...])
        yield

        def activate(pre, hidden_grad):
            value, slope = gelu_parts(pre)
            return (value.astype(bf16), (hidden_grad * slope).astype(bf16))

        count = both.shape[1] // 2
        hidden, pre_grad = by_blocks(activate, both[:, :count], both[:, count:])
        hidden1[px, :] = hidden
        pre_grad1[px, :] = pre_grad
        both = dot(side_by_side(hidden, pre_grad), back1[...])
        yield
        branch, normed_grad = (both[:, :LANES], both[:, LANES:])
        for i in range(lines):
            start = (k * lines + i + h) * ext_cols + 4
            line = x1[start : start + cols, :] + branch[i * cols : (i + 1) * cols]
            output[k * lines + i] = line[:, :channels].astype(bf16)
        product = normed_grad * unit
        gain_sum[...] += jnp.sum(product.reshape(step // 8, 8, LANES), axis=0)
        grad1[px, :] = yield from norm_backward(normed_grad, unit, inverse, gain1, channels, ones)

    together([mix1(k) for k in range(rows // lines)])

    takes = [(flat_take(grad1, cols, channels), 2 * h, rows, cols), (image_take(cot), h, rows, cols)]
    write_strips(place, outs, takes, band_combos(dims.row_count))


def clear_outside(place, flat, dims):
    h, frame_rows, ext_cols = (dims.h, dims.rows + 2 * dims.h, dims.ext_cols)
    margin = (ext_cols - dims.cols) // 2

    @pl.when(jnp.logical_not(place.has["above"]))
    def _():
        flat[0 : h * ext_cols, :] = jnp.zeros((h * ext_cols, LANES), f32)

    @pl.when(jnp.logical_not(place.has["below"]))
    def _():
        last = (frame_rows - h) * ext_cols
        flat[last:, :] = jnp.zeros((flat.shape[0] - last, LANES), f32)

    @pl.when(jnp.logical_not(place.has["left"]))
    def _():
        for r in range(frame_rows):
            flat[r * ext_cols : r * ext_cols + margin, :] = jnp.zeros((margin, LANES), f32)

    @pl.when(jnp.logical_not(place.has["right"]))
    def _():
        for r in range(frame_rows):
            flat[(r + 1) * ext_cols - margin : (r + 1) * ext_cols, :] = jnp.zeros((margin, LANES), f32)


def sums_kernel(
    dims, x1, grad1, normed1, pre_grad1, hidden1, cot, gain_part, final, taps_sum, up_sum, down_sum, output, sums
):
    output[...] = final[...]
    kernel_sums(x1, 1, dims.ext_cols, grad1, 0, dims.cols, dims.rows, dims.cols, dims.size, sums)
    store_sums(dims, sums, gain_part[...], taps_sum)
    upstream = pad_lanes(cot[...].reshape(dims.rows * dims.cols, dims.channels))
    up_sum[...] = dot_leading(normed1[...], pre_grad1[...]).T
    down_sum[...] = dot_leading(upstream, hidden1[...]).T


def store_sums(dims, sums, gain_part, target):
    taps = dims.size * dims.size
    target[...] = jnp.zeros(target.shape, f32)
    for t in range(taps):
        target[t : t + 1, :] = jnp.sum(sums[t * 8 : t * 8 + 8, :], axis=0, keepdims=True)
    target[taps : taps + 1, :] = jnp.sum(gain_part, axis=0, keepdims=True)


def third_kernel(dims, *refs):
    count = len(combos(dims.row_count))
    (grad1, cot, taps1, gains, grad_in0, grad_out0, x0, unit0, inv0, hidden0, slope0) = refs[:11]
    (taps_sum1, up_sum1, down_sum1) = refs[11:14]
    strips = refs[14 : 14 + count]
    (grad0, middle, keep, small_keep, send) = refs[14 + count : 19 + count]
    (wide_grad, cot_frame, upstream, own, sums, normed0, flow0, pre_grad0, gain_sum, small, tall, slabs) = refs[19 + count :]
    place = Place(dims.row_count, dims.col_count)
    rows, cols, channels, h, size = (dims.rows, dims.cols, dims.channels, dims.h, dims.size)
    ext_rows, ext_cols, wide = (dims.ext_rows, dims.ext_cols, dims.wide)
    skip = dims.skipped_rows(place)
    read = received(place, strips, (0, 0))
    assemble(
        place, wide_grad, lambda i: grad1[i * cols : (i + 1) * cols, 0:channels], read, 2 * h, rows, cols, channels
    )
    read_cot = received(place, strips, (rows, 2 * h))
    margin = (ext_cols - cols) // 2
    cot_frame[...] = jnp.zeros(cot_frame.shape, f32)
    for vertical, start, n in (("above", 0, h), (None, h, rows), ("below", h + rows, h)):
        for i in range(n):
            base = (start + i) * ext_cols
            line = cot[i].astype(f32) if vertical is None else read_cot(vertical, None, i)
            cot_frame[base + margin : base + margin + cols, 0:channels] = line
            cot_frame[base : base + margin, 0:channels] = read_cot(vertical, "left", i)[SIDE - margin :]
            cot_frame[base + margin + cols : base + ext_cols, 0:channels] = read_cot(vertical, "right", i)[:margin]

    used = ext_rows * ext_cols
    if dims.ext_pad > used:
        upstream[used:, :] = jnp.zeros((dims.ext_pad - used, LANES), f32)
        own[used:, :] = jnp.zeros((dims.ext_pad - used, LANES), f32)
    grad0[...] = jnp.zeros(grad0.shape, f32)
    frame = pl.multiple_of(skip * ext_cols, 8)

    def conv1(g, carry):
        at = group_start(g, ext_cols)
        total = conv_group(wide_grad, pl.multiple_of(skip * wide, 8) + at + 1, wide, ext_rows, taps1, size, True)
        col = lax.broadcasted_iota(jnp.int32, (16, LANES), 0) + (at - margin)
        inside = jnp.where(jnp.logical_and(col >= 0, col < cols), 1.0, 0.0)
        for r in range(ext_rows):
            px = pl.ds(r * ext_cols + at, 16)
            upstream[px, :] = cot_frame[pl.ds(frame + r * ext_cols + at, 16), :] + total[r]
            mine = jnp.logical_and(r + skip >= h, r + skip < h + rows)
            own[px, :] = jnp.where(mine, inside, 0.0)
        return carry

    lax.fori_loop(0, -(-ext_cols // 16), conv1, 0)
    for i in range(rows):
        line = upstream[pl.ds((i + h - skip) * ext_cols + margin, cols), :]
        middle[i * cols : (i + 1) * cols, :] = round16(line)

    gain = pad_lanes(gains[0:1, :])
    gain_sum[...] = jnp.zeros(gain_sum.shape, f32)
    ones = diagonal(jnp.ones((LANES, LANES), bf16), jnp.ones((LANES, LANES), bf16))
    half_px = dims.ext_pad // 2

    def mix0(start, n):
        spans = [(start, n), (half_px + start, n)]
        flows = [upstream[at : at + n, :].astype(bf16) for at, n in spans]
        hidden_grads = dot(side_by_side(*flows), grad_in0[...])
        yield
        count = hidden_grads.shape[1] // 2

        def slope_times(grad, slope):
            return ((grad * slope.astype(f32)).astype(bf16),)

        pre_grads = [
            by_blocks(slope_times, hidden_grads[:, k * count : (k + 1) * count], slope0[at : at + n, :])[0]
            for k, (at, n) in enumerate(spans)
        ]
        both = dot(side_by_side(*pre_grads), grad_out0[...])
        yield
        normed_grads = (both[:, :LANES], both[:, LANES:])
        for (at, n), flow, pre_grad, normed_grad in zip(spans, flows, pre_grads, normed_grads):
            mine = own[at : at + n, :]
            unit = unit0[at : at + n, :].astype(f32)
            normed0[at : at + n, :] = (unit * gain * mine).astype(bf16)
            flow0[at : at + n, :] = flow * mine.astype(bf16)
            pre_grad0[at : at + n, :] = pre_grad
            product = normed_grad * unit * mine
            gain_sum[...] += jnp.sum(product.reshape(n // 8, 8, LANES), axis=0)
            grad = yield from norm_backward(normed_grad, unit, inv0[at : at + n, :], gain, channels, ones)
            grad0[pl.ds(frame + at, n), :] = grad

    together([mix0(start, n) for start, n in pieces(half_px, dims.piece)])
    clear_outside(place, grad0, dims)
    kernel_sums(
        x0, h * wide + SIDE - h, wide, grad0, h * ext_cols + margin, ext_cols, rows, cols, size, sums
    )
    store_sums(dims, sums, gain_sum[...], small)

    taps_rows = size * size + 1
    merged = jnp.concatenate([small[0:taps_rows, :], taps_sum1[0:taps_rows, :]], axis=0) * dims.factor
    merged = fold_rows(merged, dims.small_rows, channels).astype(bf16)
    small_keep[...] = merged.astype(f32)

    layer_rows, part, half = (dims.layer_rows, dims.part, dims.half)
    units = hidden0.shape[1]
    up0 = dot_leading(normed0[...], pre_grad0[...]).T * dims.factor
    down0 = dot_leading(flow0[...], hidden0[...]).T * dims.factor
    up1 = up_sum1[...] * dims.factor
    down1 = down_sum1[...] * dims.factor
    lane = lax.broadcasted_iota(jnp.int32, (units, LANES), 1)
    slab_rows = 2 * layer_rows
    for r in range(dims.row_count):
        for layer, (u, d) in enumerate(((up0, down0), (up1, down1))):
            first = pltpu.roll(u, LANES - r * half, 1) if r else u
            shift = (half - r * half) % LANES
            second = pltpu.roll(d, shift, 1) if shift else d
            joined = jnp.where(lane < half, first, jnp.where(lane < 2 * half, second, 0.0))
            tall[layer * (units + 8) : layer * (units + 8) + units, :] = joined

        for c in range(dims.col_count):
            index = 0
            for axis, bit in dims.stages:
                index = 2 * index + ((r if axis == "row" else c) >> bit & 1)
            for layer in range(2):
                to, at = (index * slab_rows + layer * layer_rows, layer * (units + 8) + c * part)
                slabs[to : to + layer_rows, :] = tall[at : at + layer_rows, :]

    split(dims, 0, slabs, merged, keep, (send,))


def fold_rows(x, rows, used):
    n = x.shape[0]
    if rows >= n:
        return pad_rows(x, rows)
    assert used <= 96
    stride = ceil8(n - rows)
    rest = pad_rows(x[rows:], stride)
    pieces_of = pad_rows(jnp.concatenate([pltpu.roll(rest, 96 - 32 * k, 1) for k in range(3)], axis=0), rows)
    lane = lax.broadcasted_iota(jnp.int32, (rows, LANES), 1)
    return jnp.where(lane < 96, x[:rows], pieces_of)


def pad_rows(x, rows):
    if rows == x.shape[0]:
        return x
    return jnp.concatenate([x, jnp.zeros((rows - x.shape[0], LANES), x.dtype)], axis=0)


def unfold_rows(x, n):
    rows = x.shape[0]
    if rows >= n:
        return x[:n]
    stride = ceil8(n - rows)
    lane = lax.broadcasted_iota(jnp.int32, (stride, LANES), 1)
    rest = jnp.zeros((stride, LANES), x.dtype)
    for k in range(3):
        moved = pltpu.roll(x[k * stride : (k + 1) * stride], 32 + 32 * k, 1)
        rest = jnp.where(jnp.logical_and(lane >= 32 * k, lane < 32 * k + 32), moved, rest)
    return jnp.concatenate([x, rest[: n - rows]], axis=0)


def split(dims, stage, slabs, merged, keep, sends):
    group = dims.groups[stage]
    count = slabs.shape[0] >> len(group)
    mine = 0
    for axis, bit in group:
        mine = mine * 2 + lax.rem(lax.div(lax.axis_index(axis), 1 << bit), 2)
    keep[...] = slabs[pl.ds(pl.multiple_of(mine * count, 16), count), :]
    for mask, send in enumerate(sends, 1):
        other = 0
        for j in range(len(group)):
            weight = 1 << j
            digit = lax.rem(lax.div(mine, weight), 2)
            other = other + weight * (1 - digit if mask & weight else digit)
        send[0:count, :] = slabs[pl.ds(pl.multiple_of(other * count, 16), count), :].astype(bf16)
        send[count:, :] = merged


def gather_up(keep, small, gots):
    count = keep.shape[0]
    slabs = [keep[...]] + [got[0:count, :].astype(f32) for got in gots]
    sums = [small[...]] + [got[count:, :].astype(f32) for got in gots]
    if len(gots) == 1:
        return (slabs[0] + slabs[1], sums[0] + sums[1])
    return tuple((x[0] + x[1]) + (x[2] + x[3]) for x in (slabs, sums))


def stage_kernel(dims, stage, keep, small, *refs):
    before, after = (len_sends(dims.groups[stage - 1]), len_sends(dims.groups[stage]))
    gots = refs[:before]
    keep_out, small_out = refs[-3 - after : -1 - after]
    sends, total = (refs[-1 - after : -1], refs[-1])
    slabs, merged = gather_up(keep, small, gots)
    total[...] = slabs
    merged = merged.astype(bf16)
    small_out[...] = merged.astype(f32)
    split(dims, stage, total, merged, keep_out, sends)


def len_sends(group):
    return (1 << len(group)) - 1


def last_kernel(dims, keep, small, *refs):
    gots, (kernel_out, gain_out, up_out, down_out) = (refs[:-4], refs[-4:])
    total, merged = gather_up(keep, small, gots)
    merged = unfold_rows(merged, 2 * (dims.size * dims.size + 1))
    size, channels, half, part = (dims.size, dims.channels, dims.half, dims.part)
    for layer in range(2):
        block = total[layer * dims.layer_rows : layer * dims.layer_rows + part]
        up_out[layer] = block[:, :half]
        down_out[layer] = block[:, half : 2 * half]
        for t in range(size * size + 1):
            at = layer * (size * size + 1) + t
            row = merged[at : at + 1, 0:channels]
            if t < size * size:
                kernel_out[t // size, t % size, layer : layer + 1, :] = row
            else:
                gain_out[layer : layer + 1, :] = row


def image_kernel(dims, grad0, middle, taps0, after, out, ready, work):
    rows, cols, size = (dims.rows, dims.cols, dims.size)

    def conv0(g, carry):
        at = group_start(g, cols)
        total = conv_group(grad0, at + 1, dims.ext_cols, rows, taps0, size, True)
        for r in range(rows):
            work[pl.ds(r * cols + at, 16), :] = middle[pl.ds(r * cols + at, 16), :] + total[r]
        return carry

    lax.fori_loop(0, -(-cols // 16), conv0, 0)
    for r in range(rows):
        out[r] = work[r * cols : (r + 1) * cols, 0 : dims.channels].astype(bf16)
    ready[...] = jnp.zeros(ready.shape, f32)


class Dims:
    def skipped_rows(self, place):
        if self.row_count > 2:
            return 0
        return jnp.where(place.has["above"], 0, self.h)


def dims_of(image, kernels, up_weights):
    d = Dims()
    d.row_count, d.col_count = (lax.axis_size("row"), lax.axis_size("col"))
    d.rows, d.cols, d.channels = image.shape
    d.size = kernels.shape[1]
    d.h = d.size // 2
    d.ext_rows, d.ext_cols = (d.rows + (d.h if d.row_count == 2 else 2 * d.h), d.cols + 8)
    d.wide = d.cols + 2 * SIDE
    d.ext_pad = -(-d.ext_rows * d.ext_cols // 32) * 32
    d.piece = 176
    d.line_step = 4
    d.half = d.channels // d.row_count
    d.part = up_weights.shape[2] // d.col_count
    d.layer_rows = ceil8(d.part)
    d.count = d.row_count * d.col_count
    d.small_rows = 80 if d.size == 7 and d.channels <= 96 else -(-2 * (d.size * d.size + 1) // 16) * 16
    d.factor = 1.0 / math.sqrt(d.rows * d.cols * d.count)
    row_bits, col_bits = (d.row_count.bit_length() - 1, d.col_count.bit_length() - 1)
    bits = [("row", b) for b in range(row_bits)] + [("col", b) for b in range(1, col_bits)]
    d.groups = [[("col", 0)]] + [bits[i : i + 2] for i in range(0, len(bits), 2)]
    d.stages = [bit for group in d.groups for bit in group]
    return d


def swap_by(d, group, mask):
    flip = {"row": 0, "col": 0}
    for j, (axis, bit) in enumerate(group):
        if mask >> (len(group) - 1 - j) & 1:
            flip[axis] |= 1 << bit
    pairs = []
    for r in range(d.row_count):
        for c in range(d.col_count):
            pairs.append((r * d.col_count + c, (r ^ flip["row"]) * d.col_count + (c ^ flip["col"])))
    return pairs


def run(kernel, outs, scratch, *args, in_hbm=0, sems=0, busy_us=1):
    shapes = [jax.ShapeDtypeStruct(shape, kind) for shape, kind in outs]
    space = pl.BlockSpec(memory_space=pltpu.VMEM)
    far = pl.BlockSpec(memory_space=pltpu.HBM)
    held = [pltpu.VMEM(shape, kind) for shape, kind in scratch]
    if sems:
        held.append(pltpu.SemaphoreType.DMA((sems,)))
    return pl.pallas_call(
        kernel,
        out_shape=shapes,
        in_specs=[far] * in_hbm + [space] * (len(args) - in_hbm),
        out_specs=[space] * len(shapes),
        scratch_shapes=held,
        compiler_params=pltpu.CompilerParams(vmem_limit_bytes=32 * 1024 * 1024),
        cost_estimate=pl.CostEstimate(flops=int(busy_us * 1e9), bytes_accessed=1 << 18, transcendentals=0),
    )(*args)


def per_device(image, kernels, gains, up_weights, down_weights, cotangent):
    d = dims_of(image, kernels, up_weights)
    bind = functools.partial
    rows, cols, channels = image.shape
    units = up_weights.shape[2]
    tile, ext, wide = (rows * cols, d.ext_pad, (rows + 4 * d.h) * d.wide)
    frame = (rows + 2 * d.h) * d.ext_cols + 16
    taps = ((d.size * d.size * 16, LANES), bf16)
    tap_sums = ((d.size * d.size * 8, LANES), f32)
    sums_rows = ceil8(d.size * d.size + 1)

    bands, others = (band_combos(d.row_count), other_combos(d.row_count))

    def strips_of(pairs, radii):
        return [(shape, bf16) for shape in strip_shapes(pairs, rows, cols, channels, radii)]

    image, *band_strips = run(
        bind(bands_kernel, d), [(image.shape, bf16)] + strips_of(bands, (2 * d.h,)), [], image, in_hbm=1, sems=1
    )
    other_strips = run(bind(others_kernel, d), strips_of(others, (2 * d.h,)), [], image, *band_strips)
    strips = exchange(band_strips, other_strips, d.row_count, d.col_count)
    mixing = [((2 * LANES, 2 * units), bf16), ((2 * units, 2 * LANES), bf16)]
    forward0, back0, forward1, back1, grad_in0, grad_out0, taps0, taps1, gains = run(
        weights_kernel,
        mixing * 3 + [taps, taps, (gains.shape, f32)],
        [((2, channels, units), bf16), ((2, channels, units), bf16), ((d.size, d.size, 2, channels), f32)],
        up_weights,
        jnp.swapaxes(down_weights, 1, 2),
        jnp.transpose(kernels, (1, 2, 0, 3)),
        gains,
        in_hbm=4,
        sems=4,
        busy_us=2,
    )

    first = run(
        bind(first_kernel, d),
        [
            (image.shape, bf16),
            ((wide, LANES), f32),
            ((frame, LANES), f32),
            ((ext, LANES), bf16),
            ((ext, LANES), f32),
            ((ext, units), bf16),
            ((ext, units), bf16),
            ((tile, LANES), f32),
            ((tile, LANES), bf16),
            ((tile, units), bf16),
            ((tile, units), bf16),
            ((8, LANES), f32),
        ]
        + strips_of(bands, (2 * d.h, d.h)),
        [((ext, LANES), f32)],
        image,
        cotangent,
        taps0,
        taps1,
        gains,
        forward0,
        back0,
        forward1,
        back1,
        *strips,
        busy_us=15,
    )
    (final, x0, x1, unit0, inv0, hidden0, slope0, grad1, normed1, pre_grad1, hidden1, gain_part) = first[:12]
    band_strips = first[12:]
    other_strips = run(
        bind(grad_others_kernel, d), strips_of(others, (2 * d.h, d.h)), [], grad1, cotangent, *band_strips
    )
    strips = exchange(band_strips, other_strips, d.row_count, d.col_count)

    taps_sum1, up_sum1, down_sum1, output = run(
        bind(sums_kernel, d),
        [((sums_rows, LANES), f32), ((units, LANES), f32), ((units, LANES), f32), (image.shape, bf16)],
        [tap_sums],
        x1,
        grad1,
        normed1,
        pre_grad1,
        hidden1,
        cotangent,
        gain_part,
        final,
        busy_us=3,
    )

    held = d.count // 2 * 2 * d.layer_rows
    small = ((d.small_rows, LANES), f32)
    grad0, middle, keep, sums, send = run(
        bind(third_kernel, d),
        [((frame, LANES), f32), ((tile, LANES), f32), ((held, LANES), f32), small, ((held + d.small_rows, LANES), bf16)],
        [
            ((wide, LANES), f32),
            ((frame, LANES), f32),
            ((ext, LANES), f32),
            ((ext, LANES), f32),
            tap_sums,
            ((ext, LANES), bf16),
            ((ext, LANES), bf16),
            ((ext, units), bf16),
            ((8, LANES), f32),
            ((sums_rows, LANES), f32),
            ((2 * (units + 8), LANES), f32),
            ((2 * held, LANES), f32),
        ],
        grad1,
        cotangent,
        taps1,
        gains,
        grad_in0,
        grad_out0,
        x0,
        unit0,
        inv0,
        hidden0,
        slope0,
        taps_sum1,
        up_sum1,
        down_sum1,
        *strips,
        busy_us=12,
    )
    axes = ("row", "col")
    sends = [send]
    for stage, group in enumerate(d.groups):
        gots = [lax.ppermute(x, axes, swap_by(d, group, mask)) for mask, x in enumerate(sends, 1)]
        ready = []
        if stage == 1:
            gradient, *ready = run(
                bind(image_kernel, d),
                [(image.shape, bf16), ((8, LANES), f32)],
                [((tile, LANES), f32)],
                grad0,
                middle,
                taps0,
                sums,
                busy_us=3,
            )
        if stage + 1 < len(d.groups):
            after = d.groups[stage + 1]
            whole, held = (held, held >> len(after))
            keep, sums, *sends = run(
                bind(stage_kernel, d, stage + 1),
                [((held, LANES), f32), small] + [((held + d.small_rows, LANES), bf16)] * len_sends(after),
                [((whole, LANES), f32)],
                keep,
                sums,
                *gots,
                *ready,
            )
    kernel_out, gain_out, up_out, down_out = run(
        bind(last_kernel, d),
        [
            ((d.size, d.size, 2, channels), f32),
            (gains.shape, f32),
            ((2, d.part, d.half), f32),
            ((2, d.part, d.half), f32),
        ],
        [],
        keep,
        sums,
        *gots,
    )
    kernel_out = jnp.transpose(kernel_out, (2, 0, 1, 3))
    return (output, gradient, kernel_out, gain_out, jnp.swapaxes(up_out, 1, 2), down_out)


def solution(mesh):
    placed = (P("row", "col", None), P(), P(), P(), P(), P("row", "col", None))
    return jax.shard_map(
        per_device,
        mesh=mesh,
        in_specs=placed,
        out_specs=(
            P("row", "col", None),
            P("row", "col", None),
            P(),
            P(),
            P(None, "row", "col"),
            P(None, "col", "row"),
        ),
        check_vma=False,
    )
```

```python
import functools
import math

import jax
import jax.numpy as jnp
from jax import lax
from jax.experimental import pallas as pl
from jax.experimental.pallas import tpu as pltpu
from jax.sharding import PartitionSpec as P

epsilon = 1e-06
inv_sqrt_two = 0.7071067811865476
inv_sqrt_two_pi = 0.3989422804014327
log2_e = 1.4426950408889634
LANES = 128
SIDE = 8
f32, bf16 = (jnp.float32, jnp.bfloat16)


def ceil8(n):
    return -(-n // 8) * 8


def combos(row_count):
    listed = [(None, 0), (None, 1), (0, None), (0, 0), (0, 1)]
    if row_count > 2:
        listed += [(1, None), (1, 0), (1, 1)]
    return listed


def partner(index, start, count):
    if start is None:
        return index
    other = index + 1 if (index - start) % 2 == 0 else index - 1
    return other if 0 <= other < count else None


def swap_pairs(row_count, col_count, row_start, col_start):
    pairs = []
    for r in range(row_count):
        for c in range(col_count):
            pr, pc = (partner(r, row_start, row_count), partner(c, col_start, col_count))
            if pr is None:
                pr, pc = (r, c ^ 1)
            elif pc is None:
                pr, pc = (r ^ 1 if row_start is None else pr, c)
            pairs.append((r * col_count + c, pr * col_count + pc))
    return pairs


def exchange(bands, others, row_count, col_count):
    got = {}
    for strips, pairs in ((bands, band_combos(row_count)), (others, other_combos(row_count))):
        for strip, (rs, cs) in zip(strips, pairs):
            got[rs, cs] = lax.ppermute(strip, ("row", "col"), swap_pairs(row_count, col_count, rs, cs))
    return [got[pair] for pair in combos(row_count)]


class Place:
    def __init__(self, row_count, col_count):
        row, col = (lax.axis_index("row"), lax.axis_index("col"))
        self.even_row, self.even_col = (lax.rem(row, 2) == 0, lax.rem(col, 2) == 0)
        self.has = {
            "above": row > 0,
            "below": row < row_count - 1,
            "left": col > 0,
            "right": col < col_count - 1,
        }
        self.row_count = row_count


def band_combos(row_count):
    return [pair for pair in combos(row_count) if pair[1] is None]


def other_combos(row_count):
    return [pair for pair in combos(row_count) if pair[1] is not None]


def write_strips(place, outs, takes, pairs):
    for out, (rs, cs) in zip(outs, pairs):
        at = 0
        for take, radius, rows, cols in takes:
            row_sets = [slice(0, rows)] * 2
            col_sets = [slice(0, cols)] * 2
            if rs is not None:
                row_sets = [slice(rows - radius, rows), slice(0, radius)]
                if rs == 1:
                    row_sets = row_sets[::-1]
            if cs is not None:
                col_sets = [slice(cols - SIDE, cols), slice(0, SIDE)]
                if cs == 1:
                    col_sets = col_sets[::-1]
            count = row_sets[0].stop - row_sets[0].start
            for i in range(count):
                parts = {}
                for er in (0, 1):
                    for ec in (0, 1):
                        key = (row_sets[er].start + i, col_sets[ec].start, col_sets[ec].stop)
                        if key not in parts:
                            parts[key] = take(*key)
                        parts[er, ec] = parts[key]
                if cs is None:
                    pick = [parts[0, 0], parts[1, 0]]
                else:
                    pick = [jnp.where(place.even_col, parts[e, 0], parts[e, 1]) for e in (0, 1)]
                value = pick[0] if rs is None else jnp.where(place.even_row, pick[0], pick[1])
                out[at + i] = value.astype(out.dtype)
            at += count


def strip_shapes(pairs, rows, cols, channels, radii):
    shapes = []
    for rs, cs in pairs:
        height = sum(rows if rs is None else radius for radius in radii)
        shapes.append((height, cols if cs is None else SIDE, channels))
    return shapes


def received(place, strips, row_sections):
    table = dict(zip(combos(place.row_count), strips))
    full_start, band_start = row_sections

    def along(rs, cs, i):
        return table[rs, cs][(full_start if rs is None else band_start) + i].astype(f32)

    def column(rs, side, i):
        if side is None:
            return along(rs, None, i)
        near, far = (along(rs, 0, i), along(rs, 1, i))
        if side == "left":
            return jnp.where(place.even_col, far, near)
        return jnp.where(place.even_col, near, far)

    def read(vertical, side, i):
        if vertical is None:
            value = column(None, side, i)
        elif place.row_count == 2:
            value = column(0, side, i)
        else:
            near, far = (column(0, side, i), column(1, side, i))
            if vertical == "above":
                value = jnp.where(place.even_row, far, near)
            else:
                value = jnp.where(place.even_row, near, far)
        if vertical is not None:
            value = jnp.where(place.has[vertical], value, 0.0)
        if side is not None:
            value = jnp.where(place.has[side], value, 0.0)
        return value

    return read


def assemble(place, target, own, read, radius, rows, cols, channels):
    width = cols + 2 * SIDE
    target[...] = jnp.zeros(target.shape, f32)
    for vertical, start, count in (("above", 0, radius), (None, radius, rows), ("below", radius + rows, radius)):
        for i in range(count):
            base = (start + i) * width
            middle = own(i) if vertical is None else read(vertical, None, i)
            target[base + SIDE : base + SIDE + cols, 0:channels] = middle
            target[base : base + SIDE, 0:channels] = read(vertical, "left", i)
            target[base + SIDE + cols : base + width, 0:channels] = read(vertical, "right", i)


def spread_taps(kernel_ref, layer, target):
    size, channels = (kernel_ref.shape[0], kernel_ref.shape[3])
    for a in range(size):
        for b in range(size):
            t = a * size + b
            row = pad_lanes(kernel_ref[a, b, layer : layer + 1, :])
            target[t * 16 : t * 16 + 16, :] = jnp.broadcast_to(row, (16, LANES)).astype(bf16)


def tree_sum(terms):
    while len(terms) > 1:
        pairs = [terms[i] + terms[i + 1] for i in range(0, len(terms) - 1, 2)]
        terms = pairs + ([terms[-1]] if len(terms) % 2 else [])
    return terms[0]


def conv_group(src, base, stride, rows_out, taps, size, flipped=False):
    total = [None] * rows_out
    for first in range(0, size, 2):
        columns = range(first, min(first + 2, size))
        weights = []
        for b in columns:
            order = [a * size + b for a in range(size)]
            if flipped:
                order = [size * size - 1 - t for t in order]
            weights.append([taps[t * 16 : t * 16 + 16, :] for t in order])
        windows = [[] for _ in columns]
        for i in range(rows_out + size - 1):
            for window, b in zip(windows, columns):
                window.append(src[pl.ds(base + i * stride + b, 16), :].astype(bf16))
            r = i - size + 1
            if r >= 0:
                sums = [
                    tree_sum([window[r + a] * weight[a] for a in range(size)])
                    for window, weight in zip(windows, weights)
                ]
                term = tree_sum(sums).astype(f32)
                total[r] = term if total[r] is None else total[r] + term
    return total


def group_start(g, cols):
    return pl.multiple_of(jnp.minimum(g * 16, cols - 16), 8)


def kernel_sums(src, src_base, src_stride, grad, grad_base, grad_stride, rows, cols, size, sums):
    sums[...] = jnp.zeros(sums.shape, f32)
    for at in range(0, cols, 16):
        grads = [grad[pl.ds(grad_base + i * grad_stride + at, 16), :].astype(bf16) for i in range(rows)]
        for b in range(size):
            lines = [
                src[pl.ds(src_base + i * src_stride + at + b, 16), :].astype(bf16) for i in range(rows + size - 1)
            ]
            for a in range(size):
                term = tree_sum([lines[r + a] * grads[r] for r in range(rows)]).astype(f32)
                t = (a * size + b) * 8
                sums[t : t + 8, :] += term[0:8] + term[8:16]
            yield


def weight_sum(left, right, total, size):
    for start, n in pieces(left.shape[0], size):
        term = dot_leading(left[start : start + n, :], right[start : start + n, :])
        yield
        total[...] = term if start == 0 else total[...] + term


def diagonal(first, second):
    top = jnp.concatenate([first, jnp.zeros((first.shape[0], second.shape[1]), first.dtype)], axis=1)
    bottom = jnp.concatenate([jnp.zeros((second.shape[0], first.shape[1]), first.dtype), second], axis=1)
    return jnp.concatenate([top, bottom], axis=0)


def together(steps):
    steps = list(steps)
    while steps:
        steps = [step for step in steps if next(step, steps) is not steps]


def by_blocks(function, *arrays, size=16):
    count = arrays[0].shape[0]
    results = [function(*(x[i : i + size] for x in arrays)) for i in range(0, count, size)]
    return tuple(jnp.concatenate(parts, axis=0) for parts in zip(*results))


def in_channels(shape, channels):
    return lax.broadcasted_iota(jnp.int32, shape, 1) < channels


def high_low(x):
    high = x.astype(bf16)
    return (jnp.concatenate([high, (x - high.astype(f32)).astype(bf16)], axis=1),)


def side_by_side(x, y):
    return jnp.concatenate([x, y], axis=1)


def layer_norm(parts, gain, channels, ones):
    def centre(x, total):
        centred = jnp.where(in_channels(x.shape, channels), x - total * (1.0 / channels), 0.0)
        return (centred, (centred * centred).astype(bf16))

    def finish(centred, total):
        inverse = lax.rsqrt(total * (1.0 / channels) + epsilon)
        unit = centred * inverse
        return (unit, inverse, (unit * gain).astype(bf16))

    totals = [dot(by_blocks(high_low, x)[0], jnp.ones((2 * LANES, LANES), bf16)) for x in parts]
    yield
    centred, squares = zip(*(by_blocks(centre, x, total) for x, total in zip(parts, totals)))
    variances = dot(side_by_side(*squares), ones)
    yield
    return [by_blocks(finish, c, variances[:, k * LANES : (k + 1) * LANES]) for k, c in enumerate(centred)]


def norm_backward(normed_grad, unit, inverse, gain, channels, ones):
    def products(normed_grad, unit):
        m = normed_grad * gain
        return (side_by_side(m.astype(bf16), (m * unit).astype(bf16)),)

    def finish(normed_grad, unit, inverse, sums):
        along = sums[:, :LANES] + unit * sums[:, LANES:]
        grad = inverse * (normed_grad * gain - along * (1.0 / channels))
        return (round16(jnp.where(in_channels(grad.shape, channels), grad, 0.0)),)

    sums = dot(by_blocks(products, normed_grad, unit)[0], ones)
    yield
    return by_blocks(finish, normed_grad, unit, inverse, sums)[0]


def gelu_parts(v):
    p = 0.3275911 * inv_sqrt_two
    c1, c2, c3, c4, c5 = (
        0.5 * c / p ** (k + 1)
        for k, c in enumerate((0.254829592, -0.284496736, 1.421413741, -1.453152027, 1.061405429))
    )
    t = pl.reciprocal(jnp.abs(v) + 1.0 / p, approx=True)
    bell = jnp.exp2(v * v * (-0.5 * log2_e))
    tail = ((((c5 * t + c4) * t + c3) * t + c2) * t + c1) * t * bell
    cdf = jnp.where(v >= 0.0, 1.0 - tail, tail)
    return (v * cdf, cdf + v * (bell * inv_sqrt_two_pi))


def dot(x, w):
    return jnp.dot(x, w, preferred_element_type=f32)


def dot_leading(x, y):
    return lax.dot_general(x, y, (((0,), (0,)), ((), ())), preferred_element_type=f32)


def pad_lanes(x):
    rows, channels = x.shape
    return jnp.concatenate([x, jnp.zeros((rows, LANES - channels), x.dtype)], axis=1)


def pieces(total, size):
    return [(start, min(size, total - start)) for start in range(0, total, size)]


def round16(x):
    return x.astype(bf16).astype(f32)


def fetch(sources, targets, sems):
    copies = [pltpu.make_async_copy(a, b, sems.at[i]) for i, (a, b) in enumerate(zip(sources, targets))]
    for copy in copies:
        copy.start()
    for copy in copies:
        copy.wait()


def image_take(ref):
    return lambda i, lo, hi: ref[i].astype(f32)[lo:hi]


def flat_take(ref, cols, channels):
    return lambda i, lo, hi: ref[i * cols + lo : i * cols + hi, 0:channels]


def bands_kernel(dims, image_in, image, *refs):
    outs, sems = (refs[:-1], refs[-1])
    place = Place(dims.row_count, dims.col_count)
    fetch((image_in,), (image,), sems)
    takes = [(image_take(image), 2 * dims.h, dims.rows, dims.cols)]
    write_strips(place, outs, takes, band_combos(dims.row_count))


def others_kernel(dims, image, *refs):
    outs = refs[len(band_combos(dims.row_count)) :]
    place = Place(dims.row_count, dims.col_count)
    takes = [(image_take(image), 2 * dims.h, dims.rows, dims.cols)]
    write_strips(place, outs, takes, other_combos(dims.row_count))


def grad_others_kernel(dims, grad1, cot, *refs):
    outs = refs[len(band_combos(dims.row_count)) :]
    place = Place(dims.row_count, dims.col_count)
    takes = [
        (flat_take(grad1, dims.cols, dims.channels), 2 * dims.h, dims.rows, dims.cols),
        (image_take(cot), dims.h, dims.rows, dims.cols),
    ]
    write_strips(place, outs, takes, other_combos(dims.row_count))


def weights_kernel(up_in, down_t_in, kernels_in, gains_in, *refs):
    forward0, back0, forward1, back1, grad_in0, grad_out0, taps0, taps1, gains, up_w, down_w, kernels, sems = refs
    fetch((up_in, down_t_in, kernels_in, gains_in), (up_w, down_w, kernels, gains), sems)
    spread_taps(kernels, 0, taps0)
    spread_taps(kernels, 1, taps1)
    channels, units = up_w.shape[1:]
    blank = jnp.zeros((LANES - channels, units), f32)
    wide, tall = ([], [])
    for layer in range(2):
        for ref in (up_w, down_w):
            full = jnp.concatenate([ref[layer].astype(f32), blank], axis=0)
            wide.append(full.astype(bf16))
            tall.append(full.T.astype(bf16))
    (up0, down_t0, up1, down_t1), (up_t0, down0, up_t1, down1) = (wide, tall)
    forward0[...] = diagonal(up0, up0)
    back0[...] = diagonal(down0, down0)
    forward1[...] = diagonal(up1, down_t1)
    back1[...] = diagonal(down1, up_t1)
    grad_in0[...] = diagonal(down_t0, down_t0)
    grad_out0[...] = diagonal(up_t0, up_t0)


def first_kernel(dims, *refs):
    count = len(combos(dims.row_count))
    image, cot, taps0, taps1, gains, forward0, back0, forward1, back1 = refs[:9]
    strips = refs[9 : 9 + count]
    refs = refs[9 + count :]
    (output, x0, x1, unit0, inv0, hidden0, slope0, grad1, normed1, pre_grad1, hidden1, gain_sum) = refs[:12]
    outs, conv = (refs[12:-1], refs[-1])
    place = Place(dims.row_count, dims.col_count)
    rows, cols, channels, h, size = (dims.rows, dims.cols, dims.channels, dims.h, dims.size)
    ext_rows, ext_cols, wide = (dims.ext_rows, dims.ext_cols, dims.wide)
    skip = dims.skipped_rows(place)
    read = received(place, strips, (0, 0))
    assemble(place, x0, lambda i: image[i].astype(f32), read, 2 * h, rows, cols, channels)

    x1[...] = jnp.zeros(x1.shape, f32)
    if dims.ext_pad > ext_rows * ext_cols:
        conv[ext_rows * ext_cols :, :] = jnp.zeros((dims.ext_pad - ext_rows * ext_cols, LANES), f32)
    frame = pl.multiple_of(skip * ext_cols, 8)

    def conv0(g, carry):
        at = group_start(g, ext_cols)
        base = pl.multiple_of(skip * wide, 8) + at
        total = conv_group(x0, base + 1, wide, ext_rows, taps0, size)
        for r in range(ext_rows):
            conv[pl.ds(r * ext_cols + at, 16), :] = total[r]
            x1[pl.ds(frame + r * ext_cols + at, 16), :] = x0[pl.ds(base + (r + h) * wide + 4, 16), :]
        return carry

    lax.fori_loop(0, -(-ext_cols // 16), conv0, 0)
    gain = pad_lanes(gains[0:1, :])
    ones = diagonal(jnp.ones((LANES, LANES), bf16), jnp.ones((LANES, LANES), bf16))
    half = dims.ext_pad // 2

    def mix0(start, n):
        spans = [(start, n), (half + start, n)]
        parts = yield from layer_norm([conv[at : at + n, :] for at, n in spans], gain, channels, ones)
        pres = dot(side_by_side(parts[0][2], parts[1][2]), forward0[...])
        yield
        count = pres.shape[1] // 2
        hiddens = []
        for k, ((at, n), (unit, inverse, _)) in enumerate(zip(spans, parts)):
            unit0[at : at + n, :] = unit.astype(bf16)
            inv0[at : at + n, :] = inverse

            def activate(pre):
                value, slope = gelu_parts(pre)
                return (value.astype(bf16), slope.astype(bf16))

            hidden, slope = by_blocks(activate, pres[:, k * count : (k + 1) * count])
            hidden0[at : at + n, :] = hidden
            slope0[at : at + n, :] = slope
            hiddens.append(hidden)
        branches = dot(side_by_side(*hiddens), back0[...])
        yield
        for k, (at, n) in enumerate(spans):
            px = pl.ds(frame + at, n)
            x1[px, :] = round16(x1[px, :] + branches[:, k * LANES : (k + 1) * LANES])
    together([mix0(start, n) for start, n in pieces(half, dims.piece)])
    clear_outside(place, x1, dims)

    def conv1(g, carry):
        at = group_start(g, cols)
        total = conv_group(x1, at + 1, ext_cols, rows, taps1, size)
        for r in range(rows):
            conv[pl.ds(r * cols + at, 16), :] = total[r]
        return carry

    lax.fori_loop(0, -(-cols // 16), conv1, 0)
    gain1 = pad_lanes(gains[1:2, :])
    gain_sum[...] = jnp.zeros(gain_sum.shape, f32)
    lines = dims.line_step
    step = lines * cols

    def mix1(k):
        px = slice(k * step, (k + 1) * step)
        middle = k * step + step // 2
        parts = yield from layer_norm(
            [conv[k * step : middle, :], conv[middle : (k + 1) * step, :]], gain1, channels, ones
        )
        unit, inverse, normed = (jnp.concatenate(pair, axis=0) for pair in zip(*parts))
        normed1[px, :] = normed
        upstream = pad_lanes(cot[k * lines : (k + 1) * lines].reshape(step, channels))
        both = dot(side_by_side(normed, upstream), forward1[...])
        yield

        def activate(pre, hidden_grad):
            value, slope = gelu_parts(pre)
            return (value.astype(bf16), (hidden_grad * slope).astype(bf16))

        count = both.shape[1] // 2
        hidden, pre_grad = by_blocks(activate, both[:, :count], both[:, count:])
        hidden1[px, :] = hidden
        pre_grad1[px, :] = pre_grad
        both = dot(side_by_side(hidden, pre_grad), back1[...])
        yield
        branch, normed_grad = (both[:, :LANES], both[:, LANES:])
        for i in range(lines):
            start = (k * lines + i + h) * ext_cols + 4
            line = x1[start : start + cols, :] + branch[i * cols : (i + 1) * cols]
            output[k * lines + i] = line[:, :channels].astype(bf16)
        product = normed_grad * unit
        gain_sum[...] += jnp.sum(product.reshape(step // 8, 8, LANES), axis=0)
        grad1[px, :] = yield from norm_backward(normed_grad, unit, inverse, gain1, channels, ones)

    together([mix1(k) for k in range(rows // lines)])

    takes = [(flat_take(grad1, cols, channels), 2 * h, rows, cols), (image_take(cot), h, rows, cols)]
    write_strips(place, outs, takes, band_combos(dims.row_count))


def clear_outside(place, flat, dims):
    h, frame_rows, ext_cols = (dims.h, dims.rows + 2 * dims.h, dims.ext_cols)
    margin = (ext_cols - dims.cols) // 2

    @pl.when(jnp.logical_not(place.has["above"]))
    def _():
        flat[0 : h * ext_cols, :] = jnp.zeros((h * ext_cols, LANES), f32)

    @pl.when(jnp.logical_not(place.has["below"]))
    def _():
        last = (frame_rows - h) * ext_cols
        flat[last:, :] = jnp.zeros((flat.shape[0] - last, LANES), f32)

    @pl.when(jnp.logical_not(place.has["left"]))
    def _():
        for r in range(frame_rows):
            flat[r * ext_cols : r * ext_cols + margin, :] = jnp.zeros((margin, LANES), f32)

    @pl.when(jnp.logical_not(place.has["right"]))
    def _():
        for r in range(frame_rows):
            flat[(r + 1) * ext_cols - margin : (r + 1) * ext_cols, :] = jnp.zeros((margin, LANES), f32)


def sums_kernel(
    dims, x1, grad1, normed1, pre_grad1, hidden1, cot, gain_part, final, taps_sum, up_sum, down_sum, output, sums
):
    output[...] = final[...]
    together([kernel_sums(x1, 1, dims.ext_cols, grad1, 0, dims.cols, dims.rows, dims.cols, dims.size, sums)])
    store_sums(dims, sums, gain_part[...], taps_sum)
    upstream = pad_lanes(cot[...].reshape(dims.rows * dims.cols, dims.channels))
    up_sum[...] = dot_leading(normed1[...], pre_grad1[...]).T
    down_sum[...] = dot_leading(upstream, hidden1[...]).T


def store_sums(dims, sums, gain_part, target):
    taps = dims.size * dims.size
    target[...] = jnp.zeros(target.shape, f32)
    for t in range(taps):
        target[t : t + 1, :] = jnp.sum(sums[t * 8 : t * 8 + 8, :], axis=0, keepdims=True)
    target[taps : taps + 1, :] = jnp.sum(gain_part, axis=0, keepdims=True)


def third_kernel(dims, *refs):
    count = len(combos(dims.row_count))
    (grad1, cot, taps1, gains, grad_in0, grad_out0, x0, unit0, inv0, hidden0, slope0) = refs[:11]
    (taps_sum1, up_sum1, down_sum1) = refs[11:14]
    strips = refs[14 : 14 + count]
    (grad0, middle, keep, small_keep, send) = refs[14 + count : 19 + count]
    (wide_grad, cot_frame, upstream, own, sums, normed0, flow0, pre_grad0, up_acc, down_acc, gain_sum, small, tall, slabs) = refs[19 + count :]
    place = Place(dims.row_count, dims.col_count)
    rows, cols, channels, h, size = (dims.rows, dims.cols, dims.channels, dims.h, dims.size)
    ext_rows, ext_cols, wide = (dims.ext_rows, dims.ext_cols, dims.wide)
    skip = dims.skipped_rows(place)
    read = received(place, strips, (0, 0))
    assemble(
        place, wide_grad, lambda i: grad1[i * cols : (i + 1) * cols, 0:channels], read, 2 * h, rows, cols, channels
    )
    read_cot = received(place, strips, (rows, 2 * h))
    margin = (ext_cols - cols) // 2
    cot_frame[...] = jnp.zeros(cot_frame.shape, f32)
    for vertical, start, n in (("above", 0, h), (None, h, rows), ("below", h + rows, h)):
        for i in range(n):
            base = (start + i) * ext_cols
            line = cot[i].astype(f32) if vertical is None else read_cot(vertical, None, i)
            cot_frame[base + margin : base + margin + cols, 0:channels] = line
            cot_frame[base : base + margin, 0:channels] = read_cot(vertical, "left", i)[SIDE - margin :]
            cot_frame[base + margin + cols : base + ext_cols, 0:channels] = read_cot(vertical, "right", i)[:margin]

    used = ext_rows * ext_cols
    if dims.ext_pad > used:
        upstream[used:, :] = jnp.zeros((dims.ext_pad - used, LANES), f32)
        own[used:, :] = jnp.zeros((dims.ext_pad - used, LANES), f32)
    grad0[...] = jnp.zeros(grad0.shape, f32)
    frame = pl.multiple_of(skip * ext_cols, 8)

    def conv1(g, carry):
        at = group_start(g, ext_cols)
        total = conv_group(wide_grad, pl.multiple_of(skip * wide, 8) + at + 1, wide, ext_rows, taps1, size, True)
        col = lax.broadcasted_iota(jnp.int32, (16, LANES), 0) + (at - margin)
        inside = jnp.where(jnp.logical_and(col >= 0, col < cols), 1.0, 0.0)
        for r in range(ext_rows):
            px = pl.ds(r * ext_cols + at, 16)
            upstream[px, :] = cot_frame[pl.ds(frame + r * ext_cols + at, 16), :] + total[r]
            mine = jnp.logical_and(r + skip >= h, r + skip < h + rows)
            own[px, :] = jnp.where(mine, inside, 0.0)
        return carry

    lax.fori_loop(0, -(-ext_cols // 16), conv1, 0)
    for i in range(rows):
        line = upstream[pl.ds((i + h - skip) * ext_cols + margin, cols), :]
        middle[i * cols : (i + 1) * cols, :] = round16(line)

    gain = pad_lanes(gains[0:1, :])
    gain_sum[...] = jnp.zeros(gain_sum.shape, f32)
    ones = diagonal(jnp.ones((LANES, LANES), bf16), jnp.ones((LANES, LANES), bf16))
    half_px = dims.ext_pad // 2

    def mix0(start, n):
        spans = [(start, n), (half_px + start, n)]
        flows = [upstream[at : at + n, :].astype(bf16) for at, n in spans]
        hidden_grads = dot(side_by_side(*flows), grad_in0[...])
        yield
        count = hidden_grads.shape[1] // 2

        def slope_times(grad, slope):
            return ((grad * slope.astype(f32)).astype(bf16),)

        pre_grads = [
            by_blocks(slope_times, hidden_grads[:, k * count : (k + 1) * count], slope0[at : at + n, :])[0]
            for k, (at, n) in enumerate(spans)
        ]
        both = dot(side_by_side(*pre_grads), grad_out0[...])
        yield
        normed_grads = (both[:, :LANES], both[:, LANES:])
        for (at, n), flow, pre_grad, normed_grad in zip(spans, flows, pre_grads, normed_grads):
            mine = own[at : at + n, :]
            unit = unit0[at : at + n, :].astype(f32)
            normed0[at : at + n, :] = (unit * gain * mine).astype(bf16)
            flow0[at : at + n, :] = flow * mine.astype(bf16)
            pre_grad0[at : at + n, :] = pre_grad
            product = normed_grad * unit * mine
            gain_sum[...] += jnp.sum(product.reshape(n // 8, 8, LANES), axis=0)
            grad = yield from norm_backward(normed_grad, unit, inv0[at : at + n, :], gain, channels, ones)
            grad0[pl.ds(frame + at, n), :] = grad

    together([mix0(start, n) for start, n in pieces(half_px, dims.piece)])
    clear_outside(place, grad0, dims)
    at_x0, at_grad0 = (h * wide + SIDE - h, h * ext_cols + margin)
    together(
        [
            weight_sum(normed0, pre_grad0, up_acc, 2 * dims.piece),
            kernel_sums(x0, at_x0, wide, grad0, at_grad0, ext_cols, rows, cols, size, sums),
            weight_sum(flow0, hidden0, down_acc, 2 * dims.piece),
        ]
    )
    store_sums(dims, sums, gain_sum[...], small)

    taps_rows = size * size + 1
    merged = jnp.concatenate([small[0:taps_rows, :], taps_sum1[0:taps_rows, :]], axis=0) * dims.factor
    merged = fold_rows(merged, dims.small_rows, channels).astype(bf16)
    small_keep[...] = merged.astype(f32)

    layer_rows, part, half = (dims.layer_rows, dims.part, dims.half)
    units = hidden0.shape[1]
    up0 = up_acc[...].T * dims.factor
    down0 = down_acc[...].T * dims.factor
    up1 = up_sum1[...] * dims.factor
    down1 = down_sum1[...] * dims.factor
    lane = lax.broadcasted_iota(jnp.int32, (units, LANES), 1)
    slab_rows = 2 * layer_rows
    for r in range(dims.row_count):
        for layer, (u, d) in enumerate(((up0, down0), (up1, down1))):
            first = pltpu.roll(u, LANES - r * half, 1) if r else u
            shift = (half - r * half) % LANES
            second = pltpu.roll(d, shift, 1) if shift else d
            joined = jnp.where(lane < half, first, jnp.where(lane < 2 * half, second, 0.0))
            tall[layer * (units + 8) : layer * (units + 8) + units, :] = joined

        for c in range(dims.col_count):
            index = 0
            for axis, bit in dims.stages:
                index = 2 * index + ((r if axis == "row" else c) >> bit & 1)
            for layer in range(2):
                to, at = (index * slab_rows + layer * layer_rows, layer * (units + 8) + c * part)
                slabs[to : to + layer_rows, :] = tall[at : at + layer_rows, :]

    split(dims, 0, slabs, merged, keep, (send,))


def fold_rows(x, rows, used):
    n = x.shape[0]
    if rows >= n:
        return pad_rows(x, rows)
    assert used <= 96
    stride = ceil8(n - rows)
    rest = pad_rows(x[rows:], stride)
    pieces_of = pad_rows(jnp.concatenate([pltpu.roll(rest, 96 - 32 * k, 1) for k in range(3)], axis=0), rows)
    lane = lax.broadcasted_iota(jnp.int32, (rows, LANES), 1)
    return jnp.where(lane < 96, x[:rows], pieces_of)


def pad_rows(x, rows):
    if rows == x.shape[0]:
        return x
    return jnp.concatenate([x, jnp.zeros((rows - x.shape[0], LANES), x.dtype)], axis=0)


def unfold_rows(x, n):
    rows = x.shape[0]
    if rows >= n:
        return x[:n]
    stride = ceil8(n - rows)
    lane = lax.broadcasted_iota(jnp.int32, (stride, LANES), 1)
    rest = jnp.zeros((stride, LANES), x.dtype)
    for k in range(3):
        moved = pltpu.roll(x[k * stride : (k + 1) * stride], 32 + 32 * k, 1)
        rest = jnp.where(jnp.logical_and(lane >= 32 * k, lane < 32 * k + 32), moved, rest)
    return jnp.concatenate([x, rest[: n - rows]], axis=0)


def split(dims, stage, slabs, merged, keep, sends):
    group = dims.groups[stage]
    count = slabs.shape[0] >> len(group)
    mine = 0
    for axis, bit in group:
        mine = mine * 2 + lax.rem(lax.div(lax.axis_index(axis), 1 << bit), 2)
    keep[...] = slabs[pl.ds(pl.multiple_of(mine * count, 16), count), :]
    for mask, send in enumerate(sends, 1):
        other = 0
        for j in range(len(group)):
            weight = 1 << j
            digit = lax.rem(lax.div(mine, weight), 2)
            other = other + weight * (1 - digit if mask & weight else digit)
        send[0:count, :] = slabs[pl.ds(pl.multiple_of(other * count, 16), count), :].astype(bf16)
        send[count:, :] = merged


def gather_up(keep, small, gots):
    count = keep.shape[0]
    slabs = [keep[...]] + [got[0:count, :].astype(f32) for got in gots]
    sums = [small[...]] + [got[count:, :].astype(f32) for got in gots]
    if len(gots) == 1:
        return (slabs[0] + slabs[1], sums[0] + sums[1])
    return tuple((x[0] + x[1]) + (x[2] + x[3]) for x in (slabs, sums))


def stage_kernel(dims, stage, keep, small, *refs):
    before, after = (len_sends(dims.groups[stage - 1]), len_sends(dims.groups[stage]))
    gots = refs[:before]
    keep_out, small_out = refs[-3 - after : -1 - after]
    sends, total = (refs[-1 - after : -1], refs[-1])
    slabs, merged = gather_up(keep, small, gots)
    total[...] = slabs
    merged = merged.astype(bf16)
    small_out[...] = merged.astype(f32)
    split(dims, stage, total, merged, keep_out, sends)


def len_sends(group):
    return (1 << len(group)) - 1


def last_kernel(dims, keep, small, *refs):
    gots, (kernel_out, gain_out, up_out, down_out) = (refs[:-4], refs[-4:])
    total, merged = gather_up(keep, small, gots)
    merged = unfold_rows(merged, 2 * (dims.size * dims.size + 1))
    size, channels, half, part = (dims.size, dims.channels, dims.half, dims.part)
    for layer in range(2):
        block = total[layer * dims.layer_rows : layer * dims.layer_rows + part]
        up_out[layer] = block[:, :half]
        down_out[layer] = block[:, half : 2 * half]
        for t in range(size * size + 1):
            at = layer * (size * size + 1) + t
            row = merged[at : at + 1, 0:channels]
            if t < size * size:
                kernel_out[t // size, t % size, layer : layer + 1, :] = row
            else:
                gain_out[layer : layer + 1, :] = row


def image_kernel(dims, grad0, middle, taps0, after, out, ready, work):
    rows, cols, size = (dims.rows, dims.cols, dims.size)

    def conv0(g, carry):
        at = group_start(g, cols)
        total = conv_group(grad0, at + 1, dims.ext_cols, rows, taps0, size, True)
        for r in range(rows):
            work[pl.ds(r * cols + at, 16), :] = middle[pl.ds(r * cols + at, 16), :] + total[r]
        return carry

    lax.fori_loop(0, -(-cols // 16), conv0, 0)
    for r in range(rows):
        out[r] = work[r * cols : (r + 1) * cols, 0 : dims.channels].astype(bf16)
    ready[...] = jnp.zeros(ready.shape, f32)


class Dims:
    def skipped_rows(self, place):
        if self.row_count > 2:
            return 0
        return jnp.where(place.has["above"], 0, self.h)


def dims_of(image, kernels, up_weights):
    d = Dims()
    d.row_count, d.col_count = (lax.axis_size("row"), lax.axis_size("col"))
    d.rows, d.cols, d.channels = image.shape
    d.size = kernels.shape[1]
    d.h = d.size // 2
    d.ext_rows, d.ext_cols = (d.rows + (d.h if d.row_count == 2 else 2 * d.h), d.cols + 8)
    d.wide = d.cols + 2 * SIDE
    d.ext_pad = -(-d.ext_rows * d.ext_cols // 32) * 32
    d.piece = 176
    d.line_step = 4
    d.half = d.channels // d.row_count
    d.part = up_weights.shape[2] // d.col_count
    d.layer_rows = ceil8(d.part)
    d.count = d.row_count * d.col_count
    d.small_rows = 80 if d.size == 7 and d.channels <= 96 else -(-2 * (d.size * d.size + 1) // 16) * 16
    d.factor = 1.0 / math.sqrt(d.rows * d.cols * d.count)
    row_bits, col_bits = (d.row_count.bit_length() - 1, d.col_count.bit_length() - 1)
    bits = [("row", b) for b in range(row_bits)] + [("col", b) for b in range(1, col_bits)]
    d.groups = [[("col", 0)]] + [bits[i : i + 2] for i in range(0, len(bits), 2)]
    d.stages = [bit for group in d.groups for bit in group]
    return d


def swap_by(d, group, mask):
    flip = {"row": 0, "col": 0}
    for j, (axis, bit) in enumerate(group):
        if mask >> (len(group) - 1 - j) & 1:
            flip[axis] |= 1 << bit
    pairs = []
    for r in range(d.row_count):
        for c in range(d.col_count):
            pairs.append((r * d.col_count + c, (r ^ flip["row"]) * d.col_count + (c ^ flip["col"])))
    return pairs


def run(kernel, outs, scratch, *args, in_hbm=0, sems=0, busy_us=1):
    shapes = [jax.ShapeDtypeStruct(shape, kind) for shape, kind in outs]
    space = pl.BlockSpec(memory_space=pltpu.VMEM)
    far = pl.BlockSpec(memory_space=pltpu.HBM)
    held = [pltpu.VMEM(shape, kind) for shape, kind in scratch]
    if sems:
        held.append(pltpu.SemaphoreType.DMA((sems,)))
    return pl.pallas_call(
        kernel,
        out_shape=shapes,
        in_specs=[far] * in_hbm + [space] * (len(args) - in_hbm),
        out_specs=[space] * len(shapes),
        scratch_shapes=held,
        compiler_params=pltpu.CompilerParams(vmem_limit_bytes=32 * 1024 * 1024),
        cost_estimate=pl.CostEstimate(flops=int(busy_us * 1e9), bytes_accessed=1 << 18, transcendentals=0),
    )(*args)


def per_device(image, kernels, gains, up_weights, down_weights, cotangent):
    d = dims_of(image, kernels, up_weights)
    bind = functools.partial
    rows, cols, channels = image.shape
    units = up_weights.shape[2]
    tile, ext, wide = (rows * cols, d.ext_pad, (rows + 4 * d.h) * d.wide)
    frame = (rows + 2 * d.h) * d.ext_cols + 16
    taps = ((d.size * d.size * 16, LANES), bf16)
    tap_sums = ((d.size * d.size * 8, LANES), f32)
    sums_rows = ceil8(d.size * d.size + 1)

    bands, others = (band_combos(d.row_count), other_combos(d.row_count))

    def strips_of(pairs, radii):
        return [(shape, bf16) for shape in strip_shapes(pairs, rows, cols, channels, radii)]

    image, *band_strips = run(
        bind(bands_kernel, d), [(image.shape, bf16)] + strips_of(bands, (2 * d.h,)), [], image, in_hbm=1, sems=1
    )
    other_strips = run(bind(others_kernel, d), strips_of(others, (2 * d.h,)), [], image, *band_strips)
    strips = exchange(band_strips, other_strips, d.row_count, d.col_count)
    mixing = [((2 * LANES, 2 * units), bf16), ((2 * units, 2 * LANES), bf16)]
    forward0, back0, forward1, back1, grad_in0, grad_out0, taps0, taps1, gains = run(
        weights_kernel,
        mixing * 3 + [taps, taps, (gains.shape, f32)],
        [((2, channels, units), bf16), ((2, channels, units), bf16), ((d.size, d.size, 2, channels), f32)],
        up_weights,
        jnp.swapaxes(down_weights, 1, 2),
        jnp.transpose(kernels, (1, 2, 0, 3)),
        gains,
        in_hbm=4,
        sems=4,
        busy_us=2,
    )

    first = run(
        bind(first_kernel, d),
        [
            (image.shape, bf16),
            ((wide, LANES), f32),
            ((frame, LANES), f32),
            ((ext, LANES), bf16),
            ((ext, LANES), f32),
            ((ext, units), bf16),
            ((ext, units), bf16),
            ((tile, LANES), f32),
            ((tile, LANES), bf16),
            ((tile, units), bf16),
            ((tile, units), bf16),
            ((8, LANES), f32),
        ]
        + strips_of(bands, (2 * d.h, d.h)),
        [((ext, LANES), f32)],
        image,
        cotangent,
        taps0,
        taps1,
        gains,
        forward0,
        back0,
        forward1,
        back1,
        *strips,
        busy_us=15,
    )
    (final, x0, x1, unit0, inv0, hidden0, slope0, grad1, normed1, pre_grad1, hidden1, gain_part) = first[:12]
    band_strips = first[12:]
    other_strips = run(
        bind(grad_others_kernel, d), strips_of(others, (2 * d.h, d.h)), [], grad1, cotangent, *band_strips
    )
    strips = exchange(band_strips, other_strips, d.row_count, d.col_count)

    taps_sum1, up_sum1, down_sum1, output = run(
        bind(sums_kernel, d),
        [((sums_rows, LANES), f32), ((units, LANES), f32), ((units, LANES), f32), (image.shape, bf16)],
        [tap_sums],
        x1,
        grad1,
        normed1,
        pre_grad1,
        hidden1,
        cotangent,
        gain_part,
        final,
        busy_us=3,
    )

    held = d.count // 2 * 2 * d.layer_rows
    small = ((d.small_rows, LANES), f32)
    grad0, middle, keep, sums, send = run(
        bind(third_kernel, d),
        [((frame, LANES), f32), ((tile, LANES), f32), ((held, LANES), f32), small, ((held + d.small_rows, LANES), bf16)],
        [
            ((wide, LANES), f32),
            ((frame, LANES), f32),
            ((ext, LANES), f32),
            ((ext, LANES), f32),
            tap_sums,
            ((ext, LANES), bf16),
            ((ext, LANES), bf16),
            ((ext, units), bf16),
            ((LANES, units), f32),
            ((LANES, units), f32),
            ((8, LANES), f32),
            ((sums_rows, LANES), f32),
            ((2 * (units + 8), LANES), f32),
            ((2 * held, LANES), f32),
        ],
        grad1,
        cotangent,
        taps1,
        gains,
        grad_in0,
        grad_out0,
        x0,
        unit0,
        inv0,
        hidden0,
        slope0,
        taps_sum1,
        up_sum1,
        down_sum1,
        *strips,
        busy_us=12,
    )
    axes = ("row", "col")
    sends = [send]
    for stage, group in enumerate(d.groups):
        order = sorted(range(1, len(sends) + 1), key=lambda mask: (3, 1, 2).index(mask))
        gots = {mask: lax.ppermute(sends[mask - 1], axes, swap_by(d, group, mask)) for mask in order}
        gots = [gots[mask] for mask in sorted(gots)]
        ready = []
        if stage == 1:
            gradient, *ready = run(
                bind(image_kernel, d),
                [(image.shape, bf16), ((8, LANES), f32)],
                [((tile, LANES), f32)],
                grad0,
                middle,
                taps0,
                sums,
                busy_us=3,
            )
        if stage + 1 < len(d.groups):
            after = d.groups[stage + 1]
            whole, held = (held, held >> len(after))
            keep, sums, *sends = run(
                bind(stage_kernel, d, stage + 1),
                [((held, LANES), f32), small] + [((held + d.small_rows, LANES), bf16)] * len_sends(after),
                [((whole, LANES), f32)],
                keep,
                sums,
                *gots,
                *ready,
            )
    kernel_out, gain_out, up_out, down_out = run(
        bind(last_kernel, d),
        [
            ((d.size, d.size, 2, channels), f32),
            (gains.shape, f32),
            ((2, d.part, d.half), f32),
            ((2, d.part, d.half), f32),
        ],
        [],
        keep,
        sums,
        *gots,
    )
    kernel_out = jnp.transpose(kernel_out, (2, 0, 1, 3))
    return (output, gradient, kernel_out, gain_out, jnp.swapaxes(up_out, 1, 2), down_out)


def solution(mesh):
    placed = (P("row", "col", None), P(), P(), P(), P(), P("row", "col", None))
    return jax.shard_map(
        per_device,
        mesh=mesh,
        in_specs=placed,
        out_specs=(
            P("row", "col", None),
            P("row", "col", None),
            P(),
            P(),
            P(None, "row", "col"),
            P(None, "col", "row"),
        ),
        check_vma=False,
    )
```

```python
import functools
import math

import jax
import jax.numpy as jnp
from jax import lax
from jax.experimental import pallas as pl
from jax.experimental.pallas import tpu as pltpu
from jax.sharding import PartitionSpec as P

epsilon = 1e-06
inv_sqrt_two = 0.7071067811865476
inv_sqrt_two_pi = 0.3989422804014327
log2_e = 1.4426950408889634
LANES = 128
SIDE = 8
f32, bf16 = (jnp.float32, jnp.bfloat16)


def ceil8(n):
    return -(-n // 8) * 8


def combos(row_count):
    listed = [(None, 0), (None, 1), (0, None), (0, 0), (0, 1)]
    if row_count > 2:
        listed += [(1, None), (1, 0), (1, 1)]
    return listed


def partner(index, start, count):
    if start is None:
        return index
    other = index + 1 if (index - start) % 2 == 0 else index - 1
    return other if 0 <= other < count else None


def swap_pairs(row_count, col_count, row_start, col_start):
    pairs = []
    for r in range(row_count):
        for c in range(col_count):
            pr, pc = (partner(r, row_start, row_count), partner(c, col_start, col_count))
            if pr is None:
                pr, pc = (r, c ^ 1)
            elif pc is None:
                pr, pc = (r ^ 1 if row_start is None else pr, c)
            pairs.append((r * col_count + c, pr * col_count + pc))
    return pairs


def exchange(bands, others, row_count, col_count):
    got = {}
    for strips, pairs in ((bands, band_combos(row_count)), (others, other_combos(row_count))):
        for strip, (rs, cs) in zip(strips, pairs):
            got[rs, cs] = lax.ppermute(strip, ("row", "col"), swap_pairs(row_count, col_count, rs, cs))
    return [got[pair] for pair in combos(row_count)]


class Place:
    def __init__(self, row_count, col_count):
        row, col = (lax.axis_index("row"), lax.axis_index("col"))
        self.even_row, self.even_col = (lax.rem(row, 2) == 0, lax.rem(col, 2) == 0)
        self.has = {
            "above": row > 0,
            "below": row < row_count - 1,
            "left": col > 0,
            "right": col < col_count - 1,
        }
        self.row_count = row_count


def band_combos(row_count):
    return [pair for pair in combos(row_count) if pair[1] is None]


def other_combos(row_count):
    return [pair for pair in combos(row_count) if pair[1] is not None]


def write_strips(place, outs, takes, pairs):
    for out, (rs, cs) in zip(outs, pairs):
        at = 0
        for take, radius, rows, cols in takes:
            row_sets = [slice(0, rows)] * 2
            col_sets = [slice(0, cols)] * 2
            if rs is not None:
                row_sets = [slice(rows - radius, rows), slice(0, radius)]
                if rs == 1:
                    row_sets = row_sets[::-1]
            if cs is not None:
                col_sets = [slice(cols - SIDE, cols), slice(0, SIDE)]
                if cs == 1:
                    col_sets = col_sets[::-1]
            count = row_sets[0].stop - row_sets[0].start
            for i in range(count):
                parts = {}
                for er in (0, 1):
                    for ec in (0, 1):
                        key = (row_sets[er].start + i, col_sets[ec].start, col_sets[ec].stop)
                        if key not in parts:
                            parts[key] = take(*key)
                        parts[er, ec] = parts[key]
                if cs is None:
                    pick = [parts[0, 0], parts[1, 0]]
                else:
                    pick = [jnp.where(place.even_col, parts[e, 0], parts[e, 1]) for e in (0, 1)]
                value = pick[0] if rs is None else jnp.where(place.even_row, pick[0], pick[1])
                out[at + i] = value.astype(out.dtype)
            at += count


def strip_shapes(pairs, rows, cols, channels, radii):
    shapes = []
    for rs, cs in pairs:
        height = sum(rows if rs is None else radius for radius in radii)
        shapes.append((height, cols if cs is None else SIDE, channels))
    return shapes


def received(place, strips, row_sections):
    table = dict(zip(combos(place.row_count), strips))
    full_start, band_start = row_sections

    def along(rs, cs, i):
        return table[rs, cs][(full_start if rs is None else band_start) + i].astype(f32)

    def column(rs, side, i):
        if side is None:
            return along(rs, None, i)
        near, far = (along(rs, 0, i), along(rs, 1, i))
        if side == "left":
            return jnp.where(place.even_col, far, near)
        return jnp.where(place.even_col, near, far)

    def read(vertical, side, i):
        if vertical is None:
            value = column(None, side, i)
        elif place.row_count == 2:
            value = column(0, side, i)
        else:
            near, far = (column(0, side, i), column(1, side, i))
            if vertical == "above":
                value = jnp.where(place.even_row, far, near)
            else:
                value = jnp.where(place.even_row, near, far)
        if vertical is not None:
            value = jnp.where(place.has[vertical], value, 0.0)
        if side is not None:
            value = jnp.where(place.has[side], value, 0.0)
        return value

    return read


def assemble(place, target, own, read, radius, rows, cols, channels):
    width = cols + 2 * SIDE
    target[...] = jnp.zeros(target.shape, f32)
    for vertical, start, count in (("above", 0, radius), (None, radius, rows), ("below", radius + rows, radius)):
        for i in range(count):
            base = (start + i) * width
            middle = own(i) if vertical is None else read(vertical, None, i)
            target[base + SIDE : base + SIDE + cols, 0:channels] = middle
            target[base : base + SIDE, 0:channels] = read(vertical, "left", i)
            target[base + SIDE + cols : base + width, 0:channels] = read(vertical, "right", i)


def spread_taps(kernel_ref, layer, target):
    size, channels = (kernel_ref.shape[0], kernel_ref.shape[3])
    for a in range(size):
        for b in range(size):
            t = a * size + b
            row = pad_lanes(kernel_ref[a, b, layer : layer + 1, :])
            target[t * 16 : t * 16 + 16, :] = jnp.broadcast_to(row, (16, LANES)).astype(bf16)


def tree_sum(terms):
    while len(terms) > 1:
        pairs = [terms[i] + terms[i + 1] for i in range(0, len(terms) - 1, 2)]
        terms = pairs + ([terms[-1]] if len(terms) % 2 else [])
    return terms[0]


def conv_group(src, base, stride, rows_out, taps, size, flipped=False):
    total = [None] * rows_out
    for first in range(0, size, 2):
        columns = range(first, min(first + 2, size))
        weights = []
        for b in columns:
            order = [a * size + b for a in range(size)]
            if flipped:
                order = [size * size - 1 - t for t in order]
            weights.append([taps[t * 16 : t * 16 + 16, :] for t in order])
        windows = [[] for _ in columns]
        for i in range(rows_out + size - 1):
            for window, b in zip(windows, columns):
                window.append(src[pl.ds(base + i * stride + b, 16), :].astype(bf16))
            r = i - size + 1
            if r >= 0:
                sums = [
                    tree_sum([window[r + a] * weight[a] for a in range(size)])
                    for window, weight in zip(windows, weights)
                ]
                term = tree_sum(sums).astype(f32)
                total[r] = term if total[r] is None else total[r] + term
    return total


def group_start(g, cols):
    return pl.multiple_of(jnp.minimum(g * 16, cols - 16), 8)


def kernel_sums(src, src_base, src_stride, grad, grad_base, grad_stride, rows, cols, size, sums):
    sums[...] = jnp.zeros(sums.shape, f32)

    def group(g, carry):
        at = pl.multiple_of(g * 16, 16)
        grads = [grad[pl.ds(grad_base + i * grad_stride + at, 16), :].astype(bf16) for i in range(rows)]
        for b in range(size):
            lines = [
                src[pl.ds(src_base + i * src_stride + at + b, 16), :].astype(bf16) for i in range(rows + size - 1)
            ]
            for a in range(size):
                term = tree_sum([lines[r + a] * grads[r] for r in range(rows)]).astype(f32)
                t = (a * size + b) * 8
                sums[t : t + 8, :] += term[0:8] + term[8:16]
        return carry

    lax.fori_loop(0, cols // 16, group, 0)


def diagonal(first, second):
    top = jnp.concatenate([first, jnp.zeros((first.shape[0], second.shape[1]), first.dtype)], axis=1)
    bottom = jnp.concatenate([jnp.zeros((second.shape[0], first.shape[1]), first.dtype), second], axis=1)
    return jnp.concatenate([top, bottom], axis=0)


def together(steps):
    steps = list(steps)
    while steps:
        steps = [step for step in steps if next(step, steps) is not steps]


def by_blocks(function, *arrays, size=16):
    count = arrays[0].shape[0]
    results = [function(*(x[i : i + size] for x in arrays)) for i in range(0, count, size)]
    return tuple(jnp.concatenate(parts, axis=0) for parts in zip(*results))


def in_channels(shape, channels):
    return lax.broadcasted_iota(jnp.int32, shape, 1) < channels


def high_low(x):
    high = x.astype(bf16)
    return (jnp.concatenate([high, (x - high.astype(f32)).astype(bf16)], axis=1),)


def side_by_side(x, y):
    return jnp.concatenate([x, y], axis=1)


def layer_norm(parts, gain, channels, ones):
    def centre(x, total):
        centred = jnp.where(in_channels(x.shape, channels), x - total * (1.0 / channels), 0.0)
        return (centred, (centred * centred).astype(bf16))

    def finish(centred, total):
        inverse = lax.rsqrt(total * (1.0 / channels) + epsilon)
        unit = centred * inverse
        return (unit, inverse, (unit * gain).astype(bf16))

    totals = [dot(by_blocks(high_low, x)[0], jnp.ones((2 * LANES, LANES), bf16)) for x in parts]
    yield
    centred, squares = zip(*(by_blocks(centre, x, total) for x, total in zip(parts, totals)))
    variances = dot(side_by_side(*squares), ones)
    yield
    return [by_blocks(finish, c, variances[:, k * LANES : (k + 1) * LANES]) for k, c in enumerate(centred)]


def norm_backward(normed_grad, unit, inverse, gain, channels, ones):
    def products(normed_grad, unit):
        m = normed_grad * gain
        return (side_by_side(m.astype(bf16), (m * unit).astype(bf16)),)

    def finish(normed_grad, unit, inverse, sums):
        along = sums[:, :LANES] + unit * sums[:, LANES:]
        grad = inverse * (normed_grad * gain - along * (1.0 / channels))
        return (round16(jnp.where(in_channels(grad.shape, channels), grad, 0.0)),)

    sums = dot(by_blocks(products, normed_grad, unit)[0], ones)
    yield
    return by_blocks(finish, normed_grad, unit, inverse, sums)[0]


def gelu_parts(v):
    p = 0.3275911 * inv_sqrt_two
    c1, c2, c3, c4, c5 = (
        0.5 * c / p ** (k + 1)
        for k, c in enumerate((0.254829592, -0.284496736, 1.421413741, -1.453152027, 1.061405429))
    )
    t = pl.reciprocal(jnp.abs(v) + 1.0 / p, approx=True)
    bell = jnp.exp2(v * v * (-0.5 * log2_e))
    tail = ((((c5 * t + c4) * t + c3) * t + c2) * t + c1) * t * bell
    cdf = jnp.where(v >= 0.0, 1.0 - tail, tail)
    return (v * cdf, cdf + v * (bell * inv_sqrt_two_pi))


def dot(x, w):
    return jnp.dot(x, w, preferred_element_type=f32)


def dot_leading(x, y):
    return lax.dot_general(x, y, (((0,), (0,)), ((), ())), preferred_element_type=f32)


def pad_lanes(x):
    rows, channels = x.shape
    return jnp.concatenate([x, jnp.zeros((rows, LANES - channels), x.dtype)], axis=1)


def span(at, n, by=16):
    return pl.ds(pl.multiple_of(at, by), n)


def round16(x):
    return x.astype(bf16).astype(f32)


def fetch(sources, targets, sems):
    copies = [pltpu.make_async_copy(a, b, sems.at[i]) for i, (a, b) in enumerate(zip(sources, targets))]
    for copy in copies:
        copy.start()
    for copy in copies:
        copy.wait()


def image_take(ref):
    return lambda i, lo, hi: ref[i].astype(f32)[lo:hi]


def flat_take(ref, cols, channels):
    return lambda i, lo, hi: ref[i * cols + lo : i * cols + hi, 0:channels]


def bands_kernel(dims, image_in, image, *refs):
    outs, sems = (refs[:-1], refs[-1])
    place = Place(dims.row_count, dims.col_count)
    fetch((image_in,), (image,), sems)
    takes = [(image_take(image), 2 * dims.h, dims.rows, dims.cols)]
    write_strips(place, outs, takes, band_combos(dims.row_count))


def others_kernel(dims, image, *refs):
    outs = refs[len(band_combos(dims.row_count)) :]
    place = Place(dims.row_count, dims.col_count)
    takes = [(image_take(image), 2 * dims.h, dims.rows, dims.cols)]
    write_strips(place, outs, takes, other_combos(dims.row_count))


def grad_others_kernel(dims, grad1, cot, *refs):
    outs = refs[len(band_combos(dims.row_count)) :]
    place = Place(dims.row_count, dims.col_count)
    takes = [
        (flat_take(grad1, dims.cols, dims.channels), 2 * dims.h, dims.rows, dims.cols),
        (image_take(cot), dims.h, dims.rows, dims.cols),
    ]
    write_strips(place, outs, takes, other_combos(dims.row_count))


def weights_kernel(up_in, down_t_in, kernels_in, gains_in, *refs):
    forward0, back0, forward1, back1, grad_in0, grad_out0, taps0, taps1, gains, up_w, down_w, kernels, sems = refs
    fetch((up_in, down_t_in, kernels_in, gains_in), (up_w, down_w, kernels, gains), sems)
    spread_taps(kernels, 0, taps0)
    spread_taps(kernels, 1, taps1)
    channels, units = up_w.shape[1:]
    blank = jnp.zeros((LANES - channels, units), f32)
    wide, tall = ([], [])
    for layer in range(2):
        for ref in (up_w, down_w):
            full = jnp.concatenate([ref[layer].astype(f32), blank], axis=0)
            wide.append(full.astype(bf16))
            tall.append(full.T.astype(bf16))
    (up0, down_t0, up1, down_t1), (up_t0, down0, up_t1, down1) = (wide, tall)
    forward0[...] = diagonal(up0, up0)
    back0[...] = diagonal(down0, down0)
    forward1[...] = diagonal(up1, down_t1)
    back1[...] = diagonal(down1, up_t1)
    grad_in0[...] = diagonal(down_t0, down_t0)
    grad_out0[...] = diagonal(up_t0, up_t0)


def first_kernel(dims, *refs):
    count = len(combos(dims.row_count))
    image, cot, taps0, taps1, gains, forward0, back0, forward1, back1 = refs[:9]
    strips = refs[9 : 9 + count]
    refs = refs[9 + count :]
    (output, x0, x1, unit0, inv0, hidden0, slope0, grad1, normed1, pre_grad1, hidden1, gain_sum) = refs[:12]
    outs, conv = (refs[12:-1], refs[-1])
    place = Place(dims.row_count, dims.col_count)
    rows, cols, channels, h, size = (dims.rows, dims.cols, dims.channels, dims.h, dims.size)
    ext_rows, ext_cols, wide = (dims.ext_rows, dims.ext_cols, dims.wide)
    skip = dims.skipped_rows(place)
    read = received(place, strips, (0, 0))
    assemble(place, x0, lambda i: image[i].astype(f32), read, 2 * h, rows, cols, channels)

    x1[...] = jnp.zeros(x1.shape, f32)
    if dims.ext_pad > ext_rows * ext_cols:
        conv[ext_rows * ext_cols :, :] = jnp.zeros((dims.ext_pad - ext_rows * ext_cols, LANES), f32)
    frame = pl.multiple_of(skip * ext_cols, 8)

    def conv0(g, carry):
        at = group_start(g, ext_cols)
        base = pl.multiple_of(skip * wide, 8) + at
        total = conv_group(x0, base + 1, wide, ext_rows, taps0, size)
        for r in range(ext_rows):
            conv[pl.ds(r * ext_cols + at, 16), :] = total[r]
            x1[pl.ds(frame + r * ext_cols + at, 16), :] = x0[pl.ds(base + (r + h) * wide + 4, 16), :]
        return carry

    lax.fori_loop(0, -(-ext_cols // 16), conv0, 0)
    gain = pad_lanes(gains[0:1, :])
    ones = diagonal(jnp.ones((LANES, LANES), bf16), jnp.ones((LANES, LANES), bf16))
    half = dims.ext_pad // 2

    def mix0(start):
        n = dims.piece
        starts = (start, half + start)
        parts = yield from layer_norm([conv[span(at, n), :] for at in starts], gain, channels, ones)
        pres = dot(side_by_side(parts[0][2], parts[1][2]), forward0[...])
        yield
        count = pres.shape[1] // 2
        hiddens = []
        for k, (at, (unit, inverse, _)) in enumerate(zip(starts, parts)):
            unit0[span(at, n), :] = unit.astype(bf16)
            inv0[span(at, n), :] = inverse

            def activate(pre):
                value, slope = gelu_parts(pre)
                return (value.astype(bf16), slope.astype(bf16))

            hidden, slope = by_blocks(activate, pres[:, k * count : (k + 1) * count])
            hidden0[span(at, n), :] = hidden
            slope0[span(at, n), :] = slope
            hiddens.append(hidden)
        branches = dot(side_by_side(*hiddens), back0[...])
        yield
        for k, at in enumerate(starts):
            px = pl.ds(frame + pl.multiple_of(at, 16), n)
            x1[px, :] = round16(x1[px, :] + branches[:, k * LANES : (k + 1) * LANES])
    def two_pieces(i, carry):
        together([mix0((2 * i + j) * dims.piece) for j in range(2)])
        return carry

    lax.fori_loop(0, half // (2 * dims.piece), two_pieces, 0)
    clear_outside(place, x1, dims)

    def conv1(g, carry):
        at = group_start(g, cols)
        total = conv_group(x1, at + 1, ext_cols, rows, taps1, size)
        for r in range(rows):
            conv[pl.ds(r * cols + at, 16), :] = total[r]
        return carry

    lax.fori_loop(0, -(-cols // 16), conv1, 0)
    gain1 = pad_lanes(gains[1:2, :])
    gain_sum[...] = jnp.zeros(gain_sum.shape, f32)
    lines = dims.line_step
    step = lines * cols

    def mix1(k):
        px = span(k * step, step)
        half = step // 2
        parts = yield from layer_norm(
            [conv[span(k * step, half), :], conv[span(k * step + half, half), :]], gain1, channels, ones
        )
        unit, inverse, normed = (jnp.concatenate(pair, axis=0) for pair in zip(*parts))
        normed1[px, :] = normed
        upstream = pad_lanes(cot[pl.ds(k * lines, lines)].reshape(step, channels))
        both = dot(side_by_side(normed, upstream), forward1[...])
        yield

        def activate(pre, hidden_grad):
            value, slope = gelu_parts(pre)
            return (value.astype(bf16), (hidden_grad * slope).astype(bf16))

        count = both.shape[1] // 2
        hidden, pre_grad = by_blocks(activate, both[:, :count], both[:, count:])
        hidden1[px, :] = hidden
        pre_grad1[px, :] = pre_grad
        both = dot(side_by_side(hidden, pre_grad), back1[...])
        yield
        branch, normed_grad = (both[:, :LANES], both[:, LANES:])
        for i in range(lines):
            start = (k * lines + i + h) * ext_cols + 4
            line = x1[pl.ds(start, cols), :] + branch[i * cols : (i + 1) * cols]
            output[k * lines + i] = line[:, :channels].astype(bf16)
        product = normed_grad * unit
        gain_sum[...] += jnp.sum(product.reshape(step // 8, 8, LANES), axis=0)
        grad1[px, :] = yield from norm_backward(normed_grad, unit, inverse, gain1, channels, ones)

    def two_chunks(i, carry):
        together([mix1(2 * i + j) for j in range(2)])
        return carry

    lax.fori_loop(0, rows // (2 * lines), two_chunks, 0)

    takes = [(flat_take(grad1, cols, channels), 2 * h, rows, cols), (image_take(cot), h, rows, cols)]
    write_strips(place, outs, takes, band_combos(dims.row_count))


def clear_outside(place, flat, dims):
    h, frame_rows, ext_cols = (dims.h, dims.rows + 2 * dims.h, dims.ext_cols)
    margin = (ext_cols - dims.cols) // 2

    @pl.when(jnp.logical_not(place.has["above"]))
    def _():
        flat[0 : h * ext_cols, :] = jnp.zeros((h * ext_cols, LANES), f32)

    @pl.when(jnp.logical_not(place.has["below"]))
    def _():
        last = (frame_rows - h) * ext_cols
        flat[last:, :] = jnp.zeros((flat.shape[0] - last, LANES), f32)

    @pl.when(jnp.logical_not(place.has["left"]))
    def _():
        for r in range(frame_rows):
            flat[r * ext_cols : r * ext_cols + margin, :] = jnp.zeros((margin, LANES), f32)

    @pl.when(jnp.logical_not(place.has["right"]))
    def _():
        for r in range(frame_rows):
            flat[(r + 1) * ext_cols - margin : (r + 1) * ext_cols, :] = jnp.zeros((margin, LANES), f32)


def sums_kernel(
    dims, x1, grad1, normed1, pre_grad1, hidden1, cot, gain_part, final, taps_sum, up_sum, down_sum, output, sums
):
    output[...] = final[...]
    kernel_sums(x1, 1, dims.ext_cols, grad1, 0, dims.cols, dims.rows, dims.cols, dims.size, sums)
    store_sums(dims, sums, gain_part[...], taps_sum)
    upstream = pad_lanes(cot[...].reshape(dims.rows * dims.cols, dims.channels))
    up_sum[...] = dot_leading(normed1[...], pre_grad1[...]).T
    down_sum[...] = dot_leading(upstream, hidden1[...]).T


def store_sums(dims, sums, gain_part, target):
    taps = dims.size * dims.size
    target[...] = jnp.zeros(target.shape, f32)
    for t in range(taps):
        target[t : t + 1, :] = jnp.sum(sums[t * 8 : t * 8 + 8, :], axis=0, keepdims=True)
    target[taps : taps + 1, :] = jnp.sum(gain_part, axis=0, keepdims=True)


def third_kernel(dims, *refs):
    count = len(combos(dims.row_count))
    (grad1, cot, taps1, gains, grad_in0, grad_out0, x0, unit0, inv0, hidden0, slope0) = refs[:11]
    (taps_sum1, up_sum1, down_sum1) = refs[11:14]
    strips = refs[14 : 14 + count]
    (grad0, middle, keep, small_keep, send) = refs[14 + count : 19 + count]
    (wide_grad, cot_frame, upstream, own, sums, normed0, flow0, pre_grad0, gain_sum, small, tall, slabs) = refs[19 + count :]
    place = Place(dims.row_count, dims.col_count)
    rows, cols, channels, h, size = (dims.rows, dims.cols, dims.channels, dims.h, dims.size)
    ext_rows, ext_cols, wide = (dims.ext_rows, dims.ext_cols, dims.wide)
    skip = dims.skipped_rows(place)
    read = received(place, strips, (0, 0))
    assemble(
        place, wide_grad, lambda i: grad1[i * cols : (i + 1) * cols, 0:channels], read, 2 * h, rows, cols, channels
    )
    read_cot = received(place, strips, (rows, 2 * h))
    margin = (ext_cols - cols) // 2
    cot_frame[...] = jnp.zeros(cot_frame.shape, f32)
    for vertical, start, n in (("above", 0, h), (None, h, rows), ("below", h + rows, h)):
        for i in range(n):
            base = (start + i) * ext_cols
            line = cot[i].astype(f32) if vertical is None else read_cot(vertical, None, i)
            cot_frame[base + margin : base + margin + cols, 0:channels] = line
            cot_frame[base : base + margin, 0:channels] = read_cot(vertical, "left", i)[SIDE - margin :]
            cot_frame[base + margin + cols : base + ext_cols, 0:channels] = read_cot(vertical, "right", i)[:margin]

    used = ext_rows * ext_cols
    if dims.ext_pad > used:
        upstream[used:, :] = jnp.zeros((dims.ext_pad - used, LANES), f32)
        own[used:, :] = jnp.zeros((dims.ext_pad - used, LANES), f32)
    grad0[...] = jnp.zeros(grad0.shape, f32)
    frame = pl.multiple_of(skip * ext_cols, 8)

    def conv1(g, carry):
        at = group_start(g, ext_cols)
        total = conv_group(wide_grad, pl.multiple_of(skip * wide, 8) + at + 1, wide, ext_rows, taps1, size, True)
        col = lax.broadcasted_iota(jnp.int32, (16, LANES), 0) + (at - margin)
        inside = jnp.where(jnp.logical_and(col >= 0, col < cols), 1.0, 0.0)
        for r in range(ext_rows):
            px = pl.ds(r * ext_cols + at, 16)
            upstream[px, :] = cot_frame[pl.ds(frame + r * ext_cols + at, 16), :] + total[r]
            mine = jnp.logical_and(r + skip >= h, r + skip < h + rows)
            own[px, :] = jnp.where(mine, inside, 0.0)
        return carry

    lax.fori_loop(0, -(-ext_cols // 16), conv1, 0)
    for i in range(rows):
        line = upstream[pl.ds((i + h - skip) * ext_cols + margin, cols), :]
        middle[i * cols : (i + 1) * cols, :] = round16(line)

    gain = pad_lanes(gains[0:1, :])
    gain_sum[...] = jnp.zeros(gain_sum.shape, f32)
    ones = diagonal(jnp.ones((LANES, LANES), bf16), jnp.ones((LANES, LANES), bf16))
    half_px = dims.ext_pad // 2

    def mix0(start):
        n = dims.piece
        starts = (start, half_px + start)
        flows = [upstream[span(at, n), :].astype(bf16) for at in starts]
        hidden_grads = dot(side_by_side(*flows), grad_in0[...])
        yield
        count = hidden_grads.shape[1] // 2

        def slope_times(grad, slope):
            return ((grad * slope.astype(f32)).astype(bf16),)

        pre_grads = [
            by_blocks(slope_times, hidden_grads[:, k * count : (k + 1) * count], slope0[span(at, n), :])[0]
            for k, at in enumerate(starts)
        ]
        both = dot(side_by_side(*pre_grads), grad_out0[...])
        yield
        normed_grads = (both[:, :LANES], both[:, LANES:])
        for at, flow, pre_grad, normed_grad in zip(starts, flows, pre_grads, normed_grads):
            px = span(at, n)
            mine = own[px, :]
            unit = unit0[px, :].astype(f32)
            normed0[px, :] = (unit * gain * mine).astype(bf16)
            flow0[px, :] = flow * mine.astype(bf16)
            pre_grad0[px, :] = pre_grad
            product = normed_grad * unit * mine
            gain_sum[...] += jnp.sum(product.reshape(n // 8, 8, LANES), axis=0)
            grad = yield from norm_backward(normed_grad, unit, inv0[px, :], gain, channels, ones)
            grad0[pl.ds(frame + pl.multiple_of(at, 16), n), :] = grad

    def two_pieces(i, carry):
        together([mix0((2 * i + j) * dims.piece) for j in range(2)])
        return carry

    lax.fori_loop(0, half_px // (2 * dims.piece), two_pieces, 0)
    clear_outside(place, grad0, dims)
    kernel_sums(
        x0, h * wide + SIDE - h, wide, grad0, h * ext_cols + margin, ext_cols, rows, cols, size, sums
    )
    store_sums(dims, sums, gain_sum[...], small)

    taps_rows = size * size + 1
    merged = jnp.concatenate([small[0:taps_rows, :], taps_sum1[0:taps_rows, :]], axis=0) * dims.factor
    merged = fold_rows(merged, dims.small_rows, channels).astype(bf16)
    small_keep[...] = merged.astype(f32)

    layer_rows, part, half = (dims.layer_rows, dims.part, dims.half)
    units = hidden0.shape[1]
    up0 = dot_leading(normed0[...], pre_grad0[...]).T * dims.factor
    down0 = dot_leading(flow0[...], hidden0[...]).T * dims.factor
    up1 = up_sum1[...] * dims.factor
    down1 = down_sum1[...] * dims.factor
    lane = lax.broadcasted_iota(jnp.int32, (units, LANES), 1)
    slab_rows = 2 * layer_rows
    for r in range(dims.row_count):
        for layer, (u, d) in enumerate(((up0, down0), (up1, down1))):
            first = pltpu.roll(u, LANES - r * half, 1) if r else u
            shift = (half - r * half) % LANES
            second = pltpu.roll(d, shift, 1) if shift else d
            joined = jnp.where(lane < half, first, jnp.where(lane < 2 * half, second, 0.0))
            tall[layer * (units + 8) : layer * (units + 8) + units, :] = joined

        for c in range(dims.col_count):
            index = 0
            for axis, bit in dims.stages:
                index = 2 * index + ((r if axis == "row" else c) >> bit & 1)
            for layer in range(2):
                to, at = (index * slab_rows + layer * layer_rows, layer * (units + 8) + c * part)
                slabs[to : to + layer_rows, :] = tall[at : at + layer_rows, :]

    split(dims, 0, slabs, merged, keep, (send,))


def fold_rows(x, rows, used):
    n = x.shape[0]
    if rows >= n:
        return pad_rows(x, rows)
    assert used <= 96
    stride = ceil8(n - rows)
    rest = pad_rows(x[rows:], stride)
    pieces_of = pad_rows(jnp.concatenate([pltpu.roll(rest, 96 - 32 * k, 1) for k in range(3)], axis=0), rows)
    lane = lax.broadcasted_iota(jnp.int32, (rows, LANES), 1)
    return jnp.where(lane < 96, x[:rows], pieces_of)


def pad_rows(x, rows):
    if rows == x.shape[0]:
        return x
    return jnp.concatenate([x, jnp.zeros((rows - x.shape[0], LANES), x.dtype)], axis=0)


def unfold_rows(x, n):
    rows = x.shape[0]
    if rows >= n:
        return x[:n]
    stride = ceil8(n - rows)
    lane = lax.broadcasted_iota(jnp.int32, (stride, LANES), 1)
    rest = jnp.zeros((stride, LANES), x.dtype)
    for k in range(3):
        moved = pltpu.roll(x[k * stride : (k + 1) * stride], 32 + 32 * k, 1)
        rest = jnp.where(jnp.logical_and(lane >= 32 * k, lane < 32 * k + 32), moved, rest)
    return jnp.concatenate([x, rest[: n - rows]], axis=0)


def split(dims, stage, slabs, merged, keep, sends):
    group = dims.groups[stage]
    count = slabs.shape[0] >> len(group)
    mine = 0
    for axis, bit in group:
        mine = mine * 2 + lax.rem(lax.div(lax.axis_index(axis), 1 << bit), 2)
    keep[...] = slabs[pl.ds(pl.multiple_of(mine * count, 16), count), :]
    for mask, send in enumerate(sends, 1):
        other = 0
        for j in range(len(group)):
            weight = 1 << j
            digit = lax.rem(lax.div(mine, weight), 2)
            other = other + weight * (1 - digit if mask & weight else digit)
        send[0:count, :] = slabs[pl.ds(pl.multiple_of(other * count, 16), count), :].astype(bf16)
        send[count:, :] = merged


def gather_up(keep, small, gots):
    count = keep.shape[0]
    slabs = [keep[...]] + [got[0:count, :].astype(f32) for got in gots]
    sums = [small[...]] + [got[count:, :].astype(f32) for got in gots]
    if len(gots) == 1:
        return (slabs[0] + slabs[1], sums[0] + sums[1])
    return tuple((x[0] + x[1]) + (x[2] + x[3]) for x in (slabs, sums))


def stage_kernel(dims, stage, keep, small, *refs):
    before, after = (len_sends(dims.groups[stage - 1]), len_sends(dims.groups[stage]))
    gots = refs[:before]
    keep_out, small_out = refs[-3 - after : -1 - after]
    sends, total = (refs[-1 - after : -1], refs[-1])
    slabs, merged = gather_up(keep, small, gots)
    total[...] = slabs
    merged = merged.astype(bf16)
    small_out[...] = merged.astype(f32)
    split(dims, stage, total, merged, keep_out, sends)


def len_sends(group):
    return (1 << len(group)) - 1


def last_kernel(dims, keep, small, *refs):
    gots, (kernel_out, gain_out, up_out, down_out) = (refs[:-4], refs[-4:])
    total, merged = gather_up(keep, small, gots)
    merged = unfold_rows(merged, 2 * (dims.size * dims.size + 1))
    size, channels, half, part = (dims.size, dims.channels, dims.half, dims.part)
    for layer in range(2):
        block = total[layer * dims.layer_rows : layer * dims.layer_rows + part]
        up_out[layer] = block[:, :half]
        down_out[layer] = block[:, half : 2 * half]
        for t in range(size * size + 1):
            at = layer * (size * size + 1) + t
            row = merged[at : at + 1, 0:channels]
            if t < size * size:
                kernel_out[t // size, t % size, layer : layer + 1, :] = row
            else:
                gain_out[layer : layer + 1, :] = row


def image_kernel(dims, grad0, middle, taps0, after, out, ready, work):
    rows, cols, size = (dims.rows, dims.cols, dims.size)

    def conv0(g, carry):
        at = group_start(g, cols)
        total = conv_group(grad0, at + 1, dims.ext_cols, rows, taps0, size, True)
        for r in range(rows):
            work[pl.ds(r * cols + at, 16), :] = middle[pl.ds(r * cols + at, 16), :] + total[r]
        return carry

    lax.fori_loop(0, -(-cols // 16), conv0, 0)
    for r in range(rows):
        out[r] = work[r * cols : (r + 1) * cols, 0 : dims.channels].astype(bf16)
    ready[...] = jnp.zeros(ready.shape, f32)


class Dims:
    def skipped_rows(self, place):
        if self.row_count > 2:
            return 0
        return jnp.where(place.has["above"], 0, self.h)


def dims_of(image, kernels, up_weights):
    d = Dims()
    d.row_count, d.col_count = (lax.axis_size("row"), lax.axis_size("col"))
    d.rows, d.cols, d.channels = image.shape
    d.size = kernels.shape[1]
    d.h = d.size // 2
    d.ext_rows, d.ext_cols = (d.rows + (d.h if d.row_count == 2 else 2 * d.h), d.cols + 8)
    d.wide = d.cols + 2 * SIDE
    total = d.ext_rows * d.ext_cols
    d.ext_pad, d.piece = min((-(-total // (4 * p)) * 4 * p, p) for p in range(96, 209, 16))
    d.line_step = 4
    d.half = d.channels // d.row_count
    d.part = up_weights.shape[2] // d.col_count
    d.layer_rows = ceil8(d.part)
    d.count = d.row_count * d.col_count
    d.small_rows = 80 if d.size == 7 and d.channels <= 96 else -(-2 * (d.size * d.size + 1) // 16) * 16
    d.factor = 1.0 / math.sqrt(d.rows * d.cols * d.count)
    row_bits, col_bits = (d.row_count.bit_length() - 1, d.col_count.bit_length() - 1)
    bits = [("row", b) for b in range(row_bits)] + [("col", b) for b in range(1, col_bits)]
    d.groups = [[("col", 0)]] + [bits[i : i + 2] for i in range(0, len(bits), 2)]
    d.stages = [bit for group in d.groups for bit in group]
    return d


def swap_by(d, group, mask):
    flip = {"row": 0, "col": 0}
    for j, (axis, bit) in enumerate(group):
        if mask >> (len(group) - 1 - j) & 1:
            flip[axis] |= 1 << bit
    pairs = []
    for r in range(d.row_count):
        for c in range(d.col_count):
            pairs.append((r * d.col_count + c, (r ^ flip["row"]) * d.col_count + (c ^ flip["col"])))
    return pairs


def run(kernel, outs, scratch, *args, in_hbm=0, sems=0, busy_us=1):
    shapes = [jax.ShapeDtypeStruct(shape, kind) for shape, kind in outs]
    space = pl.BlockSpec(memory_space=pltpu.VMEM)
    far = pl.BlockSpec(memory_space=pltpu.HBM)
    held = [pltpu.VMEM(shape, kind) for shape, kind in scratch]
    if sems:
        held.append(pltpu.SemaphoreType.DMA((sems,)))
    return pl.pallas_call(
        kernel,
        out_shape=shapes,
        in_specs=[far] * in_hbm + [space] * (len(args) - in_hbm),
        out_specs=[space] * len(shapes),
        scratch_shapes=held,
        compiler_params=pltpu.CompilerParams(vmem_limit_bytes=32 * 1024 * 1024),
        cost_estimate=pl.CostEstimate(flops=int(busy_us * 1e9), bytes_accessed=1 << 18, transcendentals=0),
    )(*args)


def per_device(image, kernels, gains, up_weights, down_weights, cotangent):
    d = dims_of(image, kernels, up_weights)
    bind = functools.partial
    rows, cols, channels = image.shape
    units = up_weights.shape[2]
    tile, ext, wide = (rows * cols, d.ext_pad, (rows + 4 * d.h) * d.wide)
    frame = (rows + 2 * d.h) * d.ext_cols + 16 + ext - d.ext_rows * d.ext_cols
    taps = ((d.size * d.size * 16, LANES), bf16)
    tap_sums = ((d.size * d.size * 8, LANES), f32)
    sums_rows = ceil8(d.size * d.size + 1)

    bands, others = (band_combos(d.row_count), other_combos(d.row_count))

    def strips_of(pairs, radii):
        return [(shape, bf16) for shape in strip_shapes(pairs, rows, cols, channels, radii)]

    image, *band_strips = run(
        bind(bands_kernel, d), [(image.shape, bf16)] + strips_of(bands, (2 * d.h,)), [], image, in_hbm=1, sems=1
    )
    other_strips = run(bind(others_kernel, d), strips_of(others, (2 * d.h,)), [], image, *band_strips)
    strips = exchange(band_strips, other_strips, d.row_count, d.col_count)
    mixing = [((2 * LANES, 2 * units), bf16), ((2 * units, 2 * LANES), bf16)]
    forward0, back0, forward1, back1, grad_in0, grad_out0, taps0, taps1, gains = run(
        weights_kernel,
        mixing * 3 + [taps, taps, (gains.shape, f32)],
        [((2, channels, units), bf16), ((2, channels, units), bf16), ((d.size, d.size, 2, channels), f32)],
        up_weights,
        jnp.swapaxes(down_weights, 1, 2),
        jnp.transpose(kernels, (1, 2, 0, 3)),
        gains,
        in_hbm=4,
        sems=4,
        busy_us=2,
    )

    first = run(
        bind(first_kernel, d),
        [
            (image.shape, bf16),
            ((wide, LANES), f32),
            ((frame, LANES), f32),
            ((ext, LANES), bf16),
            ((ext, LANES), f32),
            ((ext, units), bf16),
            ((ext, units), bf16),
            ((tile, LANES), f32),
            ((tile, LANES), bf16),
            ((tile, units), bf16),
            ((tile, units), bf16),
            ((8, LANES), f32),
        ]
        + strips_of(bands, (2 * d.h, d.h)),
        [((ext, LANES), f32)],
        image,
        cotangent,
        taps0,
        taps1,
        gains,
        forward0,
        back0,
        forward1,
        back1,
        *strips,
        busy_us=15,
    )
    (final, x0, x1, unit0, inv0, hidden0, slope0, grad1, normed1, pre_grad1, hidden1, gain_part) = first[:12]
    band_strips = first[12:]
    other_strips = run(
        bind(grad_others_kernel, d), strips_of(others, (2 * d.h, d.h)), [], grad1, cotangent, *band_strips
    )
    strips = exchange(band_strips, other_strips, d.row_count, d.col_count)

    taps_sum1, up_sum1, down_sum1, output = run(
        bind(sums_kernel, d),
        [((sums_rows, LANES), f32), ((units, LANES), f32), ((units, LANES), f32), (image.shape, bf16)],
        [tap_sums],
        x1,
        grad1,
        normed1,
        pre_grad1,
        hidden1,
        cotangent,
        gain_part,
        final,
        busy_us=3,
    )

    held = d.count // 2 * 2 * d.layer_rows
    small = ((d.small_rows, LANES), f32)
    grad0, middle, keep, sums, send = run(
        bind(third_kernel, d),
        [((frame, LANES), f32), ((tile, LANES), f32), ((held, LANES), f32), small, ((held + d.small_rows, LANES), bf16)],
        [
            ((wide, LANES), f32),
            ((frame, LANES), f32),
            ((ext, LANES), f32),
            ((ext, LANES), f32),
            tap_sums,
            ((ext, LANES), bf16),
            ((ext, LANES), bf16),
            ((ext, units), bf16),
            ((8, LANES), f32),
            ((sums_rows, LANES), f32),
            ((2 * (units + 8), LANES), f32),
            ((2 * held, LANES), f32),
        ],
        grad1,
        cotangent,
        taps1,
        gains,
        grad_in0,
        grad_out0,
        x0,
        unit0,
        inv0,
        hidden0,
        slope0,
        taps_sum1,
        up_sum1,
        down_sum1,
        *strips,
        busy_us=12,
    )
    axes = ("row", "col")
    sends = [send]
    for stage, group in enumerate(d.groups):
        gots = [lax.ppermute(x, axes, swap_by(d, group, mask)) for mask, x in enumerate(sends, 1)]
        ready = []
        if stage == 1:
            gradient, *ready = run(
                bind(image_kernel, d),
                [(image.shape, bf16), ((8, LANES), f32)],
                [((tile, LANES), f32)],
                grad0,
                middle,
                taps0,
                sums,
                busy_us=3,
            )
        if stage + 1 < len(d.groups):
            after = d.groups[stage + 1]
            whole, held = (held, held >> len(after))
            keep, sums, *sends = run(
                bind(stage_kernel, d, stage + 1),
                [((held, LANES), f32), small] + [((held + d.small_rows, LANES), bf16)] * len_sends(after),
                [((whole, LANES), f32)],
                keep,
                sums,
                *gots,
                *ready,
            )
    kernel_out, gain_out, up_out, down_out = run(
        bind(last_kernel, d),
        [
            ((d.size, d.size, 2, channels), f32),
            (gains.shape, f32),
            ((2, d.part, d.half), f32),
            ((2, d.part, d.half), f32),
        ],
        [],
        keep,
        sums,
        *gots,
    )
    kernel_out = jnp.transpose(kernel_out, (2, 0, 1, 3))
    return (output, gradient, kernel_out, gain_out, jnp.swapaxes(up_out, 1, 2), down_out)


def solution(mesh):
    placed = (P("row", "col", None), P(), P(), P(), P(), P("row", "col", None))
    return jax.shard_map(
        per_device,
        mesh=mesh,
        in_specs=placed,
        out_specs=(
            P("row", "col", None),
            P("row", "col", None),
            P(),
            P(),
            P(None, "row", "col"),
            P(None, "col", "row"),
        ),
        check_vma=False,
    )
```

```python
import functools
import math

import jax
import jax.numpy as jnp
from jax import lax
from jax.experimental import pallas as pl
from jax.experimental.pallas import tpu as pltpu
from jax.sharding import PartitionSpec as P

epsilon = 1e-06
inv_sqrt_two = 0.7071067811865476
inv_sqrt_two_pi = 0.3989422804014327
log2_e = 1.4426950408889634
LANES = 128
SIDE = 8
f32, bf16 = (jnp.float32, jnp.bfloat16)


def ceil8(n):
    return -(-n // 8) * 8


def combos(row_count):
    listed = [(None, 0), (None, 1), (0, None), (0, 0), (0, 1)]
    if row_count > 2:
        listed += [(1, None), (1, 0), (1, 1)]
    return listed


def partner(index, start, count):
    if start is None:
        return index
    other = index + 1 if (index - start) % 2 == 0 else index - 1
    return other if 0 <= other < count else None


def swap_pairs(row_count, col_count, row_start, col_start):
    pairs = []
    for r in range(row_count):
        for c in range(col_count):
            pr, pc = (partner(r, row_start, row_count), partner(c, col_start, col_count))
            if pr is None:
                pr, pc = (r, c ^ 1)
            elif pc is None:
                pr, pc = (r ^ 1 if row_start is None else pr, c)
            pairs.append((r * col_count + c, pr * col_count + pc))
    return pairs


def exchange(bands, others, row_count, col_count):
    got = {}
    for strips, pairs in ((bands, band_combos(row_count)), (others, other_combos(row_count))):
        for strip, (rs, cs) in zip(strips, pairs):
            got[rs, cs] = lax.ppermute(strip, ("row", "col"), swap_pairs(row_count, col_count, rs, cs))
    return [got[pair] for pair in combos(row_count)]


class Place:
    def __init__(self, row_count, col_count):
        row, col = (lax.axis_index("row"), lax.axis_index("col"))
        self.even_row, self.even_col = (lax.rem(row, 2) == 0, lax.rem(col, 2) == 0)
        self.has = {
            "above": row > 0,
            "below": row < row_count - 1,
            "left": col > 0,
            "right": col < col_count - 1,
        }
        self.row_count = row_count


def band_combos(row_count):
    return [pair for pair in combos(row_count) if pair[1] is None]


def other_combos(row_count):
    return [pair for pair in combos(row_count) if pair[1] is not None]


def write_strips(place, outs, takes, pairs):
    for out, (rs, cs) in zip(outs, pairs):
        at = 0
        for take, radius, rows, cols in takes:
            row_sets = [slice(0, rows)] * 2
            col_sets = [slice(0, cols)] * 2
            if rs is not None:
                row_sets = [slice(rows - radius, rows), slice(0, radius)]
                if rs == 1:
                    row_sets = row_sets[::-1]
            if cs is not None:
                col_sets = [slice(cols - SIDE, cols), slice(0, SIDE)]
                if cs == 1:
                    col_sets = col_sets[::-1]
            count = row_sets[0].stop - row_sets[0].start
            for i in range(count):
                parts = {}
                for er in (0, 1):
                    for ec in (0, 1):
                        key = (row_sets[er].start + i, col_sets[ec].start, col_sets[ec].stop)
                        if key not in parts:
                            parts[key] = take(*key)
                        parts[er, ec] = parts[key]
                if cs is None:
                    pick = [parts[0, 0], parts[1, 0]]
                else:
                    pick = [jnp.where(place.even_col, parts[e, 0], parts[e, 1]) for e in (0, 1)]
                value = pick[0] if rs is None else jnp.where(place.even_row, pick[0], pick[1])
                out[at + i] = value.astype(out.dtype)
            at += count


def strip_shapes(pairs, rows, cols, channels, radii):
    shapes = []
    for rs, cs in pairs:
        height = sum(rows if rs is None else radius for radius in radii)
        shapes.append((height, cols if cs is None else SIDE, channels))
    return shapes


def received(place, strips, row_sections):
    table = dict(zip(combos(place.row_count), strips))
    full_start, band_start = row_sections

    def along(rs, cs, i):
        return table[rs, cs][(full_start if rs is None else band_start) + i].astype(f32)

    def column(rs, side, i):
        if side is None:
            return along(rs, None, i)
        near, far = (along(rs, 0, i), along(rs, 1, i))
        if side == "left":
            return jnp.where(place.even_col, far, near)
        return jnp.where(place.even_col, near, far)

    def read(vertical, side, i):
        if vertical is None:
            value = column(None, side, i)
        elif place.row_count == 2:
            value = column(0, side, i)
        else:
            near, far = (column(0, side, i), column(1, side, i))
            if vertical == "above":
                value = jnp.where(place.even_row, far, near)
            else:
                value = jnp.where(place.even_row, near, far)
        if vertical is not None:
            value = jnp.where(place.has[vertical], value, 0.0)
        if side is not None:
            value = jnp.where(place.has[side], value, 0.0)
        return value

    return read


def assemble(place, target, own, read, radius, rows, cols, channels):
    width = cols + 2 * SIDE
    target[...] = jnp.zeros(target.shape, f32)
    for vertical, start, count in (("above", 0, radius), (None, radius, rows), ("below", radius + rows, radius)):
        for i in range(count):
            base = (start + i) * width
            middle = own(i) if vertical is None else read(vertical, None, i)
            target[base + SIDE : base + SIDE + cols, 0:channels] = middle
            target[base : base + SIDE, 0:channels] = read(vertical, "left", i)
            target[base + SIDE + cols : base + width, 0:channels] = read(vertical, "right", i)


def spread_taps(kernel_ref, layer, target):
    size, channels = (kernel_ref.shape[0], kernel_ref.shape[3])
    for a in range(size):
        for b in range(size):
            t = a * size + b
            row = pad_lanes(kernel_ref[a, b, layer : layer + 1, :])
            target[t * 16 : t * 16 + 16, :] = jnp.broadcast_to(row, (16, LANES)).astype(bf16)


def tree_sum(terms):
    while len(terms) > 1:
        pairs = [terms[i] + terms[i + 1] for i in range(0, len(terms) - 1, 2)]
        terms = pairs + ([terms[-1]] if len(terms) % 2 else [])
    return terms[0]


def conv_group(src, base, stride, rows_out, taps, size, flipped=False):
    total = [None] * rows_out
    for first in range(0, size, 2):
        columns = range(first, min(first + 2, size))
        weights = []
        for b in columns:
            order = [a * size + b for a in range(size)]
            if flipped:
                order = [size * size - 1 - t for t in order]
            weights.append([taps[t * 16 : t * 16 + 16, :] for t in order])
        windows = [[] for _ in columns]
        for i in range(rows_out + size - 1):
            for window, b in zip(windows, columns):
                window.append(src[pl.ds(base + i * stride + b, 16), :].astype(bf16))
            r = i - size + 1
            if r >= 0:
                sums = [
                    tree_sum([window[r + a] * weight[a] for a in range(size)])
                    for window, weight in zip(windows, weights)
                ]
                term = tree_sum(sums).astype(f32)
                total[r] = term if total[r] is None else total[r] + term
    return total


def group_start(g, cols):
    return pl.multiple_of(jnp.minimum(g * 16, cols - 16), 8)


def kernel_sums(src, src_base, src_stride, grad, grad_base, grad_stride, rows, cols, size, sums):
    sums[...] = jnp.zeros(sums.shape, f32)

    def group(g, carry):
        at = pl.multiple_of(g * 16, 16)
        grads = [grad[pl.ds(grad_base + i * grad_stride + at, 16), :].astype(bf16) for i in range(rows)]
        for b in range(size):
            lines = [
                src[pl.ds(src_base + i * src_stride + at + b, 16), :].astype(bf16) for i in range(rows + size - 1)
            ]
            for a in range(size):
                term = tree_sum([lines[r + a] * grads[r] for r in range(rows)]).astype(f32)
                t = (a * size + b) * 8
                sums[t : t + 8, :] += term[0:8] + term[8:16]
        return carry

    lax.fori_loop(0, cols // 16, group, 0)


def diagonal(first, second):
    top = jnp.concatenate([first, jnp.zeros((first.shape[0], second.shape[1]), first.dtype)], axis=1)
    bottom = jnp.concatenate([jnp.zeros((second.shape[0], first.shape[1]), first.dtype), second], axis=1)
    return jnp.concatenate([top, bottom], axis=0)


def together(steps):
    steps = list(steps)
    while steps:
        steps = [step for step in steps if next(step, steps) is not steps]


def by_blocks(function, *arrays, size=16):
    count = arrays[0].shape[0]
    results = [function(*(x[i : i + size] for x in arrays)) for i in range(0, count, size)]
    return tuple(jnp.concatenate(parts, axis=0) for parts in zip(*results))


def in_channels(shape, channels):
    return lax.broadcasted_iota(jnp.int32, shape, 1) < channels


def high_low(x):
    high = x.astype(bf16)
    return (jnp.concatenate([high, (x - high.astype(f32)).astype(bf16)], axis=1),)


def side_by_side(x, y):
    return jnp.concatenate([x, y], axis=1)


def layer_norm(parts, gain, channels, ones):
    def centre(x, total):
        centred = jnp.where(in_channels(x.shape, channels), x - total * (1.0 / channels), 0.0)
        return (centred, (centred * centred).astype(bf16))

    def finish(centred, total):
        inverse = lax.rsqrt(total * (1.0 / channels) + epsilon)
        unit = centred * inverse
        return (unit, inverse, (unit * gain).astype(bf16))

    totals = [dot(by_blocks(high_low, x)[0], jnp.ones((2 * LANES, LANES), bf16)) for x in parts]
    yield
    centred, squares = zip(*(by_blocks(centre, x, total) for x, total in zip(parts, totals)))
    variances = dot(side_by_side(*squares), ones)
    yield
    return [by_blocks(finish, c, variances[:, k * LANES : (k + 1) * LANES]) for k, c in enumerate(centred)]


def norm_backward(normed_grad, unit, inverse, gain, channels, ones):
    def products(normed_grad, unit):
        m = normed_grad * gain
        return (side_by_side(m.astype(bf16), (m * unit).astype(bf16)),)

    def finish(normed_grad, unit, inverse, sums):
        along = sums[:, :LANES] + unit * sums[:, LANES:]
        grad = inverse * (normed_grad * gain - along * (1.0 / channels))
        return (round16(jnp.where(in_channels(grad.shape, channels), grad, 0.0)),)

    sums = dot(by_blocks(products, normed_grad, unit)[0], ones)
    yield
    return by_blocks(finish, normed_grad, unit, inverse, sums)[0]


def gelu_parts(v):
    p = 0.3275911 * inv_sqrt_two
    c1, c2, c3, c4, c5 = (
        0.5 * c / p ** (k + 1)
        for k, c in enumerate((0.254829592, -0.284496736, 1.421413741, -1.453152027, 1.061405429))
    )
    t = pl.reciprocal(jnp.abs(v) + 1.0 / p, approx=True)
    bell = jnp.exp2(v * v * (-0.5 * log2_e))
    tail = ((((c5 * t + c4) * t + c3) * t + c2) * t + c1) * t * bell
    cdf = jnp.where(v >= 0.0, 1.0 - tail, tail)
    return (v * cdf, cdf + v * (bell * inv_sqrt_two_pi))


def dot(x, w):
    return jnp.dot(x, w, preferred_element_type=f32)


def dot_leading(x, y):
    return lax.dot_general(x, y, (((0,), (0,)), ((), ())), preferred_element_type=f32)


def pad_lanes(x):
    rows, channels = x.shape
    return jnp.concatenate([x, jnp.zeros((rows, LANES - channels), x.dtype)], axis=1)


def pieces(total, size):
    return [(start, min(size, total - start)) for start in range(0, total, size)]


def round16(x):
    return x.astype(bf16).astype(f32)


def fetch(sources, targets, sems):
    copies = [pltpu.make_async_copy(a, b, sems.at[i]) for i, (a, b) in enumerate(zip(sources, targets))]
    for copy in copies:
        copy.start()
    for copy in copies:
        copy.wait()


def image_take(ref):
    return lambda i, lo, hi: ref[i].astype(f32)[lo:hi]


def flat_take(ref, cols, channels):
    return lambda i, lo, hi: ref[i * cols + lo : i * cols + hi, 0:channels]


def bands_kernel(dims, image_in, image, *refs):
    outs, sems = (refs[:-1], refs[-1])
    place = Place(dims.row_count, dims.col_count)
    fetch((image_in,), (image,), sems)
    takes = [(image_take(image), 2 * dims.h, dims.rows, dims.cols)]
    write_strips(place, outs, takes, band_combos(dims.row_count))


def others_kernel(dims, image, *refs):
    outs = refs[len(band_combos(dims.row_count)) :]
    place = Place(dims.row_count, dims.col_count)
    takes = [(image_take(image), 2 * dims.h, dims.rows, dims.cols)]
    write_strips(place, outs, takes, other_combos(dims.row_count))


def grad_others_kernel(dims, grad1, cot, *refs):
    outs = refs[len(band_combos(dims.row_count)) :]
    place = Place(dims.row_count, dims.col_count)
    takes = [
        (flat_take(grad1, dims.cols, dims.channels), 2 * dims.h, dims.rows, dims.cols),
        (image_take(cot), dims.h, dims.rows, dims.cols),
    ]
    write_strips(place, outs, takes, other_combos(dims.row_count))


def weights_kernel(dims, up_in, down_t_in, kernels_in, gains_in, *refs):
    forward0, back0, forward1, back1, grad_in0, grad_out0, taps0, taps1, gains, own, up_w, down_w, kernels, sems = refs
    fetch((up_in, down_t_in, kernels_in, gains_in), (up_w, down_w, kernels, gains), sems)
    spread_taps(kernels, 0, taps0)
    spread_taps(kernels, 1, taps1)
    channels, units = up_w.shape[1:]
    blank = jnp.zeros((LANES - channels, units), f32)
    wide, tall = ([], [])
    for layer in range(2):
        for ref in (up_w, down_w):
            full = jnp.concatenate([ref[layer].astype(f32), blank], axis=0)
            wide.append(full.astype(bf16))
            tall.append(full.T.astype(bf16))
    (up0, down_t0, up1, down_t1), (up_t0, down0, up_t1, down1) = (wide, tall)
    forward0[...] = diagonal(up0, up0)
    back0[...] = diagonal(down0, down0)
    forward1[...] = diagonal(up1, down_t1)
    back1[...] = diagonal(down1, up_t1)
    grad_in0[...] = diagonal(down_t0, down_t0)
    grad_out0[...] = diagonal(up_t0, up_t0)
    own_pixels(dims, own)


def own_pixels(dims, own):
    skip = dims.skipped_rows(Place(dims.row_count, dims.col_count))
    ext_rows, ext_cols, h = (dims.ext_rows, dims.ext_cols, dims.h)
    col = lax.broadcasted_iota(jnp.int32, (ext_cols, LANES), 0) - (ext_cols - dims.cols) // 2
    inside = jnp.where(jnp.logical_and(col >= 0, col < dims.cols), 1.0, 0.0)
    for r in range(ext_rows):
        mine = jnp.logical_and(r + skip >= h, r + skip < h + dims.rows)
        own[r * ext_cols : (r + 1) * ext_cols, :] = jnp.where(mine, inside, 0.0)
    used = ext_rows * ext_cols
    if dims.ext_pad > used:
        own[used:, :] = jnp.zeros((dims.ext_pad - used, LANES), f32)


def first_kernel(dims, *refs):
    count = len(combos(dims.row_count))
    image, cot, taps0, taps1, gains, forward0, back0, forward1, back1 = refs[:9]
    strips = refs[9 : 9 + count]
    refs = refs[9 + count :]
    (output, x0, x1, unit0, inv0, hidden0, slope0, grad1, normed1, pre_grad1, hidden1, gain_sum) = refs[:12]
    outs, conv = (refs[12:-1], refs[-1])
    place = Place(dims.row_count, dims.col_count)
    rows, cols, channels, h, size = (dims.rows, dims.cols, dims.channels, dims.h, dims.size)
    ext_rows, ext_cols, wide = (dims.ext_rows, dims.ext_cols, dims.wide)
    skip = dims.skipped_rows(place)
    read = received(place, strips, (0, 0))
    assemble(place, x0, lambda i: image[i].astype(f32), read, 2 * h, rows, cols, channels)

    x1[...] = jnp.zeros(x1.shape, f32)
    if dims.ext_pad > ext_rows * ext_cols:
        conv[ext_rows * ext_cols :, :] = jnp.zeros((dims.ext_pad - ext_rows * ext_cols, LANES), f32)
    frame = pl.multiple_of(skip * ext_cols, 8)

    def conv0(g, carry):
        at = group_start(g, ext_cols)
        base = pl.multiple_of(skip * wide, 8) + at
        total = conv_group(x0, base + 1, wide, ext_rows, taps0, size)
        for r in range(ext_rows):
            conv[pl.ds(r * ext_cols + at, 16), :] = total[r]
            x1[pl.ds(frame + r * ext_cols + at, 16), :] = x0[pl.ds(base + (r + h) * wide + 4, 16), :]
        return carry

    lax.fori_loop(0, -(-ext_cols // 16), conv0, 0)
    gain = pad_lanes(gains[0:1, :])
    ones = diagonal(jnp.ones((LANES, LANES), bf16), jnp.ones((LANES, LANES), bf16))
    half = dims.ext_pad // 2

    def mix0(start, n):
        spans = [(start, n), (half + start, n)]
        parts = yield from layer_norm([conv[at : at + n, :] for at, n in spans], gain, channels, ones)
        pres = dot(side_by_side(parts[0][2], parts[1][2]), forward0[...])
        yield
        count = pres.shape[1] // 2
        hiddens = []
        for k, ((at, n), (unit, inverse, _)) in enumerate(zip(spans, parts)):
            unit0[at : at + n, :] = unit.astype(bf16)
            inv0[at : at + n, :] = inverse

            def activate(pre):
                value, slope = gelu_parts(pre)
                return (value.astype(bf16), slope.astype(bf16))

            hidden, slope = by_blocks(activate, pres[:, k * count : (k + 1) * count])
            hidden0[at : at + n, :] = hidden
            slope0[at : at + n, :] = slope
            hiddens.append(hidden)
        branches = dot(side_by_side(*hiddens), back0[...])
        yield
        for k, (at, n) in enumerate(spans):
            px = pl.ds(frame + at, n)
            x1[px, :] = round16(x1[px, :] + branches[:, k * LANES : (k + 1) * LANES])
    together([mix0(start, n) for start, n in pieces(half, dims.piece)])
    clear_outside(place, x1, dims)

    def conv1(g, carry):
        at = group_start(g, cols)
        total = conv_group(x1, at + 1, ext_cols, rows, taps1, size)
        for r in range(rows):
            conv[pl.ds(r * cols + at, 16), :] = total[r]
        return carry

    lax.fori_loop(0, -(-cols // 16), conv1, 0)
    gain1 = pad_lanes(gains[1:2, :])
    gain_sum[...] = jnp.zeros(gain_sum.shape, f32)
    lines = dims.line_step
    step = lines * cols

    def mix1(k):
        px = slice(k * step, (k + 1) * step)
        middle = k * step + step // 2
        parts = yield from layer_norm(
            [conv[k * step : middle, :], conv[middle : (k + 1) * step, :]], gain1, channels, ones
        )
        unit, inverse, normed = (jnp.concatenate(pair, axis=0) for pair in zip(*parts))
        normed1[px, :] = normed
        upstream = pad_lanes(cot[k * lines : (k + 1) * lines].reshape(step, channels))
        both = dot(side_by_side(normed, upstream), forward1[...])
        yield

        def activate(pre, hidden_grad):
            value, slope = gelu_parts(pre)
            return (value.astype(bf16), (hidden_grad * slope).astype(bf16))

        count = both.shape[1] // 2
        hidden, pre_grad = by_blocks(activate, both[:, :count], both[:, count:])
        hidden1[px, :] = hidden
        pre_grad1[px, :] = pre_grad
        both = dot(side_by_side(hidden, pre_grad), back1[...])
        yield
        branch, normed_grad = (both[:, :LANES], both[:, LANES:])
        for i in range(lines):
            start = (k * lines + i + h) * ext_cols + 4
            line = x1[start : start + cols, :] + branch[i * cols : (i + 1) * cols]
            output[k * lines + i] = line[:, :channels].astype(bf16)
        product = normed_grad * unit
        gain_sum[...] += jnp.sum(product.reshape(step // 8, 8, LANES), axis=0)
        grad1[px, :] = yield from norm_backward(normed_grad, unit, inverse, gain1, channels, ones)

    together([mix1(k) for k in range(rows // lines)])

    takes = [(flat_take(grad1, cols, channels), 2 * h, rows, cols), (image_take(cot), h, rows, cols)]
    write_strips(place, outs, takes, band_combos(dims.row_count))


def clear_outside(place, flat, dims):
    h, frame_rows, ext_cols = (dims.h, dims.rows + 2 * dims.h, dims.ext_cols)
    margin = (ext_cols - dims.cols) // 2

    @pl.when(jnp.logical_not(place.has["above"]))
    def _():
        flat[0 : h * ext_cols, :] = jnp.zeros((h * ext_cols, LANES), f32)

    @pl.when(jnp.logical_not(place.has["below"]))
    def _():
        last = (frame_rows - h) * ext_cols
        flat[last:, :] = jnp.zeros((flat.shape[0] - last, LANES), f32)

    @pl.when(jnp.logical_not(place.has["left"]))
    def _():
        for r in range(frame_rows):
            flat[r * ext_cols : r * ext_cols + margin, :] = jnp.zeros((margin, LANES), f32)

    @pl.when(jnp.logical_not(place.has["right"]))
    def _():
        for r in range(frame_rows):
            flat[(r + 1) * ext_cols - margin : (r + 1) * ext_cols, :] = jnp.zeros((margin, LANES), f32)


def sums_kernel(
    dims, x1, grad1, normed1, pre_grad1, hidden1, cot, gain_part, final, taps_sum, joined, output, sums
):
    output[...] = final[...]
    kernel_sums(x1, 1, dims.ext_cols, grad1, 0, dims.cols, dims.rows, dims.cols, dims.size, sums)
    store_sums(dims, sums, gain_part[...], taps_sum)
    upstream = pad_lanes(cot[...].reshape(dims.rows * dims.cols, dims.channels))
    up = dot_leading(normed1[...], pre_grad1[...]).T * dims.factor
    down = dot_leading(upstream, hidden1[...]).T * dims.factor
    join_sums(dims, up, down, joined)


def join_sums(dims, up, down, target):
    units, half = (up.shape[0], dims.half)
    lane = lax.broadcasted_iota(jnp.int32, (units, LANES), 1)
    for r in range(dims.row_count):
        first = pltpu.roll(up, LANES - r * half, 1) if r else up
        shift = (half - r * half) % LANES
        second = pltpu.roll(down, shift, 1) if shift else down
        both = jnp.where(lane < half, first, jnp.where(lane < 2 * half, second, 0.0))
        target[r * units : (r + 1) * units, :] = both
    target[dims.row_count * units :, :] = jnp.zeros((8, LANES), f32)


def store_sums(dims, sums, gain_part, target):
    taps = dims.size * dims.size
    target[...] = jnp.zeros(target.shape, f32)
    for t in range(taps):
        target[t : t + 1, :] = jnp.sum(sums[t * 8 : t * 8 + 8, :], axis=0, keepdims=True)
    target[taps : taps + 1, :] = jnp.sum(gain_part, axis=0, keepdims=True)


def third_kernel(dims, *refs):
    count = len(combos(dims.row_count))
    (grad1, cot, taps1, gains, grad_in0, grad_out0, x0, unit0, inv0, hidden0, slope0) = refs[:11]
    (own, taps_sum1, joined1) = refs[11:14]
    strips = refs[14 : 14 + count]
    (grad0, upstream, keep, small_keep, send) = refs[14 + count : 19 + count]
    (wide_grad, cot_frame, sums, normed0, flow0, pre_grad0, gain_sum, small, tall, slabs) = refs[19 + count :]
    place = Place(dims.row_count, dims.col_count)
    rows, cols, channels, h, size = (dims.rows, dims.cols, dims.channels, dims.h, dims.size)
    ext_rows, ext_cols, wide = (dims.ext_rows, dims.ext_cols, dims.wide)
    skip = dims.skipped_rows(place)
    read = received(place, strips, (0, 0))
    assemble(
        place, wide_grad, lambda i: grad1[i * cols : (i + 1) * cols, 0:channels], read, 2 * h, rows, cols, channels
    )
    read_cot = received(place, strips, (rows, 2 * h))
    margin = (ext_cols - cols) // 2
    cot_frame[...] = jnp.zeros(cot_frame.shape, f32)
    for vertical, start, n in (("above", 0, h), (None, h, rows), ("below", h + rows, h)):
        for i in range(n):
            base = (start + i) * ext_cols
            line = cot[i].astype(f32) if vertical is None else read_cot(vertical, None, i)
            cot_frame[base + margin : base + margin + cols, 0:channels] = line
            cot_frame[base : base + margin, 0:channels] = read_cot(vertical, "left", i)[SIDE - margin :]
            cot_frame[base + margin + cols : base + ext_cols, 0:channels] = read_cot(vertical, "right", i)[:margin]

    used = ext_rows * ext_cols
    if dims.ext_pad > used:
        upstream[used:, :] = jnp.zeros((dims.ext_pad - used, LANES), f32)
    grad0[...] = jnp.zeros(grad0.shape, f32)
    frame = pl.multiple_of(skip * ext_cols, 8)

    def conv1(g, carry):
        at = group_start(g, ext_cols)
        total = conv_group(wide_grad, pl.multiple_of(skip * wide, 8) + at + 1, wide, ext_rows, taps1, size, True)
        for r in range(ext_rows):
            px = pl.ds(r * ext_cols + at, 16)
            upstream[px, :] = cot_frame[pl.ds(frame + r * ext_cols + at, 16), :] + total[r]
        return carry

    lax.fori_loop(0, -(-ext_cols // 16), conv1, 0)
    gain = pad_lanes(gains[0:1, :])
    gain_sum[...] = jnp.zeros(gain_sum.shape, f32)
    ones = diagonal(jnp.ones((LANES, LANES), bf16), jnp.ones((LANES, LANES), bf16))
    half_px = dims.ext_pad // 2

    def mix0(start, n):
        spans = [(start, n), (half_px + start, n)]
        flows = [upstream[at : at + n, :].astype(bf16) for at, n in spans]
        hidden_grads = dot(side_by_side(*flows), grad_in0[...])
        yield
        count = hidden_grads.shape[1] // 2

        def slope_times(grad, slope):
            return ((grad * slope.astype(f32)).astype(bf16),)

        pre_grads = [
            by_blocks(slope_times, hidden_grads[:, k * count : (k + 1) * count], slope0[at : at + n, :])[0]
            for k, (at, n) in enumerate(spans)
        ]
        both = dot(side_by_side(*pre_grads), grad_out0[...])
        yield
        normed_grads = (both[:, :LANES], both[:, LANES:])
        for (at, n), flow, pre_grad, normed_grad in zip(spans, flows, pre_grads, normed_grads):
            mine = own[at : at + n, :]
            unit = unit0[at : at + n, :].astype(f32)
            normed0[at : at + n, :] = (unit * gain * mine).astype(bf16)
            flow0[at : at + n, :] = flow * mine.astype(bf16)
            pre_grad0[at : at + n, :] = pre_grad
            product = normed_grad * unit * mine
            gain_sum[...] += jnp.sum(product.reshape(n // 8, 8, LANES), axis=0)
            grad = yield from norm_backward(normed_grad, unit, inv0[at : at + n, :], gain, channels, ones)
            grad0[pl.ds(frame + at, n), :] = grad

    together([mix0(start, n) for start, n in pieces(half_px, dims.piece)])
    clear_outside(place, grad0, dims)
    kernel_sums(
        x0, h * wide + SIDE - h, wide, grad0, h * ext_cols + margin, ext_cols, rows, cols, size, sums
    )
    store_sums(dims, sums, gain_sum[...], small)

    taps_rows = size * size + 1
    merged = jnp.concatenate([small[0:taps_rows, :], taps_sum1[0:taps_rows, :]], axis=0) * dims.factor
    merged = fold_rows(merged, dims.small_rows, channels).astype(bf16)
    small_keep[...] = merged.astype(f32)

    layer_rows, part = (dims.layer_rows, dims.part)
    units = hidden0.shape[1]
    up0 = dot_leading(normed0[...], pre_grad0[...]).T * dims.factor
    down0 = dot_leading(flow0[...], hidden0[...]).T * dims.factor
    join_sums(dims, up0, down0, tall)
    slab_rows = 2 * layer_rows
    for r in range(dims.row_count):
        for c in range(dims.col_count):
            index = 0
            for axis, bit in dims.stages:
                index = 2 * index + ((r if axis == "row" else c) >> bit & 1)
            for layer, source in ((0, tall), (1, joined1)):
                to, at = (index * slab_rows + layer * layer_rows, r * units + c * part)
                slabs[to : to + layer_rows, :] = source[at : at + layer_rows, :]

    split(dims, 0, slabs, merged, keep, (send,))


def fold_rows(x, rows, used):
    n = x.shape[0]
    if rows >= n:
        return pad_rows(x, rows)
    assert used <= 96
    stride = ceil8(n - rows)
    rest = pad_rows(x[rows:], stride)
    pieces_of = pad_rows(jnp.concatenate([pltpu.roll(rest, 96 - 32 * k, 1) for k in range(3)], axis=0), rows)
    lane = lax.broadcasted_iota(jnp.int32, (rows, LANES), 1)
    return jnp.where(lane < 96, x[:rows], pieces_of)


def pad_rows(x, rows):
    if rows == x.shape[0]:
        return x
    return jnp.concatenate([x, jnp.zeros((rows - x.shape[0], LANES), x.dtype)], axis=0)


def unfold_rows(x, n):
    rows = x.shape[0]
    if rows >= n:
        return x[:n]
    stride = ceil8(n - rows)
    lane = lax.broadcasted_iota(jnp.int32, (stride, LANES), 1)
    rest = jnp.zeros((stride, LANES), x.dtype)
    for k in range(3):
        moved = pltpu.roll(x[k * stride : (k + 1) * stride], 32 + 32 * k, 1)
        rest = jnp.where(jnp.logical_and(lane >= 32 * k, lane < 32 * k + 32), moved, rest)
    return jnp.concatenate([x, rest[: n - rows]], axis=0)


def split(dims, stage, slabs, merged, keep, sends):
    group = dims.groups[stage]
    count = slabs.shape[0] >> len(group)
    mine = 0
    for axis, bit in group:
        mine = mine * 2 + lax.rem(lax.div(lax.axis_index(axis), 1 << bit), 2)
    keep[...] = slabs[pl.ds(pl.multiple_of(mine * count, 16), count), :]
    for mask, send in enumerate(sends, 1):
        other = 0
        for j in range(len(group)):
            weight = 1 << j
            digit = lax.rem(lax.div(mine, weight), 2)
            other = other + weight * (1 - digit if mask & weight else digit)
        send[0:count, :] = slabs[pl.ds(pl.multiple_of(other * count, 16), count), :].astype(bf16)
        send[count:, :] = merged


def gather_up(keep, small, gots):
    count = keep.shape[0]
    slabs = [keep[...]] + [got[0:count, :].astype(f32) for got in gots]
    sums = [small[...]] + [got[count:, :].astype(f32) for got in gots]
    if len(gots) == 1:
        return (slabs[0] + slabs[1], sums[0] + sums[1])
    return tuple((x[0] + x[1]) + (x[2] + x[3]) for x in (slabs, sums))


def stage_kernel(dims, stage, keep, small, *refs):
    before, after = (len_sends(dims.groups[stage - 1]), len_sends(dims.groups[stage]))
    gots = refs[:before]
    keep_out, small_out = refs[-3 - after : -1 - after]
    sends, total = (refs[-1 - after : -1], refs[-1])
    slabs, merged = gather_up(keep, small, gots)
    total[...] = slabs
    merged = merged.astype(bf16)
    small_out[...] = merged.astype(f32)
    split(dims, stage, total, merged, keep_out, sends)


def len_sends(group):
    return (1 << len(group)) - 1


def last_kernel(dims, keep, small, *refs):
    gots, (kernel_out, gain_out, up_out, down_out) = (refs[:-4], refs[-4:])
    total, merged = gather_up(keep, small, gots)
    merged = unfold_rows(merged, 2 * (dims.size * dims.size + 1))
    size, channels, half, part = (dims.size, dims.channels, dims.half, dims.part)
    for layer in range(2):
        block = total[layer * dims.layer_rows : layer * dims.layer_rows + part]
        up_out[layer] = block[:, :half]
        down_out[layer] = block[:, half : 2 * half]
        for t in range(size * size + 1):
            at = layer * (size * size + 1) + t
            row = merged[at : at + 1, 0:channels]
            if t < size * size:
                kernel_out[t // size, t % size, layer : layer + 1, :] = row
            else:
                gain_out[layer : layer + 1, :] = row


def image_kernel(dims, grad0, upstream, taps0, after, out, ready, work):
    rows, cols, size = (dims.rows, dims.cols, dims.size)
    skip = dims.skipped_rows(Place(dims.row_count, dims.col_count))
    margin = (dims.ext_cols - cols) // 2

    def conv0(g, carry):
        at = group_start(g, cols)
        total = conv_group(grad0, at + 1, dims.ext_cols, rows, taps0, size, True)
        for r in range(rows):
            line = upstream[pl.ds((r + dims.h - skip) * dims.ext_cols + margin + at, 16), :]
            work[pl.ds(r * cols + at, 16), :] = round16(line) + total[r]
        return carry

    lax.fori_loop(0, -(-cols // 16), conv0, 0)
    for r in range(rows):
        out[r] = work[r * cols : (r + 1) * cols, 0 : dims.channels].astype(bf16)
    ready[...] = jnp.zeros(ready.shape, f32)


class Dims:
    def skipped_rows(self, place):
        if self.row_count > 2:
            return 0
        return jnp.where(place.has["above"], 0, self.h)


def dims_of(image, kernels, up_weights):
    d = Dims()
    d.row_count, d.col_count = (lax.axis_size("row"), lax.axis_size("col"))
    d.rows, d.cols, d.channels = image.shape
    d.size = kernels.shape[1]
    d.h = d.size // 2
    d.ext_rows, d.ext_cols = (d.rows + (d.h if d.row_count == 2 else 2 * d.h), d.cols + 8)
    d.wide = d.cols + 2 * SIDE
    d.ext_pad = -(-d.ext_rows * d.ext_cols // 32) * 32
    d.piece = 176
    d.line_step = 4
    d.half = d.channels // d.row_count
    d.part = up_weights.shape[2] // d.col_count
    d.layer_rows = ceil8(d.part)
    d.count = d.row_count * d.col_count
    d.small_rows = 80 if d.size == 7 and d.channels <= 96 else -(-2 * (d.size * d.size + 1) // 16) * 16
    d.factor = 1.0 / math.sqrt(d.rows * d.cols * d.count)
    row_bits, col_bits = (d.row_count.bit_length() - 1, d.col_count.bit_length() - 1)
    bits = [("row", b) for b in range(row_bits)] + [("col", b) for b in range(1, col_bits)]
    d.groups = [[("col", 0)]] + [bits[i : i + 2] for i in range(0, len(bits), 2)]
    d.stages = [bit for group in d.groups for bit in group]
    return d


def swap_by(d, group, mask):
    flip = {"row": 0, "col": 0}
    for j, (axis, bit) in enumerate(group):
        if mask >> (len(group) - 1 - j) & 1:
            flip[axis] |= 1 << bit
    pairs = []
    for r in range(d.row_count):
        for c in range(d.col_count):
            pairs.append((r * d.col_count + c, (r ^ flip["row"]) * d.col_count + (c ^ flip["col"])))
    return pairs


def run(kernel, outs, scratch, *args, in_hbm=0, sems=0, busy_us=1):
    shapes = [jax.ShapeDtypeStruct(shape, kind) for shape, kind in outs]
    space = pl.BlockSpec(memory_space=pltpu.VMEM)
    far = pl.BlockSpec(memory_space=pltpu.HBM)
    held = [pltpu.VMEM(shape, kind) for shape, kind in scratch]
    if sems:
        held.append(pltpu.SemaphoreType.DMA((sems,)))
    return pl.pallas_call(
        kernel,
        out_shape=shapes,
        in_specs=[far] * in_hbm + [space] * (len(args) - in_hbm),
        out_specs=[space] * len(shapes),
        scratch_shapes=held,
        compiler_params=pltpu.CompilerParams(vmem_limit_bytes=32 * 1024 * 1024),
        cost_estimate=pl.CostEstimate(flops=int(busy_us * 1e9), bytes_accessed=1 << 18, transcendentals=0),
    )(*args)


def per_device(image, kernels, gains, up_weights, down_weights, cotangent):
    d = dims_of(image, kernels, up_weights)
    bind = functools.partial
    rows, cols, channels = image.shape
    units = up_weights.shape[2]
    tile, ext, wide = (rows * cols, d.ext_pad, (rows + 4 * d.h) * d.wide)
    frame = (rows + 2 * d.h) * d.ext_cols + 16
    taps = ((d.size * d.size * 16, LANES), bf16)
    tap_sums = ((d.size * d.size * 8, LANES), f32)
    sums_rows = ceil8(d.size * d.size + 1)

    bands, others = (band_combos(d.row_count), other_combos(d.row_count))

    def strips_of(pairs, radii):
        return [(shape, bf16) for shape in strip_shapes(pairs, rows, cols, channels, radii)]

    image, *band_strips = run(
        bind(bands_kernel, d), [(image.shape, bf16)] + strips_of(bands, (2 * d.h,)), [], image, in_hbm=1, sems=1
    )
    other_strips = run(bind(others_kernel, d), strips_of(others, (2 * d.h,)), [], image, *band_strips)
    strips = exchange(band_strips, other_strips, d.row_count, d.col_count)
    mixing = [((2 * LANES, 2 * units), bf16), ((2 * units, 2 * LANES), bf16)]
    forward0, back0, forward1, back1, grad_in0, grad_out0, taps0, taps1, gains, own = run(
        bind(weights_kernel, d),
        mixing * 3 + [taps, taps, (gains.shape, f32), ((ext, LANES), f32)],
        [((2, channels, units), bf16), ((2, channels, units), bf16), ((d.size, d.size, 2, channels), f32)],
        up_weights,
        jnp.swapaxes(down_weights, 1, 2),
        jnp.transpose(kernels, (1, 2, 0, 3)),
        gains,
        in_hbm=4,
        sems=4,
        busy_us=2,
    )

    first = run(
        bind(first_kernel, d),
        [
            (image.shape, bf16),
            ((wide, LANES), f32),
            ((frame, LANES), f32),
            ((ext, LANES), bf16),
            ((ext, LANES), f32),
            ((ext, units), bf16),
            ((ext, units), bf16),
            ((tile, LANES), f32),
            ((tile, LANES), bf16),
            ((tile, units), bf16),
            ((tile, units), bf16),
            ((8, LANES), f32),
        ]
        + strips_of(bands, (2 * d.h, d.h)),
        [((ext, LANES), f32)],
        image,
        cotangent,
        taps0,
        taps1,
        gains,
        forward0,
        back0,
        forward1,
        back1,
        *strips,
        busy_us=15,
    )
    (final, x0, x1, unit0, inv0, hidden0, slope0, grad1, normed1, pre_grad1, hidden1, gain_part) = first[:12]
    band_strips = first[12:]
    other_strips = run(
        bind(grad_others_kernel, d), strips_of(others, (2 * d.h, d.h)), [], grad1, cotangent, *band_strips
    )
    strips = exchange(band_strips, other_strips, d.row_count, d.col_count)

    joined = ((d.row_count * units + 8, LANES), f32)
    taps_sum1, joined1, output = run(
        bind(sums_kernel, d),
        [((sums_rows, LANES), f32), joined, (image.shape, bf16)],
        [tap_sums],
        x1,
        grad1,
        normed1,
        pre_grad1,
        hidden1,
        cotangent,
        gain_part,
        final,
        busy_us=3,
    )

    held = d.count // 2 * 2 * d.layer_rows
    small = ((d.small_rows, LANES), f32)
    grad0, upstream, keep, sums, send = run(
        bind(third_kernel, d),
        [((frame, LANES), f32), ((ext, LANES), f32), ((held, LANES), f32), small, ((held + d.small_rows, LANES), bf16)],
        [
            ((wide, LANES), f32),
            ((frame, LANES), f32),
            tap_sums,
            ((ext, LANES), bf16),
            ((ext, LANES), bf16),
            ((ext, units), bf16),
            ((8, LANES), f32),
            ((sums_rows, LANES), f32),
            joined,
            ((2 * held, LANES), f32),
        ],
        grad1,
        cotangent,
        taps1,
        gains,
        grad_in0,
        grad_out0,
        x0,
        unit0,
        inv0,
        hidden0,
        slope0,
        own,
        taps_sum1,
        joined1,
        *strips,
        busy_us=12,
    )
    axes = ("row", "col")
    sends = [send]
    for stage, group in enumerate(d.groups):
        gots = [lax.ppermute(x, axes, swap_by(d, group, mask)) for mask, x in enumerate(sends, 1)]
        ready = []
        if stage == 1:
            gradient, *ready = run(
                bind(image_kernel, d),
                [(image.shape, bf16), ((8, LANES), f32)],
                [((tile, LANES), f32)],
                grad0,
                upstream,
                taps0,
                sums,
                busy_us=3,
            )
        if stage + 1 < len(d.groups):
            after = d.groups[stage + 1]
            whole, held = (held, held >> len(after))
            keep, sums, *sends = run(
                bind(stage_kernel, d, stage + 1),
                [((held, LANES), f32), small] + [((held + d.small_rows, LANES), bf16)] * len_sends(after),
                [((whole, LANES), f32)],
                keep,
                sums,
                *gots,
                *ready,
            )
    kernel_out, gain_out, up_out, down_out = run(
        bind(last_kernel, d),
        [
            ((d.size, d.size, 2, channels), f32),
            (gains.shape, f32),
            ((2, d.part, d.half), f32),
            ((2, d.part, d.half), f32),
        ],
        [],
        keep,
        sums,
        *gots,
    )
    kernel_out = jnp.transpose(kernel_out, (2, 0, 1, 3))
    return (output, gradient, kernel_out, gain_out, jnp.swapaxes(up_out, 1, 2), down_out)


def solution(mesh):
    placed = (P("row", "col", None), P(), P(), P(), P(), P("row", "col", None))
    return jax.shard_map(
        per_device,
        mesh=mesh,
        in_specs=placed,
        out_specs=(
            P("row", "col", None),
            P("row", "col", None),
            P(),
            P(),
            P(None, "row", "col"),
            P(None, "col", "row"),
        ),
        check_vma=False,
    )
```

```python
import functools
import math

import jax
import jax.numpy as jnp
from jax import lax
from jax.experimental import pallas as pl
from jax.experimental.pallas import tpu as pltpu
from jax.sharding import PartitionSpec as P

epsilon = 1e-06
inv_sqrt_two = 0.7071067811865476
inv_sqrt_two_pi = 0.3989422804014327
log2_e = 1.4426950408889634
LANES = 128
SIDE = 8
f32, bf16 = (jnp.float32, jnp.bfloat16)


def ceil8(n):
    return -(-n // 8) * 8


def combos(row_count):
    listed = [(None, 0), (None, 1), (0, None), (0, 0), (0, 1)]
    if row_count > 2:
        listed += [(1, None), (1, 0), (1, 1)]
    return listed


def partner(index, start, count):
    if start is None:
        return index
    other = index + 1 if (index - start) % 2 == 0 else index - 1
    return other if 0 <= other < count else None


def swap_pairs(row_count, col_count, row_start, col_start):
    pairs = []
    for r in range(row_count):
        for c in range(col_count):
            pr, pc = (partner(r, row_start, row_count), partner(c, col_start, col_count))
            if pr is None:
                pr, pc = (r, c ^ 1)
            elif pc is None:
                pr, pc = (r ^ 1 if row_start is None else pr, c)
            pairs.append((r * col_count + c, pr * col_count + pc))
    return pairs


def exchange(bands, others, row_count, col_count):
    got = {}
    for strips, pairs in ((bands, band_combos(row_count)), (others, other_combos(row_count))):
        for strip, (rs, cs) in zip(strips, pairs):
            got[rs, cs] = lax.ppermute(strip, ("row", "col"), swap_pairs(row_count, col_count, rs, cs))
    return [got[pair] for pair in combos(row_count)]


class Place:
    def __init__(self, row_count, col_count):
        row, col = (lax.axis_index("row"), lax.axis_index("col"))
        self.even_row, self.even_col = (lax.rem(row, 2) == 0, lax.rem(col, 2) == 0)
        self.has = {
            "above": row > 0,
            "below": row < row_count - 1,
            "left": col > 0,
            "right": col < col_count - 1,
        }
        self.row_count = row_count


def band_combos(row_count):
    return [pair for pair in combos(row_count) if pair[1] is None]


def other_combos(row_count):
    return [pair for pair in combos(row_count) if pair[1] is not None]


def write_strips(place, outs, takes, pairs):
    for out, (rs, cs) in zip(outs, pairs):
        at = 0
        for take, radius, rows, cols in takes:
            row_sets = [slice(0, rows)] * 2
            col_sets = [slice(0, cols)] * 2
            if rs is not None:
                row_sets = [slice(rows - radius, rows), slice(0, radius)]
                if rs == 1:
                    row_sets = row_sets[::-1]
            if cs is not None:
                col_sets = [slice(cols - SIDE, cols), slice(0, SIDE)]
                if cs == 1:
                    col_sets = col_sets[::-1]
            count = row_sets[0].stop - row_sets[0].start
            for i in range(count):
                parts = {}
                for er in (0, 1):
                    for ec in (0, 1):
                        key = (row_sets[er].start + i, col_sets[ec].start, col_sets[ec].stop)
                        if key not in parts:
                            parts[key] = take(*key)
                        parts[er, ec] = parts[key]
                if cs is None:
                    pick = [parts[0, 0], parts[1, 0]]
                else:
                    pick = [jnp.where(place.even_col, parts[e, 0], parts[e, 1]) for e in (0, 1)]
                value = pick[0] if rs is None else jnp.where(place.even_row, pick[0], pick[1])
                out[at + i] = value.astype(out.dtype)
            at += count


def strip_shapes(pairs, rows, cols, channels, radii):
    shapes = []
    for rs, cs in pairs:
        height = sum(rows if rs is None else radius for radius in radii)
        shapes.append((height, cols if cs is None else SIDE, channels))
    return shapes


def received(place, strips, row_sections):
    table = dict(zip(combos(place.row_count), strips))
    full_start, band_start = row_sections

    def along(rs, cs, i):
        return table[rs, cs][(full_start if rs is None else band_start) + i].astype(f32)

    def column(rs, side, i):
        if side is None:
            return along(rs, None, i)
        near, far = (along(rs, 0, i), along(rs, 1, i))
        if side == "left":
            return jnp.where(place.even_col, far, near)
        return jnp.where(place.even_col, near, far)

    def read(vertical, side, i):
        if vertical is None:
            value = column(None, side, i)
        elif place.row_count == 2:
            value = column(0, side, i)
        else:
            near, far = (column(0, side, i), column(1, side, i))
            if vertical == "above":
                value = jnp.where(place.even_row, far, near)
            else:
                value = jnp.where(place.even_row, near, far)
        if vertical is not None:
            value = jnp.where(place.has[vertical], value, 0.0)
        if side is not None:
            value = jnp.where(place.has[side], value, 0.0)
        return value

    return read


def assemble(place, target, own, read, radius, rows, cols, channels):
    width = cols + 2 * SIDE
    target[...] = jnp.zeros(target.shape, f32)
    for vertical, start, count in (("above", 0, radius), (None, radius, rows), ("below", radius + rows, radius)):
        for i in range(count):
            base = (start + i) * width
            middle = own(i) if vertical is None else read(vertical, None, i)
            target[base + SIDE : base + SIDE + cols, 0:channels] = middle
            target[base : base + SIDE, 0:channels] = read(vertical, "left", i)
            target[base + SIDE + cols : base + width, 0:channels] = read(vertical, "right", i)


def spread_taps(kernel_ref, layer, target):
    size, channels = (kernel_ref.shape[0], kernel_ref.shape[3])
    for a in range(size):
        for b in range(size):
            t = a * size + b
            row = pad_lanes(kernel_ref[a, b, layer : layer + 1, :])
            target[t * 16 : t * 16 + 16, :] = jnp.broadcast_to(row, (16, LANES)).astype(bf16)


def tree_sum(terms):
    while len(terms) > 1:
        pairs = [terms[i] + terms[i + 1] for i in range(0, len(terms) - 1, 2)]
        terms = pairs + ([terms[-1]] if len(terms) % 2 else [])
    return terms[0]


def conv_group(src, base, stride, rows_out, taps, size, flipped=False):
    total = [None] * rows_out
    for first in range(0, size, 2):
        columns = range(first, min(first + 2, size))
        weights = []
        for b in columns:
            order = [a * size + b for a in range(size)]
            if flipped:
                order = [size * size - 1 - t for t in order]
            weights.append([taps[t * 16 : t * 16 + 16, :] for t in order])
        windows = [[] for _ in columns]
        for i in range(rows_out + size - 1):
            for window, b in zip(windows, columns):
                window.append(src[pl.ds(base + i * stride + b, 16), :].astype(bf16))
            r = i - size + 1
            if r >= 0:
                sums = [
                    tree_sum([window[r + a] * weight[a] for a in range(size)])
                    for window, weight in zip(windows, weights)
                ]
                term = tree_sum(sums).astype(f32)
                total[r] = term if total[r] is None else total[r] + term
    return total


def group_start(g, cols):
    return pl.multiple_of(jnp.minimum(g * 16, cols - 16), 8)


def kernel_sums(src, src_base, src_stride, grad, grad_base, grad_stride, rows, cols, size, sums):
    sums[...] = jnp.zeros(sums.shape, f32)

    def group(g, carry):
        at = pl.multiple_of(g * 16, 16)
        grads = [grad[pl.ds(grad_base + i * grad_stride + at, 16), :].astype(bf16) for i in range(rows)]
        for b in range(size):
            lines = [
                src[pl.ds(src_base + i * src_stride + at + b, 16), :].astype(bf16) for i in range(rows + size - 1)
            ]
            for a in range(size):
                term = tree_sum([lines[r + a] * grads[r] for r in range(rows)]).astype(f32)
                t = (a * size + b) * 8
                sums[t : t + 8, :] += term[0:8] + term[8:16]
        return carry

    lax.fori_loop(0, cols // 16, group, 0)


def diagonal(first, second):
    top = jnp.concatenate([first, jnp.zeros((first.shape[0], second.shape[1]), first.dtype)], axis=1)
    bottom = jnp.concatenate([jnp.zeros((second.shape[0], first.shape[1]), first.dtype), second], axis=1)
    return jnp.concatenate([top, bottom], axis=0)


def together(steps):
    steps = list(steps)
    while steps:
        steps = [step for step in steps if next(step, steps) is not steps]


def by_blocks(function, *arrays, size=16):
    count = arrays[0].shape[0]
    results = [function(*(x[i : i + size] for x in arrays)) for i in range(0, count, size)]
    return tuple(jnp.concatenate(parts, axis=0) for parts in zip(*results))


def in_channels(shape, channels):
    return lax.broadcasted_iota(jnp.int32, shape, 1) < channels


def high_low(x):
    high = x.astype(bf16)
    return (jnp.concatenate([high, (x - high.astype(f32)).astype(bf16)], axis=1),)


def side_by_side(x, y):
    return jnp.concatenate([x, y], axis=1)


def layer_norm(parts, gain, channels, ones):
    def centre(x, total):
        centred = jnp.where(in_channels(x.shape, channels), x - total * (1.0 / channels), 0.0)
        return (centred, (centred * centred).astype(bf16))

    def finish(centred, total):
        inverse = lax.rsqrt(total * (1.0 / channels) + epsilon)
        unit = centred * inverse
        return (unit, inverse, (unit * gain).astype(bf16))

    totals = [dot(by_blocks(high_low, x)[0], jnp.ones((2 * LANES, LANES), bf16)) for x in parts]
    yield
    centred, squares = zip(*(by_blocks(centre, x, total) for x, total in zip(parts, totals)))
    variances = dot(side_by_side(*squares), ones)
    yield
    return [by_blocks(finish, c, variances[:, k * LANES : (k + 1) * LANES]) for k, c in enumerate(centred)]


def norm_backward(normed_grad, unit, inverse, gain, channels, ones):
    def products(normed_grad, unit):
        m = normed_grad * gain
        return (side_by_side(m.astype(bf16), (m * unit).astype(bf16)),)

    def finish(normed_grad, unit, inverse, sums):
        along = sums[:, :LANES] + unit * sums[:, LANES:]
        grad = inverse * (normed_grad * gain - along * (1.0 / channels))
        return (round16(jnp.where(in_channels(grad.shape, channels), grad, 0.0)),)

    sums = dot(by_blocks(products, normed_grad, unit)[0], ones)
    yield
    return by_blocks(finish, normed_grad, unit, inverse, sums)[0]


def gelu_parts(v):
    p = 0.3275911 * inv_sqrt_two
    c1, c2, c3, c4, c5 = (
        0.5 * c / p ** (k + 1)
        for k, c in enumerate((0.254829592, -0.284496736, 1.421413741, -1.453152027, 1.061405429))
    )
    t = pl.reciprocal(jnp.abs(v) + 1.0 / p, approx=True)
    bell = jnp.exp2(v * v * (-0.5 * log2_e))
    tail = ((((c5 * t + c4) * t + c3) * t + c2) * t + c1) * t * bell
    cdf = jnp.where(v >= 0.0, 1.0 - tail, tail)
    return (v * cdf, cdf + v * (bell * inv_sqrt_two_pi))


def dot(x, w):
    return jnp.dot(x, w, preferred_element_type=f32)


def dot_leading(x, y):
    return lax.dot_general(x, y, (((0,), (0,)), ((), ())), preferred_element_type=f32)


def pad_lanes(x):
    rows, channels = x.shape
    return jnp.concatenate([x, jnp.zeros((rows, LANES - channels), x.dtype)], axis=1)


def pieces(total, size):
    return [(start, min(size, total - start)) for start in range(0, total, size)]


def round16(x):
    return x.astype(bf16).astype(f32)


def fetch(sources, targets, sems):
    copies = [pltpu.make_async_copy(a, b, sems.at[i]) for i, (a, b) in enumerate(zip(sources, targets))]
    for copy in copies:
        copy.start()
    for copy in copies:
        copy.wait()


def image_take(ref):
    return lambda i, lo, hi: ref[i].astype(f32)[lo:hi]


def flat_take(ref, cols, channels):
    return lambda i, lo, hi: ref[i * cols + lo : i * cols + hi, 0:channels]


def bands_kernel(dims, image_in, image, *refs):
    outs, sems = (refs[:-1], refs[-1])
    place = Place(dims.row_count, dims.col_count)
    fetch((image_in,), (image,), sems)
    takes = [(image_take(image), 2 * dims.h, dims.rows, dims.cols)]
    write_strips(place, outs, takes, band_combos(dims.row_count))


def others_kernel(dims, image, *refs):
    outs = refs[len(band_combos(dims.row_count)) :]
    place = Place(dims.row_count, dims.col_count)
    takes = [(image_take(image), 2 * dims.h, dims.rows, dims.cols)]
    write_strips(place, outs, takes, other_combos(dims.row_count))


def grad_others_kernel(dims, grad1, cot, *refs):
    outs = refs[len(band_combos(dims.row_count)) :]
    place = Place(dims.row_count, dims.col_count)
    takes = [
        (flat_take(grad1, dims.cols, dims.channels), 2 * dims.h, dims.rows, dims.cols),
        (image_take(cot), dims.h, dims.rows, dims.cols),
    ]
    write_strips(place, outs, takes, other_combos(dims.row_count))


def weights_kernel(dims, up_in, down_t_in, kernels_in, gains_in, *refs):
    forward0, back0, forward1, back1, grad_in0, grad_out0, taps0, taps1, gains, own, up_w, down_w, kernels, sems = refs
    fetch((up_in, down_t_in, kernels_in, gains_in), (up_w, down_w, kernels, gains), sems)
    spread_taps(kernels, 0, taps0)
    spread_taps(kernels, 1, taps1)
    channels, units = up_w.shape[1:]
    blank = jnp.zeros((LANES - channels, units), f32)
    wide, tall = ([], [])
    for layer in range(2):
        for ref in (up_w, down_w):
            full = jnp.concatenate([ref[layer].astype(f32), blank], axis=0)
            wide.append(full.astype(bf16))
            tall.append(full.T.astype(bf16))
    (up0, down_t0, up1, down_t1), (up_t0, down0, up_t1, down1) = (wide, tall)
    forward0[...] = diagonal(up0, up0)
    back0[...] = diagonal(down0, down0)
    forward1[...] = diagonal(up1, down_t1)
    back1[...] = diagonal(down1, up_t1)
    grad_in0[...] = diagonal(down_t0, down_t0)
    grad_out0[...] = diagonal(up_t0, up_t0)
    own_pixels(dims, own)


def own_pixels(dims, own):
    skip = dims.skipped_rows(Place(dims.row_count, dims.col_count))
    ext_rows, ext_cols, h = (dims.ext_rows, dims.ext_cols, dims.h)
    col = lax.broadcasted_iota(jnp.int32, (ext_cols, LANES), 0) - (ext_cols - dims.cols) // 2
    inside = jnp.where(jnp.logical_and(col >= 0, col < dims.cols), 1.0, 0.0)
    for r in range(ext_rows):
        mine = jnp.logical_and(r + skip >= h, r + skip < h + dims.rows)
        own[r * ext_cols : (r + 1) * ext_cols, :] = jnp.where(mine, inside, 0.0)
    used = ext_rows * ext_cols
    if dims.ext_pad > used:
        own[used:, :] = jnp.zeros((dims.ext_pad - used, LANES), f32)


def first_kernel(dims, *refs):
    count = len(combos(dims.row_count))
    image, cot, taps0, taps1, gains, forward0, back0, forward1, back1 = refs[:9]
    strips = refs[9 : 9 + count]
    refs = refs[9 + count :]
    (output, x0, x1, unit0, inv0, hidden0, slope0, grad1, normed1, pre_grad1, hidden1, gain_sum) = refs[:12]
    outs, conv = (refs[12:-1], refs[-1])
    place = Place(dims.row_count, dims.col_count)
    rows, cols, channels, h, size = (dims.rows, dims.cols, dims.channels, dims.h, dims.size)
    ext_rows, ext_cols, wide = (dims.ext_rows, dims.ext_cols, dims.wide)
    skip = dims.skipped_rows(place)
    read = received(place, strips, (0, 0))
    assemble(place, x0, lambda i: image[i].astype(f32), read, 2 * h, rows, cols, channels)

    x1[...] = jnp.zeros(x1.shape, f32)
    if dims.ext_pad > ext_rows * ext_cols:
        conv[ext_rows * ext_cols :, :] = jnp.zeros((dims.ext_pad - ext_rows * ext_cols, LANES), f32)
    frame = pl.multiple_of(skip * ext_cols, 8)

    def conv0(g, carry):
        at = group_start(g, ext_cols)
        base = pl.multiple_of(skip * wide, 8) + at
        total = conv_group(x0, base + 1, wide, ext_rows, taps0, size)
        for r in range(ext_rows):
            conv[pl.ds(r * ext_cols + at, 16), :] = total[r]
            x1[pl.ds(frame + r * ext_cols + at, 16), :] = x0[pl.ds(base + (r + h) * wide + 4, 16), :]
        return carry

    lax.fori_loop(0, -(-ext_cols // 16), conv0, 0)
    gain = pad_lanes(gains[0:1, :])
    ones = diagonal(jnp.ones((LANES, LANES), bf16), jnp.ones((LANES, LANES), bf16))
    half = dims.ext_pad // 2

    def mix0(start, n):
        spans = [(start, n), (half + start, n)]
        parts = yield from layer_norm([conv[at : at + n, :] for at, n in spans], gain, channels, ones)
        pres = dot(side_by_side(parts[0][2], parts[1][2]), forward0[...])
        yield
        count = pres.shape[1] // 2
        hiddens = []
        for k, ((at, n), (unit, inverse, _)) in enumerate(zip(spans, parts)):
            unit0[at : at + n, :] = unit.astype(bf16)
            inv0[at : at + n, :] = inverse

            def activate(pre):
                value, slope = gelu_parts(pre)
                return (value.astype(bf16), slope.astype(bf16))

            hidden, slope = by_blocks(activate, pres[:, k * count : (k + 1) * count])
            hidden0[at : at + n, :] = hidden
            slope0[at : at + n, :] = slope
            hiddens.append(hidden)
        branches = dot(side_by_side(*hiddens), back0[...])
        yield
        for k, (at, n) in enumerate(spans):
            px = pl.ds(frame + at, n)
            x1[px, :] = round16(x1[px, :] + branches[:, k * LANES : (k + 1) * LANES])
    together([mix0(start, n) for start, n in pieces(half, dims.piece)])
    clear_outside(place, x1, dims)

    def conv1(g, carry):
        at = group_start(g, cols)
        total = conv_group(x1, at + 1, ext_cols, rows, taps1, size)
        for r in range(rows):
            conv[pl.ds(r * cols + at, 16), :] = total[r]
        return carry

    lax.fori_loop(0, -(-cols // 16), conv1, 0)
    gain1 = pad_lanes(gains[1:2, :])
    gain_sum[...] = jnp.zeros(gain_sum.shape, f32)
    lines = dims.line_step
    step = lines * cols

    def mix1(k):
        px = slice(k * step, (k + 1) * step)
        middle = k * step + step // 2
        parts = yield from layer_norm(
            [conv[k * step : middle, :], conv[middle : (k + 1) * step, :]], gain1, channels, ones
        )
        unit, inverse, normed = (jnp.concatenate(pair, axis=0) for pair in zip(*parts))
        normed1[px, :] = normed
        upstream = pad_lanes(cot[k * lines : (k + 1) * lines].reshape(step, channels))
        both = dot(side_by_side(normed, upstream), forward1[...])
        yield

        def activate(pre, hidden_grad):
            value, slope = gelu_parts(pre)
            return (value.astype(bf16), (hidden_grad * slope).astype(bf16))

        count = both.shape[1] // 2
        hidden, pre_grad = by_blocks(activate, both[:, :count], both[:, count:])
        hidden1[px, :] = hidden
        pre_grad1[px, :] = pre_grad
        both = dot(side_by_side(hidden, pre_grad), back1[...])
        yield
        branch, normed_grad = (both[:, :LANES], both[:, LANES:])
        for i in range(lines):
            start = (k * lines + i + h) * ext_cols + 4
            line = x1[start : start + cols, :] + branch[i * cols : (i + 1) * cols]
            output[k * lines + i] = line[:, :channels].astype(bf16)
        product = normed_grad * unit
        gain_sum[...] += jnp.sum(product.reshape(step // 8, 8, LANES), axis=0)
        grad1[px, :] = yield from norm_backward(normed_grad, unit, inverse, gain1, channels, ones)

    together([mix1(k) for k in range(rows // lines)])

    takes = [(flat_take(grad1, cols, channels), 2 * h, rows, cols), (image_take(cot), h, rows, cols)]
    write_strips(place, outs, takes, band_combos(dims.row_count))


def clear_outside(place, flat, dims):
    h, frame_rows, ext_cols = (dims.h, dims.rows + 2 * dims.h, dims.ext_cols)
    margin = (ext_cols - dims.cols) // 2

    @pl.when(jnp.logical_not(place.has["above"]))
    def _():
        flat[0 : h * ext_cols, :] = jnp.zeros((h * ext_cols, LANES), f32)

    @pl.when(jnp.logical_not(place.has["below"]))
    def _():
        last = (frame_rows - h) * ext_cols
        flat[last:, :] = jnp.zeros((flat.shape[0] - last, LANES), f32)

    @pl.when(jnp.logical_not(place.has["left"]))
    def _():
        for r in range(frame_rows):
            flat[r * ext_cols : r * ext_cols + margin, :] = jnp.zeros((margin, LANES), f32)

    @pl.when(jnp.logical_not(place.has["right"]))
    def _():
        for r in range(frame_rows):
            flat[(r + 1) * ext_cols - margin : (r + 1) * ext_cols, :] = jnp.zeros((margin, LANES), f32)


def sums_kernel(
    dims, x1, grad1, normed1, pre_grad1, hidden1, cot, gain_part, final, taps_sum, joined, output, sums
):
    output[...] = final[...]
    kernel_sums(x1, 1, dims.ext_cols, grad1, 0, dims.cols, dims.rows, dims.cols, dims.size, sums)
    store_sums(dims, sums, gain_part[...], taps_sum)
    upstream = pad_lanes(cot[...].reshape(dims.rows * dims.cols, dims.channels))
    up = dot_leading(normed1[...], pre_grad1[...]).T * dims.factor
    down = dot_leading(upstream, hidden1[...]).T * dims.factor
    join_sums(dims, up, down, joined)


def join_sums(dims, up, down, target):
    units, half = (up.shape[0], dims.half)
    lane = lax.broadcasted_iota(jnp.int32, (units, LANES), 1)
    for r in range(dims.row_count):
        first = pltpu.roll(up, LANES - r * half, 1) if r else up
        shift = (half - r * half) % LANES
        second = pltpu.roll(down, shift, 1) if shift else down
        both = jnp.where(lane < half, first, jnp.where(lane < 2 * half, second, 0.0))
        target[r * units : (r + 1) * units, :] = both
    target[dims.row_count * units :, :] = jnp.zeros((8, LANES), f32)


def store_sums(dims, sums, gain_part, target):
    taps = dims.size * dims.size
    target[...] = jnp.zeros(target.shape, f32)
    for t in range(taps):
        target[t : t + 1, :] = jnp.sum(sums[t * 8 : t * 8 + 8, :], axis=0, keepdims=True)
    target[taps : taps + 1, :] = jnp.sum(gain_part, axis=0, keepdims=True)


def third_kernel(dims, *refs):
    count = len(combos(dims.row_count))
    (grad1, cot, taps1, gains, grad_in0, grad_out0, x0, unit0, inv0, hidden0, slope0) = refs[:11]
    (own, taps_sum1, joined1) = refs[11:14]
    strips = refs[14 : 14 + count]
    (grad0, upstream, keep, small_keep, send) = refs[14 + count : 19 + count]
    (wide_grad, cot_frame, sums, normed0, flow0, pre_grad0, gain_sum, small, tall, slabs) = refs[19 + count :]
    place = Place(dims.row_count, dims.col_count)
    rows, cols, channels, h, size = (dims.rows, dims.cols, dims.channels, dims.h, dims.size)
    ext_rows, ext_cols, wide = (dims.ext_rows, dims.ext_cols, dims.wide)
    skip = dims.skipped_rows(place)
    read = received(place, strips, (0, 0))
    assemble(
        place, wide_grad, lambda i: grad1[i * cols : (i + 1) * cols, 0:channels], read, 2 * h, rows, cols, channels
    )
    read_cot = received(place, strips, (rows, 2 * h))
    margin = (ext_cols - cols) // 2
    cot_frame[...] = jnp.zeros(cot_frame.shape, f32)
    for vertical, start, n in (("above", 0, h), (None, h, rows), ("below", h + rows, h)):
        for i in range(n):
            base = (start + i) * ext_cols
            line = cot[i].astype(f32) if vertical is None else read_cot(vertical, None, i)
            cot_frame[base + margin : base + margin + cols, 0:channels] = line
            cot_frame[base : base + margin, 0:channels] = read_cot(vertical, "left", i)[SIDE - margin :]
            cot_frame[base + margin + cols : base + ext_cols, 0:channels] = read_cot(vertical, "right", i)[:margin]

    used = ext_rows * ext_cols
    if dims.ext_pad > used:
        upstream[used:, :] = jnp.zeros((dims.ext_pad - used, LANES), f32)
    grad0[...] = jnp.zeros(grad0.shape, f32)
    frame = pl.multiple_of(skip * ext_cols, 8)

    def conv1(g, carry):
        at = group_start(g, ext_cols)
        total = conv_group(wide_grad, pl.multiple_of(skip * wide, 8) + at + 1, wide, ext_rows, taps1, size, True)
        for r in range(ext_rows):
            px = pl.ds(r * ext_cols + at, 16)
            upstream[px, :] = cot_frame[pl.ds(frame + r * ext_cols + at, 16), :] + total[r]
        return carry

    lax.fori_loop(0, -(-ext_cols // 16), conv1, 0)
    gain = pad_lanes(gains[0:1, :])
    gain_sum[...] = jnp.zeros(gain_sum.shape, f32)
    ones = diagonal(jnp.ones((LANES, LANES), bf16), jnp.ones((LANES, LANES), bf16))
    half_px = dims.ext_pad // 2

    def mix0(start, n):
        spans = [(start, n), (half_px + start, n)]
        flows = [upstream[at : at + n, :].astype(bf16) for at, n in spans]
        hidden_grads = dot(side_by_side(*flows), grad_in0[...])
        yield
        count = hidden_grads.shape[1] // 2

        def slope_times(grad, slope):
            return ((grad * slope.astype(f32)).astype(bf16),)

        pre_grads = [
            by_blocks(slope_times, hidden_grads[:, k * count : (k + 1) * count], slope0[at : at + n, :])[0]
            for k, (at, n) in enumerate(spans)
        ]
        both = dot(side_by_side(*pre_grads), grad_out0[...])
        yield
        normed_grads = (both[:, :LANES], both[:, LANES:])
        for (at, n), flow, pre_grad, normed_grad in zip(spans, flows, pre_grads, normed_grads):
            mine = own[at : at + n, :]
            unit = unit0[at : at + n, :].astype(f32)
            normed0[at : at + n, :] = (unit * gain * mine).astype(bf16)
            flow0[at : at + n, :] = flow * mine.astype(bf16)
            pre_grad0[at : at + n, :] = pre_grad
            product = normed_grad * unit * mine
            gain_sum[...] += jnp.sum(product.reshape(n // 8, 8, LANES), axis=0)
            grad = yield from norm_backward(normed_grad, unit, inv0[at : at + n, :], gain, channels, ones)
            grad0[pl.ds(frame + at, n), :] = grad

    together([mix0(start, n) for start, n in pieces(half_px, dims.back_piece)])
    clear_outside(place, grad0, dims)
    kernel_sums(
        x0, h * wide + SIDE - h, wide, grad0, h * ext_cols + margin, ext_cols, rows, cols, size, sums
    )
    store_sums(dims, sums, gain_sum[...], small)

    taps_rows = size * size + 1
    merged = jnp.concatenate([small[0:taps_rows, :], taps_sum1[0:taps_rows, :]], axis=0) * dims.factor
    merged = fold_rows(merged, dims.small_rows, channels).astype(bf16)
    small_keep[...] = merged.astype(f32)

    layer_rows, part = (dims.layer_rows, dims.part)
    units = hidden0.shape[1]
    up0 = dot_leading(normed0[...], pre_grad0[...]).T * dims.factor
    down0 = dot_leading(flow0[...], hidden0[...]).T * dims.factor
    join_sums(dims, up0, down0, tall)
    slab_rows = 2 * layer_rows
    for r in range(dims.row_count):
        for c in range(dims.col_count):
            index = 0
            for axis, bit in dims.stages:
                index = 2 * index + ((r if axis == "row" else c) >> bit & 1)
            for layer, source in ((0, tall), (1, joined1)):
                to, at = (index * slab_rows + layer * layer_rows, r * units + c * part)
                slabs[to : to + layer_rows, :] = source[at : at + layer_rows, :]

    split(dims, 0, slabs, merged, keep, (send,))


def fold_rows(x, rows, used):
    n = x.shape[0]
    if rows >= n:
        return pad_rows(x, rows)
    assert used <= 96
    stride = ceil8(n - rows)
    rest = pad_rows(x[rows:], stride)
    pieces_of = pad_rows(jnp.concatenate([pltpu.roll(rest, 96 - 32 * k, 1) for k in range(3)], axis=0), rows)
    lane = lax.broadcasted_iota(jnp.int32, (rows, LANES), 1)
    return jnp.where(lane < 96, x[:rows], pieces_of)


def pad_rows(x, rows):
    if rows == x.shape[0]:
        return x
    return jnp.concatenate([x, jnp.zeros((rows - x.shape[0], LANES), x.dtype)], axis=0)


def unfold_rows(x, n):
    rows = x.shape[0]
    if rows >= n:
        return x[:n]
    stride = ceil8(n - rows)
    lane = lax.broadcasted_iota(jnp.int32, (stride, LANES), 1)
    rest = jnp.zeros((stride, LANES), x.dtype)
    for k in range(3):
        moved = pltpu.roll(x[k * stride : (k + 1) * stride], 32 + 32 * k, 1)
        rest = jnp.where(jnp.logical_and(lane >= 32 * k, lane < 32 * k + 32), moved, rest)
    return jnp.concatenate([x, rest[: n - rows]], axis=0)


def split(dims, stage, slabs, merged, keep, sends):
    group = dims.groups[stage]
    count = slabs.shape[0] >> len(group)
    mine = 0
    for axis, bit in group:
        mine = mine * 2 + lax.rem(lax.div(lax.axis_index(axis), 1 << bit), 2)
    keep[...] = slabs[pl.ds(pl.multiple_of(mine * count, 16), count), :]
    for mask, send in enumerate(sends, 1):
        other = 0
        for j in range(len(group)):
            weight = 1 << j
            digit = lax.rem(lax.div(mine, weight), 2)
            other = other + weight * (1 - digit if mask & weight else digit)
        send[0:count, :] = slabs[pl.ds(pl.multiple_of(other * count, 16), count), :].astype(bf16)
        send[count:, :] = merged


def gather_up(keep, small, gots):
    count = keep.shape[0]
    slabs = [keep[...]] + [got[0:count, :].astype(f32) for got in gots]
    sums = [small[...]] + [got[count:, :].astype(f32) for got in gots]
    if len(gots) == 1:
        return (slabs[0] + slabs[1], sums[0] + sums[1])
    return tuple((x[0] + x[1]) + (x[2] + x[3]) for x in (slabs, sums))


def stage_kernel(dims, stage, keep, small, *refs):
    before, after = (len_sends(dims.groups[stage - 1]), len_sends(dims.groups[stage]))
    gots = refs[:before]
    keep_out, small_out = refs[-3 - after : -1 - after]
    sends, total = (refs[-1 - after : -1], refs[-1])
    slabs, merged = gather_up(keep, small, gots)
    total[...] = slabs
    merged = merged.astype(bf16)
    small_out[...] = merged.astype(f32)
    split(dims, stage, total, merged, keep_out, sends)


def len_sends(group):
    return (1 << len(group)) - 1


def last_kernel(dims, keep, small, *refs):
    gots, (kernel_out, gain_out, up_out, down_out) = (refs[:-4], refs[-4:])
    total, merged = gather_up(keep, small, gots)
    merged = unfold_rows(merged, 2 * (dims.size * dims.size + 1))
    size, channels, half, part = (dims.size, dims.channels, dims.half, dims.part)
    for layer in range(2):
        block = total[layer * dims.layer_rows : layer * dims.layer_rows + part]
        up_out[layer] = block[:, :half]
        down_out[layer] = block[:, half : 2 * half]
        for t in range(size * size + 1):
            at = layer * (size * size + 1) + t
            row = merged[at : at + 1, 0:channels]
            if t < size * size:
                kernel_out[t // size, t % size, layer : layer + 1, :] = row
            else:
                gain_out[layer : layer + 1, :] = row


def image_kernel(dims, grad0, upstream, taps0, after, out, ready, work):
    rows, cols, size = (dims.rows, dims.cols, dims.size)
    skip = dims.skipped_rows(Place(dims.row_count, dims.col_count))
    margin = (dims.ext_cols - cols) // 2

    def conv0(g, carry):
        at = group_start(g, cols)
        total = conv_group(grad0, at + 1, dims.ext_cols, rows, taps0, size, True)
        for r in range(rows):
            line = upstream[pl.ds((r + dims.h - skip) * dims.ext_cols + margin + at, 16), :]
            work[pl.ds(r * cols + at, 16), :] = round16(line) + total[r]
        return carry

    lax.fori_loop(0, -(-cols // 16), conv0, 0)
    for r in range(rows):
        out[r] = work[r * cols : (r + 1) * cols, 0 : dims.channels].astype(bf16)
    ready[...] = jnp.zeros(ready.shape, f32)


class Dims:
    def skipped_rows(self, place):
        if self.row_count > 2:
            return 0
        return jnp.where(place.has["above"], 0, self.h)


def dims_of(image, kernels, up_weights):
    d = Dims()
    d.row_count, d.col_count = (lax.axis_size("row"), lax.axis_size("col"))
    d.rows, d.cols, d.channels = image.shape
    d.size = kernels.shape[1]
    d.h = d.size // 2
    d.ext_rows, d.ext_cols = (d.rows + (d.h if d.row_count == 2 else 2 * d.h), d.cols + 8)
    d.wide = d.cols + 2 * SIDE
    d.ext_pad = -(-d.ext_rows * d.ext_cols // 32) * 32
    d.piece = 176
    d.back_piece = 128
    d.line_step = 2
    d.half = d.channels // d.row_count
    d.part = up_weights.shape[2] // d.col_count
    d.layer_rows = ceil8(d.part)
    d.count = d.row_count * d.col_count
    d.small_rows = 80 if d.size == 7 and d.channels <= 96 else -(-2 * (d.size * d.size + 1) // 16) * 16
    d.factor = 1.0 / math.sqrt(d.rows * d.cols * d.count)
    row_bits, col_bits = (d.row_count.bit_length() - 1, d.col_count.bit_length() - 1)
    bits = [("row", b) for b in range(row_bits)] + [("col", b) for b in range(1, col_bits)]
    d.groups = [[("col", 0)]] + [bits[i : i + 2] for i in range(0, len(bits), 2)]
    d.stages = [bit for group in d.groups for bit in group]
    return d


def swap_by(d, group, mask):
    flip = {"row": 0, "col": 0}
    for j, (axis, bit) in enumerate(group):
        if mask >> (len(group) - 1 - j) & 1:
            flip[axis] |= 1 << bit
    pairs = []
    for r in range(d.row_count):
        for c in range(d.col_count):
            pairs.append((r * d.col_count + c, (r ^ flip["row"]) * d.col_count + (c ^ flip["col"])))
    return pairs


def run(kernel, outs, scratch, *args, in_hbm=0, sems=0, busy_us=1):
    shapes = [jax.ShapeDtypeStruct(shape, kind) for shape, kind in outs]
    space = pl.BlockSpec(memory_space=pltpu.VMEM)
    far = pl.BlockSpec(memory_space=pltpu.HBM)
    held = [pltpu.VMEM(shape, kind) for shape, kind in scratch]
    if sems:
        held.append(pltpu.SemaphoreType.DMA((sems,)))
    return pl.pallas_call(
        kernel,
        out_shape=shapes,
        in_specs=[far] * in_hbm + [space] * (len(args) - in_hbm),
        out_specs=[space] * len(shapes),
        scratch_shapes=held,
        compiler_params=pltpu.CompilerParams(vmem_limit_bytes=32 * 1024 * 1024),
        cost_estimate=pl.CostEstimate(flops=int(busy_us * 1e9), bytes_accessed=1 << 18, transcendentals=0),
    )(*args)


def per_device(image, kernels, gains, up_weights, down_weights, cotangent):
    d = dims_of(image, kernels, up_weights)
    bind = functools.partial
    rows, cols, channels = image.shape
    units = up_weights.shape[2]
    tile, ext, wide = (rows * cols, d.ext_pad, (rows + 4 * d.h) * d.wide)
    frame = (rows + 2 * d.h) * d.ext_cols + 16
    taps = ((d.size * d.size * 16, LANES), bf16)
    tap_sums = ((d.size * d.size * 8, LANES), f32)
    sums_rows = ceil8(d.size * d.size + 1)

    bands, others = (band_combos(d.row_count), other_combos(d.row_count))

    def strips_of(pairs, radii):
        return [(shape, bf16) for shape in strip_shapes(pairs, rows, cols, channels, radii)]

    image, *band_strips = run(
        bind(bands_kernel, d), [(image.shape, bf16)] + strips_of(bands, (2 * d.h,)), [], image, in_hbm=1, sems=1
    )
    other_strips = run(bind(others_kernel, d), strips_of(others, (2 * d.h,)), [], image, *band_strips)
    strips = exchange(band_strips, other_strips, d.row_count, d.col_count)
    mixing = [((2 * LANES, 2 * units), bf16), ((2 * units, 2 * LANES), bf16)]
    forward0, back0, forward1, back1, grad_in0, grad_out0, taps0, taps1, gains, own = run(
        bind(weights_kernel, d),
        mixing * 3 + [taps, taps, (gains.shape, f32), ((ext, LANES), f32)],
        [((2, channels, units), bf16), ((2, channels, units), bf16), ((d.size, d.size, 2, channels), f32)],
        up_weights,
        jnp.swapaxes(down_weights, 1, 2),
        jnp.transpose(kernels, (1, 2, 0, 3)),
        gains,
        in_hbm=4,
        sems=4,
        busy_us=2,
    )

    first = run(
        bind(first_kernel, d),
        [
            (image.shape, bf16),
            ((wide, LANES), f32),
            ((frame, LANES), f32),
            ((ext, LANES), bf16),
            ((ext, LANES), f32),
            ((ext, units), bf16),
            ((ext, units), bf16),
            ((tile, LANES), f32),
            ((tile, LANES), bf16),
            ((tile, units), bf16),
            ((tile, units), bf16),
            ((8, LANES), f32),
        ]
        + strips_of(bands, (2 * d.h, d.h)),
        [((ext, LANES), f32)],
        image,
        cotangent,
        taps0,
        taps1,
        gains,
        forward0,
        back0,
        forward1,
        back1,
        *strips,
        busy_us=15,
    )
    (final, x0, x1, unit0, inv0, hidden0, slope0, grad1, normed1, pre_grad1, hidden1, gain_part) = first[:12]
    band_strips = first[12:]
    other_strips = run(
        bind(grad_others_kernel, d), strips_of(others, (2 * d.h, d.h)), [], grad1, cotangent, *band_strips
    )
    strips = exchange(band_strips, other_strips, d.row_count, d.col_count)

    joined = ((d.row_count * units + 8, LANES), f32)
    taps_sum1, joined1, output = run(
        bind(sums_kernel, d),
        [((sums_rows, LANES), f32), joined, (image.shape, bf16)],
        [tap_sums],
        x1,
        grad1,
        normed1,
        pre_grad1,
        hidden1,
        cotangent,
        gain_part,
        final,
        busy_us=3,
    )

    held = d.count // 2 * 2 * d.layer_rows
    small = ((d.small_rows, LANES), f32)
    grad0, upstream, keep, sums, send = run(
        bind(third_kernel, d),
        [((frame, LANES), f32), ((ext, LANES), f32), ((held, LANES), f32), small, ((held + d.small_rows, LANES), bf16)],
        [
            ((wide, LANES), f32),
            ((frame, LANES), f32),
            tap_sums,
            ((ext, LANES), bf16),
            ((ext, LANES), bf16),
            ((ext, units), bf16),
            ((8, LANES), f32),
            ((sums_rows, LANES), f32),
            joined,
            ((2 * held, LANES), f32),
        ],
        grad1,
        cotangent,
        taps1,
        gains,
        grad_in0,
        grad_out0,
        x0,
        unit0,
        inv0,
        hidden0,
        slope0,
        own,
        taps_sum1,
        joined1,
        *strips,
        busy_us=12,
    )
    axes = ("row", "col")
    sends = [send]
    for stage, group in enumerate(d.groups):
        gots = [lax.ppermute(x, axes, swap_by(d, group, mask)) for mask, x in enumerate(sends, 1)]
        ready = []
        if stage == 1:
            gradient, *ready = run(
                bind(image_kernel, d),
                [(image.shape, bf16), ((8, LANES), f32)],
                [((tile, LANES), f32)],
                grad0,
                upstream,
                taps0,
                sums,
                busy_us=3,
            )
        if stage + 1 < len(d.groups):
            after = d.groups[stage + 1]
            whole, held = (held, held >> len(after))
            keep, sums, *sends = run(
                bind(stage_kernel, d, stage + 1),
                [((held, LANES), f32), small] + [((held + d.small_rows, LANES), bf16)] * len_sends(after),
                [((whole, LANES), f32)],
                keep,
                sums,
                *gots,
                *ready,
            )
    kernel_out, gain_out, up_out, down_out = run(
        bind(last_kernel, d),
        [
            ((d.size, d.size, 2, channels), f32),
            (gains.shape, f32),
            ((2, d.part, d.half), f32),
            ((2, d.part, d.half), f32),
        ],
        [],
        keep,
        sums,
        *gots,
    )
    kernel_out = jnp.transpose(kernel_out, (2, 0, 1, 3))
    return (output, gradient, kernel_out, gain_out, jnp.swapaxes(up_out, 1, 2), down_out)


def solution(mesh):
    placed = (P("row", "col", None), P(), P(), P(), P(), P("row", "col", None))
    return jax.shard_map(
        per_device,
        mesh=mesh,
        in_specs=placed,
        out_specs=(
            P("row", "col", None),
            P("row", "col", None),
            P(),
            P(),
            P(None, "row", "col"),
            P(None, "col", "row"),
        ),
        check_vma=False,
    )
```

```python
import functools
import math

import jax
import jax.numpy as jnp
from jax import lax
from jax.experimental import pallas as pl
from jax.experimental.pallas import tpu as pltpu
from jax.sharding import PartitionSpec as P

epsilon = 1e-06
inv_sqrt_two = 0.7071067811865476
inv_sqrt_two_pi = 0.3989422804014327
log2_e = 1.4426950408889634
LANES = 128
SIDE = 8
f32, bf16 = (jnp.float32, jnp.bfloat16)


def ceil8(n):
    return -(-n // 8) * 8


def combos(row_count):
    listed = [(None, 0), (None, 1), (0, None), (0, 0), (0, 1)]
    if row_count > 2:
        listed += [(1, None), (1, 0), (1, 1)]
    return listed


def partner(index, start, count):
    if start is None:
        return index
    other = index + 1 if (index - start) % 2 == 0 else index - 1
    return other if 0 <= other < count else None


def swap_pairs(row_count, col_count, row_start, col_start):
    pairs = []
    for r in range(row_count):
        for c in range(col_count):
            pr, pc = (partner(r, row_start, row_count), partner(c, col_start, col_count))
            if pr is None:
                pr, pc = (r, c ^ 1)
            elif pc is None:
                pr, pc = (r ^ 1 if row_start is None else pr, c)
            pairs.append((r * col_count + c, pr * col_count + pc))
    return pairs


def exchange(bands, others, row_count, col_count):
    got = {}
    for strips, pairs in ((bands, band_combos(row_count)), (others, other_combos(row_count))):
        for strip, (rs, cs) in zip(strips, pairs):
            got[rs, cs] = lax.ppermute(strip, ("row", "col"), swap_pairs(row_count, col_count, rs, cs))
    return [got[pair] for pair in combos(row_count)]


class Place:
    def __init__(self, row_count, col_count):
        row, col = (lax.axis_index("row"), lax.axis_index("col"))
        self.even_row, self.even_col = (lax.rem(row, 2) == 0, lax.rem(col, 2) == 0)
        self.has = {
            "above": row > 0,
            "below": row < row_count - 1,
            "left": col > 0,
            "right": col < col_count - 1,
        }
        self.row_count = row_count


def band_combos(row_count):
    return [pair for pair in combos(row_count) if pair[1] is None]


def other_combos(row_count):
    return [pair for pair in combos(row_count) if pair[1] is not None]


def write_strips(place, outs, takes, pairs):
    for out, (rs, cs) in zip(outs, pairs):
        at = 0
        for take, radius, rows, cols in takes:
            row_sets = [slice(0, rows)] * 2
            col_sets = [slice(0, cols)] * 2
            if rs is not None:
                row_sets = [slice(rows - radius, rows), slice(0, radius)]
                if rs == 1:
                    row_sets = row_sets[::-1]
            if cs is not None:
                col_sets = [slice(cols - SIDE, cols), slice(0, SIDE)]
                if cs == 1:
                    col_sets = col_sets[::-1]
            count = row_sets[0].stop - row_sets[0].start
            for i in range(count):
                parts = {}
                for er in (0, 1):
                    for ec in (0, 1):
                        key = (row_sets[er].start + i, col_sets[ec].start, col_sets[ec].stop)
                        if key not in parts:
                            parts[key] = take(*key)
                        parts[er, ec] = parts[key]
                if cs is None:
                    pick = [parts[0, 0], parts[1, 0]]
                else:
                    pick = [jnp.where(place.even_col, parts[e, 0], parts[e, 1]) for e in (0, 1)]
                value = pick[0] if rs is None else jnp.where(place.even_row, pick[0], pick[1])
                out[at + i] = value.astype(out.dtype)
            at += count


def strip_shapes(pairs, rows, cols, channels, radii):
    shapes = []
    for rs, cs in pairs:
        height = sum(rows if rs is None else radius for radius in radii)
        shapes.append((height, cols if cs is None else SIDE, channels))
    return shapes


def received(place, strips, row_sections):
    table = dict(zip(combos(place.row_count), strips))
    full_start, band_start = row_sections

    def along(rs, cs, i):
        return table[rs, cs][(full_start if rs is None else band_start) + i].astype(f32)

    def column(rs, side, i):
        if side is None:
            return along(rs, None, i)
        near, far = (along(rs, 0, i), along(rs, 1, i))
        if side == "left":
            return jnp.where(place.even_col, far, near)
        return jnp.where(place.even_col, near, far)

    def read(vertical, side, i):
        if vertical is None:
            value = column(None, side, i)
        elif place.row_count == 2:
            value = column(0, side, i)
        else:
            near, far = (column(0, side, i), column(1, side, i))
            if vertical == "above":
                value = jnp.where(place.even_row, far, near)
            else:
                value = jnp.where(place.even_row, near, far)
        if vertical is not None:
            value = jnp.where(place.has[vertical], value, 0.0)
        if side is not None:
            value = jnp.where(place.has[side], value, 0.0)
        return value

    return read


def assemble(place, target, own, read, radius, rows, cols, channels):
    width = cols + 2 * SIDE
    target[...] = jnp.zeros(target.shape, f32)
    for vertical, start, count in (("above", 0, radius), (None, radius, rows), ("below", radius + rows, radius)):
        for i in range(count):
            base = (start + i) * width
            middle = own(i) if vertical is None else read(vertical, None, i)
            target[base + SIDE : base + SIDE + cols, 0:channels] = middle
            target[base : base + SIDE, 0:channels] = read(vertical, "left", i)
            target[base + SIDE + cols : base + width, 0:channels] = read(vertical, "right", i)


def spread_taps(kernel_ref, layer, target):
    size, channels = (kernel_ref.shape[0], kernel_ref.shape[3])
    for a in range(size):
        for b in range(size):
            t = a * size + b
            row = pad_lanes(kernel_ref[a, b, layer : layer + 1, :])
            target[t * 16 : t * 16 + 16, :] = jnp.broadcast_to(row, (16, LANES)).astype(bf16)


def tree_sum(terms):
    while len(terms) > 1:
        pairs = [terms[i] + terms[i + 1] for i in range(0, len(terms) - 1, 2)]
        terms = pairs + ([terms[-1]] if len(terms) % 2 else [])
    return terms[0]


def conv_group(src, base, stride, rows_out, taps, size, flipped=False):
    total = [None] * rows_out
    for first in range(0, size, 2):
        columns = range(first, min(first + 2, size))
        weights = []
        for b in columns:
            order = [a * size + b for a in range(size)]
            if flipped:
                order = [size * size - 1 - t for t in order]
            weights.append([taps[t * 16 : t * 16 + 16, :] for t in order])
        windows = [[] for _ in columns]
        for i in range(rows_out + size - 1):
            for window, b in zip(windows, columns):
                window.append(src[pl.ds(base + i * stride + b, 16), :].astype(bf16))
            r = i - size + 1
            if r >= 0:
                sums = [
                    tree_sum([window[r + a] * weight[a] for a in range(size)])
                    for window, weight in zip(windows, weights)
                ]
                term = tree_sum(sums).astype(f32)
                total[r] = term if total[r] is None else total[r] + term
    return total


def group_start(g, cols):
    return pl.multiple_of(jnp.minimum(g * 16, cols - 16), 8)


def kernel_sums(src, src_base, src_stride, grad, grad_base, grad_stride, rows, cols, size, sums):
    sums[...] = jnp.zeros(sums.shape, f32)

    def group(g, carry):
        at = pl.multiple_of(g * 16, 16)
        grads = [grad[pl.ds(grad_base + i * grad_stride + at, 16), :].astype(bf16) for i in range(rows)]
        for b in range(size):
            lines = [
                src[pl.ds(src_base + i * src_stride + at + b, 16), :].astype(bf16) for i in range(rows + size - 1)
            ]
            for a in range(size):
                term = tree_sum([lines[r + a] * grads[r] for r in range(rows)]).astype(f32)
                t = (a * size + b) * 8
                sums[t : t + 8, :] += term[0:8] + term[8:16]
        return carry

    lax.fori_loop(0, cols // 16, group, 0)


def diagonal(first, second):
    top = jnp.concatenate([first, jnp.zeros((first.shape[0], second.shape[1]), first.dtype)], axis=1)
    bottom = jnp.concatenate([jnp.zeros((second.shape[0], first.shape[1]), first.dtype), second], axis=1)
    return jnp.concatenate([top, bottom], axis=0)


def together(steps):
    steps = list(steps)
    while steps:
        steps = [step for step in steps if next(step, steps) is not steps]


def by_blocks(function, *arrays, size=16):
    count = arrays[0].shape[0]
    results = [function(*(x[i : i + size] for x in arrays)) for i in range(0, count, size)]
    return tuple(jnp.concatenate(parts, axis=0) for parts in zip(*results))


def in_channels(shape, channels):
    return lax.broadcasted_iota(jnp.int32, shape, 1) < channels


def high_low(x):
    high = x.astype(bf16)
    return (jnp.concatenate([high, (x - high.astype(f32)).astype(bf16)], axis=1),)


def side_by_side(x, y):
    return jnp.concatenate([x, y], axis=1)


def layer_norm(parts, gain, channels, ones):
    def centre(x, total):
        centred = jnp.where(in_channels(x.shape, channels), x - total * (1.0 / channels), 0.0)
        return (centred, (centred * centred).astype(bf16))

    def finish(centred, total):
        inverse = lax.rsqrt(total * (1.0 / channels) + epsilon)
        unit = centred * inverse
        return (unit, inverse, (unit * gain).astype(bf16))

    totals = [dot(by_blocks(high_low, x)[0], jnp.ones((2 * LANES, LANES), bf16)) for x in parts]
    yield
    centred, squares = zip(*(by_blocks(centre, x, total) for x, total in zip(parts, totals)))
    variances = dot(side_by_side(*squares), ones)
    yield
    return [by_blocks(finish, c, variances[:, k * LANES : (k + 1) * LANES]) for k, c in enumerate(centred)]


def norm_backward(normed_grad, unit, inverse, gain, channels, ones):
    def products(normed_grad, unit):
        m = normed_grad * gain
        return (side_by_side(m.astype(bf16), (m * unit).astype(bf16)),)

    def finish(normed_grad, unit, inverse, sums):
        along = sums[:, :LANES] + unit * sums[:, LANES:]
        grad = inverse * (normed_grad * gain - along * (1.0 / channels))
        return (round16(jnp.where(in_channels(grad.shape, channels), grad, 0.0)),)

    sums = dot(by_blocks(products, normed_grad, unit)[0], ones)
    yield
    return by_blocks(finish, normed_grad, unit, inverse, sums)[0]


def gelu_parts(v):
    p = 0.3275911 * inv_sqrt_two
    c1, c2, c3, c4, c5 = (
        0.5 * c / p ** (k + 1)
        for k, c in enumerate((0.254829592, -0.284496736, 1.421413741, -1.453152027, 1.061405429))
    )
    t = pl.reciprocal(jnp.abs(v) + 1.0 / p, approx=True)
    bell = jnp.exp2(v * v * (-0.5 * log2_e))
    tail = ((((c5 * t + c4) * t + c3) * t + c2) * t + c1) * t * bell
    cdf = jnp.where(v >= 0.0, 1.0 - tail, tail)
    return (v * cdf, cdf + v * (bell * inv_sqrt_two_pi))


def dot(x, w):
    return jnp.dot(x, w, preferred_element_type=f32)


def dot_leading(x, y):
    return lax.dot_general(x, y, (((0,), (0,)), ((), ())), preferred_element_type=f32)


def pad_lanes(x):
    rows, channels = x.shape
    return jnp.concatenate([x, jnp.zeros((rows, LANES - channels), x.dtype)], axis=1)


def pieces(total, size):
    return [(start, min(size, total - start)) for start in range(0, total, size)]


def round16(x):
    return x.astype(bf16).astype(f32)


def fetch(sources, targets, sems):
    copies = [pltpu.make_async_copy(a, b, sems.at[i]) for i, (a, b) in enumerate(zip(sources, targets))]
    for copy in copies:
        copy.start()
    for copy in copies:
        copy.wait()


def image_take(ref):
    return lambda i, lo, hi: ref[i].astype(f32)[lo:hi]


def flat_take(ref, cols, channels):
    return lambda i, lo, hi: ref[i * cols + lo : i * cols + hi, 0:channels]


def bands_kernel(dims, image_in, image, *refs):
    outs, sems = (refs[:-1], refs[-1])
    place = Place(dims.row_count, dims.col_count)
    fetch((image_in,), (image,), sems)
    takes = [(image_take(image), 2 * dims.h, dims.rows, dims.cols)]
    write_strips(place, outs, takes, band_combos(dims.row_count))


def others_kernel(dims, image, *refs):
    outs = refs[len(band_combos(dims.row_count)) :]
    place = Place(dims.row_count, dims.col_count)
    takes = [(image_take(image), 2 * dims.h, dims.rows, dims.cols)]
    write_strips(place, outs, takes, other_combos(dims.row_count))


def grad_others_kernel(dims, grad1, cot, *refs):
    outs = refs[len(band_combos(dims.row_count)) :]
    place = Place(dims.row_count, dims.col_count)
    takes = [
        (flat_take(grad1, dims.cols, dims.channels), 2 * dims.h, dims.rows, dims.cols),
        (image_take(cot), dims.h, dims.rows, dims.cols),
    ]
    write_strips(place, outs, takes, other_combos(dims.row_count))


def weights_kernel(dims, up_in, down_t_in, kernels_in, gains_in, *refs):
    forward0, back0, forward1, back1, grad_in0, grad_out0, taps0, taps1, gains, own, up_w, down_w, kernels, sems = refs
    fetch((up_in, down_t_in, kernels_in, gains_in), (up_w, down_w, kernels, gains), sems)
    spread_taps(kernels, 0, taps0)
    spread_taps(kernels, 1, taps1)
    channels, units = up_w.shape[1:]
    blank = jnp.zeros((LANES - channels, units), f32)
    wide, tall = ([], [])
    for layer in range(2):
        for ref in (up_w, down_w):
            full = jnp.concatenate([ref[layer].astype(f32), blank], axis=0)
            wide.append(full.astype(bf16))
            tall.append(full.T.astype(bf16))
    (up0, down_t0, up1, down_t1), (up_t0, down0, up_t1, down1) = (wide, tall)
    forward0[...] = diagonal(up0, up0)
    back0[...] = diagonal(down0, down0)
    forward1[...] = diagonal(up1, down_t1)
    back1[...] = diagonal(down1, up_t1)
    grad_in0[...] = diagonal(down_t0, down_t0)
    grad_out0[...] = diagonal(up_t0, up_t0)
    own_pixels(dims, own)


def own_pixels(dims, own):
    skip = dims.skipped_rows(Place(dims.row_count, dims.col_count))
    ext_rows, ext_cols, h = (dims.ext_rows, dims.ext_cols, dims.h)
    col = lax.broadcasted_iota(jnp.int32, (ext_cols, LANES), 0) - (ext_cols - dims.cols) // 2
    inside = jnp.where(jnp.logical_and(col >= 0, col < dims.cols), 1.0, 0.0)
    for r in range(ext_rows):
        mine = jnp.logical_and(r + skip >= h, r + skip < h + dims.rows)
        own[r * ext_cols : (r + 1) * ext_cols, :] = jnp.where(mine, inside, 0.0)
    used = ext_rows * ext_cols
    if dims.ext_pad > used:
        own[used:, :] = jnp.zeros((dims.ext_pad - used, LANES), f32)


def first_kernel(dims, *refs):
    count = len(combos(dims.row_count))
    image, cot, taps0, taps1, gains, forward0, back0, forward1, back1 = refs[:9]
    strips = refs[9 : 9 + count]
    refs = refs[9 + count :]
    (output, x0, x1, unit0, inv0, hidden0, slope0, grad1, normed1, pre_grad1, hidden1, gain_sum) = refs[:12]
    outs, conv = (refs[12:-1], refs[-1])
    place = Place(dims.row_count, dims.col_count)
    rows, cols, channels, h, size = (dims.rows, dims.cols, dims.channels, dims.h, dims.size)
    ext_rows, ext_cols, wide = (dims.ext_rows, dims.ext_cols, dims.wide)
    skip = dims.skipped_rows(place)
    read = received(place, strips, (0, 0))
    assemble(place, x0, lambda i: image[i].astype(f32), read, 2 * h, rows, cols, channels)

    x1[...] = jnp.zeros(x1.shape, f32)
    if dims.ext_pad > ext_rows * ext_cols:
        conv[ext_rows * ext_cols :, :] = jnp.zeros((dims.ext_pad - ext_rows * ext_cols, LANES), f32)
    frame = pl.multiple_of(skip * ext_cols, 8)

    def conv0(g, carry):
        at = group_start(g, ext_cols)
        base = pl.multiple_of(skip * wide, 8) + at
        total = conv_group(x0, base + 1, wide, ext_rows, taps0, size)
        for r in range(ext_rows):
            conv[pl.ds(r * ext_cols + at, 16), :] = total[r]
            x1[pl.ds(frame + r * ext_cols + at, 16), :] = x0[pl.ds(base + (r + h) * wide + 4, 16), :]
        return carry

    lax.fori_loop(0, -(-ext_cols // 16), conv0, 0)
    gain = pad_lanes(gains[0:1, :])
    ones = diagonal(jnp.ones((LANES, LANES), bf16), jnp.ones((LANES, LANES), bf16))
    half = dims.ext_pad // 2

    def mix0(start, n):
        spans = [(start, n), (half + start, n)]
        parts = yield from layer_norm([conv[at : at + n, :] for at, n in spans], gain, channels, ones)
        pres = dot(side_by_side(parts[0][2], parts[1][2]), forward0[...])
        yield
        count = pres.shape[1] // 2
        hiddens = []
        for k, ((at, n), (unit, inverse, _)) in enumerate(zip(spans, parts)):
            unit0[at : at + n, :] = unit.astype(bf16)
            inv0[at : at + n, :] = inverse

            def activate(pre):
                value, slope = gelu_parts(pre)
                return (value.astype(bf16), slope.astype(bf16))

            hidden, slope = by_blocks(activate, pres[:, k * count : (k + 1) * count])
            hidden0[at : at + n, :] = hidden
            slope0[at : at + n, :] = slope
            hiddens.append(hidden)
        branches = dot(side_by_side(*hiddens), back0[...])
        yield
        for k, (at, n) in enumerate(spans):
            px = pl.ds(frame + at, n)
            x1[px, :] = round16(x1[px, :] + branches[:, k * LANES : (k + 1) * LANES])
    together([mix0(start, n) for start, n in pieces(half, dims.piece)])
    clear_outside(place, x1, dims)

    def conv1(g, carry):
        at = group_start(g, cols)
        total = conv_group(x1, at + 1, ext_cols, rows, taps1, size)
        for r in range(rows):
            conv[pl.ds(r * cols + at, 16), :] = total[r]
        return carry

    lax.fori_loop(0, -(-cols // 16), conv1, 0)
    gain1 = pad_lanes(gains[1:2, :])
    gain_sum[...] = jnp.zeros(gain_sum.shape, f32)
    lines = dims.line_step
    step = lines * cols

    def mix1(k):
        px = slice(k * step, (k + 1) * step)
        middle = k * step + step // 2
        parts = yield from layer_norm(
            [conv[k * step : middle, :], conv[middle : (k + 1) * step, :]], gain1, channels, ones
        )
        unit, inverse, normed = (jnp.concatenate(pair, axis=0) for pair in zip(*parts))
        normed1[px, :] = normed
        upstream = pad_lanes(cot[k * lines : (k + 1) * lines].reshape(step, channels))
        both = dot(side_by_side(normed, upstream), forward1[...])
        yield

        def activate(pre, hidden_grad):
            value, slope = gelu_parts(pre)
            return (value.astype(bf16), (hidden_grad * slope).astype(bf16))

        count = both.shape[1] // 2
        hidden, pre_grad = by_blocks(activate, both[:, :count], both[:, count:])
        hidden1[px, :] = hidden
        pre_grad1[px, :] = pre_grad
        both = dot(side_by_side(hidden, pre_grad), back1[...])
        yield
        branch, normed_grad = (both[:, :LANES], both[:, LANES:])
        for i in range(lines):
            start = (k * lines + i + h) * ext_cols + 4
            line = x1[start : start + cols, :] + branch[i * cols : (i + 1) * cols]
            output[k * lines + i] = line[:, :channels].astype(bf16)
        product = normed_grad * unit
        gain_sum[...] += jnp.sum(product.reshape(step // 8, 8, LANES), axis=0)
        grad1[px, :] = yield from norm_backward(normed_grad, unit, inverse, gain1, channels, ones)

    together([mix1(k) for k in range(rows // lines)])

    takes = [(flat_take(grad1, cols, channels), 2 * h, rows, cols), (image_take(cot), h, rows, cols)]
    write_strips(place, outs, takes, band_combos(dims.row_count))


def clear_outside(place, flat, dims):
    h, frame_rows, ext_cols = (dims.h, dims.rows + 2 * dims.h, dims.ext_cols)
    margin = (ext_cols - dims.cols) // 2

    @pl.when(jnp.logical_not(place.has["above"]))
    def _():
        flat[0 : h * ext_cols, :] = jnp.zeros((h * ext_cols, LANES), f32)

    @pl.when(jnp.logical_not(place.has["below"]))
    def _():
        last = (frame_rows - h) * ext_cols
        flat[last:, :] = jnp.zeros((flat.shape[0] - last, LANES), f32)

    @pl.when(jnp.logical_not(place.has["left"]))
    def _():
        for r in range(frame_rows):
            flat[r * ext_cols : r * ext_cols + margin, :] = jnp.zeros((margin, LANES), f32)

    @pl.when(jnp.logical_not(place.has["right"]))
    def _():
        for r in range(frame_rows):
            flat[(r + 1) * ext_cols - margin : (r + 1) * ext_cols, :] = jnp.zeros((margin, LANES), f32)


def sums_kernel(
    dims, x1, grad1, normed1, pre_grad1, hidden1, cot, gain_part, final, taps_sum, joined, output, sums
):
    output[...] = final[...]
    kernel_sums(x1, 1, dims.ext_cols, grad1, 0, dims.cols, dims.rows, dims.cols, dims.size, sums)
    store_sums(dims, sums, gain_part[...], taps_sum)
    upstream = pad_lanes(cot[...].reshape(dims.rows * dims.cols, dims.channels))
    up = dot_leading(normed1[...], pre_grad1[...]).T * dims.factor
    down = dot_leading(upstream, hidden1[...]).T * dims.factor
    join_sums(dims, up, down, joined)


def join_sums(dims, up, down, target):
    units, half = (up.shape[0], dims.half)
    lane = lax.broadcasted_iota(jnp.int32, (units, LANES), 1)
    for r in range(dims.row_count):
        first = pltpu.roll(up, LANES - r * half, 1) if r else up
        shift = (half - r * half) % LANES
        second = pltpu.roll(down, shift, 1) if shift else down
        both = jnp.where(lane < half, first, jnp.where(lane < 2 * half, second, 0.0))
        target[r * units : (r + 1) * units, :] = both
    target[dims.row_count * units :, :] = jnp.zeros((8, LANES), f32)


def store_sums(dims, sums, gain_part, target):
    taps = dims.size * dims.size
    target[...] = jnp.zeros(target.shape, f32)
    for t in range(taps):
        target[t : t + 1, :] = jnp.sum(sums[t * 8 : t * 8 + 8, :], axis=0, keepdims=True)
    target[taps : taps + 1, :] = jnp.sum(gain_part, axis=0, keepdims=True)


def third_kernel(dims, *refs):
    count = len(combos(dims.row_count))
    (grad1, cot, taps1, gains, grad_in0, grad_out0, x0, unit0, inv0, hidden0, slope0) = refs[:11]
    (own, taps_sum1, joined1) = refs[11:14]
    strips = refs[14 : 14 + count]
    (grad0, upstream, keep, small_keep, send) = refs[14 + count : 19 + count]
    (wide_grad, cot_frame, sums, normed0, flow0, pre_grad0, gain_sum, small, tall, slabs) = refs[19 + count :]
    place = Place(dims.row_count, dims.col_count)
    rows, cols, channels, h, size = (dims.rows, dims.cols, dims.channels, dims.h, dims.size)
    ext_rows, ext_cols, wide = (dims.ext_rows, dims.ext_cols, dims.wide)
    skip = dims.skipped_rows(place)
    read = received(place, strips, (0, 0))
    assemble(
        place, wide_grad, lambda i: grad1[i * cols : (i + 1) * cols, 0:channels], read, 2 * h, rows, cols, channels
    )
    read_cot = received(place, strips, (rows, 2 * h))
    margin = (ext_cols - cols) // 2
    cot_frame[...] = jnp.zeros(cot_frame.shape, f32)
    for vertical, start, n in (("above", 0, h), (None, h, rows), ("below", h + rows, h)):
        for i in range(n):
            base = (start + i) * ext_cols
            line = cot[i].astype(f32) if vertical is None else read_cot(vertical, None, i)
            cot_frame[base + margin : base + margin + cols, 0:channels] = line
            cot_frame[base : base + margin, 0:channels] = read_cot(vertical, "left", i)[SIDE - margin :]
            cot_frame[base + margin + cols : base + ext_cols, 0:channels] = read_cot(vertical, "right", i)[:margin]

    used = ext_rows * ext_cols
    if dims.ext_pad > used:
        upstream[used:, :] = jnp.zeros((dims.ext_pad - used, LANES), f32)
    grad0[...] = jnp.zeros(grad0.shape, f32)
    frame = pl.multiple_of(skip * ext_cols, 8)

    def conv1(g, carry):
        at = group_start(g, ext_cols)
        total = conv_group(wide_grad, pl.multiple_of(skip * wide, 8) + at + 1, wide, ext_rows, taps1, size, True)
        for r in range(ext_rows):
            px = pl.ds(r * ext_cols + at, 16)
            upstream[px, :] = cot_frame[pl.ds(frame + r * ext_cols + at, 16), :] + total[r]
        return carry

    lax.fori_loop(0, -(-ext_cols // 16), conv1, 0)
    gain = pad_lanes(gains[0:1, :])
    gain_sum[...] = jnp.zeros(gain_sum.shape, f32)
    ones = diagonal(jnp.ones((LANES, LANES), bf16), jnp.ones((LANES, LANES), bf16))
    half_px = dims.ext_pad // 2

    def mix0(start, n):
        spans = [(start, n), (half_px + start, n)]
        flows = [upstream[at : at + n, :].astype(bf16) for at, n in spans]
        hidden_grads = dot(side_by_side(*flows), grad_in0[...])
        yield
        count = hidden_grads.shape[1] // 2

        def slope_times(grad, slope):
            return ((grad * slope.astype(f32)).astype(bf16),)

        pre_grads = [
            by_blocks(slope_times, hidden_grads[:, k * count : (k + 1) * count], slope0[at : at + n, :])[0]
            for k, (at, n) in enumerate(spans)
        ]
        both = dot(side_by_side(*pre_grads), grad_out0[...])
        yield
        normed_grads = (both[:, :LANES], both[:, LANES:])
        for (at, n), flow, pre_grad, normed_grad in zip(spans, flows, pre_grads, normed_grads):
            mine = own[at : at + n, :]
            unit = unit0[at : at + n, :].astype(f32)
            normed0[at : at + n, :] = (unit * gain * mine).astype(bf16)
            flow0[at : at + n, :] = flow * mine.astype(bf16)
            pre_grad0[at : at + n, :] = pre_grad
            product = normed_grad * unit * mine
            gain_sum[...] += jnp.sum(product.reshape(n // 8, 8, LANES), axis=0)
            grad = yield from norm_backward(normed_grad, unit, inv0[at : at + n, :], gain, channels, ones)
            grad0[pl.ds(frame + at, n), :] = grad

    together([mix0(start, n) for start, n in pieces(half_px, dims.piece)])
    clear_outside(place, grad0, dims)
    kernel_sums(
        x0, h * wide + SIDE - h, wide, grad0, h * ext_cols + margin, ext_cols, rows, cols, size, sums
    )
    store_sums(dims, sums, gain_sum[...], small)

    taps_rows = size * size + 1
    merged = jnp.concatenate([small[0:taps_rows, :], taps_sum1[0:taps_rows, :]], axis=0) * dims.factor
    merged = fold_rows(merged, dims.small_rows, channels).astype(bf16)
    small_keep[...] = merged.astype(f32)

    layer_rows, part = (dims.layer_rows, dims.part)
    units = hidden0.shape[1]
    up0 = dot_leading(normed0[...], pre_grad0[...]).T * dims.factor
    down0 = dot_leading(flow0[...], hidden0[...]).T * dims.factor
    join_sums(dims, up0, down0, tall)
    slab_rows = 2 * layer_rows
    for r in range(dims.row_count):
        for c in range(dims.col_count):
            index = 0
            for axis, bit in dims.stages:
                index = 2 * index + ((r if axis == "row" else c) >> bit & 1)
            for layer, source in ((0, tall), (1, joined1)):
                to, at = (index * slab_rows + layer * layer_rows, r * units + c * part)
                slabs[to : to + layer_rows, :] = source[at : at + layer_rows, :]

    split(dims, 0, slabs, merged, keep, (send,))


def fold_rows(x, rows, used):
    n = x.shape[0]
    if rows >= n:
        return pad_rows(x, rows)
    assert used <= 96
    stride = ceil8(n - rows)
    rest = pad_rows(x[rows:], stride)
    pieces_of = pad_rows(jnp.concatenate([pltpu.roll(rest, 96 - 32 * k, 1) for k in range(3)], axis=0), rows)
    lane = lax.broadcasted_iota(jnp.int32, (rows, LANES), 1)
    return jnp.where(lane < 96, x[:rows], pieces_of)


def pad_rows(x, rows):
    if rows == x.shape[0]:
        return x
    return jnp.concatenate([x, jnp.zeros((rows - x.shape[0], LANES), x.dtype)], axis=0)


def unfold_rows(x, n):
    rows = x.shape[0]
    if rows >= n:
        return x[:n]
    stride = ceil8(n - rows)
    lane = lax.broadcasted_iota(jnp.int32, (stride, LANES), 1)
    rest = jnp.zeros((stride, LANES), x.dtype)
    for k in range(3):
        moved = pltpu.roll(x[k * stride : (k + 1) * stride], 32 + 32 * k, 1)
        rest = jnp.where(jnp.logical_and(lane >= 32 * k, lane < 32 * k + 32), moved, rest)
    return jnp.concatenate([x, rest[: n - rows]], axis=0)


def split(dims, stage, slabs, merged, keep, sends):
    group = dims.groups[stage]
    count = slabs.shape[0] >> len(group)
    mine = 0
    for axis, bit in group:
        mine = mine * 2 + lax.rem(lax.div(lax.axis_index(axis), 1 << bit), 2)
    keep[...] = slabs[pl.ds(pl.multiple_of(mine * count, 16), count), :]
    for mask, send in enumerate(sends, 1):
        other = 0
        for j in range(len(group)):
            weight = 1 << j
            digit = lax.rem(lax.div(mine, weight), 2)
            other = other + weight * (1 - digit if mask & weight else digit)
        send[0:count, :] = slabs[pl.ds(pl.multiple_of(other * count, 16), count), :].astype(bf16)
        send[count:, :] = merged


def gather_up(keep, small, gots):
    count = keep.shape[0]
    slabs = [keep[...]] + [got[0:count, :].astype(f32) for got in gots]
    sums = [small[...]] + [got[count:, :].astype(f32) for got in gots]
    if len(gots) == 1:
        return (slabs[0] + slabs[1], sums[0] + sums[1])
    return tuple((x[0] + x[1]) + (x[2] + x[3]) for x in (slabs, sums))


def stage_kernel(dims, stage, keep, small, *refs):
    before, after = (len_sends(dims.groups[stage - 1]), len_sends(dims.groups[stage]))
    gots = refs[:before]
    keep_out, small_out = refs[-3 - after : -1 - after]
    sends, total = (refs[-1 - after : -1], refs[-1])
    slabs, merged = gather_up(keep, small, gots)
    total[...] = slabs
    merged = merged.astype(bf16)
    small_out[...] = merged.astype(f32)
    split(dims, stage, total, merged, keep_out, sends)


def len_sends(group):
    return (1 << len(group)) - 1


def last_kernel(dims, keep, small, *refs):
    gots, (kernel_out, gain_out, up_out, down_out) = (refs[:-4], refs[-4:])
    total, merged = gather_up(keep, small, gots)
    merged = unfold_rows(merged, 2 * (dims.size * dims.size + 1))
    size, channels, half, part = (dims.size, dims.channels, dims.half, dims.part)
    for layer in range(2):
        block = total[layer * dims.layer_rows : layer * dims.layer_rows + part]
        up_out[layer] = block[:, :half]
        down_out[layer] = block[:, half : 2 * half]
        for t in range(size * size + 1):
            at = layer * (size * size + 1) + t
            row = merged[at : at + 1, 0:channels]
            if t < size * size:
                kernel_out[t // size, t % size, layer : layer + 1, :] = row
            else:
                gain_out[layer : layer + 1, :] = row


def image_kernel(dims, grad0, upstream, taps0, after, out, ready, work):
    rows, cols, size = (dims.rows, dims.cols, dims.size)
    skip = dims.skipped_rows(Place(dims.row_count, dims.col_count))
    margin = (dims.ext_cols - cols) // 2

    def conv0(g, carry):
        at = group_start(g, cols)
        total = conv_group(grad0, at + 1, dims.ext_cols, rows, taps0, size, True)
        for r in range(rows):
            line = upstream[pl.ds((r + dims.h - skip) * dims.ext_cols + margin + at, 16), :]
            work[pl.ds(r * cols + at, 16), :] = round16(line) + total[r]
        return carry

    lax.fori_loop(0, -(-cols // 16), conv0, 0)
    for r in range(rows):
        out[r] = work[r * cols : (r + 1) * cols, 0 : dims.channels].astype(bf16)
    ready[...] = jnp.zeros(ready.shape, f32)


class Dims:
    def skipped_rows(self, place):
        if self.row_count > 2:
            return 0
        return jnp.where(place.has["above"], 0, self.h)


def dims_of(image, kernels, up_weights):
    d = Dims()
    d.row_count, d.col_count = (lax.axis_size("row"), lax.axis_size("col"))
    d.rows, d.cols, d.channels = image.shape
    d.size = kernels.shape[1]
    d.h = d.size // 2
    d.ext_rows, d.ext_cols = (d.rows + (d.h if d.row_count == 2 else 2 * d.h), d.cols + 8)
    d.wide = d.cols + 2 * SIDE
    d.ext_pad = -(-d.ext_rows * d.ext_cols // 32) * 32
    d.piece = 176
    d.line_step = 4
    d.half = d.channels // d.row_count
    d.part = up_weights.shape[2] // d.col_count
    d.layer_rows = ceil8(d.part)
    d.count = d.row_count * d.col_count
    d.small_rows = 80 if d.size == 7 and d.channels <= 96 else -(-2 * (d.size * d.size + 1) // 16) * 16
    d.factor = 1.0 / math.sqrt(d.rows * d.cols * d.count)
    row_bits, col_bits = (d.row_count.bit_length() - 1, d.col_count.bit_length() - 1)
    bits = [("row", b) for b in range(row_bits)] + [("col", b) for b in range(1, col_bits)]
    d.groups = [[("col", 0)]] + [bits[i : i + 2][::-1] for i in range(0, len(bits), 2)]
    d.stages = [bit for group in d.groups for bit in group]
    return d


def swap_by(d, group, mask):
    flip = {"row": 0, "col": 0}
    for j, (axis, bit) in enumerate(group):
        if mask >> (len(group) - 1 - j) & 1:
            flip[axis] |= 1 << bit
    pairs = []
    for r in range(d.row_count):
        for c in range(d.col_count):
            pairs.append((r * d.col_count + c, (r ^ flip["row"]) * d.col_count + (c ^ flip["col"])))
    return pairs


def run(kernel, outs, scratch, *args, in_hbm=0, sems=0, busy_us=1):
    shapes = [jax.ShapeDtypeStruct(shape, kind) for shape, kind in outs]
    space = pl.BlockSpec(memory_space=pltpu.VMEM)
    far = pl.BlockSpec(memory_space=pltpu.HBM)
    held = [pltpu.VMEM(shape, kind) for shape, kind in scratch]
    if sems:
        held.append(pltpu.SemaphoreType.DMA((sems,)))
    return pl.pallas_call(
        kernel,
        out_shape=shapes,
        in_specs=[far] * in_hbm + [space] * (len(args) - in_hbm),
        out_specs=[space] * len(shapes),
        scratch_shapes=held,
        compiler_params=pltpu.CompilerParams(vmem_limit_bytes=32 * 1024 * 1024),
        cost_estimate=pl.CostEstimate(flops=int(busy_us * 1e9), bytes_accessed=1 << 18, transcendentals=0),
    )(*args)


def per_device(image, kernels, gains, up_weights, down_weights, cotangent):
    d = dims_of(image, kernels, up_weights)
    bind = functools.partial
    rows, cols, channels = image.shape
    units = up_weights.shape[2]
    tile, ext, wide = (rows * cols, d.ext_pad, (rows + 4 * d.h) * d.wide)
    frame = (rows + 2 * d.h) * d.ext_cols + 16
    taps = ((d.size * d.size * 16, LANES), bf16)
    tap_sums = ((d.size * d.size * 8, LANES), f32)
    sums_rows = ceil8(d.size * d.size + 1)

    bands, others = (band_combos(d.row_count), other_combos(d.row_count))

    def strips_of(pairs, radii):
        return [(shape, bf16) for shape in strip_shapes(pairs, rows, cols, channels, radii)]

    image, *band_strips = run(
        bind(bands_kernel, d), [(image.shape, bf16)] + strips_of(bands, (2 * d.h,)), [], image, in_hbm=1, sems=1
    )
    other_strips = run(bind(others_kernel, d), strips_of(others, (2 * d.h,)), [], image, *band_strips)
    strips = exchange(band_strips, other_strips, d.row_count, d.col_count)
    mixing = [((2 * LANES, 2 * units), bf16), ((2 * units, 2 * LANES), bf16)]
    forward0, back0, forward1, back1, grad_in0, grad_out0, taps0, taps1, gains, own = run(
        bind(weights_kernel, d),
        mixing * 3 + [taps, taps, (gains.shape, f32), ((ext, LANES), f32)],
        [((2, channels, units), bf16), ((2, channels, units), bf16), ((d.size, d.size, 2, channels), f32)],
        up_weights,
        jnp.swapaxes(down_weights, 1, 2),
        jnp.transpose(kernels, (1, 2, 0, 3)),
        gains,
        in_hbm=4,
        sems=4,
        busy_us=2,
    )

    first = run(
        bind(first_kernel, d),
        [
            (image.shape, bf16),
            ((wide, LANES), f32),
            ((frame, LANES), f32),
            ((ext, LANES), bf16),
            ((ext, LANES), f32),
            ((ext, units), bf16),
            ((ext, units), bf16),
            ((tile, LANES), f32),
            ((tile, LANES), bf16),
            ((tile, units), bf16),
            ((tile, units), bf16),
            ((8, LANES), f32),
        ]
        + strips_of(bands, (2 * d.h, d.h)),
        [((ext, LANES), f32)],
        image,
        cotangent,
        taps0,
        taps1,
        gains,
        forward0,
        back0,
        forward1,
        back1,
        *strips,
        busy_us=15,
    )
    (final, x0, x1, unit0, inv0, hidden0, slope0, grad1, normed1, pre_grad1, hidden1, gain_part) = first[:12]
    band_strips = first[12:]
    other_strips = run(
        bind(grad_others_kernel, d), strips_of(others, (2 * d.h, d.h)), [], grad1, cotangent, *band_strips
    )
    strips = exchange(band_strips, other_strips, d.row_count, d.col_count)

    joined = ((d.row_count * units + 8, LANES), f32)
    taps_sum1, joined1, output = run(
        bind(sums_kernel, d),
        [((sums_rows, LANES), f32), joined, (image.shape, bf16)],
        [tap_sums],
        x1,
        grad1,
        normed1,
        pre_grad1,
        hidden1,
        cotangent,
        gain_part,
        final,
        busy_us=3,
    )

    held = d.count // 2 * 2 * d.layer_rows
    small = ((d.small_rows, LANES), f32)
    grad0, upstream, keep, sums, send = run(
        bind(third_kernel, d),
        [((frame, LANES), f32), ((ext, LANES), f32), ((held, LANES), f32), small, ((held + d.small_rows, LANES), bf16)],
        [
            ((wide, LANES), f32),
            ((frame, LANES), f32),
            tap_sums,
            ((ext, LANES), bf16),
            ((ext, LANES), bf16),
            ((ext, units), bf16),
            ((8, LANES), f32),
            ((sums_rows, LANES), f32),
            joined,
            ((2 * held, LANES), f32),
        ],
        grad1,
        cotangent,
        taps1,
        gains,
        grad_in0,
        grad_out0,
        x0,
        unit0,
        inv0,
        hidden0,
        slope0,
        own,
        taps_sum1,
        joined1,
        *strips,
        busy_us=12,
    )
    axes = ("row", "col")
    sends = [send]
    for stage, group in enumerate(d.groups):
        gots = [lax.ppermute(x, axes, swap_by(d, group, mask)) for mask, x in enumerate(sends, 1)]
        ready = []
        if stage == 1:
            gradient, *ready = run(
                bind(image_kernel, d),
                [(image.shape, bf16), ((8, LANES), f32)],
                [((tile, LANES), f32)],
                grad0,
                upstream,
                taps0,
                sums,
                busy_us=3,
            )
        if stage + 1 < len(d.groups):
            after = d.groups[stage + 1]
            whole, held = (held, held >> len(after))
            keep, sums, *sends = run(
                bind(stage_kernel, d, stage + 1),
                [((held, LANES), f32), small] + [((held + d.small_rows, LANES), bf16)] * len_sends(after),
                [((whole, LANES), f32)],
                keep,
                sums,
                *gots,
                *ready,
            )
    kernel_out, gain_out, up_out, down_out = run(
        bind(last_kernel, d),
        [
            ((d.size, d.size, 2, channels), f32),
            (gains.shape, f32),
            ((2, d.part, d.half), f32),
            ((2, d.part, d.half), f32),
        ],
        [],
        keep,
        sums,
        *gots,
    )
    kernel_out = jnp.transpose(kernel_out, (2, 0, 1, 3))
    return (output, gradient, kernel_out, gain_out, jnp.swapaxes(up_out, 1, 2), down_out)


def solution(mesh):
    placed = (P("row", "col", None), P(), P(), P(), P(), P("row", "col", None))
    return jax.shard_map(
        per_device,
        mesh=mesh,
        in_specs=placed,
        out_specs=(
            P("row", "col", None),
            P("row", "col", None),
            P(),
            P(),
            P(None, "row", "col"),
            P(None, "col", "row"),
        ),
        check_vma=False,
    )
```

```python
import functools
import math

import jax
import jax.numpy as jnp
from jax import lax
from jax.experimental import pallas as pl
from jax.experimental.pallas import tpu as pltpu
from jax.sharding import PartitionSpec as P

epsilon = 1e-06
inv_sqrt_two = 0.7071067811865476
inv_sqrt_two_pi = 0.3989422804014327
log2_e = 1.4426950408889634
LANES = 128
SIDE = 8
f32, bf16 = (jnp.float32, jnp.bfloat16)


def ceil8(n):
    return -(-n // 8) * 8


def combos(row_count):
    listed = [(None, 0), (None, 1), (0, None), (0, 0), (0, 1)]
    if row_count > 2:
        listed += [(1, None), (1, 0), (1, 1)]
    return listed


def partner(index, start, count):
    if start is None:
        return index
    other = index + 1 if (index - start) % 2 == 0 else index - 1
    return other if 0 <= other < count else None


def swap_pairs(row_count, col_count, row_start, col_start):
    pairs = []
    for r in range(row_count):
        for c in range(col_count):
            pr, pc = (partner(r, row_start, row_count), partner(c, col_start, col_count))
            if pr is None:
                pr, pc = (r, c ^ 1)
            elif pc is None:
                pr, pc = (r ^ 1 if row_start is None else pr, c)
            pairs.append((r * col_count + c, pr * col_count + pc))
    return pairs


def exchange(bands, others, row_count, col_count):
    got = {}
    for strips, pairs in ((bands, band_combos(row_count)), (others, other_combos(row_count))):
        for strip, (rs, cs) in zip(strips, pairs):
            got[rs, cs] = lax.ppermute(strip, ("row", "col"), swap_pairs(row_count, col_count, rs, cs))
    return [got[pair] for pair in combos(row_count)]


class Place:
    def __init__(self, row_count, col_count):
        row, col = (lax.axis_index("row"), lax.axis_index("col"))
        self.even_row, self.even_col = (lax.rem(row, 2) == 0, lax.rem(col, 2) == 0)
        self.has = {
            "above": row > 0,
            "below": row < row_count - 1,
            "left": col > 0,
            "right": col < col_count - 1,
        }
        self.row_count = row_count


def band_combos(row_count):
    return [pair for pair in combos(row_count) if pair[1] is None]


def other_combos(row_count):
    return [pair for pair in combos(row_count) if pair[1] is not None]


def write_strips(place, outs, takes, pairs):
    for out, (rs, cs) in zip(outs, pairs):
        at = 0
        for take, radius, rows, cols in takes:
            row_sets = [slice(0, rows)] * 2
            col_sets = [slice(0, cols)] * 2
            if rs is not None:
                row_sets = [slice(rows - radius, rows), slice(0, radius)]
                if rs == 1:
                    row_sets = row_sets[::-1]
            if cs is not None:
                col_sets = [slice(cols - SIDE, cols), slice(0, SIDE)]
                if cs == 1:
                    col_sets = col_sets[::-1]
            count = row_sets[0].stop - row_sets[0].start
            for i in range(count):
                parts = {}
                for er in (0, 1):
                    for ec in (0, 1):
                        key = (row_sets[er].start + i, col_sets[ec].start, col_sets[ec].stop)
                        if key not in parts:
                            parts[key] = take(*key)
                        parts[er, ec] = parts[key]
                if cs is None:
                    pick = [parts[0, 0], parts[1, 0]]
                else:
                    pick = [jnp.where(place.even_col, parts[e, 0], parts[e, 1]) for e in (0, 1)]
                value = pick[0] if rs is None else jnp.where(place.even_row, pick[0], pick[1])
                out[at + i] = value.astype(out.dtype)
            at += count


def strip_shapes(pairs, rows, cols, channels, radii):
    shapes = []
    for rs, cs in pairs:
        height = sum(rows if rs is None else radius for radius in radii)
        shapes.append((height, cols if cs is None else SIDE, channels))
    return shapes


def received(place, strips, row_sections):
    table = dict(zip(combos(place.row_count), strips))
    full_start, band_start = row_sections

    def along(rs, cs, i):
        return table[rs, cs][(full_start if rs is None else band_start) + i].astype(f32)

    def column(rs, side, i):
        if side is None:
            return along(rs, None, i)
        near, far = (along(rs, 0, i), along(rs, 1, i))
        if side == "left":
            return jnp.where(place.even_col, far, near)
        return jnp.where(place.even_col, near, far)

    def read(vertical, side, i):
        if vertical is None:
            value = column(None, side, i)
        elif place.row_count == 2:
            value = column(0, side, i)
        else:
            near, far = (column(0, side, i), column(1, side, i))
            if vertical == "above":
                value = jnp.where(place.even_row, far, near)
            else:
                value = jnp.where(place.even_row, near, far)
        if vertical is not None:
            value = jnp.where(place.has[vertical], value, 0.0)
        if side is not None:
            value = jnp.where(place.has[side], value, 0.0)
        return value

    return read


def assemble(place, target, own, read, radius, rows, cols, channels):
    width = cols + 2 * SIDE
    for vertical, start, count in (("above", 0, radius), (None, radius, rows), ("below", radius + rows, radius)):
        for i in range(count):
            base = (start + i) * width
            middle = own(i) if vertical is None else read(vertical, None, i)
            target[base + SIDE : base + SIDE + cols, :] = pad_lanes(middle)
            target[base : base + SIDE, :] = pad_lanes(read(vertical, "left", i))
            target[base + SIDE + cols : base + width, :] = pad_lanes(read(vertical, "right", i))


def spread_taps(kernel_ref, layer, target):
    size, channels = (kernel_ref.shape[0], kernel_ref.shape[3])
    for a in range(size):
        for b in range(size):
            t = a * size + b
            row = pad_lanes(kernel_ref[a, b, layer : layer + 1, :])
            target[t * 16 : t * 16 + 16, :] = jnp.broadcast_to(row, (16, LANES)).astype(bf16)


def tree_sum(terms):
    while len(terms) > 1:
        pairs = [terms[i] + terms[i + 1] for i in range(0, len(terms) - 1, 2)]
        terms = pairs + ([terms[-1]] if len(terms) % 2 else [])
    return terms[0]


def conv_group(src, base, stride, rows_out, taps, size, flipped=False):
    total = [None] * rows_out
    for first in range(0, size, 2):
        columns = range(first, min(first + 2, size))
        weights = []
        for b in columns:
            order = [a * size + b for a in range(size)]
            if flipped:
                order = [size * size - 1 - t for t in order]
            weights.append([taps[t * 16 : t * 16 + 16, :] for t in order])
        windows = [[] for _ in columns]
        for i in range(rows_out + size - 1):
            for window, b in zip(windows, columns):
                window.append(src[pl.ds(base + i * stride + b, 16), :].astype(bf16))
            r = i - size + 1
            if r >= 0:
                sums = [
                    tree_sum([window[r + a] * weight[a] for a in range(size)])
                    for window, weight in zip(windows, weights)
                ]
                term = tree_sum(sums).astype(f32)
                total[r] = term if total[r] is None else total[r] + term
    return total


def group_start(g, cols):
    return pl.multiple_of(jnp.minimum(g * 16, cols - 16), 8)


def kernel_sums(src, src_base, src_stride, grad, grad_base, grad_stride, rows, cols, size, sums):
    sums[...] = jnp.zeros(sums.shape, f32)

    def group(g, carry):
        at = pl.multiple_of(g * 16, 16)
        grads = [grad[pl.ds(grad_base + i * grad_stride + at, 16), :].astype(bf16) for i in range(rows)]
        for b in range(size):
            lines = [
                src[pl.ds(src_base + i * src_stride + at + b, 16), :].astype(bf16) for i in range(rows + size - 1)
            ]
            for a in range(size):
                term = tree_sum([lines[r + a] * grads[r] for r in range(rows)]).astype(f32)
                t = (a * size + b) * 8
                sums[t : t + 8, :] += term[0:8] + term[8:16]
        return carry

    lax.fori_loop(0, cols // 16, group, 0)


def diagonal(first, second):
    top = jnp.concatenate([first, jnp.zeros((first.shape[0], second.shape[1]), first.dtype)], axis=1)
    bottom = jnp.concatenate([jnp.zeros((second.shape[0], first.shape[1]), first.dtype), second], axis=1)
    return jnp.concatenate([top, bottom], axis=0)


def together(steps):
    steps = list(steps)
    while steps:
        steps = [step for step in steps if next(step, steps) is not steps]


def by_blocks(function, *arrays, size=16):
    count = arrays[0].shape[0]
    results = [function(*(x[i : i + size] for x in arrays)) for i in range(0, count, size)]
    return tuple(jnp.concatenate(parts, axis=0) for parts in zip(*results))


def in_channels(shape, channels):
    return lax.broadcasted_iota(jnp.int32, shape, 1) < channels


def high_low(x):
    high = x.astype(bf16)
    return (jnp.concatenate([high, (x - high.astype(f32)).astype(bf16)], axis=1),)


def side_by_side(x, y):
    return jnp.concatenate([x, y], axis=1)


def layer_norm(parts, gain, channels, ones):
    def centre(x, total):
        centred = jnp.where(in_channels(x.shape, channels), x - total * (1.0 / channels), 0.0)
        return (centred, (centred * centred).astype(bf16))

    def finish(centred, total):
        inverse = lax.rsqrt(total * (1.0 / channels) + epsilon)
        unit = centred * inverse
        return (unit, inverse, (unit * gain).astype(bf16))

    totals = [dot(by_blocks(high_low, x)[0], jnp.ones((2 * LANES, LANES), bf16)) for x in parts]
    yield
    centred, squares = zip(*(by_blocks(centre, x, total) for x, total in zip(parts, totals)))
    variances = dot(side_by_side(*squares), ones)
    yield
    return [by_blocks(finish, c, variances[:, k * LANES : (k + 1) * LANES]) for k, c in enumerate(centred)]


def norm_backward(normed_grad, unit, inverse, gain, channels, ones):
    def products(normed_grad, unit):
        m = normed_grad * gain
        return (side_by_side(m.astype(bf16), (m * unit).astype(bf16)),)

    def finish(normed_grad, unit, inverse, sums):
        along = sums[:, :LANES] + unit * sums[:, LANES:]
        grad = inverse * (normed_grad * gain - along * (1.0 / channels))
        return (round16(jnp.where(in_channels(grad.shape, channels), grad, 0.0)),)

    sums = dot(by_blocks(products, normed_grad, unit)[0], ones)
    yield
    return by_blocks(finish, normed_grad, unit, inverse, sums)[0]


def gelu_parts(v):
    p = 0.3275911 * inv_sqrt_two
    c1, c2, c3, c4, c5 = (
        0.5 * c / p ** (k + 1)
        for k, c in enumerate((0.254829592, -0.284496736, 1.421413741, -1.453152027, 1.061405429))
    )
    t = pl.reciprocal(jnp.abs(v) + 1.0 / p, approx=True)
    bell = jnp.exp2(v * v * (-0.5 * log2_e))
    tail = ((((c5 * t + c4) * t + c3) * t + c2) * t + c1) * t * bell
    cdf = jnp.where(v >= 0.0, 1.0 - tail, tail)
    return (v * cdf, cdf + v * (bell * inv_sqrt_two_pi))


def dot(x, w):
    return jnp.dot(x, w, preferred_element_type=f32)


def dot_leading(x, y):
    return lax.dot_general(x, y, (((0,), (0,)), ((), ())), preferred_element_type=f32)


def pad_lanes(x):
    rows, channels = x.shape
    return jnp.concatenate([x, jnp.zeros((rows, LANES - channels), x.dtype)], axis=1)


def pieces(total, size):
    return [(start, min(size, total - start)) for start in range(0, total, size)]


def round16(x):
    return x.astype(bf16).astype(f32)


def fetch(sources, targets, sems):
    copies = [pltpu.make_async_copy(a, b, sems.at[i]) for i, (a, b) in enumerate(zip(sources, targets))]
    for copy in copies:
        copy.start()
    for copy in copies:
        copy.wait()


def image_take(ref):
    return lambda i, lo, hi: ref[i].astype(f32)[lo:hi]


def flat_take(ref, cols, channels):
    return lambda i, lo, hi: ref[i * cols + lo : i * cols + hi, 0:channels]


def bands_kernel(dims, image_in, image, *refs):
    outs, sems = (refs[:-1], refs[-1])
    place = Place(dims.row_count, dims.col_count)
    fetch((image_in,), (image,), sems)
    takes = [(image_take(image), 2 * dims.h, dims.rows, dims.cols)]
    write_strips(place, outs, takes, band_combos(dims.row_count))


def others_kernel(dims, image, *refs):
    outs = refs[len(band_combos(dims.row_count)) :]
    place = Place(dims.row_count, dims.col_count)
    takes = [(image_take(image), 2 * dims.h, dims.rows, dims.cols)]
    write_strips(place, outs, takes, other_combos(dims.row_count))


def grad_others_kernel(dims, grad1, cot, *refs):
    outs = refs[len(band_combos(dims.row_count)) :]
    place = Place(dims.row_count, dims.col_count)
    takes = [
        (flat_take(grad1, dims.cols, dims.channels), 2 * dims.h, dims.rows, dims.cols),
        (image_take(cot), dims.h, dims.rows, dims.cols),
    ]
    write_strips(place, outs, takes, other_combos(dims.row_count))


def weights_kernel(dims, up_in, down_t_in, kernels_in, gains_in, *refs):
    forward0, back0, forward1, back1, grad_in0, grad_out0, taps0, taps1, gains, own, up_w, down_w, kernels, sems = refs
    fetch((up_in, down_t_in, kernels_in, gains_in), (up_w, down_w, kernels, gains), sems)
    spread_taps(kernels, 0, taps0)
    spread_taps(kernels, 1, taps1)
    channels, units = up_w.shape[1:]
    blank = jnp.zeros((LANES - channels, units), f32)
    wide, tall = ([], [])
    for layer in range(2):
        for ref in (up_w, down_w):
            full = jnp.concatenate([ref[layer].astype(f32), blank], axis=0)
            wide.append(full.astype(bf16))
            tall.append(full.T.astype(bf16))
    (up0, down_t0, up1, down_t1), (up_t0, down0, up_t1, down1) = (wide, tall)
    forward0[...] = diagonal(up0, up0)
    back0[...] = diagonal(down0, down0)
    forward1[...] = diagonal(up1, down_t1)
    back1[...] = diagonal(down1, up_t1)
    grad_in0[...] = diagonal(down_t0, down_t0)
    grad_out0[...] = diagonal(up_t0, up_t0)
    own_pixels(dims, own)


def own_pixels(dims, own):
    skip = dims.skipped_rows(Place(dims.row_count, dims.col_count))
    ext_rows, ext_cols, h = (dims.ext_rows, dims.ext_cols, dims.h)
    col = lax.broadcasted_iota(jnp.int32, (ext_cols, LANES), 0) - (ext_cols - dims.cols) // 2
    inside = jnp.where(jnp.logical_and(col >= 0, col < dims.cols), 1.0, 0.0)
    for r in range(ext_rows):
        mine = jnp.logical_and(r + skip >= h, r + skip < h + dims.rows)
        own[r * ext_cols : (r + 1) * ext_cols, :] = jnp.where(mine, inside, 0.0)
    used = ext_rows * ext_cols
    if dims.ext_pad > used:
        own[used:, :] = jnp.zeros((dims.ext_pad - used, LANES), f32)


def first_kernel(dims, *refs):
    count = len(combos(dims.row_count))
    image, cot, taps0, taps1, gains, forward0, back0, forward1, back1 = refs[:9]
    strips = refs[9 : 9 + count]
    refs = refs[9 + count :]
    (output, x0, x1, unit0, inv0, hidden0, slope0, grad1, normed1, pre_grad1, hidden1, gain_sum) = refs[:12]
    outs, conv = (refs[12:-1], refs[-1])
    place = Place(dims.row_count, dims.col_count)
    rows, cols, channels, h, size = (dims.rows, dims.cols, dims.channels, dims.h, dims.size)
    ext_rows, ext_cols, wide = (dims.ext_rows, dims.ext_cols, dims.wide)
    skip = dims.skipped_rows(place)
    read = received(place, strips, (0, 0))
    assemble(place, x0, lambda i: image[i].astype(f32), read, 2 * h, rows, cols, channels)

    x1[...] = jnp.zeros(x1.shape, f32)
    if dims.ext_pad > ext_rows * ext_cols:
        conv[ext_rows * ext_cols :, :] = jnp.zeros((dims.ext_pad - ext_rows * ext_cols, LANES), f32)
    frame = pl.multiple_of(skip * ext_cols, 8)

    def conv0(g, carry):
        at = group_start(g, ext_cols)
        base = pl.multiple_of(skip * wide, 8) + at
        total = conv_group(x0, base + 1, wide, ext_rows, taps0, size)
        for r in range(ext_rows):
            conv[pl.ds(r * ext_cols + at, 16), :] = total[r]
            x1[pl.ds(frame + r * ext_cols + at, 16), :] = x0[pl.ds(base + (r + h) * wide + 4, 16), :]
        return carry

    lax.fori_loop(0, -(-ext_cols // 16), conv0, 0)
    gain = pad_lanes(gains[0:1, :])
    ones = diagonal(jnp.ones((LANES, LANES), bf16), jnp.ones((LANES, LANES), bf16))
    half = dims.ext_pad // 2

    def mix0(start, n):
        spans = [(start, n), (half + start, n)]
        parts = yield from layer_norm([conv[at : at + n, :] for at, n in spans], gain, channels, ones)
        pres = dot(side_by_side(parts[0][2], parts[1][2]), forward0[...])
        yield
        count = pres.shape[1] // 2
        hiddens = []
        for k, ((at, n), (unit, inverse, _)) in enumerate(zip(spans, parts)):
            unit0[at : at + n, :] = unit.astype(bf16)
            inv0[at : at + n, :] = inverse

            def activate(pre):
                value, slope = gelu_parts(pre)
                return (value.astype(bf16), slope.astype(bf16))

            hidden, slope = by_blocks(activate, pres[:, k * count : (k + 1) * count])
            hidden0[at : at + n, :] = hidden
            slope0[at : at + n, :] = slope
            hiddens.append(hidden)
        branches = dot(side_by_side(*hiddens), back0[...])
        yield
        for k, (at, n) in enumerate(spans):
            px = pl.ds(frame + at, n)
            x1[px, :] = round16(x1[px, :] + branches[:, k * LANES : (k + 1) * LANES])
    together([mix0(start, n) for start, n in pieces(half, dims.piece)])
    clear_outside(place, x1, dims)

    def conv1(g, carry):
        at = group_start(g, cols)
        total = conv_group(x1, at + 1, ext_cols, rows, taps1, size)
        for r in range(rows):
            conv[pl.ds(r * cols + at, 16), :] = total[r]
        return carry

    lax.fori_loop(0, -(-cols // 16), conv1, 0)
    gain1 = pad_lanes(gains[1:2, :])
    gain_sum[...] = jnp.zeros(gain_sum.shape, f32)
    lines = dims.line_step
    step = lines * cols

    def mix1(k):
        px = slice(k * step, (k + 1) * step)
        middle = k * step + step // 2
        parts = yield from layer_norm(
            [conv[k * step : middle, :], conv[middle : (k + 1) * step, :]], gain1, channels, ones
        )
        unit, inverse, normed = (jnp.concatenate(pair, axis=0) for pair in zip(*parts))
        normed1[px, :] = normed
        upstream = pad_lanes(cot[k * lines : (k + 1) * lines].reshape(step, channels))
        both = dot(side_by_side(normed, upstream), forward1[...])
        yield

        def activate(pre, hidden_grad):
            value, slope = gelu_parts(pre)
            return (value.astype(bf16), (hidden_grad * slope).astype(bf16))

        count = both.shape[1] // 2
        hidden, pre_grad = by_blocks(activate, both[:, :count], both[:, count:])
        hidden1[px, :] = hidden
        pre_grad1[px, :] = pre_grad
        both = dot(side_by_side(hidden, pre_grad), back1[...])
        yield
        branch, normed_grad = (both[:, :LANES], both[:, LANES:])
        for i in range(lines):
            start = (k * lines + i + h) * ext_cols + 4
            line = x1[start : start + cols, :] + branch[i * cols : (i + 1) * cols]
            output[k * lines + i] = line[:, :channels].astype(bf16)
        product = normed_grad * unit
        gain_sum[...] += jnp.sum(product.reshape(step // 8, 8, LANES), axis=0)
        grad1[px, :] = yield from norm_backward(normed_grad, unit, inverse, gain1, channels, ones)

    together([mix1(k) for k in range(rows // lines)])

    takes = [(flat_take(grad1, cols, channels), 2 * h, rows, cols), (image_take(cot), h, rows, cols)]
    write_strips(place, outs, takes, band_combos(dims.row_count))


def clear_outside(place, flat, dims):
    h, frame_rows, ext_cols = (dims.h, dims.rows + 2 * dims.h, dims.ext_cols)
    margin = (ext_cols - dims.cols) // 2

    @pl.when(jnp.logical_not(place.has["above"]))
    def _():
        flat[0 : h * ext_cols, :] = jnp.zeros((h * ext_cols, LANES), f32)

    @pl.when(jnp.logical_not(place.has["below"]))
    def _():
        last = (frame_rows - h) * ext_cols
        flat[last:, :] = jnp.zeros((flat.shape[0] - last, LANES), f32)

    @pl.when(jnp.logical_not(place.has["left"]))
    def _():
        for r in range(frame_rows):
            flat[r * ext_cols : r * ext_cols + margin, :] = jnp.zeros((margin, LANES), f32)

    @pl.when(jnp.logical_not(place.has["right"]))
    def _():
        for r in range(frame_rows):
            flat[(r + 1) * ext_cols - margin : (r + 1) * ext_cols, :] = jnp.zeros((margin, LANES), f32)


def sums_kernel(
    dims, x1, grad1, normed1, pre_grad1, hidden1, cot, gain_part, final, taps_sum, joined, output, sums
):
    output[...] = final[...]
    kernel_sums(x1, 1, dims.ext_cols, grad1, 0, dims.cols, dims.rows, dims.cols, dims.size, sums)
    store_sums(dims, sums, gain_part[...], taps_sum)
    upstream = pad_lanes(cot[...].reshape(dims.rows * dims.cols, dims.channels))
    up = dot_leading(normed1[...], pre_grad1[...]).T * dims.factor
    down = dot_leading(upstream, hidden1[...]).T * dims.factor
    join_sums(dims, up, down, joined)


def join_sums(dims, up, down, target):
    units, half = (up.shape[0], dims.half)
    lane = lax.broadcasted_iota(jnp.int32, (units, LANES), 1)
    for r in range(dims.row_count):
        first = pltpu.roll(up, LANES - r * half, 1) if r else up
        shift = (half - r * half) % LANES
        second = pltpu.roll(down, shift, 1) if shift else down
        both = jnp.where(lane < half, first, jnp.where(lane < 2 * half, second, 0.0))
        target[r * units : (r + 1) * units, :] = both
    target[dims.row_count * units :, :] = jnp.zeros((8, LANES), f32)


def store_sums(dims, sums, gain_part, target):
    taps = dims.size * dims.size
    target[...] = jnp.zeros(target.shape, f32)
    for t in range(taps):
        target[t : t + 1, :] = jnp.sum(sums[t * 8 : t * 8 + 8, :], axis=0, keepdims=True)
    target[taps : taps + 1, :] = jnp.sum(gain_part, axis=0, keepdims=True)


def third_kernel(dims, *refs):
    count = len(combos(dims.row_count))
    (grad1, cot, taps1, gains, grad_in0, grad_out0, x0, unit0, inv0, hidden0, slope0) = refs[:11]
    (own, taps_sum1, joined1) = refs[11:14]
    strips = refs[14 : 14 + count]
    (grad0, upstream, keep, small_keep, send) = refs[14 + count : 19 + count]
    (wide_grad, cot_frame, sums, normed0, flow0, pre_grad0, gain_sum, small, tall, slabs) = refs[19 + count :]
    place = Place(dims.row_count, dims.col_count)
    rows, cols, channels, h, size = (dims.rows, dims.cols, dims.channels, dims.h, dims.size)
    ext_rows, ext_cols, wide = (dims.ext_rows, dims.ext_cols, dims.wide)
    skip = dims.skipped_rows(place)
    read = received(place, strips, (0, 0))
    assemble(
        place, wide_grad, lambda i: grad1[i * cols : (i + 1) * cols, 0:channels], read, 2 * h, rows, cols, channels
    )
    read_cot = received(place, strips, (rows, 2 * h))
    margin = (ext_cols - cols) // 2
    cot_frame[...] = jnp.zeros(cot_frame.shape, f32)
    for vertical, start, n in (("above", 0, h), (None, h, rows), ("below", h + rows, h)):
        for i in range(n):
            base = (start + i) * ext_cols
            line = cot[i].astype(f32) if vertical is None else read_cot(vertical, None, i)
            cot_frame[base + margin : base + margin + cols, 0:channels] = line
            cot_frame[base : base + margin, 0:channels] = read_cot(vertical, "left", i)[SIDE - margin :]
            cot_frame[base + margin + cols : base + ext_cols, 0:channels] = read_cot(vertical, "right", i)[:margin]

    used = ext_rows * ext_cols
    if dims.ext_pad > used:
        upstream[used:, :] = jnp.zeros((dims.ext_pad - used, LANES), f32)
    grad0[...] = jnp.zeros(grad0.shape, f32)
    frame = pl.multiple_of(skip * ext_cols, 8)

    def conv1(g, carry):
        at = group_start(g, ext_cols)
        total = conv_group(wide_grad, pl.multiple_of(skip * wide, 8) + at + 1, wide, ext_rows, taps1, size, True)
        for r in range(ext_rows):
            px = pl.ds(r * ext_cols + at, 16)
            upstream[px, :] = cot_frame[pl.ds(frame + r * ext_cols + at, 16), :] + total[r]
        return carry

    lax.fori_loop(0, -(-ext_cols // 16), conv1, 0)
    gain = pad_lanes(gains[0:1, :])
    gain_sum[...] = jnp.zeros(gain_sum.shape, f32)
    ones = diagonal(jnp.ones((LANES, LANES), bf16), jnp.ones((LANES, LANES), bf16))
    half_px = dims.ext_pad // 2

    def mix0(start, n):
        spans = [(start, n), (half_px + start, n)]
        flows = [upstream[at : at + n, :].astype(bf16) for at, n in spans]
        hidden_grads = dot(side_by_side(*flows), grad_in0[...])
        yield
        count = hidden_grads.shape[1] // 2

        def slope_times(grad, slope):
            return ((grad * slope.astype(f32)).astype(bf16),)

        pre_grads = [
            by_blocks(slope_times, hidden_grads[:, k * count : (k + 1) * count], slope0[at : at + n, :])[0]
            for k, (at, n) in enumerate(spans)
        ]
        both = dot(side_by_side(*pre_grads), grad_out0[...])
        yield
        normed_grads = (both[:, :LANES], both[:, LANES:])
        for (at, n), flow, pre_grad, normed_grad in zip(spans, flows, pre_grads, normed_grads):
            mine = own[at : at + n, :]
            unit = unit0[at : at + n, :].astype(f32)
            normed0[at : at + n, :] = (unit * gain * mine).astype(bf16)
            flow0[at : at + n, :] = flow * mine.astype(bf16)
            pre_grad0[at : at + n, :] = pre_grad
            product = normed_grad * unit * mine
            gain_sum[...] += jnp.sum(product.reshape(n // 8, 8, LANES), axis=0)
            grad = yield from norm_backward(normed_grad, unit, inv0[at : at + n, :], gain, channels, ones)
            grad0[pl.ds(frame + at, n), :] = grad

    together([mix0(start, n) for start, n in pieces(half_px, dims.piece)])
    clear_outside(place, grad0, dims)
    kernel_sums(
        x0, h * wide + SIDE - h, wide, grad0, h * ext_cols + margin, ext_cols, rows, cols, size, sums
    )
    store_sums(dims, sums, gain_sum[...], small)

    taps_rows = size * size + 1
    merged = jnp.concatenate([small[0:taps_rows, :], taps_sum1[0:taps_rows, :]], axis=0) * dims.factor
    merged = fold_rows(merged, dims.small_rows, channels).astype(bf16)
    small_keep[...] = merged.astype(f32)

    layer_rows, part = (dims.layer_rows, dims.part)
    units = hidden0.shape[1]
    up0 = dot_leading(normed0[...], pre_grad0[...]).T * dims.factor
    down0 = dot_leading(flow0[...], hidden0[...]).T * dims.factor
    join_sums(dims, up0, down0, tall)
    slab_rows = 2 * layer_rows
    for r in range(dims.row_count):
        for c in range(dims.col_count):
            index = 0
            for axis, bit in dims.stages:
                index = 2 * index + ((r if axis == "row" else c) >> bit & 1)
            for layer, source in ((0, tall), (1, joined1)):
                to, at = (index * slab_rows + layer * layer_rows, r * units + c * part)
                slabs[to : to + layer_rows, :] = source[at : at + layer_rows, :]

    split(dims, 0, slabs, merged, keep, (send,))


def fold_rows(x, rows, used):
    n = x.shape[0]
    if rows >= n:
        return pad_rows(x, rows)
    assert used <= 96
    stride = ceil8(n - rows)
    rest = pad_rows(x[rows:], stride)
    pieces_of = pad_rows(jnp.concatenate([pltpu.roll(rest, 96 - 32 * k, 1) for k in range(3)], axis=0), rows)
    lane = lax.broadcasted_iota(jnp.int32, (rows, LANES), 1)
    return jnp.where(lane < 96, x[:rows], pieces_of)


def pad_rows(x, rows):
    if rows == x.shape[0]:
        return x
    return jnp.concatenate([x, jnp.zeros((rows - x.shape[0], LANES), x.dtype)], axis=0)


def unfold_rows(x, n):
    rows = x.shape[0]
    if rows >= n:
        return x[:n]
    stride = ceil8(n - rows)
    lane = lax.broadcasted_iota(jnp.int32, (stride, LANES), 1)
    rest = jnp.zeros((stride, LANES), x.dtype)
    for k in range(3):
        moved = pltpu.roll(x[k * stride : (k + 1) * stride], 32 + 32 * k, 1)
        rest = jnp.where(jnp.logical_and(lane >= 32 * k, lane < 32 * k + 32), moved, rest)
    return jnp.concatenate([x, rest[: n - rows]], axis=0)


def split(dims, stage, slabs, merged, keep, sends):
    group = dims.groups[stage]
    count = slabs.shape[0] >> len(group)
    mine = 0
    for axis, bit in group:
        mine = mine * 2 + lax.rem(lax.div(lax.axis_index(axis), 1 << bit), 2)
    keep[...] = slabs[pl.ds(pl.multiple_of(mine * count, 16), count), :]
    for mask, send in enumerate(sends, 1):
        other = 0
        for j in range(len(group)):
            weight = 1 << j
            digit = lax.rem(lax.div(mine, weight), 2)
            other = other + weight * (1 - digit if mask & weight else digit)
        send[0:count, :] = slabs[pl.ds(pl.multiple_of(other * count, 16), count), :].astype(bf16)
        send[count:, :] = merged


def gather_up(keep, small, gots):
    count = keep.shape[0]
    slabs = [keep[...]] + [got[0:count, :].astype(f32) for got in gots]
    sums = [small[...]] + [got[count:, :].astype(f32) for got in gots]
    if len(gots) == 1:
        return (slabs[0] + slabs[1], sums[0] + sums[1])
    return tuple((x[0] + x[1]) + (x[2] + x[3]) for x in (slabs, sums))


def stage_kernel(dims, stage, keep, small, *refs):
    before, after = (len_sends(dims.groups[stage - 1]), len_sends(dims.groups[stage]))
    gots = refs[:before]
    keep_out, small_out = refs[-3 - after : -1 - after]
    sends, total = (refs[-1 - after : -1], refs[-1])
    slabs, merged = gather_up(keep, small, gots)
    total[...] = slabs
    merged = merged.astype(bf16)
    small_out[...] = merged.astype(f32)
    split(dims, stage, total, merged, keep_out, sends)


def len_sends(group):
    return (1 << len(group)) - 1


def last_kernel(dims, keep, small, *refs):
    gots, (kernel_out, gain_out, up_out, down_out) = (refs[:-4], refs[-4:])
    total, merged = gather_up(keep, small, gots)
    merged = unfold_rows(merged, 2 * (dims.size * dims.size + 1))
    size, channels, half, part = (dims.size, dims.channels, dims.half, dims.part)
    for layer in range(2):
        block = total[layer * dims.layer_rows : layer * dims.layer_rows + part]
        up_out[layer] = block[:, :half]
        down_out[layer] = block[:, half : 2 * half]
        for t in range(size * size + 1):
            at = layer * (size * size + 1) + t
            row = merged[at : at + 1, 0:channels]
            if t < size * size:
                kernel_out[t // size, t % size, layer : layer + 1, :] = row
            else:
                gain_out[layer : layer + 1, :] = row


def image_kernel(dims, grad0, upstream, taps0, after, out, ready, work):
    rows, cols, size = (dims.rows, dims.cols, dims.size)
    skip = dims.skipped_rows(Place(dims.row_count, dims.col_count))
    margin = (dims.ext_cols - cols) // 2

    def conv0(g, carry):
        at = group_start(g, cols)
        total = conv_group(grad0, at + 1, dims.ext_cols, rows, taps0, size, True)
        for r in range(rows):
            line = upstream[pl.ds((r + dims.h - skip) * dims.ext_cols + margin + at, 16), :]
            work[pl.ds(r * cols + at, 16), :] = round16(line) + total[r]
        return carry

    lax.fori_loop(0, -(-cols // 16), conv0, 0)
    for r in range(rows):
        out[r] = work[r * cols : (r + 1) * cols, 0 : dims.channels].astype(bf16)
    ready[...] = jnp.zeros(ready.shape, f32)


class Dims:
    def skipped_rows(self, place):
        if self.row_count > 2:
            return 0
        return jnp.where(place.has["above"], 0, self.h)


def dims_of(image, kernels, up_weights):
    d = Dims()
    d.row_count, d.col_count = (lax.axis_size("row"), lax.axis_size("col"))
    d.rows, d.cols, d.channels = image.shape
    d.size = kernels.shape[1]
    d.h = d.size // 2
    d.ext_rows, d.ext_cols = (d.rows + (d.h if d.row_count == 2 else 2 * d.h), d.cols + 8)
    d.wide = d.cols + 2 * SIDE
    d.ext_pad = -(-d.ext_rows * d.ext_cols // 32) * 32
    d.piece = 176
    d.line_step = 4
    d.half = d.channels // d.row_count
    d.part = up_weights.shape[2] // d.col_count
    d.layer_rows = ceil8(d.part)
    d.count = d.row_count * d.col_count
    d.small_rows = 80 if d.size == 7 and d.channels <= 96 else -(-2 * (d.size * d.size + 1) // 16) * 16
    d.factor = 1.0 / math.sqrt(d.rows * d.cols * d.count)
    row_bits, col_bits = (d.row_count.bit_length() - 1, d.col_count.bit_length() - 1)
    bits = [("row", b) for b in range(row_bits)] + [("col", b) for b in range(1, col_bits)]
    d.groups = [[("col", 0)]] + [bits[i : i + 2][::-1] for i in range(0, len(bits), 2)]
    d.stages = [bit for group in d.groups for bit in group]
    return d


def swap_by(d, group, mask):
    flip = {"row": 0, "col": 0}
    for j, (axis, bit) in enumerate(group):
        if mask >> (len(group) - 1 - j) & 1:
            flip[axis] |= 1 << bit
    pairs = []
    for r in range(d.row_count):
        for c in range(d.col_count):
            pairs.append((r * d.col_count + c, (r ^ flip["row"]) * d.col_count + (c ^ flip["col"])))
    return pairs


def run(kernel, outs, scratch, *args, in_hbm=0, sems=0, busy_us=1):
    shapes = [jax.ShapeDtypeStruct(shape, kind) for shape, kind in outs]
    space = pl.BlockSpec(memory_space=pltpu.VMEM)
    far = pl.BlockSpec(memory_space=pltpu.HBM)
    held = [pltpu.VMEM(shape, kind) for shape, kind in scratch]
    if sems:
        held.append(pltpu.SemaphoreType.DMA((sems,)))
    return pl.pallas_call(
        kernel,
        out_shape=shapes,
        in_specs=[far] * in_hbm + [space] * (len(args) - in_hbm),
        out_specs=[space] * len(shapes),
        scratch_shapes=held,
        compiler_params=pltpu.CompilerParams(vmem_limit_bytes=32 * 1024 * 1024),
        cost_estimate=pl.CostEstimate(flops=int(busy_us * 1e9), bytes_accessed=1 << 18, transcendentals=0),
    )(*args)


def per_device(image, kernels, gains, up_weights, down_weights, cotangent):
    d = dims_of(image, kernels, up_weights)
    bind = functools.partial
    rows, cols, channels = image.shape
    units = up_weights.shape[2]
    tile, ext, wide = (rows * cols, d.ext_pad, (rows + 4 * d.h) * d.wide)
    frame = (rows + 2 * d.h) * d.ext_cols + 16
    taps = ((d.size * d.size * 16, LANES), bf16)
    tap_sums = ((d.size * d.size * 8, LANES), f32)
    sums_rows = ceil8(d.size * d.size + 1)

    bands, others = (band_combos(d.row_count), other_combos(d.row_count))

    def strips_of(pairs, radii):
        return [(shape, bf16) for shape in strip_shapes(pairs, rows, cols, channels, radii)]

    image, *band_strips = run(
        bind(bands_kernel, d), [(image.shape, bf16)] + strips_of(bands, (2 * d.h,)), [], image, in_hbm=1, sems=1
    )
    other_strips = run(bind(others_kernel, d), strips_of(others, (2 * d.h,)), [], image, *band_strips)
    strips = exchange(band_strips, other_strips, d.row_count, d.col_count)
    mixing = [((2 * LANES, 2 * units), bf16), ((2 * units, 2 * LANES), bf16)]
    forward0, back0, forward1, back1, grad_in0, grad_out0, taps0, taps1, gains, own = run(
        bind(weights_kernel, d),
        mixing * 3 + [taps, taps, (gains.shape, f32), ((ext, LANES), f32)],
        [((2, channels, units), bf16), ((2, channels, units), bf16), ((d.size, d.size, 2, channels), f32)],
        up_weights,
        jnp.swapaxes(down_weights, 1, 2),
        jnp.transpose(kernels, (1, 2, 0, 3)),
        gains,
        in_hbm=4,
        sems=4,
        busy_us=2,
    )

    first = run(
        bind(first_kernel, d),
        [
            (image.shape, bf16),
            ((wide, LANES), f32),
            ((frame, LANES), f32),
            ((ext, LANES), bf16),
            ((ext, LANES), f32),
            ((ext, units), bf16),
            ((ext, units), bf16),
            ((tile, LANES), f32),
            ((tile, LANES), bf16),
            ((tile, units), bf16),
            ((tile, units), bf16),
            ((8, LANES), f32),
        ]
        + strips_of(bands, (2 * d.h, d.h)),
        [((ext, LANES), f32)],
        image,
        cotangent,
        taps0,
        taps1,
        gains,
        forward0,
        back0,
        forward1,
        back1,
        *strips,
        busy_us=15,
    )
    (final, x0, x1, unit0, inv0, hidden0, slope0, grad1, normed1, pre_grad1, hidden1, gain_part) = first[:12]
    band_strips = first[12:]
    other_strips = run(
        bind(grad_others_kernel, d), strips_of(others, (2 * d.h, d.h)), [], grad1, cotangent, *band_strips
    )
    strips = exchange(band_strips, other_strips, d.row_count, d.col_count)

    joined = ((d.row_count * units + 8, LANES), f32)
    taps_sum1, joined1, output = run(
        bind(sums_kernel, d),
        [((sums_rows, LANES), f32), joined, (image.shape, bf16)],
        [tap_sums],
        x1,
        grad1,
        normed1,
        pre_grad1,
        hidden1,
        cotangent,
        gain_part,
        final,
        busy_us=3,
    )

    held = d.count // 2 * 2 * d.layer_rows
    small = ((d.small_rows, LANES), f32)
    grad0, upstream, keep, sums, send = run(
        bind(third_kernel, d),
        [((frame, LANES), f32), ((ext, LANES), f32), ((held, LANES), f32), small, ((held + d.small_rows, LANES), bf16)],
        [
            ((wide, LANES), f32),
            ((frame, LANES), f32),
            tap_sums,
            ((ext, LANES), bf16),
            ((ext, LANES), bf16),
            ((ext, units), bf16),
            ((8, LANES), f32),
            ((sums_rows, LANES), f32),
            joined,
            ((2 * held, LANES), f32),
        ],
        grad1,
        cotangent,
        taps1,
        gains,
        grad_in0,
        grad_out0,
        x0,
        unit0,
        inv0,
        hidden0,
        slope0,
        own,
        taps_sum1,
        joined1,
        *strips,
        busy_us=12,
    )
    axes = ("row", "col")
    sends = [send]
    for stage, group in enumerate(d.groups):
        gots = [lax.ppermute(x, axes, swap_by(d, group, mask)) for mask, x in enumerate(sends, 1)]
        ready = []
        if stage == 1:
            gradient, *ready = run(
                bind(image_kernel, d),
                [(image.shape, bf16), ((8, LANES), f32)],
                [((tile, LANES), f32)],
                grad0,
                upstream,
                taps0,
                sums,
                busy_us=3,
            )
        if stage + 1 < len(d.groups):
            after = d.groups[stage + 1]
            whole, held = (held, held >> len(after))
            keep, sums, *sends = run(
                bind(stage_kernel, d, stage + 1),
                [((held, LANES), f32), small] + [((held + d.small_rows, LANES), bf16)] * len_sends(after),
                [((whole, LANES), f32)],
                keep,
                sums,
                *gots,
                *ready,
            )
    kernel_out, gain_out, up_out, down_out = run(
        bind(last_kernel, d),
        [
            ((d.size, d.size, 2, channels), f32),
            (gains.shape, f32),
            ((2, d.part, d.half), f32),
            ((2, d.part, d.half), f32),
        ],
        [],
        keep,
        sums,
        *gots,
    )
    kernel_out = jnp.transpose(kernel_out, (2, 0, 1, 3))
    return (output, gradient, kernel_out, gain_out, jnp.swapaxes(up_out, 1, 2), down_out)


def solution(mesh):
    placed = (P("row", "col", None), P(), P(), P(), P(), P("row", "col", None))
    return jax.shard_map(
        per_device,
        mesh=mesh,
        in_specs=placed,
        out_specs=(
            P("row", "col", None),
            P("row", "col", None),
            P(),
            P(),
            P(None, "row", "col"),
            P(None, "col", "row"),
        ),
        check_vma=False,
    )
```
